32 devices in a mesh: shard: 8 (over z, y), rep: 4 (over x, core).
Axes of the slice: x: 2, y: 2, z: 4, core: 2. Of those that a mesh axis runs over, the one named last changes fastest.
Arguments:
- tokens: bfloat16 [4, 8, 1024, 1024], P('rep', 'shard'), may hold values from -6 to 6
- cotangent: bfloat16 [4, 8, 1024, 1024], P('rep', 'shard'), may hold values from -6 to 6
- routes: int32 [4, 8, 1024, 8], P('rep', 'shard'), may hold values from 0 to 15, all different within a row; in each aligned block of 1024 rows (0 to 1023, 1024 to 2047, ..., all dimensions but the last counted through in order) at most 640 rows name the same one
- branch: int32 [4, 8], P('rep', 'shard'), may hold values from 512 to 4096, as said below
- attn_gain: bfloat16 [1024], P('shard'), may hold values from 0.5 to 1.5
- query_key_value_weight: bfloat16 [1024, 2048], P('shard'), may hold values from -0.1875 to 0.1875
- w_attn_out: bfloat16 [1024, 1024], P('shard'), may hold values from -6 to 6
- ffn_gain: bfloat16 [1024], P('shard'), may hold values from 0.5 to 1.5
- w_router: bfloat16 [1024, 16], P('shard'), may hold values from -0.375 to 0.375
- w_in: bfloat16 [1024, 16384], P('shard'), may hold values from -0.1875 to 0.1875
- w_out: bfloat16 [1024, 8192], P('shard'), may hold values from -0.25 to 0.25
- adam_first: float32 [4, 8, 3541248], P('rep', 'shard'), may hold values from -0.00030517578 to 0.00030517578
- adam_second: float32 [4, 8, 3541248], P('rep', 'shard'), may hold values from 1.7649145e-10 to 7.059658e-09
- outer_mom: float32 [8, 3541248], P('shard'), may hold values from -0.15625 to 0.15625
Outputs:
- block_out: bfloat16 [4, 8, 1024, 1024], P('rep', 'shard')
- grad_tokens: float32 [4, 8, 1024, 1024], P('rep', 'shard')
- weight_grad: float32 [8, 3541248], P('shard')
- grad_norm: float32 [], replicated
- new_adam_first: float32 [4, 8, 3541248], P('rep', 'shard')
- new_adam_second: float32 [4, 8, 3541248], P('rep', 'shard')
- new_outer_mom: float32 [8, 3541248], P('shard')
- weight_update: float32 [8, 3541248], P('shard')
The draws below stay inside these ranges and needn't reach their ends.
Inputs may be any that keep to these rules, and one draw needn't show every extreme that they name: `routes`: among the tokens of one device, no expert is named by more than 640 of them, and some expert reaches 640. `branch`: in every prompt group one continuation follows the whole prompt.
All inputs are finite; a program needn't handle non-finite values.
Results may differ from the reference program's by a relative error of at most 0.023.
Values may be sent and summed in bfloat16 or wider, within the bound.
A program may use at most 576 MiB of HBM per device.

```python
import math
import jax
import jax.numpy as jnp
import numpy as np
from jax import lax

MODEL_DIMENSION = 1024
QUERY_HEADS = 16
KEY_VALUE_HEADS = 8
HEAD_SIZE = 64
F = 512
EXPERTS = 16
TOP = 8
GROUP_SIZE = 8
CONTINUATION_LEN = 512
PROMPT_PER_SHARD = 512
STEP = 10
PROMPT_LENGTH = 4096
TOKENS_PER_SHARD = 1024
CAP = 640
REPS = 4
SHARDS = 8
FLAT_DEV = 3541248


def draw_branch(key, part):
    first_key, second_key = jax.random.split(key)
    drawn_len = jax.random.randint(first_key, (REPS, SHARDS), PROMPT_PER_SHARD, PROMPT_LENGTH + 1)
    chosen = jax.random.randint(second_key, (REPS, SHARDS // GROUP_SIZE, 1), 0, GROUP_SIZE)
    lanes_row = jnp.arange(GROUP_SIZE)[None, None, :]
    whole_one = (lanes_row == chosen).reshape(REPS, SHARDS)
    return jnp.where(whole_one, PROMPT_LENGTH, drawn_len).astype(jnp.int32)


def block_scale(stream_key, shape, pieces, low, largest):
    def one(position, blocks):
        heights = jax.random.uniform(jax.random.fold_in(jax.random.fold_in(stream_key, 6), position), (blocks,), jnp.float32, low / len(pieces), largest / len(pieces))
        return jnp.repeat(jnp.exp(heights), shape[position] // blocks).reshape((-1,) + (1,) * (len(shape) - position - 1))

    gain = one(*pieces[0])
    for cut in pieces[1:]:
        gain = gain * one(*cut)
    return gain


def shared_out(stream_key, own, number, rows, count, top, most, skew):
    ranking = jax.random.permutation(stream_key, count)
    packed, usual = load_shares(count, rows * top, most, skew, True), load_shares(count, rows * top, most, skew, False)
    places = jnp.arange(count)

    def named(lengths, turn):
        used = int((lengths > 0).sum())
        fixed = max(1, used // 4)
        moved = fixed + (places - fixed + turn * (used - fixed)) % max(1, count - fixed)
        return jnp.zeros((count,), jnp.int32).at[ranking[jnp.where(places < fixed, places, moved)]].set(jnp.asarray(lengths, jnp.int32))

    lengths = jnp.where(number % 4 == 0, named(packed, number // 4), named(usual, number - number // 4 - 1))
    mixed = jax.random.permutation(jax.random.fold_in(own, 3), count)
    giver, sink = mixed[0:count // 2 * 2:2], mixed[1:count // 2 * 2:2]
    room = jnp.minimum(lengths[giver] - 1, most - lengths[sink]) // 2
    room = jnp.where((giver == ranking[0]) | (sink == ranking[0]) | (lengths[sink] == 0), 0, jnp.maximum(room, 0))
    moved = jax.random.randint(jax.random.fold_in(own, 4), (count // 2,), 0, 1 << 20) % (room + 1)
    lengths = lengths.at[giver].add(-moved).at[sink].add(moved)
    labels = jnp.searchsorted(jnp.cumsum(lengths), jnp.arange(rows * top), side="right").astype(jnp.int32)
    grid = labels.reshape(top, rows).T
    grid = grid[jax.random.permutation(jax.random.fold_in(own, 1), rows)]
    turn = jax.random.randint(jax.random.fold_in(own, 2), (rows, 1), 0, top)
    return jnp.take_along_axis(grid, (jnp.arange(top)[None, :] + turn) % top, axis=1)


def load_shares(count, total, bound, skew, full):
    portions = [(1 << 20) // math.isqrt(standing ** skew) + 1 for standing in range(1, count + 1)]
    largest = bound if full else min(bound, max(-(-total // count), total * portions[0] // sum(portions)))
    least = 1 if total - largest >= count - 1 else 0
    holding, rest = [largest] + [least] * (count - 1), total - largest - least * (count - 1)
    while rest > 0:
        candidates = [i for i in range(1, count) if holding[i] < largest] or [i for i in range(1, count) if holding[i] < bound]
        mass, left = sum([portions[i] for i in candidates]), rest
        for i in candidates:
            addition = min(bound - holding[i], max(1, left * portions[i] // mass), rest)
            holding[i] = holding[i] + addition
            rest = rest - addition
    return np.array(holding)


def centred(own_key, extent, deviation, reach, pieces=(), kind=jnp.bfloat16):
    gain = block_scale(own_key, extent, pieces, -0.22, 0.18) if pieces else 1.0
    entries = jax.random.normal(own_key, extent, jnp.float32) * deviation * gain
    return jnp.minimum(jnp.maximum(entries, -reach), reach).astype(kind)


def setup_inputs(seed: int = 0) -> dict:
    streams_of = jax.random.split(jax.random.key(seed), 15)
    tokens = centred(streams_of[0], (REPS, SHARDS, TOKENS_PER_SHARD, MODEL_DIMENSION), 1.0, 6.0, ((0, 4), (1, 8)))
    cotangent = centred(streams_of[1], (REPS, SHARDS, TOKENS_PER_SHARD, MODEL_DIMENSION), 1.0, 6.0, ((0, 4), (1, 8)))
    routes_keys = jax.random.split(jax.random.fold_in(streams_of[2], 1), REPS * SHARDS * TOKENS_PER_SHARD // TOKENS_PER_SHARD)
    routes_turns = jax.random.permutation(jax.random.fold_in(streams_of[2], 3), REPS * SHARDS * TOKENS_PER_SHARD // TOKENS_PER_SHARD)
    routes = jax.vmap(lambda own, number: shared_out(jax.random.fold_in(streams_of[2], 2), own, number, TOKENS_PER_SHARD, EXPERTS, TOP, CAP, 1))(routes_keys, routes_turns).reshape((REPS, SHARDS, TOKENS_PER_SHARD, TOP))
    branch = draw_branch(jax.random.fold_in(streams_of[14], 71), 0)
    attn_gain = jnp.clip(1.0 + 0.1 * jax.random.normal(streams_of[4], (MODEL_DIMENSION,), jnp.float32), 0.5, 1.5).astype(jnp.bfloat16)
    query_key_value_weight = centred(streams_of[5], (MODEL_DIMENSION, (QUERY_HEADS + 2 * KEY_VALUE_HEADS) * HEAD_SIZE), MODEL_DIMENSION ** -0.5, 0.1875, ((0, 8),))
    w_attn_out = centred(streams_of[6], (MODEL_DIMENSION, QUERY_HEADS * HEAD_SIZE), (max(1, QUERY_HEADS * HEAD_SIZE * 2 // PROMPT_LENGTH)) ** -0.5, 6.0, ((0, 8),))
    ffn_gain = jnp.clip(1.0 + 0.1 * jax.random.normal(streams_of[7], (MODEL_DIMENSION,), jnp.float32), 0.5, 1.5).astype(jnp.bfloat16)
    w_router = centred(streams_of[8], (MODEL_DIMENSION, EXPERTS), (MODEL_DIMENSION // 4) ** -0.5, 0.375, ((0, 8),))
    w_in = centred(streams_of[9], (MODEL_DIMENSION, EXPERTS * 2 * F), MODEL_DIMENSION ** -0.5, 0.1875, ((0, 8),))
    w_out = centred(streams_of[10], (MODEL_DIMENSION, EXPERTS * F), F ** -0.5, 0.25, ((0, 8),))
    adam_first = centred(streams_of[11], (REPS, SHARDS, FLAT_DEV), (0.11 * (FLAT_DEV * SHARDS) ** -0.5), 0.00030517578, ((0, 4), (1, 8)), jnp.float32)
    adam_second = jnp.clip(jnp.exp(math.log(7.059658191366225e-09) - 3.6888795 * jax.random.uniform(streams_of[12], (REPS, SHARDS, FLAT_DEV), jnp.float32) ** block_scale(streams_of[12], (REPS, SHARDS, FLAT_DEV), ((0, 4), (1, 8)), -0.2, 0.2)), 1.7649144645748294e-10, 7.059658191366225e-09)
    outer_mom = centred(streams_of[13], (SHARDS, FLAT_DEV), 0.01, 0.15625, ((0, 8),), jnp.float32)
    return dict(tokens=tokens, cotangent=cotangent, routes=routes, branch=branch, attn_gain=attn_gain, query_key_value_weight=query_key_value_weight, w_attn_out=w_attn_out, ffn_gain=ffn_gain, w_router=w_router, w_in=w_in, w_out=w_out, adam_first=adam_first, adam_second=adam_second, outer_mom=outer_mom)


EPSILON = 1e-06
NEGATIVE = -1e+30
ROPE_BASE = 10000.0
BETA_ONE = 0.9
BETA_TWO = 0.95
ADAM_EPS = 1e-08
INNER_RATE = 0.01
DECAY_RATE = 0.1
OUTER_RATE = 0.7
OUTER_MOMENTUM = 0.9
CLIP_NORM = 1.0
HIGHEST = lax.Precision.HIGHEST

@jax.custom_vjp
def narrow_values(v):
    return lax.optimization_barrier(v.astype(jnp.bfloat16)).astype(jnp.float32)

@jax.custom_vjp
def low_back(v):
    return v

def low_keep(v):
    return (narrow_values(v), None)

def low_pass(kept, grad):
    return (grad,)

def back_keep(v):
    return (v, None)

def back_low(kept, grad):
    return (narrow_values(grad),)
narrow_values.defvjp(low_keep, low_pass)
low_back.defvjp(back_keep, back_low)

def rope_angles(positions, head_dim):
    half_dim = head_dim // 2
    inverse_freq = ROPE_BASE ** (-(jnp.arange(half_dim, dtype=jnp.float32) * 2.0) / head_dim)
    return positions.astype(jnp.float32)[:, None] * inverse_freq[None, :]

def apply_rotary(value_rows, rotary_angles):
    half_dim = value_rows.shape[-1] // 2
    cosine = jnp.cos(rotary_angles)[:, None, :]
    sine = jnp.sin(rotary_angles)[:, None, :]
    front = value_rows[..., :half_dim]
    back_half = value_rows[..., half_dim:]
    return jnp.concatenate([front * cosine - back_half * sine, back_half * cosine + front * sine], axis=-1)

def attention(query_vector, key_rows, value_rows, allowed):
    row_block = query_vector.shape[0]
    grouped_rows = query_vector.reshape(row_block, KEY_VALUE_HEADS, QUERY_HEADS // KEY_VALUE_HEADS, HEAD_SIZE)
    raw = jnp.einsum('qhgd,khd->hgqk', grouped_rows, key_rows, precision=HIGHEST) * HEAD_SIZE ** (-0.5)
    raw = low_back(raw)
    probs = jax.nn.softmax(jnp.where(allowed[None, None], raw, NEGATIVE), axis=-1)
    probs = narrow_values(probs)
    result = jnp.einsum('hgqk,khd->qhgd', probs, value_rows, precision=HIGHEST)
    return result.reshape(row_block, QUERY_HEADS * HEAD_SIZE)

def dispatch(route_dev):
    flat_ids = route_dev.reshape(-1).astype(jnp.int32)
    onehot = (flat_ids[:, None] == jnp.arange(EXPERTS, dtype=jnp.int32)[None, :]).astype(jnp.int32)
    running = jnp.cumsum(onehot, axis=0)
    slots = lax.optimization_barrier(jnp.sum((running - 1) * onehot, axis=1))
    row_of = (flat_ids * CAP + slots).astype(jnp.int32)
    owners = (jnp.arange(flat_ids.shape[0], dtype=jnp.int32) // TOP).astype(jnp.int32)
    token_of_row = jnp.zeros((EXPERTS * CAP,), jnp.int32).at[row_of].set(owners)
    return (row_of, token_of_row)

def group_forward(params, x_group, route_group, branch_group):
    attn_gain, query_key_value_weight, w_attn_out, ffn_gain, w_router, w_in, w_out = params
    scale_one = lax.rsqrt(lax.optimization_barrier(jnp.mean(x_group * x_group, axis=-1, keepdims=True)) + EPSILON)
    normed = narrow_values(x_group * scale_one * attn_gain)
    projected_rows = low_back(jnp.einsum('std,de->ste', normed, query_key_value_weight, precision=HIGHEST))
    prompt_pos = jnp.arange(GROUP_SIZE, dtype=jnp.int32)[:, None] * PROMPT_PER_SHARD + jnp.arange(PROMPT_PER_SHARD, dtype=jnp.int32)[None, :]
    cont_pos = branch_group[:, None] + jnp.arange(CONTINUATION_LEN, dtype=jnp.int32)[None, :]
    positions = jnp.concatenate([prompt_pos, cont_pos], axis=1).reshape(-1)
    rotary_angles = rope_angles(positions, HEAD_SIZE)
    query_total_width = QUERY_HEADS * HEAD_SIZE
    key_value_width = KEY_VALUE_HEADS * HEAD_SIZE
    flattened_projection = projected_rows.reshape(GROUP_SIZE * TOKENS_PER_SHARD, -1)
    query_matrix = narrow_values(apply_rotary(flattened_projection[:, :query_total_width].reshape(-1, QUERY_HEADS, HEAD_SIZE), rotary_angles)).reshape(GROUP_SIZE, TOKENS_PER_SHARD, QUERY_HEADS, HEAD_SIZE)
    key_rows = narrow_values(apply_rotary(flattened_projection[:, query_total_width:query_total_width + key_value_width].reshape(-1, KEY_VALUE_HEADS, HEAD_SIZE), rotary_angles)).reshape(GROUP_SIZE, TOKENS_PER_SHARD, KEY_VALUE_HEADS, HEAD_SIZE)
    value_rows = narrow_values(flattened_projection[:, query_total_width + key_value_width:]).reshape(GROUP_SIZE, TOKENS_PER_SHARD, KEY_VALUE_HEADS, HEAD_SIZE)
    prompt_key_rows = key_rows[:, :PROMPT_PER_SHARD].reshape(PROMPT_LENGTH, KEY_VALUE_HEADS, HEAD_SIZE)
    prompt_value_rows = value_rows[:, :PROMPT_PER_SHARD].reshape(PROMPT_LENGTH, KEY_VALUE_HEADS, HEAD_SIZE)
    key_index = jnp.arange(PROMPT_LENGTH, dtype=jnp.int32)

    def prompt_part(args):
        query_rows, index = args
        limit = index * PROMPT_PER_SHARD + jnp.arange(PROMPT_PER_SHARD, dtype=jnp.int32) + 1
        allowed = key_index[None, :] < limit[:, None]
        return attention(query_rows, prompt_key_rows, prompt_value_rows, allowed)
    prompt_out = lax.map(jax.checkpoint(prompt_part), (query_matrix[:, :PROMPT_PER_SHARD], jnp.arange(GROUP_SIZE, dtype=jnp.int32)))
    all_index = jnp.arange(PROMPT_LENGTH + CONTINUATION_LEN, dtype=jnp.int32)
    cont_index = jnp.arange(CONTINUATION_LEN, dtype=jnp.int32)

    def cont_part(args):
        query_rows, own_keys, own_values, cut = args
        all_keys = jnp.concatenate([prompt_key_rows, own_keys], axis=0)
        all_values = jnp.concatenate([prompt_value_rows, own_values], axis=0)
        allowed = (all_index[None, :] < cut) | (all_index[None, :] >= PROMPT_LENGTH) & (all_index[None, :] - PROMPT_LENGTH <= cont_index[:, None])
        return attention(query_rows, all_keys, all_values, allowed)
    cont_out = lax.map(jax.checkpoint(cont_part), (query_matrix[:, PROMPT_PER_SHARD:], key_rows[:, PROMPT_PER_SHARD:], value_rows[:, PROMPT_PER_SHARD:], branch_group))
    attn_out = jnp.concatenate([prompt_out, cont_out], axis=1)
    attn_low = narrow_values(low_back(attn_out))
    branch_out = low_back(jnp.einsum('stc,dc->std', attn_low, w_attn_out, precision=HIGHEST))
    x_mid = x_group + branch_out
    w_in_grid = w_in.reshape(MODEL_DIMENSION, EXPERTS, 2 * F)
    w_out_grid = w_out.reshape(MODEL_DIMENSION, EXPERTS, F)

    def expert_part(args):
        x_dev, route_dev = args
        scale_two = lax.rsqrt(lax.optimization_barrier(jnp.mean(x_dev * x_dev, axis=-1, keepdims=True)) + EPSILON)
        normed_two = narrow_values(x_dev * scale_two * ffn_gain)
        logits = low_back(jnp.dot(normed_two, w_router, precision=HIGHEST))
        route_hot = (route_dev[:, :, None] == jnp.arange(EXPERTS, dtype=jnp.int32)[None, None, :]).astype(jnp.float32)
        picked = lax.optimization_barrier(jnp.sum(route_hot * logits[:, None, :], axis=-1))
        gates = jax.nn.softmax(picked, axis=-1)
        row_of, token_of_row = dispatch(route_dev)
        expert_in = normed_two[token_of_row].reshape(EXPERTS, CAP, MODEL_DIMENSION)
        gate_up = low_back(jnp.einsum('ecd,def->ecf', expert_in, w_in_grid, precision=HIGHEST))
        hidden = narrow_values(jax.nn.silu(gate_up[..., :F]) * gate_up[..., F:])
        expert_out = low_back(jnp.einsum('ecf,def->ecd', hidden, w_out_grid, precision=HIGHEST)).reshape(EXPERTS * CAP, MODEL_DIMENSION)
        routed = expert_out[row_of].reshape(TOKENS_PER_SHARD, TOP, MODEL_DIMENSION)
        return x_dev + lax.optimization_barrier(jnp.sum(gates[:, :, None] * routed, axis=1))
    return lax.map(jax.checkpoint(expert_part), (x_mid, route_group))

def flatten(arrays):
    return jnp.concatenate([portion.reshape(SHARDS, -1) for portion in arrays], axis=1)

def reference(tokens, cotangent, routes, branch, attn_gain, query_key_value_weight, w_attn_out, ffn_gain, w_router, w_in, w_out, adam_first, adam_second, outer_mom):
    params = tuple((portion.astype(jnp.float32) for portion in (attn_gain, query_key_value_weight, w_attn_out, ffn_gain, w_router, w_in, w_out)))
    groups_all = REPS * SHARDS // GROUP_SIZE
    x_all = tokens.astype(jnp.float32).reshape(groups_all, GROUP_SIZE, TOKENS_PER_SHARD, MODEL_DIMENSION)
    route_all = routes.reshape(groups_all, GROUP_SIZE, TOKENS_PER_SHARD, TOP)
    branch_all = branch.reshape(groups_all, GROUP_SIZE)

    def forward(x_values, weights):

        def one_group(args):
            x_group, route_group, branch_group = args
            return group_forward(weights, x_group, route_group, branch_group)
        return lax.map(jax.checkpoint(one_group), (x_values, route_all, branch_all))
    result, pullback = jax.vjp(forward, x_all, params)
    grad_x, grad_params = pullback(cotangent.astype(jnp.float32).reshape(x_all.shape))
    grads = flatten(grad_params)
    grad_norm = jnp.sqrt(jnp.sum(grads * grads))
    clipped = grads * (CLIP_NORM / jnp.maximum(grad_norm, CLIP_NORM))
    new_first = BETA_ONE * adam_first + (1.0 - BETA_ONE) * clipped[None]
    new_second = BETA_TWO * adam_second + (1.0 - BETA_TWO) * (clipped * clipped)[None]
    weights_flat = flatten(params)
    step_delta = -INNER_RATE * (new_first / (1.0 - BETA_ONE ** STEP) / (jnp.sqrt(new_second / (1.0 - BETA_TWO ** STEP)) + ADAM_EPS) + DECAY_RATE * weights_flat[None])
    pseudo = -lax.optimization_barrier(jnp.mean(step_delta, axis=0))
    new_mom = OUTER_MOMENTUM * outer_mom + pseudo
    weight_update = -OUTER_RATE * (pseudo + OUTER_MOMENTUM * new_mom)
    block_out = result.reshape(tokens.shape).astype(jnp.bfloat16)
    return (block_out, grad_x.reshape(tokens.shape), grads, grad_norm, new_first, new_second, new_mom, weight_update)
```

```python
import functools

import jax
import jax.numpy as jnp
from jax import lax
from jax.experimental import pallas as pl
from jax.experimental.pallas import tpu as pltpu
from jax.sharding import PartitionSpec as P

QUERY_HEADS = 16
KEY_VALUE_HEADS = 8
HEAD_SIZE = 64
F = 512
EXPERTS = 16
TOP = 8
GROUP_SIZE = 8
CONTINUATION_LEN = 512
STEP = 10

EPSILON = 1e-06
NEGATIVE = -1e30
ROPE_BASE = 10000.0
BETA_ONE = 0.9
BETA_TWO = 0.95
ADAM_EPS = 1e-08
INNER_RATE = 0.01
DECAY_RATE = 0.1
OUTER_RATE = 0.7
OUTER_MOMENTUM = 0.9
CLIP_NORM = 1.0

LOG2E = 1.4426950408889634
LANES = 128
MIB = 1 << 20
BF16 = jnp.bfloat16
F32 = jnp.float32
PER_KEY = QUERY_HEADS // KEY_VALUE_HEADS
Q_WIDTH = QUERY_HEADS * HEAD_SIZE
KV_WIDTH = KEY_VALUE_HEADS * HEAD_SIZE


def dot(left, right, dims):
    return lax.dot_general(left, right, ((dims[:1], dims[1:]), ((), ())), preferred_element_type=F32)


def split_three(value):
    high = value.astype(BF16)
    rest = value - high.astype(F32)
    middle = rest.astype(BF16)
    low = (rest - middle.astype(F32)).astype(BF16)
    return high, middle, low


def augment_query(q_ref, start, width):
    rows = jnp.concatenate([q_ref[g, :, start : start + width] for g in range(PER_KEY)], axis=1)
    scaled = rows.astype(F32) * (HEAD_SIZE**-0.5 * LOG2E)
    high = scaled.astype(BF16)
    low = (scaled - high.astype(F32)).astype(BF16)
    return rows, high, low


def causal(width, columns):
    key_pos = lax.broadcasted_iota(jnp.int32, (width, columns), 0)
    query_pos = lax.broadcasted_iota(jnp.int32, (width, columns), 1) % width
    return key_pos <= query_pos


def attn_forward_kernel(where_ref, q_ref, kv_ref, own_ref, o_ref, lse_ref, peak_ref, sum_ref, acc_ref):
    block = own_ref.shape[-1]
    columns = PER_KEY * block
    shard_pos = where_ref[0]
    branch = where_ref[1]

    def advance(query, key, value, mask):
        scores = dot(jnp.concatenate([key, key], axis=0), query, (0, 0))
        if mask is not None:
            scores = jnp.where(mask, scores, NEGATIVE)
        old = peak_ref[...]
        new = jnp.maximum(old, jnp.max(scores, axis=0, keepdims=True))
        probs = jnp.exp2(scores - new).astype(BF16)
        shrink = jnp.exp2(old - new)
        ones = jnp.ones((16, block), BF16)
        part = dot(jnp.concatenate([value, ones], axis=0), probs, (1, 0))
        peak_ref[...] = new
        sum_ref[...] = sum_ref[...] * shrink + part[HEAD_SIZE : HEAD_SIZE + 1]
        acc_ref[...] = acc_ref[...] * shrink + part[:HEAD_SIZE]

    def begin(start):
        _, high, low = augment_query(q_ref, start, block)
        peak_ref[...] = jnp.full_like(peak_ref, NEGATIVE)
        sum_ref[...] = jnp.zeros_like(sum_ref)
        acc_ref[...] = jnp.zeros_like(acc_ref)
        return jnp.concatenate([high, low], axis=0)

    def finish(start):
        total = sum_ref[...]
        result = acc_ref[...] / total
        lse = peak_ref[...] + jnp.log2(total)
        for g in range(PER_KEY):
            o_ref[g, :, start : start + block] = result[:, g * block : (g + 1) * block]
            lse_ref[0, g : g + 1, start : start + block] = lse[:, g * block : (g + 1) * block]

    def full(query):
        def body(index, carry):
            advance(query, kv_ref[index, 0, 0], kv_ref[index, 1, 0], None)
            return carry

        return body

    query = begin(0)
    lax.fori_loop(0, shard_pos, full(query), 0)
    advance(query, kv_ref[shard_pos, 0, 0], kv_ref[shard_pos, 1, 0], causal(block, columns))
    finish(0)

    query = begin(block)
    whole = branch // block
    lax.fori_loop(0, whole, full(query), 0)

    @pl.when(branch % block != 0)
    def _():
        key_pos = lax.broadcasted_iota(jnp.int32, (block, columns), 0)
        advance(query, kv_ref[whole, 0, 0], kv_ref[whole, 1, 0], key_pos < branch % block)

    advance(query, own_ref[0, 0], own_ref[1, 0], causal(block, columns))
    finish(block)


def attn_forward(where, query, prompt_kv, own_kv):
    tokens = query.shape[-1]
    block = own_kv.shape[-1]
    columns = PER_KEY * block
    parts = prompt_kv.shape[0]
    return pl.pallas_call(
        attn_forward_kernel,
        grid=(query.shape[0] // PER_KEY,),
        in_specs=[
            pl.BlockSpec(memory_space=pltpu.SMEM),
            pl.BlockSpec((PER_KEY, HEAD_SIZE, tokens), lambda h: (h, 0, 0)),
            pl.BlockSpec((parts, 2, 1, HEAD_SIZE, block), lambda h: (0, 0, h, 0, 0)),
            pl.BlockSpec((2, 1, HEAD_SIZE, block), lambda h: (0, h, 0, 0)),
        ],
        out_specs=[
            pl.BlockSpec((PER_KEY, HEAD_SIZE, tokens), lambda h: (h, 0, 0)),
            pl.BlockSpec((1, PER_KEY, tokens), lambda h: (h, 0, 0)),
        ],
        out_shape=[
            jax.ShapeDtypeStruct(query.shape, F32),
            jax.ShapeDtypeStruct((query.shape[0] // PER_KEY, PER_KEY, tokens), F32),
        ],
        scratch_shapes=[
            pltpu.VMEM((1, columns), F32),
            pltpu.VMEM((1, columns), F32),
            pltpu.VMEM((HEAD_SIZE, columns), F32),
        ],
        compiler_params=pltpu.CompilerParams(vmem_limit_bytes=48 * MIB),
        cost_estimate=pl.CostEstimate(
            flops=4 * tokens * parts * block * query.shape[0] * HEAD_SIZE,
            bytes_accessed=16 * MIB,
            transcendentals=query.shape[0] * tokens * parts * block,
        ),
        name="attn_forward",
    )(where, query, prompt_kv, own_kv)


def attn_backward_kernel(
    where_ref, q_ref, kv_ref, own_ref, go_ref, lse_ref, delta_ref, dq_ref, dkv_ref, down_ref, dkv_acc, dq_acc
):
    block = own_ref.shape[-1]
    columns = PER_KEY * block
    shard_pos = where_ref[0]
    branch = where_ref[1]
    ones = jnp.ones((16, block), BF16)
    pad = jnp.zeros((16 - 3, columns), BF16)

    def begin(start):
        rows, high, low = augment_query(q_ref, start, block)

        def lanes(ref):
            return jnp.concatenate([ref[0, g : g + 1, start : start + block] for g in range(PER_KEY)], axis=1)

        lse = split_three(-lanes(lse_ref))
        delta = split_three(-lanes(delta_ref))
        grad = jnp.concatenate([go_ref[g, :, start : start + block] for g in range(PER_KEY)], axis=1)
        query = jnp.concatenate([high, low, *lse, pad], axis=0)
        grad_plus = jnp.concatenate([grad, *delta, pad], axis=0)
        dq_acc[...] = jnp.zeros_like(dq_acc)
        scaled = (rows.astype(F32) * HEAD_SIZE**-0.5).astype(BF16)
        return query, scaled, grad_plus, grad

    def terms(state, key, value, mask):
        query, scaled, grad_plus, grad = state
        scores = dot(jnp.concatenate([key, key, ones], axis=0), query, (0, 0))
        if mask is not None:
            scores = jnp.where(mask, scores, NEGATIVE)
        probs = jnp.exp2(scores)
        grad_probs = dot(jnp.concatenate([value, ones], axis=0), grad_plus, (0, 0))
        grad_scores = (probs * grad_probs).astype(BF16)
        dq_acc[...] += dot(key, grad_scores, (1, 0))
        return dot(scaled, grad_scores, (1, 1)), dot(grad, probs.astype(BF16), (1, 1))

    def add(index, state, mask):
        dk, dv = terms(state, kv_ref[index, 0, 0], kv_ref[index, 1, 0], mask)
        dkv_acc[index, 0] += dk
        dkv_acc[index, 1] += dv

    def finish(start):
        total = dq_acc[...] * HEAD_SIZE**-0.5
        for g in range(PER_KEY):
            dq_ref[g, :, start : start + block] = total[:, g * block : (g + 1) * block]

    def full(state):
        def body(index, carry):
            add(index, state, None)
            return carry

        return body

    dkv_acc[...] = jnp.zeros_like(dkv_acc)
    state = begin(0)
    lax.fori_loop(0, shard_pos, full(state), 0)
    add(shard_pos, state, causal(block, columns))
    finish(0)

    state = begin(block)
    whole = branch // block
    lax.fori_loop(0, whole, full(state), 0)

    @pl.when(branch % block != 0)
    def _():
        key_pos = lax.broadcasted_iota(jnp.int32, (block, columns), 0)
        add(whole, state, key_pos < branch % block)

    dk, dv = terms(state, own_ref[0, 0], own_ref[1, 0], causal(block, columns))
    down_ref[0, 0] = dk
    down_ref[1, 0] = dv
    finish(block)
    dkv_ref[:, :, 0] = dkv_acc[...].astype(BF16)


def attn_backward(where, query, prompt_kv, own_kv, grad_out, lse, delta):
    tokens = query.shape[-1]
    block = own_kv.shape[-1]
    columns = PER_KEY * block
    parts = prompt_kv.shape[0]
    by_head = pl.BlockSpec((PER_KEY, HEAD_SIZE, tokens), lambda h: (h, 0, 0))
    by_parts = pl.BlockSpec((parts, 2, 1, HEAD_SIZE, block), lambda h: (0, 0, h, 0, 0))
    by_own = pl.BlockSpec((2, 1, HEAD_SIZE, block), lambda h: (0, h, 0, 0))
    by_row = pl.BlockSpec((1, PER_KEY, tokens), lambda h: (h, 0, 0))
    return pl.pallas_call(
        attn_backward_kernel,
        grid=(query.shape[0] // PER_KEY,),
        in_specs=[pl.BlockSpec(memory_space=pltpu.SMEM), by_head, by_parts, by_own, by_head, by_row, by_row],
        out_specs=[by_head, by_parts, by_own],
        out_shape=[
            jax.ShapeDtypeStruct(query.shape, F32),
            jax.ShapeDtypeStruct(prompt_kv.shape, BF16),
            jax.ShapeDtypeStruct(own_kv.shape, F32),
        ],
        scratch_shapes=[
            pltpu.VMEM((parts, 2, HEAD_SIZE, block), F32),
            pltpu.VMEM((HEAD_SIZE, columns), F32),
        ],
        compiler_params=pltpu.CompilerParams(vmem_limit_bytes=56 * MIB),
        cost_estimate=pl.CostEstimate(
            flops=10 * tokens * parts * block * query.shape[0] * HEAD_SIZE,
            bytes_accessed=32 * MIB,
            transcendentals=query.shape[0] * tokens * parts * block,
        ),
        name="attn_backward",
    )(where, query, prompt_kv, own_kv, grad_out, lse, delta)


ORDER = ((0, 0), (0, 1), (3, 0), (2, 0), (3, 1), (2, 1), (1, 0), (1, 1))


def experts_kernel(
    x_hbm,
    top_hbm,
    gates_ref,
    in_ref,
    out_ref,
    all_x,
    dx_own,
    dx_core,
    dx_far,
    y_all,
    dgu_all,
    gh_all,
    dg_all,
    x_buf,
    top_buf,
    y_buf,
    dx_buf,
    dgu_buf,
    gh_buf,
    relay,
    y_acc,
    dx_acc,
    gates_all,
    gates_now,
    dg_now,
    dg_mine,
    in_sem,
    out_sem,
    copy_sem,
    send_sem,
    recv_sem,
    small_send,
    small_recv,
):
    tile = x_buf.shape[1]
    count = in_ref.shape[1] // (2 * F)
    step = pl.program_id(0)
    steps = len(ORDER)
    slot = lax.rem(step, 2)
    me = lax.axis_index("rep")
    home = [me, me + 1 - 2 * lax.rem(me, 2), lax.rem(me + 2, 4), 3 - me]

    def remote(source, target, send, receive, relation):
        return pltpu.make_async_remote_copy(
            src_ref=source,
            dst_ref=target,
            send_sem=send,
            recv_sem=receive,
            device_id={"rep": home[relation]},
            device_id_type=pl.DeviceIdType.MESH,
        )

    def half(ref, half_index, *lead):
        return ref.at[(*lead, pl.ds(half_index * tile, tile))]

    def to_core(h):
        return remote(half(x_hbm, h), half(all_x, h, me), send_sem.at[0, h], recv_sem.at[0, h], 1)

    def to_far(h):
        return remote(half(x_hbm, h), half(all_x, h, me), send_sem.at[1, h], recv_sem.at[1, h], 2)

    def forward(h):
        part = half(all_x, h, home[2])
        return remote(part, part, send_sem.at[2, h], recv_sem.at[2, h], 1)

    def give(kind, h, buffer):
        if kind == 3:
            return remote(buffer, relay.at[h], send_sem.at[3, h], recv_sem.at[3, h], 1)
        if kind == 2:
            return remote(buffer, half(dx_far, h), send_sem.at[4, h], recv_sem.at[4, h], 2)
        return remote(buffer, half(dx_core, h), send_sem.at[5, h], recv_sem.at[5, h], 1)

    def small_gates(k):
        return remote(gates_ref.at[home[k]], gates_all.at[me], small_send.at[0, k], small_recv.at[0, k], k)

    def small_back(k):
        return remote(dg_mine.at[home[k]], dg_all.at[me], small_send.at[1, k], small_recv.at[1, k], k)

    def load_x(i):
        kind, h = ORDER[i]
        source = half(x_hbm, h) if kind == 0 else half(all_x, h, home[kind])
        return pltpu.make_async_copy(source, x_buf.at[i % 2], in_sem.at[i % 2, 0])

    def load_top(i):
        kind, h = ORDER[i]
        return pltpu.make_async_copy(half(top_hbm, h, home[kind]), top_buf.at[i % 2], in_sem.at[i % 2, 1])

    def stores(i):
        kind, h = ORDER[i]
        out = []
        for n, (buffer, target) in enumerate(((y_buf, y_all), (dgu_buf, dgu_all), (gh_buf, gh_all))):
            out.append(
                pltpu.make_async_copy(buffer.at[i % 2], half(target, h, home[kind]), out_sem.at[i % 2, n])
            )
        return out

    def store_dx(i):
        kind, h = ORDER[i]
        if kind == 0:
            return pltpu.make_async_copy(dx_buf.at[i % 2], half(dx_own, h), out_sem.at[i % 2, 3])
        return give(kind, h, dx_buf.at[i % 2])

    def finish(i):
        for copy in stores(i):
            copy.wait()
        if ORDER[i][0] == 0:
            store_dx(i).wait()
        else:
            store_dx(i).wait_send()

    own_copy = pltpu.make_async_copy(x_hbm, all_x.at[me], copy_sem)
    for i in range(steps):
        kind, h = ORDER[i]

        @pl.when(step == i)
        def _(i=i, kind=kind, h=h):
            if i == 0:
                barrier = pltpu.get_barrier_semaphore()
                for k in (1, 2, 3):
                    pl.semaphore_signal(
                        barrier, inc=1, device_id={"rep": home[k]}, device_id_type=pl.DeviceIdType.MESH
                    )
                pl.semaphore_wait(barrier, 3)
                for n in (0, 1):
                    to_far(n).start()
                for n in (0, 1):
                    to_core(n).start()
                for k in (1, 2, 3):
                    small_gates(k).start()
                own_copy.start()
                load_top(0).start()
                load_x(0).start()
                gates_all[me] = gates_ref[me]
            if i == 2:
                for k in (1, 2, 3):
                    small_gates(k).wait_recv()
                to_far(0).wait_recv()
                forward(0).start()
                forward(0).wait_recv()
                load_x(2).start()
            if i == 3:
                to_far(1).wait_recv()
                forward(1).start()
            if i == 4:
                forward(1).wait_recv()
                load_x(4).start()
            if i == 5:
                to_core(0).wait_recv()
                to_core(1).wait_recv()
            load_x(i).wait()
            load_top(i).wait()
            if i + 1 < steps:
                load_top(i + 1).start()
                if i + 1 not in (2, 4):
                    load_x(i + 1).start()
            if i >= 2:
                finish(i - 2)
            gates_now[...] = jnp.transpose(gates_all[home[kind]][:, h * tile : (h + 1) * tile])

    x = x_buf[slot]
    top = top_buf[slot]
    columns = []
    for e in range(count):
        w_in = in_ref[:, e * 2 * F : (e + 1) * 2 * F]
        w_out = out_ref[:, e * F : (e + 1) * F]
        gate_up = dot(x, w_in, (1, 0))
        g = gate_up[:, :F]
        u = gate_up[:, F:]
        sig = jax.nn.sigmoid(g)
        act = g * sig
        hidden = (act * u).astype(BF16).astype(F32)
        raw = dot(top, w_out, (1, 0))
        columns.append(jnp.sum(hidden * raw, axis=1, keepdims=True))
        gate = gates_now[:, e : e + 1]
        gated = (hidden * gate).astype(BF16)
        gh_buf[slot, :, e * F : (e + 1) * F] = gated
        grad_hidden = raw * gate
        dg = (grad_hidden * u * sig * (1.0 + g * (1.0 - sig))).astype(BF16)
        du = (grad_hidden * act).astype(BF16)
        dgu = jnp.concatenate([dg, du], axis=1)
        dgu_buf[slot, :, e * 2 * F : (e + 1) * 2 * F] = dgu
        y = dot(gated, w_out, (1, 1))
        dx = dot(dgu, w_in, (1, 1))
        if e == 0:
            y_acc[...] = y
            dx_acc[...] = dx
        elif e < count - 1:
            y_acc[...] += y
            dx_acc[...] += dx
        else:
            y_buf[slot] = (y_acc[...] + y).astype(BF16)
            dx_acc[...] += dx
    columns.append(jnp.zeros((tile, 8 - count), F32))
    dg_now[...] = jnp.transpose(jnp.concatenate(columns, axis=1))

    for i in range(steps):
        kind, h = ORDER[i]

        @pl.when(step == i)
        def _(i=i, kind=kind, h=h):
            dg_mine[home[kind], :, h * tile : (h + 1) * tile] = dg_now[...]
            if kind == 2:
                give(3, h, dx_buf.at[0]).wait_recv()
                dx_buf[i % 2] = (dx_acc[...] + relay[h].astype(F32)).astype(BF16)
            else:
                dx_buf[i % 2] = dx_acc[...].astype(BF16)
            store_dx(i).start()
            for copy in stores(i):
                copy.start()
            if i == steps - 1:
                own_back = pltpu.make_async_copy(dg_mine.at[me], dg_all.at[me], small_send.at[1, 0])
                own_back.start()
                for k in (1, 2, 3):
                    small_back(k).start()
                finish(i - 1)
                finish(i)
                own_copy.wait()
                own_back.wait()
                for n in (0, 1):
                    to_far(n).wait_send()
                    to_core(n).wait_send()
                    forward(n).wait_send()
                    give(2, n, dx_buf.at[0]).wait_recv()
                    give(1, n, dx_buf.at[0]).wait_recv()
                for k in (1, 2, 3):
                    small_gates(k).wait_send()
                    small_back(k).wait()


def experts(x, all_top, gates, w_in, w_out):
    rows, width = x.shape
    reps = all_top.shape[0]
    count = w_in.shape[1] // (2 * F)
    tile = rows // 2
    anywhere = pl.BlockSpec(memory_space=pl.ANY)
    fixed = lambda n: pl.BlockSpec((width, n), lambda i: (0, 0), pipeline_mode=pl.Buffered(1))
    small = pl.BlockSpec((reps, 8, rows), lambda i: (0, 0, 0))
    dma = pltpu.SemaphoreType.DMA
    return pl.pallas_call(
        experts_kernel,
        grid=(len(ORDER),),
        in_specs=[anywhere, anywhere, small, fixed(count * 2 * F), fixed(count * F)],
        out_specs=[anywhere] * 8,
        out_shape=[
            jax.ShapeDtypeStruct((reps, rows, width), BF16),
            jax.ShapeDtypeStruct((rows, width), BF16),
            jax.ShapeDtypeStruct((rows, width), BF16),
            jax.ShapeDtypeStruct((rows, width), BF16),
            jax.ShapeDtypeStruct((reps, rows, width), BF16),
            jax.ShapeDtypeStruct((reps, rows, count * 2 * F), BF16),
            jax.ShapeDtypeStruct((reps, rows, count * F), BF16),
            jax.ShapeDtypeStruct((reps, 8, rows), F32),
        ],
        scratch_shapes=[
            pltpu.VMEM((2, tile, width), BF16),
            pltpu.VMEM((2, tile, width), BF16),
            pltpu.VMEM((2, tile, width), BF16),
            pltpu.VMEM((2, tile, width), BF16),
            pltpu.VMEM((2, tile, count * 2 * F), BF16),
            pltpu.VMEM((2, tile, count * F), BF16),
            pltpu.VMEM((2, tile, width), BF16),
            pltpu.VMEM((tile, width), F32),
            pltpu.VMEM((tile, width), F32),
            pltpu.VMEM((reps, 8, rows), F32),
            pltpu.VMEM((tile, 8), F32),
            pltpu.VMEM((8, tile), F32),
            pltpu.VMEM((reps, 8, rows), F32),
            dma((2, 2)),
            dma((2, 4)),
            dma,
            dma((6, 2)),
            dma((6, 2)),
            dma((2, 4)),
            dma((2, 4)),
        ],
        compiler_params=pltpu.CompilerParams(
            vmem_limit_bytes=58 * MIB, collective_id=1, has_side_effects=True
        ),
        cost_estimate=pl.CostEstimate(
            flops=12 * reps * rows * width * count * F,
            bytes_accessed=80 * MIB,
            transcendentals=reps * rows * count * F,
        ),
        name="experts",
    )(x, all_top, gates, w_in, w_out)


def flatten_kernel(starts, lead_ref, *refs):
    parts, flat_ref, square_ref = refs[: len(starts)], refs[len(starts)], refs[len(starts) + 1]
    scratch, sems = refs[len(starts) + 2 : -1], refs[-1]
    step = pl.program_id(0)
    steps = pl.num_programs(0)
    slot = lax.rem(step, 2)
    flat = flat_ref.reshape(flat_ref.shape[1] // LANES, LANES)
    lead_places = ((0, 0, 1), (1, starts[2] - 17 , 1), (2, starts[2] - 16, 16))

    def copies(index, where):
        out = []
        for n, (start, buffer) in enumerate(zip(starts, scratch)):
            size = buffer.shape[1]
            out.append(pltpu.make_async_copy(buffer.at[where], flat.at[pl.ds(start + index * size, size)], sems.at[where, n]))
        return out

    @pl.when(step == 0)
    def _():
        square_ref[...] = jnp.sum(lead_ref[...] * lead_ref[...], keepdims=True).reshape(1, 1) + jnp.zeros_like(square_ref)
        for n, (source, target, size) in enumerate(lead_places):
            copy = pltpu.make_async_copy(lead_ref.at[pl.ds(source, size)], flat.at[pl.ds(target, size)], sems.at[2, n])
            copy.start()
            copy.wait()

    @pl.when(step >= 2)
    def _():
        for copy in copies(step - 2, slot):
            copy.wait()

    total = jnp.zeros((8, LANES), F32)
    for part, buffer in zip(parts, scratch):
        rows = part.shape[-2]
        wide = buffer.shape[1] // rows
        reps = part.shape[0] if len(part.shape) == 3 else 1
        each = wide // reps
        for r in range(reps):
            for c in range(each):
                lanes = slice(c * LANES, (c + 1) * LANES)
                value = (part[r, :, lanes] if len(part.shape) == 3 else part[:, lanes]).astype(F32)
                buffer[slot, pl.ds(r * each + c, rows, stride=wide), :] = value
                square = value * value
                for k in range(0, rows, 8):
                    total += square[k : k + 8]
    square_ref[...] += jnp.sum(total, keepdims=True).reshape(1, 1)
    for copy in copies(step, slot):
        copy.start()

    @pl.when(step == steps - 1)
    def _():
        if True:
            for copy in copies(step - 1, 1 - slot):
                copy.wait()
        for copy in copies(step, slot):
            copy.wait()

def flatten(size, lead, *parts, tile=16):
    rows = parts[0].shape[-2]
    widths = [p.shape[-1] * (p.shape[0] if p.ndim == 3 else 1) // LANES for p in parts]
    starts, at = [], 1
    for n, w in enumerate(widths):
        if n == 2: at += 1 + 16
        starts.append(at); at += rows * w
    specs = [pl.BlockSpec((p.shape[0], tile, p.shape[2]), lambda i: (0, i, 0)) if p.ndim == 3 else pl.BlockSpec((tile, p.shape[1]), lambda i: (i, 0)) for p in parts]
    return pl.pallas_call(
        functools.partial(flatten_kernel, starts),
        grid=(rows // tile,),
        in_specs=[pl.BlockSpec(lead.shape, lambda i: (0, 0))] + specs,
        out_specs=[pl.BlockSpec(memory_space=pl.ANY), pl.BlockSpec((1, 1), lambda i: (0, 0))],
        out_shape=[jax.ShapeDtypeStruct((1, size), F32), jax.ShapeDtypeStruct((1, 1), F32)],
        scratch_shapes=[pltpu.VMEM((2, tile * w, LANES), F32) for w in widths] + [pltpu.SemaphoreType.DMA((3, 4))],
        compiler_params=pltpu.CompilerParams(vmem_limit_bytes=48 * MIB),
        name="flatten",
    )(lead, *parts)

def optimizer_math(grad, first, second, weight, scale):
    clipped = grad * scale
    new_first = BETA_ONE * first + (1.0 - BETA_ONE) * clipped
    new_second = BETA_TWO * second + (1.0 - BETA_TWO) * clipped * clipped
    root = jnp.sqrt(new_second * (1.0 / (1.0 - BETA_TWO**STEP))) + ADAM_EPS
    step = -INNER_RATE * (new_first * (1.0 / (1.0 - BETA_ONE**STEP)) / root + DECAY_RATE * weight)
    return new_first, new_second, step

CHUNK=1024
def stream(body, ins, outs, rows):
    whole = rows // CHUNK
    pipe = pltpu.emit_pipeline(body, grid=(whole,), in_specs=[pl.BlockSpec((CHUNK, LANES), lambda i: (i, 0))] * len(ins), out_specs=[pl.BlockSpec((CHUNK, LANES), lambda i: (i, 0))] * len(outs))
    pipe(*ins, *outs)

def adam_kernel(scale_ref, g, f, s, w, nf, ns, st, tg, tf, ts, tw, tnf, tns, tst, sems):
    rows = g.shape[-1] // LANES
    def view(r):
        return r.reshape(rows, LANES)
    scale = scale_ref[0]
    def body(gr, fr, sr, wr, nfr, nsr, str_):
        a, b, c = optimizer_math(gr[...], fr[...], sr[...], wr[...], scale)
        nfr[...] = a; nsr[...] = b; str_[...] = c.astype(BF16)
    ins = [view(r) for r in (g, f, s, w)]
    outs = [view(nf), view(ns), st]
    stream(body, ins, outs, rows)
    done = rows // CHUNK * CHUNK
    rest = rows - done
    for n, (r, t) in enumerate(zip(ins, (tg, tf, ts, tw))):
        pltpu.make_async_copy(r.at[pl.ds(done, rest)], t.at[pl.ds(0, rest)], sems.at[n]).start()
    for n, (r, t) in enumerate(zip(ins, (tg, tf, ts, tw))):
        pltpu.make_async_copy(r.at[pl.ds(done, rest)], t.at[pl.ds(0, rest)], sems.at[n]).wait()
    body(tg, tf, ts, tw, tnf, tns, tst)
    tail = st.shape[0] - done
    cs = [pltpu.make_async_copy(tnf.at[pl.ds(0, rest)], outs[0].at[pl.ds(done, rest)], sems.at[0]),
          pltpu.make_async_copy(tns.at[pl.ds(0, rest)], outs[1].at[pl.ds(done, rest)], sems.at[1]),
          pltpu.make_async_copy(tst.at[pl.ds(0, tail)], outs[2].at[pl.ds(done, tail)], sems.at[2])]
    for c in cs: c.start()
    for c in cs: c.wait()

def adam(scale, g, f, s, w):
    n = g.shape[-1]
    rows = n // LANES
    pad = -(-rows // 16) * 16
    tail = pad - rows // CHUNK * CHUNK
    anys = pl.BlockSpec(memory_space=pl.ANY)
    return pl.pallas_call(adam_kernel, in_specs=[pl.BlockSpec(memory_space=pltpu.SMEM)] + [anys] * 4, out_specs=[anys] * 3,
      out_shape=[jax.ShapeDtypeStruct(f.shape, F32), jax.ShapeDtypeStruct(s.shape, F32), jax.ShapeDtypeStruct((pad, LANES), BF16)],
      scratch_shapes=[pltpu.VMEM((tail, LANES), F32)] * 6 + [pltpu.VMEM((tail, LANES), BF16), pltpu.SemaphoreType.DMA((4,))],
      compiler_params=pltpu.CompilerParams(vmem_limit_bytes=48 * MIB), name="adam")(scale, g, f, s, w)

def outer_kernel(reps, st, mom, nm, up, ts, tm, tnm, tup, sems):
    rows = mom.shape[-1] // LANES
    def body(sr, mr, nmr, upr):
        pseudo = sr[...].astype(F32) * (-1.0 / reps)
        new = OUTER_MOMENTUM * mr[...] + pseudo
        nmr[...] = new
        upr[...] = -OUTER_RATE * (pseudo + OUTER_MOMENTUM * new)
    view = lambda r: r.reshape(rows, LANES)
    m, a, b = view(mom), view(nm), view(up)
    stream(body, [st, m], [a, b], rows)
    done = rows // CHUNK * CHUNK
    rest = rows - done
    tail = st.shape[0] - done
    cs = [pltpu.make_async_copy(st.at[pl.ds(done, tail)], ts.at[pl.ds(0, tail)], sems.at[0]),
          pltpu.make_async_copy(m.at[pl.ds(done, rest)], tm.at[pl.ds(0, rest)], sems.at[1])]
    for c in cs: c.start()
    for c in cs: c.wait()
    body(ts, tm, tnm, tup)
    cs = [pltpu.make_async_copy(tnm.at[pl.ds(0, rest)], a.at[pl.ds(done, rest)], sems.at[0]),
          pltpu.make_async_copy(tup.at[pl.ds(0, rest)], b.at[pl.ds(done, rest)], sems.at[1])]
    for c in cs: c.start()
    for c in cs: c.wait()

def outer(reps, st, mom):
    rows = mom.shape[-1] // LANES
    tail = st.shape[0] - rows // CHUNK * CHUNK
    anys = pl.BlockSpec(memory_space=pl.ANY)
    return pl.pallas_call(functools.partial(outer_kernel, reps), in_specs=[anys] * 2, out_specs=[anys] * 2,
      out_shape=[jax.ShapeDtypeStruct(mom.shape, F32)] * 2,
      scratch_shapes=[pltpu.VMEM((tail, LANES), BF16)] + [pltpu.VMEM((tail, LANES), F32)] * 3 + [pltpu.SemaphoreType.DMA((2,))],
      compiler_params=pltpu.CompilerParams(vmem_limit_bytes=48 * MIB), name="outer")(st, mom)


def rms_scale(rows):
    return lax.rsqrt(jnp.mean(rows * rows, axis=-1, keepdims=True) + EPSILON)


def rms_backward(rows, scale, gain, grad_out):
    grad_gain = jnp.sum(grad_out * rows * scale, axis=0)
    inner = jnp.sum(grad_out * gain * rows, axis=-1, keepdims=True)
    grad_in = scale * gain * grad_out - rows * scale * scale * scale * inner / rows.shape[-1]
    return grad_in, grad_gain


def rotate(rows, cosine, sine):
    half = HEAD_SIZE // 2
    front, back = rows[:, :half], rows[:, half:]
    return jnp.concatenate([front * cosine - back * sine, back * cosine + front * sine], axis=1)


def per_device(
    tokens,
    cotangent,
    routes,
    branch,
    attn_gain,
    query_key_value_weight,
    w_attn_out,
    ffn_gain,
    w_router,
    w_in,
    w_out,
    adam_first,
    adam_second,
    outer_mom,
):
    shards = lax.axis_size("shard")
    reps = lax.axis_size("rep")
    count = tokens.shape[2]
    width = tokens.shape[3]
    prompt = count - CONTINUATION_LEN
    local = EXPERTS // reps
    groups = None
    if shards > GROUP_SIZE:
        groups = [list(range(i, i + GROUP_SIZE)) for i in range(0, shards, GROUP_SIZE)]
    shard_pos = lax.axis_index("shard") % GROUP_SIZE
    rep_pos = lax.axis_index("rep")
    branch_len = branch.reshape(())
    x_in = tokens.reshape(count, width).astype(F32)
    top_low = cotangent.reshape(count, width)
    grad_top = top_low.astype(F32)
    route_ids = routes.reshape(count, TOP)
    gather = functools.partial(lax.all_gather, axis_name="shard", axis=0, tiled=True)

    flat_path = width // shards == LANES and outer_mom.shape[-1] % LANES == 0

    gains = gather(jnp.stack([attn_gain, ffn_gain], axis=1)).astype(F32)
    attn_gain_full, ffn_gain_full = gains[:, 0], gains[:, 1]
    qkv_full = gather(query_key_value_weight)

    attn_scale = rms_scale(x_in)
    normed_attn = (x_in * attn_scale * attn_gain_full).astype(BF16)
    positions = jnp.concatenate(
        [
            shard_pos * prompt + jnp.arange(prompt, dtype=jnp.int32),
            branch_len + jnp.arange(CONTINUATION_LEN, dtype=jnp.int32),
        ]
    )
    half = HEAD_SIZE // 2
    inverse_freq = ROPE_BASE ** (-(jnp.arange(half, dtype=F32) * 2.0) / HEAD_SIZE)
    angles = inverse_freq[:, None] * positions.astype(F32)[None, :]
    cosine, sine = jnp.cos(angles)[None], jnp.sin(angles)[None]

    def project(start, size, spin):
        rows = dot(qkv_full[:, start : start + size], normed_attn, (0, 1))
        rows = rows.reshape(size // HEAD_SIZE, HEAD_SIZE, count)
        return (rotate(rows, cosine, sine) if spin else rows).astype(BF16)

    key_value = jnp.stack(
        [project(Q_WIDTH, KV_WIDTH, True), project(Q_WIDTH + KV_WIDTH, KV_WIDTH, False)]
    )
    pieces = 2
    per_piece = KEY_VALUE_HEADS // pieces
    kv_piece = [slice(i * per_piece, (i + 1) * per_piece) for i in range(pieces)]
    q_piece = [slice(p.start * PER_KEY, p.stop * PER_KEY) for p in kv_piece]
    prompt_kv = [
        lax.all_gather(key_value[:, p, :, :prompt], "shard", axis=0, tiled=False, axis_index_groups=groups)
        for p in kv_piece
    ]
    own_kv = [key_value[:, p, :, prompt:] for p in kv_piece]
    query_all = project(0, Q_WIDTH, True)
    query = [query_all[p] for p in q_piece]
    attn_out_full = gather(w_attn_out)
    router_full = gather(w_router)
    w_in_mine = gather(lax.dynamic_slice_in_dim(w_in, rep_pos * local * 2 * F, local * 2 * F, 1))
    w_out_mine = gather(lax.dynamic_slice_in_dim(w_out, rep_pos * local * F, local * F, 1))
    all_top = lax.all_gather(top_low, "rep", axis=0, tiled=False)
    where = jnp.stack([shard_pos.astype(jnp.int32), branch_len])
    attn, lse = zip(*[attn_forward(where, *part) for part in zip(query, prompt_kv, own_kv)])
    attn = jnp.concatenate(attn, axis=0)
    attn_low = attn.astype(BF16).reshape(Q_WIDTH, count)
    x_mid = x_in + dot(attn_low, attn_out_full, (0, 1))

    ffn_scale = rms_scale(x_mid)
    normed_ffn = (x_mid * ffn_scale * ffn_gain_full).astype(BF16)
    logits = dot(normed_ffn, router_full, (1, 0))
    chosen = jnp.any(route_ids[:, :, None] == jnp.arange(EXPERTS, dtype=jnp.int32), axis=1)
    gates = jax.nn.softmax(jnp.where(chosen, logits, NEGATIVE), axis=-1)
    gates = jnp.where(chosen, gates, 0.0)

    gates_out = jnp.pad(gates.T.reshape(reps, local, count), ((0, 0), (0, 8 - local), (0, 0)))
    all_normed, dx_own, dx_core, dx_far, y_part, dgu, gated, dgate_part = experts(
        normed_ffn, all_top, gates_out, w_in_mine, w_out_mine
    )
    grad_from_experts = dx_own.astype(F32) + dx_core.astype(F32) + dx_far.astype(F32)
    grad_gates = dgate_part[:, :local].reshape(EXPERTS, count).T
    y_sum = lax.psum_scatter(y_part, "rep", scatter_dimension=0, tiled=False).astype(F32)
    block_out = (x_mid + y_sum).astype(BF16)

    def expert_term(left, right):
        term = dot(left.reshape(reps * count, width), right.reshape(reps * count, -1), (0, 0)).astype(BF16)
        rows = lax.psum_scatter(term, "shard", scatter_dimension=0, tiled=True)
        return lax.all_gather(rows, "rep", axis=0, tiled=False)

    expert_in = expert_term(all_normed, dgu)
    expert_out = expert_term(all_top, gated)

    grad_logits = (gates * (grad_gates - jnp.sum(gates * grad_gates, axis=-1, keepdims=True))).astype(BF16)
    grad_router_w = dot(normed_ffn, grad_logits, (0, 0))
    grad_normed_ffn = grad_from_experts + dot(grad_logits, router_full, (1, 1))
    grad_mid_norm, grad_ffn_gain = rms_backward(x_mid, ffn_scale, ffn_gain_full, grad_normed_ffn)
    grad_mid = grad_top + grad_mid_norm
    grad_branch = grad_mid.astype(BF16)
    grad_attn_w = dot(grad_branch, attn_low, (0, 1))
    grad_attn = dot(attn_out_full, grad_branch, (0, 1)).astype(BF16).reshape(QUERY_HEADS, HEAD_SIZE, count)
    early = jnp.concatenate([grad_attn_w, grad_ffn_gain[:, None], grad_router_w], axis=1).astype(BF16)
    early = jnp.pad(early, ((0, 0), (0, -early.shape[1] % LANES)))
    early = lax.psum_scatter(early, "shard", scatter_dimension=0, tiled=True)

    delta = jnp.sum(grad_attn.astype(F32) * attn, axis=1).reshape(KEY_VALUE_HEADS, PER_KEY, count)
    grad_query, grad_kv = [], []
    for n in range(pieces):
        dq, dkv, own = attn_backward(
            where, query[n], prompt_kv[n], own_kv[n], grad_attn[q_piece[n]], lse[n], delta[kv_piece[n]]
        )
        dkv = lax.psum_scatter(dkv, "shard", scatter_dimension=0, tiled=False, axis_index_groups=groups)
        grad_query.append(dq)
        grad_kv.append(jnp.concatenate([dkv.astype(F32), own], axis=-1))
    grad_query = jnp.concatenate(grad_query, axis=0)
    grad_kv = jnp.concatenate(grad_kv, axis=1)
    grad_projected = jnp.concatenate(
        [rotate(grad_query, cosine, -sine), rotate(grad_kv[0], cosine, -sine), grad_kv[1]], axis=0
    ).astype(BF16).reshape(Q_WIDTH + 2 * KV_WIDTH, count)
    grad_qkv_w = dot(normed_attn, grad_projected, (0, 1))
    grad_normed_attn = dot(grad_projected, qkv_full, (0, 1))
    grad_x_norm, grad_attn_gain = rms_backward(x_in, attn_scale, attn_gain_full, grad_normed_attn)
    grad_input = grad_mid + grad_x_norm

    late = jnp.concatenate([grad_qkv_w, grad_attn_gain[:, None]], axis=1).astype(BF16)
    late = jnp.pad(late, ((0, 0), (0, -late.shape[1] % LANES)))
    late = lax.psum_scatter(late, "shard", scatter_dimension=0, tiled=True)
    both = lax.psum(jnp.concatenate([early, late], axis=1), "rep")
    early, late = both[:, : early.shape[1]], both[:, early.shape[1] :]
    qkv_rows, attn_gain_rows = late[:, : Q_WIDTH + 2 * KV_WIDTH], late[:, Q_WIDTH + 2 * KV_WIDTH]
    attn_rows, ffn_gain_rows = early[:, :Q_WIDTH], early[:, Q_WIDTH]
    router_rows = early[:, Q_WIDTH + 1 : Q_WIDTH + 1 + EXPERTS]
    if flat_path:
        size = outer_mom.shape[-1]

        def lead(first, second, rest):
            return jnp.concatenate([first[None], second[None], rest.reshape(-1, LANES)], axis=0).astype(F32)

        weight_flat, _ = flatten(
            size, lead(attn_gain, ffn_gain, w_router), query_key_value_weight, w_attn_out, w_in, w_out
        )
        total_grad, square = flatten(
            size, lead(attn_gain_rows, ffn_gain_rows, router_rows), qkv_rows, attn_rows, expert_in, expert_out
        )
        norm_square = lax.psum(square.reshape(()), "shard")
    else:
        weight_flat = jnp.concatenate(
            [
                portion.astype(F32).reshape(-1)
                for portion in (attn_gain, query_key_value_weight, w_attn_out, ffn_gain, w_router, w_in, w_out)
            ]
        )
        total_grad = jnp.concatenate(
            [
                portion.astype(F32).reshape(-1)
                for portion in (
                    attn_gain_rows,
                    qkv_rows,
                    attn_rows,
                    ffn_gain_rows,
                    router_rows,
                    expert_in.transpose(1, 0, 2),
                    expert_out.transpose(1, 0, 2),
                )
            ]
        )
        norm_square = lax.psum(jnp.sum(total_grad * total_grad), "shard")
    grad_norm = jnp.sqrt(norm_square)
    clip_scale = CLIP_NORM / jnp.maximum(grad_norm, CLIP_NORM)
    if flat_path:
        new_first, new_second, step = adam(
            clip_scale.reshape(1), total_grad, adam_first, adam_second, weight_flat
        )
        new_mom, weight_update = outer(reps, lax.psum(step, "rep"), outer_mom)
    else:
        new_first, new_second, step = optimizer_math(
            total_grad, adam_first.reshape(-1), adam_second.reshape(-1), weight_flat, clip_scale
        )
        pseudo = -(lax.psum(step.astype(BF16), "rep").astype(F32) / reps)
        new_mom = OUTER_MOMENTUM * outer_mom.reshape(-1) + pseudo
        weight_update = -OUTER_RATE * (pseudo + OUTER_MOMENTUM * new_mom)
    return (
        block_out.reshape(tokens.shape),
        grad_input.reshape(tokens.shape),
        total_grad.reshape(outer_mom.shape),
        grad_norm,
        new_first.reshape(adam_first.shape),
        new_second.reshape(adam_second.shape),
        new_mom.reshape(outer_mom.shape),
        weight_update.reshape(outer_mom.shape),
    )


def solution(mesh):
    by_token = P("rep", "shard", None, None)
    by_state = P("rep", "shard", None)
    by_row = P("shard", None)
    placed = (
        by_token,
        by_token,
        by_token,
        P("rep", "shard"),
        P("shard"),
        by_row,
        by_row,
        P("shard"),
        by_row,
        by_row,
        by_row,
        by_state,
        by_state,
        by_row,
    )
    return jax.shard_map(
        per_device,
        mesh=mesh,
        in_specs=placed,
        out_specs=(by_token, by_token, by_row, P(), by_state, by_state, by_row, by_row),
        check_vma=False,
    )
```

```python
import functools

import jax
import jax.numpy as jnp
from jax import lax
from jax.experimental import pallas as pl
from jax.experimental.pallas import tpu as pltpu
from jax.sharding import PartitionSpec as P

QUERY_HEADS = 16
KEY_VALUE_HEADS = 8
HEAD_SIZE = 64
F = 512
EXPERTS = 16
TOP = 8
GROUP_SIZE = 8
CONTINUATION_LEN = 512
STEP = 10

EPSILON = 1e-06
NEGATIVE = -1e30
ROPE_BASE = 10000.0
BETA_ONE = 0.9
BETA_TWO = 0.95
ADAM_EPS = 1e-08
INNER_RATE = 0.01
DECAY_RATE = 0.1
OUTER_RATE = 0.7
OUTER_MOMENTUM = 0.9
CLIP_NORM = 1.0

LOG2E = 1.4426950408889634
LANES = 128
MIB = 1 << 20
BF16 = jnp.bfloat16
F32 = jnp.float32
PER_KEY = QUERY_HEADS // KEY_VALUE_HEADS
Q_WIDTH = QUERY_HEADS * HEAD_SIZE
KV_WIDTH = KEY_VALUE_HEADS * HEAD_SIZE


def dot(left, right, dims):
    return lax.dot_general(left, right, ((dims[:1], dims[1:]), ((), ())), preferred_element_type=F32)


def split_three(value):
    high = value.astype(BF16)
    rest = value - high.astype(F32)
    middle = rest.astype(BF16)
    low = (rest - middle.astype(F32)).astype(BF16)
    return high, middle, low


def augment_query(q_ref, start, width):
    rows = jnp.concatenate([q_ref[g, :, start : start + width] for g in range(PER_KEY)], axis=1)
    scaled = rows.astype(F32) * (HEAD_SIZE**-0.5 * LOG2E)
    high = scaled.astype(BF16)
    low = (scaled - high.astype(F32)).astype(BF16)
    return rows, high, low


def block_of(ref, index, block):
    span = pl.ds(pl.multiple_of(index * block, block), block)
    return ref[0, 0, :, span], ref[1, 0, :, span]


def causal(width, columns):
    key_pos = lax.broadcasted_iota(jnp.int32, (width, columns), 0)
    query_pos = lax.broadcasted_iota(jnp.int32, (width, columns), 1) % width
    return key_pos <= query_pos


def attn_forward_kernel(where_ref, q_ref, kv_ref, own_ref, o_ref, lse_ref, peak_ref, sum_ref, acc_ref):
    block = own_ref.shape[-1]
    columns = PER_KEY * block
    shard_pos = where_ref[0]
    branch = where_ref[1]

    def advance(query, key, value, mask):
        scores = dot(jnp.concatenate([key, key], axis=0), query, (0, 0))
        if mask is not None:
            scores = jnp.where(mask, scores, NEGATIVE)
        old = peak_ref[...]
        new = jnp.maximum(old, jnp.max(scores, axis=0, keepdims=True))
        probs = jnp.exp2(scores - new).astype(BF16)
        shrink = jnp.exp2(old - new)
        ones = jnp.ones((16, block), BF16)
        part = dot(jnp.concatenate([value, ones], axis=0), probs, (1, 0))
        peak_ref[...] = new
        sum_ref[...] = sum_ref[...] * shrink + part[HEAD_SIZE : HEAD_SIZE + 1]
        acc_ref[...] = acc_ref[...] * shrink + part[:HEAD_SIZE]

    def begin(start):
        _, high, low = augment_query(q_ref, start, block)
        peak_ref[...] = jnp.full_like(peak_ref, NEGATIVE)
        sum_ref[...] = jnp.zeros_like(sum_ref)
        acc_ref[...] = jnp.zeros_like(acc_ref)
        return jnp.concatenate([high, low], axis=0)

    def finish(start):
        total = sum_ref[...]
        result = acc_ref[...] / total
        lse = peak_ref[...] + jnp.log2(total)
        for g in range(PER_KEY):
            o_ref[g, :, start : start + block] = result[:, g * block : (g + 1) * block]
            lse_ref[0, g : g + 1, start : start + block] = lse[:, g * block : (g + 1) * block]

    def full(query):
        def body(index, carry):
            advance(query, *block_of(kv_ref, index, block), None)
            return carry

        return body

    query = begin(0)
    lax.fori_loop(0, shard_pos, full(query), 0)
    advance(query, *block_of(kv_ref, shard_pos, block), causal(block, columns))
    finish(0)

    query = begin(block)
    whole = branch // block
    lax.fori_loop(0, whole, full(query), 0)

    @pl.when(branch % block != 0)
    def _():
        key_pos = lax.broadcasted_iota(jnp.int32, (block, columns), 0)
        advance(query, *block_of(kv_ref, whole, block), key_pos < branch % block)

    advance(query, own_ref[0, 0], own_ref[1, 0], causal(block, columns))
    finish(block)


def attn_forward(where, query, prompt_kv, own_kv):
    tokens = query.shape[-1]
    block = own_kv.shape[-1]
    columns = PER_KEY * block
    keys = prompt_kv.shape[-1]
    return pl.pallas_call(
        attn_forward_kernel,
        grid=(query.shape[0] // PER_KEY,),
        in_specs=[
            pl.BlockSpec(memory_space=pltpu.SMEM),
            pl.BlockSpec((PER_KEY, HEAD_SIZE, tokens), lambda h: (h, 0, 0)),
            pl.BlockSpec((2, 1, HEAD_SIZE, keys), lambda h: (0, h, 0, 0)),
            pl.BlockSpec((2, 1, HEAD_SIZE, block), lambda h: (0, h, 0, 0)),
        ],
        out_specs=[
            pl.BlockSpec((PER_KEY, HEAD_SIZE, tokens), lambda h: (h, 0, 0)),
            pl.BlockSpec((1, PER_KEY, tokens), lambda h: (h, 0, 0)),
        ],
        out_shape=[
            jax.ShapeDtypeStruct(query.shape, F32),
            jax.ShapeDtypeStruct((query.shape[0] // PER_KEY, PER_KEY, tokens), F32),
        ],
        scratch_shapes=[
            pltpu.VMEM((1, columns), F32),
            pltpu.VMEM((1, columns), F32),
            pltpu.VMEM((HEAD_SIZE, columns), F32),
        ],
        compiler_params=pltpu.CompilerParams(vmem_limit_bytes=48 * MIB),
        cost_estimate=pl.CostEstimate(
            flops=4 * tokens * keys * query.shape[0] * HEAD_SIZE,
            bytes_accessed=16 * MIB,
            transcendentals=query.shape[0] * tokens * keys,
        ),
        name="attn_forward",
    )(where, query, prompt_kv, own_kv)


def attn_backward_kernel(
    where_ref, q_ref, kv_ref, own_ref, go_ref, lse_ref, delta_ref, dq_ref, dkv_ref, down_ref, dkv_acc, dq_acc
):
    block = own_ref.shape[-1]
    columns = PER_KEY * block
    shard_pos = where_ref[0]
    branch = where_ref[1]
    ones = jnp.ones((16, block), BF16)
    pad = jnp.zeros((16 - 3, columns), BF16)

    def begin(start):
        rows, high, low = augment_query(q_ref, start, block)

        def lanes(ref):
            return jnp.concatenate([ref[0, g : g + 1, start : start + block] for g in range(PER_KEY)], axis=1)

        lse = split_three(-lanes(lse_ref))
        delta = split_three(-lanes(delta_ref))
        grad = jnp.concatenate([go_ref[g, :, start : start + block] for g in range(PER_KEY)], axis=1)
        query = jnp.concatenate([high, low, *lse, pad], axis=0)
        grad_plus = jnp.concatenate([grad, *delta, pad], axis=0)
        dq_acc[...] = jnp.zeros_like(dq_acc)
        scaled = (rows.astype(F32) * HEAD_SIZE**-0.5).astype(BF16)
        return query, scaled, grad_plus, grad

    def terms(state, key, value, mask):
        query, scaled, grad_plus, grad = state
        scores = dot(jnp.concatenate([key, key, ones], axis=0), query, (0, 0))
        if mask is not None:
            scores = jnp.where(mask, scores, NEGATIVE)
        probs = jnp.exp2(scores)
        grad_probs = dot(jnp.concatenate([value, ones], axis=0), grad_plus, (0, 0))
        grad_scores = (probs * grad_probs).astype(BF16)
        dq_acc[...] += dot(key, grad_scores, (1, 0))
        return dot(scaled, grad_scores, (1, 1)), dot(grad, probs.astype(BF16), (1, 1))

    def add(index, state, mask):
        dk, dv = terms(state, *block_of(kv_ref, index, block), mask)
        span = pl.ds(pl.multiple_of(index * block, block), block)
        dkv_acc[0, :, span] += dk
        dkv_acc[1, :, span] += dv

    def finish(start):
        total = dq_acc[...] * HEAD_SIZE**-0.5
        for g in range(PER_KEY):
            dq_ref[g, :, start : start + block] = total[:, g * block : (g + 1) * block]

    def full(state):
        def body(index, carry):
            add(index, state, None)
            return carry

        return body

    dkv_acc[...] = jnp.zeros_like(dkv_acc)
    state = begin(0)
    lax.fori_loop(0, shard_pos, full(state), 0)
    add(shard_pos, state, causal(block, columns))
    finish(0)

    state = begin(block)
    whole = branch // block
    lax.fori_loop(0, whole, full(state), 0)

    @pl.when(branch % block != 0)
    def _():
        key_pos = lax.broadcasted_iota(jnp.int32, (block, columns), 0)
        add(whole, state, key_pos < branch % block)

    dk, dv = terms(state, own_ref[0, 0], own_ref[1, 0], causal(block, columns))
    down_ref[0, 0] = dk
    down_ref[1, 0] = dv
    finish(block)
    dkv_ref[:, 0] = dkv_acc[...].astype(BF16)


def attn_backward(where, query, prompt_kv, own_kv, grad_out, lse, delta):
    tokens = query.shape[-1]
    block = own_kv.shape[-1]
    columns = PER_KEY * block
    keys = prompt_kv.shape[-1]
    by_head = pl.BlockSpec((PER_KEY, HEAD_SIZE, tokens), lambda h: (h, 0, 0))
    by_keys = pl.BlockSpec((2, 1, HEAD_SIZE, keys), lambda h: (0, h, 0, 0))
    by_own = pl.BlockSpec((2, 1, HEAD_SIZE, block), lambda h: (0, h, 0, 0))
    by_row = pl.BlockSpec((1, PER_KEY, tokens), lambda h: (h, 0, 0))
    return pl.pallas_call(
        attn_backward_kernel,
        grid=(query.shape[0] // PER_KEY,),
        in_specs=[pl.BlockSpec(memory_space=pltpu.SMEM), by_head, by_keys, by_own, by_head, by_row, by_row],
        out_specs=[by_head, by_keys, by_own],
        out_shape=[
            jax.ShapeDtypeStruct(query.shape, F32),
            jax.ShapeDtypeStruct(prompt_kv.shape, BF16),
            jax.ShapeDtypeStruct(own_kv.shape, F32),
        ],
        scratch_shapes=[
            pltpu.VMEM((2, HEAD_SIZE, keys), F32),
            pltpu.VMEM((HEAD_SIZE, columns), F32),
        ],
        compiler_params=pltpu.CompilerParams(vmem_limit_bytes=56 * MIB),
        cost_estimate=pl.CostEstimate(
            flops=10 * tokens * keys * query.shape[0] * HEAD_SIZE,
            bytes_accessed=32 * MIB,
            transcendentals=query.shape[0] * tokens * keys,
        ),
        name="attn_backward",
    )(where, query, prompt_kv, own_kv, grad_out, lse, delta)


MESH = pl.DeviceIdType.MESH
LINE = 4
TOKEN_PARTS = 4


def start_kernel(
    x_ref,
    w_ref,
    top_ref,
    tok_all,
    w_all,
    top_all,
    own_sem,
    line_recv,
    right_send,
    left_send,
    y_send,
    y_recv,
    x_send,
    x_recv,
    core_send,
    core_recv,
    top_send,
    top_recv,
):
    part = tok_all.shape[1] // TOKEN_PARTS
    quarter = w_all.shape[2]
    half = top_ref.shape[0] // 2
    me = lax.axis_index("shard")
    place, column = me // 2, lax.rem(me, 2)
    rep = lax.axis_index("rep")
    far, core = lax.rem(rep + 2, 4), rep + 1 - 2 * lax.rem(rep, 2)
    to_right, to_left, to_y = {"shard": me + 2}, {"shard": me - 2}, {"shard": me + 1 - 2 * column}
    to_far, to_core = {"rep": far}, {"rep": core}
    weights, mirrored = 0, TOKEN_PARTS + 1
    last = TOKEN_PARTS
    streams = TOKEN_PARTS + 2

    def piece(i, origin, side):
        if i == weights:
            return w_all.at[2 * origin + side, rep]
        k = (i if i != mirrored else last) - 1
        return tok_all.at[2 * origin + side, pl.ds(k * part, part)]

    def side_of(i):
        return 1 - column if i == mirrored else column

    def own(i):
        if i == weights:
            return w_ref.at[pl.ds(pl.multiple_of(rep * quarter, quarter), quarter)]
        if i == mirrored:
            return piece(i, place, 1 - column)
        return x_ref.at[pl.ds((i - 1) * part, part)]

    def remote(source, target, send, receive, device):
        return pltpu.make_async_remote_copy(
            src_ref=source, dst_ref=target, send_sem=send, recv_sem=receive, device_id=device, device_id_type=MESH
        )

    def source(i, origin, at_home):
        return own(i) if at_home else piece(i, origin, side_of(i))

    def right(i, origin, at_home=False):
        return remote(
            source(i, origin, at_home),
            piece(i, origin, side_of(i)),
            right_send.at[i, origin],
            line_recv.at[i, origin],
            to_right,
        )

    def left(i, origin, at_home=False):
        return remote(
            source(i, origin, at_home),
            piece(i, origin, side_of(i)),
            left_send.at[i, origin],
            line_recv.at[i, origin],
            to_left,
        )

    def abreast(i, origin, at_home=False):
        return remote(
            source(i, origin, at_home), piece(i, origin, column), y_send.at[i, origin], y_recv.at[i, origin], to_y
        )

    def over_x(origin, side, at_home=False):
        target = piece(weights, origin, side)
        source_ref = own(weights) if at_home else target
        return remote(source_ref, target, x_send.at[origin, side], x_recv.at[origin, side], to_far)

    def over_core(group, origin, side, at_home=False):
        target = w_all.at[2 * origin + side, rep if group == 0 else far]
        source_ref = own(weights) if at_home else target
        return remote(
            source_ref, target, core_send.at[group, origin, side], core_recv.at[group, origin, side], to_core
        )

    def top_far(h):
        return remote(
            top_ref.at[pl.ds(h * half, half)],
            top_all.at[2, pl.ds(h * half, half)],
            top_send.at[0, h],
            top_recv.at[0, h],
            to_far,
        )

    def top_core(h):
        return remote(
            top_ref.at[pl.ds(h * half, half)],
            top_all.at[1, pl.ds(h * half, half)],
            top_send.at[1, h],
            top_recv.at[1, h],
            to_core,
        )

    def top_diagonal(h):
        return remote(
            top_all.at[2, pl.ds(h * half, half)],
            top_all.at[3, pl.ds(h * half, half)],
            top_send.at[2, h],
            top_recv.at[2, h],
            to_core,
        )

    has_right, has_left = place < LINE - 1, place > 0
    barrier = pltpu.get_barrier_semaphore()

    def greet(device):
        pl.semaphore_signal(barrier, inc=1, device_id=device, device_id_type=MESH)

    for device in (to_y, to_far, to_core):
        greet(device)

    @pl.when(has_right)
    def _():
        greet(to_right)

    @pl.when(has_left)
    def _():
        greet(to_left)

    pl.semaphore_wait(barrier, 3 + has_right.astype(jnp.int32) + has_left.astype(jnp.int32))

    def along(i, origin, at_home=False):
        @pl.when(has_right)
        def _():
            right(i, origin, at_home).start()

        @pl.when(has_left)
        def _():
            left(i, origin, at_home).start()

    order = [weights, last] + list(range(1, last))
    for i in order:
        along(i, place, True)
        abreast(i, place, True).start()
        if i == weights:
            over_x(place, column, True).start()
            over_core(0, place, column, True).start()
            for h in (0, 1):
                top_far(h).start()
    for h in (0, 1):
        top_core(h).start()
    own_copies = [
        pltpu.make_async_copy(own(i), piece(i, place, column), own_sem.at[i]) for i in range(streams - 1)
    ]
    own_copies.append(pltpu.make_async_copy(top_ref, top_all.at[0], own_sem.at[streams - 1]))
    for copy in own_copies:
        copy.start()
    abreast(last, place).wait_recv()
    along(mirrored, place, True)

    def weights_across(origin):
        abreast(weights, origin).wait_recv()
        over_x(origin, 1 - column).start()
        over_core(0, origin, 1 - column).start()

    weights_across(place)
    for d in range(1, LINE):
        before, after = place - d, place + d
        from_left, from_right = before >= 0, after < LINE
        for i in [weights, last, mirrored] + list(range(1, last)):

            @pl.when(from_left)
            def _(i=i):
                right(i, before).wait_recv()

                @pl.when(has_right)
                def _():
                    right(i, before).start()

                if i != last and i != mirrored:
                    abreast(i, before).start()
                if i == weights:
                    over_x(before, column).start()
                    over_core(0, before, column).start()

            @pl.when(from_right)
            def _(i=i):
                left(i, after).wait_recv()

                @pl.when(has_left)
                def _():
                    left(i, after).start()

                if i != last and i != mirrored:
                    abreast(i, after).start()
                if i == weights:
                    over_x(after, column).start()
                    over_core(0, after, column).start()

        @pl.when(from_left)
        def _():
            weights_across(before)

        @pl.when(from_right)
        def _():
            weights_across(after)

        if d >= 2:
            h = d - 2
            top_far(h).wait_recv()
            top_diagonal(h).start()

    for origin in range(LINE):
        for side in (0, 1):
            remote(
                w_all.at[2 * origin + side, far],
                w_all.at[2 * origin + side, far],
                x_send.at[origin, side],
                x_recv.at[origin, side],
                to_far,
            ).wait_recv()
            over_core(1, origin, side).start()

    for origin in range(LINE):
        for i in range(1, last):
            abreast(i, origin).wait_recv()
        for side in (0, 1):
            for group in (0, 1):
                over_core(group, origin, side).wait_recv()
    for h in (0, 1):
        top_core(h).wait_recv()
        top_diagonal(h).wait_recv()
        for copy in (top_far(h), top_core(h), top_diagonal(h)):
            copy.wait_send()
    for copy in own_copies:
        copy.wait()
    for origin in range(LINE):
        for i in range(streams):

            @pl.when(has_right & (origin <= place))
            def _(i=i, origin=origin):
                right(i, origin).wait_send()

            @pl.when(has_left & (origin >= place))
            def _(i=i, origin=origin):
                left(i, origin).wait_send()

            if i != last and i != mirrored:
                abreast(i, origin).wait_send()
        for side in (0, 1):
            over_x(origin, side).wait_send()
            for group in (0, 1):
                over_core(group, origin, side).wait_send()
    abreast(last, place).wait_send()


def start_gather(x, small, top):
    rows, width = x.shape
    prompt = rows - CONTINUATION_LEN
    own_rows, columns = small.shape
    dma = pltpu.SemaphoreType.DMA
    streams = TOKEN_PARTS + 2
    anywhere = pl.BlockSpec(memory_space=pl.ANY)
    return pl.pallas_call(
        start_kernel,
        in_specs=[anywhere] * 3,
        out_specs=[anywhere] * 3,
        out_shape=[
            jax.ShapeDtypeStruct((2 * LINE, prompt, width), BF16),
            jax.ShapeDtypeStruct((2 * LINE, 4, own_rows // 4, columns), BF16),
            jax.ShapeDtypeStruct((4, rows, width), BF16),
        ],
        scratch_shapes=[
            dma((streams,)),
            dma((streams, LINE)),
            dma((streams, LINE)),
            dma((streams, LINE)),
            dma((streams, LINE)),
            dma((streams, LINE)),
            dma((LINE, 2)),
            dma((LINE, 2)),
            dma((2, LINE, 2)),
            dma((2, LINE, 2)),
            dma((3, 2)),
            dma((3, 2)),
        ],
        compiler_params=pltpu.CompilerParams(collective_id=2, has_side_effects=True),
        cost_estimate=pl.CostEstimate(flops=0, bytes_accessed=64 * MIB, transcendentals=0),
        name="start_gather",
    )(x, small, top)


ORDER = ((0, 0), (0, 1), (3, 0), (2, 0), (3, 1), (2, 1), (1, 0), (1, 1))
Y_PLACE = (0, 2, 1, 3)


def experts_kernel(
    x_hbm,
    top_hbm,
    gates_ref,
    w_ref,
    all_x,
    dx_own,
    dx_core,
    dx_far,
    y_all,
    dgu_all,
    gh_all,
    dg_all,
    x_buf,
    top_buf,
    y_buf,
    dx_buf,
    dgu_buf,
    gh_buf,
    relay,
    y_acc,
    dx_acc,
    gates_all,
    gates_now,
    dg_now,
    dg_mine,
    in_sem,
    out_sem,
    copy_sem,
    send_sem,
    recv_sem,
    small_send,
    small_recv,
):
    tile = x_buf.shape[1]
    count = w_ref.shape[1] // (3 * F)
    step = pl.program_id(0)
    steps = len(ORDER)
    slot = lax.rem(step, 2)
    me = lax.axis_index("rep")
    home = [me, me + 1 - 2 * lax.rem(me, 2), lax.rem(me + 2, 4), 3 - me]

    def remote(source, target, send, receive, relation):
        return pltpu.make_async_remote_copy(
            src_ref=source,
            dst_ref=target,
            send_sem=send,
            recv_sem=receive,
            device_id={"rep": home[relation]},
            device_id_type=MESH,
        )

    def half(ref, half_index, *lead):
        return ref.at[(*lead, pl.ds(half_index * tile, tile))]

    def to_core(h):
        return remote(half(x_hbm, h), half(all_x, h, me), send_sem.at[0, h], recv_sem.at[0, h], 1)

    def to_far(h):
        return remote(half(x_hbm, h), half(all_x, h, me), send_sem.at[1, h], recv_sem.at[1, h], 2)

    def forward(h):
        part = half(all_x, h, home[2])
        return remote(part, part, send_sem.at[2, h], recv_sem.at[2, h], 1)

    def give(kind, h, buffer):
        if kind == 3:
            return remote(buffer, relay.at[h], send_sem.at[3, h], recv_sem.at[3, h], 1)
        if kind == 2:
            return remote(buffer, half(dx_far, h), send_sem.at[4, h], recv_sem.at[4, h], 2)
        return remote(buffer, half(dx_core, h), send_sem.at[5, h], recv_sem.at[5, h], 1)

    def small_gates(k):
        return remote(gates_ref.at[home[k]], gates_all.at[me], small_send.at[0, k], small_recv.at[0, k], k)

    def small_back(k):
        return remote(dg_mine.at[home[k]], dg_all.at[me], small_send.at[1, k], small_recv.at[1, k], k)

    def load_x(i):
        kind, h = ORDER[i]
        source = half(x_hbm, h) if kind == 0 else half(all_x, h, home[kind])
        return pltpu.make_async_copy(source, x_buf.at[i % 2], in_sem.at[i % 2, 0])

    def load_top(i):
        kind, h = ORDER[i]
        return pltpu.make_async_copy(half(top_hbm, h, kind), top_buf.at[i % 2], in_sem.at[i % 2, 1])

    def stores(i):
        kind, h = ORDER[i]
        out = []
        places = (y_buf, y_all, Y_PLACE[kind]), (dgu_buf, dgu_all, home[kind]), (gh_buf, gh_all, kind)
        for n, (buffer, target, place) in enumerate(places):
            out.append(pltpu.make_async_copy(buffer.at[i % 2], half(target, h, place), out_sem.at[i % 2, n]))
        return out

    def store_dx(i):
        kind, h = ORDER[i]
        if kind == 0:
            return pltpu.make_async_copy(dx_buf.at[i % 2], half(dx_own, h), out_sem.at[i % 2, 3])
        return give(kind, h, dx_buf.at[i % 2])

    def finish(i):
        for copy in stores(i):
            copy.wait()
        if ORDER[i][0] == 0:
            store_dx(i).wait()
        else:
            store_dx(i).wait_send()

    own_copy = pltpu.make_async_copy(x_hbm, all_x.at[me], copy_sem)
    for i in range(steps):
        kind, h = ORDER[i]

        @pl.when(step == i)
        def _(i=i, kind=kind, h=h):
            if i == 0:
                barrier = pltpu.get_barrier_semaphore()
                for k in (1, 2, 3):
                    pl.semaphore_signal(
                        barrier, inc=1, device_id={"rep": home[k]}, device_id_type=MESH
                    )
                pl.semaphore_wait(barrier, 3)
                for n in (0, 1):
                    to_far(n).start()
                for n in (0, 1):
                    to_core(n).start()
                for k in (1, 2, 3):
                    small_gates(k).start()
                own_copy.start()
                load_top(0).start()
                load_x(0).start()
                gates_all[me] = gates_ref[me]
            if i == 2:
                for k in (1, 2, 3):
                    small_gates(k).wait_recv()
                to_far(0).wait_recv()
                forward(0).start()
                forward(0).wait_recv()
                load_x(2).start()
            if i == 3:
                to_far(1).wait_recv()
                forward(1).start()
            if i == 4:
                forward(1).wait_recv()
                load_x(4).start()
            if i == 5:
                to_core(0).wait_recv()
                to_core(1).wait_recv()
            load_x(i).wait()
            load_top(i).wait()
            if i + 1 < steps:
                load_top(i + 1).start()
                if i + 1 not in (2, 4):
                    load_x(i + 1).start()
            if i >= 2:
                finish(i - 2)
            gates_now[...] = jnp.transpose(gates_all[home[kind]][:, h * tile : (h + 1) * tile])

    x = x_buf[slot]
    top = top_buf[slot]
    columns = []
    for e in range(count):
        w_in = w_ref[:, e * 2 * F : (e + 1) * 2 * F]
        w_out = w_ref[:, (count * 2 + e) * F : (count * 2 + e + 1) * F]
        gate_up = dot(x, w_in, (1, 0))
        g = gate_up[:, :F]
        u = gate_up[:, F:]
        sig = jax.nn.sigmoid(g)
        act = g * sig
        hidden = (act * u).astype(BF16).astype(F32)
        raw = dot(top, w_out, (1, 0))
        columns.append(jnp.sum(hidden * raw, axis=1, keepdims=True))
        gate = gates_now[:, e : e + 1]
        gated = (hidden * gate).astype(BF16)
        gh_buf[slot, :, e * F : (e + 1) * F] = gated
        grad_hidden = raw * gate
        dg = (grad_hidden * u * sig * (1.0 + g * (1.0 - sig))).astype(BF16)
        du = (grad_hidden * act).astype(BF16)
        dgu = jnp.concatenate([dg, du], axis=1)
        dgu_buf[slot, :, e * 2 * F : (e + 1) * 2 * F] = dgu
        y = dot(gated, w_out, (1, 1))
        dx = dot(dgu, w_in, (1, 1))
        if e == 0:
            y_acc[...] = y
            dx_acc[...] = dx
        elif e < count - 1:
            y_acc[...] += y
            dx_acc[...] += dx
        else:
            y_buf[slot] = (y_acc[...] + y).astype(BF16)
            dx_acc[...] += dx
    columns.append(jnp.zeros((tile, 8 - count), F32))
    dg_now[...] = jnp.transpose(jnp.concatenate(columns, axis=1))

    for i in range(steps):
        kind, h = ORDER[i]

        @pl.when(step == i)
        def _(i=i, kind=kind, h=h):
            dg_mine[home[kind], :, h * tile : (h + 1) * tile] = dg_now[...]
            if kind == 2:
                give(3, h, dx_buf.at[0]).wait_recv()
                dx_buf[i % 2] = (dx_acc[...] + relay[h].astype(F32)).astype(BF16)
            else:
                dx_buf[i % 2] = dx_acc[...].astype(BF16)
            store_dx(i).start()
            for copy in stores(i):
                copy.start()
            if i == steps - 1:
                own_back = pltpu.make_async_copy(dg_mine.at[me], dg_all.at[me], small_send.at[1, 0])
                own_back.start()
                for k in (1, 2, 3):
                    small_back(k).start()
                finish(i - 1)
                finish(i)
                own_copy.wait()
                own_back.wait()
                for n in (0, 1):
                    to_far(n).wait_send()
                    to_core(n).wait_send()
                    forward(n).wait_send()
                    give(2, n, dx_buf.at[0]).wait_recv()
                    give(1, n, dx_buf.at[0]).wait_recv()
                for k in (1, 2, 3):
                    small_gates(k).wait_send()
                    small_back(k).wait()


def experts(x, all_top, gates, weights):
    rows, width = x.shape
    reps = all_top.shape[0]
    count = weights.shape[1] // (3 * F)
    tile = rows // 2
    anywhere = pl.BlockSpec(memory_space=pl.ANY)
    fixed = pl.BlockSpec(weights.shape, lambda i: (0, 0), pipeline_mode=pl.Buffered(1))
    small = pl.BlockSpec((reps, 8, rows), lambda i: (0, 0, 0))
    dma = pltpu.SemaphoreType.DMA
    return pl.pallas_call(
        experts_kernel,
        grid=(len(ORDER),),
        in_specs=[anywhere, anywhere, small, fixed],
        out_specs=[anywhere] * 8,
        out_shape=[
            jax.ShapeDtypeStruct((reps, rows, width), BF16),
            jax.ShapeDtypeStruct((rows, width), BF16),
            jax.ShapeDtypeStruct((rows, width), BF16),
            jax.ShapeDtypeStruct((rows, width), BF16),
            jax.ShapeDtypeStruct((reps, rows, width), BF16),
            jax.ShapeDtypeStruct((reps, rows, count * 2 * F), BF16),
            jax.ShapeDtypeStruct((reps, rows, count * F), BF16),
            jax.ShapeDtypeStruct((reps, 8, rows), F32),
        ],
        scratch_shapes=[
            pltpu.VMEM((2, tile, width), BF16),
            pltpu.VMEM((2, tile, width), BF16),
            pltpu.VMEM((2, tile, width), BF16),
            pltpu.VMEM((2, tile, width), BF16),
            pltpu.VMEM((2, tile, count * 2 * F), BF16),
            pltpu.VMEM((2, tile, count * F), BF16),
            pltpu.VMEM((2, tile, width), BF16),
            pltpu.VMEM((tile, width), F32),
            pltpu.VMEM((tile, width), F32),
            pltpu.VMEM((reps, 8, rows), F32),
            pltpu.VMEM((tile, 8), F32),
            pltpu.VMEM((8, tile), F32),
            pltpu.VMEM((reps, 8, rows), F32),
            dma((2, 2)),
            dma((2, 4)),
            dma,
            dma((6, 2)),
            dma((6, 2)),
            dma((2, 4)),
            dma((2, 4)),
        ],
        compiler_params=pltpu.CompilerParams(
            vmem_limit_bytes=58 * MIB, collective_id=1, has_side_effects=True
        ),
        cost_estimate=pl.CostEstimate(
            flops=12 * reps * rows * width * count * F,
            bytes_accessed=80 * MIB,
            transcendentals=reps * rows * count * F,
        ),
        name="experts",
    )(x, all_top, gates, weights)


def flatten_kernel(starts, lead_ref, *refs):
    parts, flat_ref, square_ref = refs[: len(starts)], refs[len(starts)], refs[len(starts) + 1]
    scratch, sems = refs[len(starts) + 2 : -1], refs[-1]
    step = pl.program_id(0)
    steps = pl.num_programs(0)
    slot = lax.rem(step, 2)
    flat = flat_ref.reshape(flat_ref.shape[1] // LANES, LANES)
    lead_places = ((0, 0, 1), (1, starts[2] - 17 , 1), (2, starts[2] - 16, 16))

    def copies(index, where):
        out = []
        for n, (start, buffer) in enumerate(zip(starts, scratch)):
            size = buffer.shape[1]
            out.append(pltpu.make_async_copy(buffer.at[where], flat.at[pl.ds(start + index * size, size)], sems.at[where, n]))
        return out

    @pl.when(step == 0)
    def _():
        square_ref[...] = jnp.sum(lead_ref[...] * lead_ref[...], keepdims=True).reshape(1, 1) + jnp.zeros_like(square_ref)
        for n, (source, target, size) in enumerate(lead_places):
            copy = pltpu.make_async_copy(lead_ref.at[pl.ds(source, size)], flat.at[pl.ds(target, size)], sems.at[2, n])
            copy.start()
            copy.wait()

    @pl.when(step >= 2)
    def _():
        for copy in copies(step - 2, slot):
            copy.wait()

    total = jnp.zeros((8, LANES), F32)
    for part, buffer in zip(parts, scratch):
        rows = part.shape[-2]
        wide = buffer.shape[1] // rows
        reps = part.shape[0] if len(part.shape) == 3 else 1
        each = wide // reps
        for r in range(reps):
            for c in range(each):
                lanes = slice(c * LANES, (c + 1) * LANES)
                value = (part[r, :, lanes] if len(part.shape) == 3 else part[:, lanes]).astype(F32)
                buffer[slot, pl.ds(r * each + c, rows, stride=wide), :] = value
                square = value * value
                for k in range(0, rows, 8):
                    total += square[k : k + 8]
    square_ref[...] += jnp.sum(total, keepdims=True).reshape(1, 1)
    for copy in copies(step, slot):
        copy.start()

    @pl.when(step == steps - 1)
    def _():
        for copy in copies(step - 1, 1 - slot):
            copy.wait()
        for copy in copies(step, slot):
            copy.wait()

def flatten(size, lead, parts, tile=16):
    rows = parts[0][0].shape[-2]
    widths = [columns * (p.shape[0] if p.ndim == 3 else 1) // LANES for p, columns, _ in parts]
    starts, at = [], 1
    for n, w in enumerate(widths):
        if n == 2: at += 1 + 16
        starts.append(at); at += rows * w
    specs = []
    for p, columns, place in parts:
        if p.ndim == 3:
            specs.append(pl.BlockSpec((p.shape[0], tile, columns), lambda i, place=place: (0, i, place)))
        else:
            specs.append(pl.BlockSpec((tile, columns), lambda i, place=place: (i, place)))
    return pl.pallas_call(
        functools.partial(flatten_kernel, starts),
        grid=(rows // tile,),
        in_specs=[pl.BlockSpec(lead.shape, lambda i: (0, 0))] + specs,
        out_specs=[pl.BlockSpec(memory_space=pl.ANY), pl.BlockSpec((1, 1), lambda i: (0, 0))],
        out_shape=[jax.ShapeDtypeStruct((1, size), F32), jax.ShapeDtypeStruct((1, 1), F32)],
        scratch_shapes=[pltpu.VMEM((2, tile * w, LANES), F32) for w in widths] + [pltpu.SemaphoreType.DMA((3, 4))],
        compiler_params=pltpu.CompilerParams(vmem_limit_bytes=48 * MIB),
        name="flatten",
    )(lead, *[p for p, _, _ in parts])

HALF_ROWS = 1056


def moments(grad, first, second, scale):
    clipped = grad * scale
    new_first = BETA_ONE * first + (1.0 - BETA_ONE) * clipped
    new_second = BETA_TWO * second + (1.0 - BETA_TWO) * clipped * clipped
    return new_first, new_second


def inner_step(new_first, new_second, weight):
    root = jnp.sqrt(new_second * (1.0 / (1.0 - BETA_TWO**STEP))) + ADAM_EPS
    return -INNER_RATE * (new_first * (1.0 / (1.0 - BETA_ONE**STEP)) / root + DECAY_RATE * weight)


def flat_chunks(rows):
    chunks, at, half_at = [], 0, 0
    while at < rows:
        size = min(2 * HALF_ROWS, rows - at)
        half = -(-size // 32) * 16
        chunks.append((at, size, half_at, half))
        at, half_at = at + size, half_at + half
    return chunks


def step_kernel(
    square_ref,
    g_ref,
    f_ref,
    s_ref,
    w_ref,
    norm_ref,
    total,
    g_buf,
    f_buf,
    s_buf,
    w_buf,
    step_buf,
    near_buf,
    far_buf,
    sum_buf,
    square_mine,
    square_all,
    in_sem,
    near_send,
    near_recv,
    far_send,
    far_recv,
    back_send,
    back_recv,
    own_sem,
    square_send,
    square_recv,
):
    rows = g_ref.shape[-1] // LANES
    chunks = flat_chunks(rows)
    count = len(chunks)
    shards = lax.axis_size("shard")
    shard, rep = lax.axis_index("shard"), lax.axis_index("rep")
    side = lax.rem(rep, 2)
    to_core, to_far = {"rep": rep + 1 - 2 * side}, {"rep": lax.rem(rep + 2, 4)}

    def other(k):
        return {"shard": lax.rem(shard + k, shards)}

    barrier = pltpu.get_barrier_semaphore()
    greeted = [to_core, to_far] + [other(k) for k in range(1, shards)]
    for device in greeted:
        pl.semaphore_signal(barrier, inc=1, device_id=device, device_id_type=MESH)

    def loads(i):
        at, size, _, _ = chunks[i]
        pairs = (g_ref, g_buf), (f_ref.at[0], f_buf), (s_ref.at[0], s_buf), (w_ref, w_buf)
        return [
            pltpu.make_async_copy(
                ref.at[:, pl.ds(at * LANES, size * LANES)],
                buf.at[i % 2, :, pl.ds(0, size * LANES)],
                in_sem.at[i % 2, n],
            )
            for n, (ref, buf) in enumerate(pairs)
        ]

    def remote(source, target, send, receive, device):
        return pltpu.make_async_remote_copy(
            src_ref=source, dst_ref=target, send_sem=send, recv_sem=receive, device_id=device, device_id_type=MESH
        )

    def near(i):
        _, _, at, half = chunks[i]
        span = pl.ds(at, half)
        return remote(step_buf.at[1 - side, span], near_buf.at[span], near_send.at[i], near_recv.at[i], to_core)

    def far(i):
        _, _, at, half = chunks[i]
        span = pl.ds(at, half)
        return remote(step_buf.at[side, span], far_buf.at[span], far_send.at[i], far_recv.at[i], to_far)

    def back(i):
        _, _, at, half = chunks[i]
        span = pl.ds(at, half)
        return remote(sum_buf.at[span], total.at[side, span], back_send.at[i], back_recv.at[i], to_core)

    def keep(i):
        _, _, at, half = chunks[i]
        span = pl.ds(at, half)
        return pltpu.make_async_copy(sum_buf.at[span], total.at[side, span], own_sem.at[i])

    for copy in loads(0):
        copy.start()
    pl.semaphore_wait(barrier, len(greeted))

    def square_copy(k):
        return remote(square_mine, square_all.at[shard], square_send.at[k], square_recv.at[shard], other(k))

    square_mine[...] = jnp.broadcast_to(square_ref[...], square_mine.shape)
    square_all[shard] = square_mine[...]
    for k in range(1, shards):
        square_copy(k).start()
    for k in range(1, shards):
        source = lax.rem(shard + k, shards)
        remote(
            square_mine, square_all.at[source], square_send.at[k], square_recv.at[source], other(k)
        ).wait_recv()
    norm = jnp.sqrt(jnp.sum(square_all[...], axis=0))
    norm_ref[...] = norm[:1, :1]
    scale = (CLIP_NORM / jnp.maximum(norm, CLIP_NORM))[:1]

    def blocks(size):
        return 48 if size % 48 == 0 else 16

    def compute(i):
        _, _, at, half = chunks[i]
        block = blocks(half)
        for h in (0, 1):

            def body(j, carry):
                here = pl.multiple_of(j * block, 16)
                span = pl.ds(pl.multiple_of((h * half + here) * LANES, LANES), block * LANES)
                grad, first, second, weight = (
                    buf[i % 2, :, span].reshape(block, LANES) for buf in (g_buf, f_buf, s_buf, w_buf)
                )
                new_first, new_second = moments(grad, first, second, scale)
                step = inner_step(new_first, new_second, weight)
                step_buf[h, pl.ds(at + here, block)] = step.astype(BF16)
                return carry

            lax.fori_loop(0, half // block, body, 0)

    def add(i, left, right, target):
        _, _, at, half = chunks[i]
        block = blocks(half)

        def body(j, carry):
            span = pl.ds(pl.multiple_of(at + j * block, 16), block)
            target[span] = (left[span].astype(F32) + right[span].astype(F32)).astype(BF16)
            return carry

        lax.fori_loop(0, half // block, body, 0)

    for i in range(count + 2):
        if i < count:
            for copy in loads(i):
                copy.wait()
            if i + 1 < count:
                for copy in loads(i + 1):
                    copy.start()
            compute(i)
            near(i).start()
        if 1 <= i <= count:
            near(i - 1).wait_recv()
            add(i - 1, step_buf.at[side], near_buf, step_buf.at[side])
            far(i - 1).start()
        if i >= 2:
            far(i - 2).wait_recv()
            add(i - 2, step_buf.at[side], far_buf, sum_buf)
            back(i - 2).start()
            keep(i - 2).start()
    for k in range(1, shards):
        square_copy(k).wait_send()
    for i in range(count):
        near(i).wait_send()
        far(i).wait_send()
        back(i).wait_send()
        keep(i).wait()
        _, _, at, half = chunks[i]
        span = pl.ds(at, half)
        remote(
            sum_buf.at[span], total.at[1 - side, span], back_send.at[i], back_recv.at[i], to_core
        ).wait_recv()


def summed_step(square, grad, first, second, weight):
    rows = grad.shape[-1] // LANES
    chunks = flat_chunks(rows)
    count = len(chunks)
    halves = sum(chunk[3] for chunk in chunks)
    size = chunks[0][3] * 2
    shards = lax.axis_size("shard")
    dma = pltpu.SemaphoreType.DMA
    anywhere = pl.BlockSpec(memory_space=pl.ANY)
    return pl.pallas_call(
        step_kernel,
        in_specs=[pl.BlockSpec(memory_space=pltpu.VMEM)] + [anywhere] * 4,
        out_specs=[pl.BlockSpec(memory_space=pltpu.VMEM), anywhere],
        out_shape=[jax.ShapeDtypeStruct((1, 1), F32), jax.ShapeDtypeStruct((2, halves, LANES), BF16)],
        scratch_shapes=[pltpu.VMEM((2, 1, size * LANES), F32)] * 4
        + [
            pltpu.VMEM((2, halves, LANES), BF16),
            pltpu.VMEM((halves, LANES), BF16),
            pltpu.VMEM((halves, LANES), BF16),
            pltpu.VMEM((halves, LANES), BF16),
            pltpu.VMEM((8, LANES), F32),
            pltpu.VMEM((shards, 8, LANES), F32),
            dma((2, 4)),
        ]
        + [dma((count,))] * 7
        + [dma((shards,))] * 2,
        compiler_params=pltpu.CompilerParams(
            vmem_limit_bytes=48 * MIB, collective_id=3, has_side_effects=True
        ),
        cost_estimate=pl.CostEstimate(flops=0, bytes_accessed=64 * MIB, transcendentals=0),
        name="summed_step",
    )(square, grad, first, second, weight)


def update_kernel(
    reps, norm_ref, g, f, s, total, mom, nf, ns, nm, up, tg, tf, ts, tm, tt, tnf, tns, tnm, tup, sems
):
    rows = g.shape[-1] // LANES
    chunks = flat_chunks(rows)
    whole = [c for c in chunks if c[1] == 2 * HALF_ROWS]
    scale = CLIP_NORM / jnp.maximum(norm_ref[...], CLIP_NORM)

    def body(g_ref, f_ref, s_ref, t_ref, m_ref, nf_ref, ns_ref, nm_ref, up_ref):
        half = t_ref.shape[1]
        size = g_ref.shape[0]
        nf_ref[...], ns_ref[...] = moments(g_ref[...], f_ref[...], s_ref[...], scale)
        for h in (0, 1):
            span = slice(h * half, min((h + 1) * half, size))
            pseudo = t_ref[h, : span.stop - span.start].astype(F32) * (-1.0 / reps)
            new = OUTER_MOMENTUM * m_ref[span] + pseudo
            nm_ref[span] = new
            up_ref[span] = -OUTER_RATE * (pseudo + OUTER_MOMENTUM * new)

    def view(ref):
        return ref.reshape(rows, LANES)

    ins, outs = [view(g), view(f), view(s), total, view(mom)], [view(r) for r in (nf, ns, nm, up)]
    wide = pl.BlockSpec((2 * HALF_ROWS, LANES), lambda i: (i, 0))
    halves = pl.BlockSpec((2, HALF_ROWS, LANES), lambda i: (0, i, 0))
    if whole:
        pltpu.emit_pipeline(
            body, grid=(len(whole),), in_specs=[wide, wide, wide, halves, wide], out_specs=[wide] * 4
        )(*ins, *outs)
    for at, size, half_at, half in chunks[len(whole) :]:

        def part(n, ref):
            return ref.at[:, pl.ds(half_at, half)] if n == 3 else ref.at[pl.ds(at, size)]

        copies = [
            pltpu.make_async_copy(part(n, ref), buf, sems.at[n]) for n, (ref, buf) in enumerate(zip(ins, (tg, tf, ts, tt, tm)))
        ]
        for copy in copies:
            copy.start()
        for copy in copies:
            copy.wait()
        body(tg, tf, ts, tt, tm, tnf, tns, tnm, tup)
        copies = [
            pltpu.make_async_copy(buf, ref.at[pl.ds(at, size)], sems.at[n])
            for n, (buf, ref) in enumerate(zip((tnf, tns, tnm, tup), outs))
        ]
        for copy in copies:
            copy.start()
        for copy in copies:
            copy.wait()


def update(reps, norm, grad, first, second, total, mom):
    _, size, _, half = flat_chunks(grad.shape[-1] // LANES)[-1]
    anywhere = pl.BlockSpec(memory_space=pl.ANY)
    tail = pltpu.VMEM((size, LANES), F32)
    return pl.pallas_call(
        functools.partial(update_kernel, reps),
        in_specs=[pl.BlockSpec(memory_space=pltpu.VMEM)] + [anywhere] * 5,
        out_specs=[anywhere] * 4,
        out_shape=[jax.ShapeDtypeStruct(ref.shape, F32) for ref in (first, second, mom, mom)],
        scratch_shapes=[tail] * 4
        + [pltpu.VMEM((2, half, LANES), BF16)]
        + [tail] * 4
        + [pltpu.SemaphoreType.DMA((5,))],
        compiler_params=pltpu.CompilerParams(vmem_limit_bytes=48 * MIB),
        cost_estimate=pl.CostEstimate(flops=0, bytes_accessed=120 * MIB, transcendentals=0),
        name="update",
    )(norm, grad, first, second, total, mom)


def rms_scale(rows):
    return lax.rsqrt(jnp.mean(rows * rows, axis=-1, keepdims=True) + EPSILON)


def rms_backward(rows, scale, gain, grad_out):
    grad_gain = jnp.sum(grad_out * rows * scale, axis=0)
    inner = jnp.sum(grad_out * gain * rows, axis=-1, keepdims=True)
    grad_in = scale * gain * grad_out - rows * scale * scale * scale * inner / rows.shape[-1]
    return grad_in, grad_gain


def rotate(rows, cosine, sine):
    half = HEAD_SIZE // 2
    front, back = rows[:, :half], rows[:, half:]
    return jnp.concatenate([front * cosine - back * sine, back * cosine + front * sine], axis=1)


def per_device(
    tokens,
    cotangent,
    routes,
    branch,
    attn_gain,
    query_key_value_weight,
    w_attn_out,
    ffn_gain,
    w_router,
    w_in,
    w_out,
    adam_first,
    adam_second,
    outer_mom,
):
    shards = lax.axis_size("shard")
    reps = lax.axis_size("rep")
    count = tokens.shape[2]
    width = tokens.shape[3]
    prompt = count - CONTINUATION_LEN
    local = EXPERTS // reps
    groups = None
    if shards > GROUP_SIZE:
        groups = [list(range(i, i + GROUP_SIZE)) for i in range(0, shards, GROUP_SIZE)]
    shard_pos = lax.axis_index("shard") % GROUP_SIZE
    rep_pos = lax.axis_index("rep")
    branch_len = branch.reshape(())
    x_in = tokens.reshape(count, width).astype(F32)
    top_low = cotangent.reshape(count, width)
    grad_top = top_low.astype(F32)
    route_ids = routes.reshape(count, TOP)
    gather = functools.partial(lax.all_gather, axis_name="shard", axis=0, tiled=True)
    rows = width // shards
    qkv_columns = Q_WIDTH + 2 * KV_WIDTH
    fast = shards == 2 * LINE and reps == 4 and rows == LANES
    flat_path = fast and outer_mom.shape[-1] % LANES == 0

    small = jnp.concatenate(
        [query_key_value_weight, w_attn_out, w_router, attn_gain[:, None], ffn_gain[:, None]], axis=1
    )
    small = jnp.pad(small, ((0, 0), (0, -small.shape[1] % LANES)))
    tokens_low = tokens.reshape(count, width)
    if fast:
        prompt_low, small_full, all_top = start_gather(tokens_low, small, top_low)
        small_full = small_full.reshape(width, small.shape[1])
    else:
        prompt_low = lax.all_gather(tokens_low[:prompt], "shard", axis=0, tiled=False, axis_index_groups=groups)
        small_full = gather(small)
        by_rep = lax.all_gather(top_low, "rep", axis=0, tiled=False)
        core_pos = rep_pos + 1 - 2 * (rep_pos % 2)
        all_top = jnp.stack([top_low] + [by_rep[i] for i in (core_pos, (rep_pos + 2) % 4, 3 - rep_pos)])
    prompt_low = prompt_low.reshape(GROUP_SIZE * prompt, width)
    qkv_full = small_full[:, :qkv_columns]
    attn_out_full = small_full[:, qkv_columns : qkv_columns + Q_WIDTH]
    router_full = small_full[:, qkv_columns + Q_WIDTH : qkv_columns + Q_WIDTH + EXPERTS]
    gains = small_full[:, qkv_columns + Q_WIDTH + EXPERTS :].astype(F32)
    attn_gain_full, ffn_gain_full = gains[:, 0], gains[:, 1]
    w_both = jnp.concatenate(
        [
            lax.dynamic_slice_in_dim(w_in, rep_pos * local * 2 * F, local * 2 * F, 1),
            lax.dynamic_slice_in_dim(w_out, rep_pos * local * F, local * F, 1),
        ],
        axis=1,
    )
    w_both, prompt_low = lax.optimization_barrier((w_both, prompt_low))
    w_both = gather(w_both)

    def normed(values):
        scale = rms_scale(values)
        return (values * scale * attn_gain_full).astype(BF16), scale

    def angles_of(positions):
        half = HEAD_SIZE // 2
        inverse_freq = ROPE_BASE ** (-(jnp.arange(half, dtype=F32) * 2.0) / HEAD_SIZE)
        angles = inverse_freq[:, None] * positions.astype(F32)[None, :]
        return jnp.cos(angles)[None], jnp.sin(angles)[None]

    def project(source, start, size, turn):
        rows = dot(qkv_full[:, start : start + size], source, (0, 1))
        rows = rows.reshape(size // HEAD_SIZE, HEAD_SIZE, source.shape[0])
        return (rotate(rows, *turn) if turn is not None else rows).astype(BF16)

    def keys_values(source, turn):
        return jnp.stack([project(source, Q_WIDTH, KV_WIDTH, turn), project(source, Q_WIDTH + KV_WIDTH, KV_WIDTH, None)])

    normed_attn, attn_scale = normed(x_in)
    normed_prompt, _ = normed(prompt_low.astype(F32))
    prompt_turn = angles_of(jnp.arange(GROUP_SIZE * prompt, dtype=jnp.int32))
    own_turn = angles_of(
        jnp.concatenate(
            [
                shard_pos * prompt + jnp.arange(prompt, dtype=jnp.int32),
                branch_len + jnp.arange(CONTINUATION_LEN, dtype=jnp.int32),
            ]
        )
    )
    continued_turn = tuple(part[..., prompt:] for part in own_turn)
    prompt_kv = keys_values(normed_prompt, prompt_turn)
    own_kv = keys_values(normed_attn[prompt:], continued_turn)
    query = project(normed_attn, 0, Q_WIDTH, own_turn)
    where = jnp.stack([shard_pos.astype(jnp.int32), branch_len])
    attn, lse = attn_forward(where, query, prompt_kv, own_kv)
    attn_low = attn.astype(BF16).reshape(Q_WIDTH, count)
    x_mid = x_in + dot(attn_low, attn_out_full, (0, 1))

    ffn_scale = rms_scale(x_mid)
    normed_ffn = (x_mid * ffn_scale * ffn_gain_full).astype(BF16)
    logits = dot(normed_ffn, router_full, (1, 0))
    chosen = jnp.any(route_ids[:, :, None] == jnp.arange(EXPERTS, dtype=jnp.int32), axis=1)
    gates = jax.nn.softmax(jnp.where(chosen, logits, NEGATIVE), axis=-1)
    gates = jnp.where(chosen, gates, 0.0)

    gates_out = jnp.pad(gates.T.reshape(reps, local, count), ((0, 0), (0, 8 - local), (0, 0)))
    all_normed, dx_own, dx_core, dx_far, y_part, dgu, gated, dgate_part = experts(
        normed_ffn, all_top, gates_out, w_both
    )
    grad_from_experts = dx_own.astype(F32) + dx_core.astype(F32) + dx_far.astype(F32)
    grad_gates = dgate_part[:, :local].reshape(EXPERTS, count).T
    to_core = [(i, i + 1 - 2 * (i % 2)) for i in range(reps)]
    to_far = [(i, (i + 2) % reps) for i in range(reps)]
    y_near = y_part[:2].astype(F32) + lax.ppermute(y_part[2:], "rep", to_core).astype(F32)
    y_sum = y_near[0] + lax.ppermute(y_near[1].astype(BF16), "rep", to_far).astype(F32)
    block_out = (x_mid + y_sum).astype(BF16)

    def rep_sum(values):
        for pairs in (to_core, to_far):
            values = (values.astype(F32) + lax.ppermute(values, "rep", pairs).astype(F32)).astype(BF16)
        return values

    def expert_term(left, right):
        return dot(left.reshape(reps * count, width), right.reshape(reps * count, -1), (0, 0)).astype(BF16)

    grad_logits = (gates * (grad_gates - jnp.sum(gates * grad_gates, axis=-1, keepdims=True))).astype(BF16)
    grad_router_w = dot(normed_ffn, grad_logits, (0, 0))
    grad_normed_ffn = grad_from_experts + dot(grad_logits, router_full, (1, 1))
    grad_mid_norm, grad_ffn_gain = rms_backward(x_mid, ffn_scale, ffn_gain_full, grad_normed_ffn)
    grad_mid = grad_top + grad_mid_norm
    grad_branch = grad_mid.astype(BF16)
    grad_attn_w = dot(grad_branch, attn_low, (0, 1))
    grad_attn = dot(attn_out_full, grad_branch, (0, 1)).astype(BF16).reshape(QUERY_HEADS, HEAD_SIZE, count)
    early = jnp.concatenate(
        [
            expert_term(all_normed, dgu),
            expert_term(all_top, gated),
            grad_attn_w.astype(BF16),
            grad_router_w.astype(BF16),
            grad_ffn_gain[:, None].astype(BF16),
        ],
        axis=1,
    )
    early = jnp.pad(early, ((0, 0), (0, -early.shape[1] % LANES)))
    grad_attn, early = lax.optimization_barrier((grad_attn, early))
    early = lax.psum_scatter(early, "shard", scatter_dimension=0, tiled=True)
    expert_columns = local * 3 * F
    expert_rows = lax.all_gather(early[:, :expert_columns], "rep", axis=0, tiled=False)
    early = rep_sum(early[:, expert_columns:])
    attn_rows, router_rows = early[:, :Q_WIDTH], early[:, Q_WIDTH : Q_WIDTH + EXPERTS]
    ffn_gain_rows = early[:, Q_WIDTH + EXPERTS]

    delta = jnp.sum(grad_attn.astype(F32) * attn, axis=1).reshape(KEY_VALUE_HEADS, PER_KEY, count)
    grad_query, grad_prompt_kv, grad_own_kv = attn_backward(
        where, query, prompt_kv, own_kv, grad_attn, lse, delta
    )

    def turn_back(values, turn):
        spun = rotate(values, turn[0], -turn[1])
        return spun.astype(BF16).reshape(-1, values.shape[-1])

    grad_query = turn_back(grad_query, own_turn)
    grad_prompt_kv = jnp.concatenate(
        [
            turn_back(grad_prompt_kv[0].astype(F32), prompt_turn),
            grad_prompt_kv[1].reshape(KV_WIDTH, GROUP_SIZE * prompt),
        ],
        axis=0,
    )
    grad_own_kv = jnp.concatenate(
        [turn_back(grad_own_kv[0], continued_turn), grad_own_kv[1].astype(BF16).reshape(KV_WIDTH, -1)], axis=0
    )
    late = jnp.concatenate(
        [
            dot(normed_attn, grad_query, (0, 1)).astype(BF16),
            (dot(normed_prompt, grad_prompt_kv, (0, 1)) + dot(normed_attn[prompt:], grad_own_kv, (0, 1))).astype(BF16),
        ],
        axis=1,
    )
    late = lax.psum_scatter(late, "shard", scatter_dimension=0, tiled=True)
    late, grad_prompt_kv = lax.optimization_barrier((late, grad_prompt_kv))
    qkv_rows = rep_sum(late)
    attn_gain_rows = jnp.sum(
        qkv_rows.astype(F32) * query_key_value_weight.astype(F32), axis=1
    ) / attn_gain.astype(F32)

    grad_prompt_kv = lax.psum_scatter(
        grad_prompt_kv, "shard", scatter_dimension=1, tiled=True, axis_index_groups=groups
    )
    grad_projected = jnp.concatenate(
        [grad_query, jnp.concatenate([grad_prompt_kv, grad_own_kv], axis=1)], axis=0
    )
    grad_normed_attn = dot(grad_projected, qkv_full, (0, 1))
    grad_x_norm, _ = rms_backward(x_in, attn_scale, attn_gain_full, grad_normed_attn)
    grad_input = grad_mid + grad_x_norm

    in_columns = local * 2 * F
    if flat_path:
        size = outer_mom.shape[-1]

        def lead(first, second, rest):
            parts = [first[None].astype(F32), second[None].astype(F32), rest.reshape(-1, LANES).astype(F32)]
            return jnp.concatenate(parts, axis=0)

        def whole(values):
            return values, values.shape[-1], 0

        weight_flat, _ = flatten(
            size,
            lead(attn_gain, ffn_gain, w_router),
            [whole(query_key_value_weight), whole(w_attn_out), whole(w_in), whole(w_out)],
        )
        total_grad, square = flatten(
            size,
            lead(attn_gain_rows, ffn_gain_rows, router_rows),
            [
                whole(qkv_rows),
                whole(attn_rows),
                (expert_rows, in_columns, 0),
                (expert_rows, expert_columns - in_columns, in_columns // (expert_columns - in_columns)),
            ],
        )
        grad_norm, step_sum = summed_step(square, total_grad, adam_first, adam_second, weight_flat)
        new_first, new_second, new_mom, weight_update = update(
            reps, grad_norm, total_grad, adam_first, adam_second, step_sum, outer_mom
        )
        grad_norm = grad_norm.reshape(())
    else:
        weight_flat = jnp.concatenate(
            [
                portion.astype(F32).reshape(-1)
                for portion in (attn_gain, query_key_value_weight, w_attn_out, ffn_gain, w_router, w_in, w_out)
            ]
        )
        total_grad = jnp.concatenate(
            [
                portion.astype(F32).reshape(-1)
                for portion in (
                    attn_gain_rows,
                    qkv_rows,
                    attn_rows,
                    ffn_gain_rows,
                    router_rows,
                    expert_rows[:, :, :in_columns].transpose(1, 0, 2),
                    expert_rows[:, :, in_columns:].transpose(1, 0, 2),
                )
            ]
        )
        grad_norm = jnp.sqrt(lax.psum(jnp.sum(total_grad * total_grad), "shard"))
        new_first, new_second = moments(
            total_grad,
            adam_first.reshape(-1),
            adam_second.reshape(-1),
            CLIP_NORM / jnp.maximum(grad_norm, CLIP_NORM),
        )
        step = inner_step(new_first, new_second, weight_flat)
        pseudo = -(lax.psum(step.astype(BF16), "rep").astype(F32) / reps)
        new_mom = OUTER_MOMENTUM * outer_mom.reshape(-1) + pseudo
        weight_update = -OUTER_RATE * (pseudo + OUTER_MOMENTUM * new_mom)
    return (
        block_out.reshape(tokens.shape),
        grad_input.reshape(tokens.shape),
        total_grad.reshape(outer_mom.shape),
        grad_norm,
        new_first.reshape(adam_first.shape),
        new_second.reshape(adam_second.shape),
        new_mom.reshape(outer_mom.shape),
        weight_update.reshape(outer_mom.shape),
    )


def solution(mesh):
    by_token = P("rep", "shard", None, None)
    by_state = P("rep", "shard", None)
    by_row = P("shard", None)
    placed = (
        by_token,
        by_token,
        by_token,
        P("rep", "shard"),
        P("shard"),
        by_row,
        by_row,
        P("shard"),
        by_row,
        by_row,
        by_row,
        by_state,
        by_state,
        by_row,
    )
    return jax.shard_map(
        per_device,
        mesh=mesh,
        in_specs=placed,
        out_specs=(by_token, by_token, by_row, P(), by_state, by_state, by_row, by_row),
        check_vma=False,
    )
```

```python
import functools

import jax
import jax.numpy as jnp
from jax import lax
from jax.experimental import pallas as pl
from jax.experimental.pallas import tpu as pltpu
from jax.sharding import PartitionSpec as P

QUERY_HEADS = 16
KEY_VALUE_HEADS = 8
HEAD_SIZE = 64
F = 512
EXPERTS = 16
TOP = 8
GROUP_SIZE = 8
CONTINUATION_LEN = 512
STEP = 10

EPSILON = 1e-06
NEGATIVE = -1e30
ROPE_BASE = 10000.0
BETA_ONE = 0.9
BETA_TWO = 0.95
ADAM_EPS = 1e-08
INNER_RATE = 0.01
DECAY_RATE = 0.1
OUTER_RATE = 0.7
OUTER_MOMENTUM = 0.9
CLIP_NORM = 1.0

LOG2E = 1.4426950408889634
LANES = 128
MIB = 1 << 20
BF16 = jnp.bfloat16
F32 = jnp.float32
PER_KEY = QUERY_HEADS // KEY_VALUE_HEADS
Q_WIDTH = QUERY_HEADS * HEAD_SIZE
KV_WIDTH = KEY_VALUE_HEADS * HEAD_SIZE


def dot(left, right, dims):
    return lax.dot_general(left, right, ((dims[:1], dims[1:]), ((), ())), preferred_element_type=F32)


def split_three(value):
    high = value.astype(BF16)
    rest = value - high.astype(F32)
    middle = rest.astype(BF16)
    low = (rest - middle.astype(F32)).astype(BF16)
    return high, middle, low


def augment_query(q_ref, start, width):
    rows = jnp.concatenate([q_ref[g, :, start : start + width] for g in range(PER_KEY)], axis=1)
    scaled = rows.astype(F32) * (HEAD_SIZE**-0.5 * LOG2E)
    high = scaled.astype(BF16)
    low = (scaled - high.astype(F32)).astype(BF16)
    return rows, high, low


def block_of(ref, index, block):
    span = pl.ds(pl.multiple_of(index * block, block), block)
    return ref[0, 0, :, span], ref[1, 0, :, span]


def causal(width, columns):
    key_pos = lax.broadcasted_iota(jnp.int32, (width, columns), 0)
    query_pos = lax.broadcasted_iota(jnp.int32, (width, columns), 1) % width
    return key_pos <= query_pos


def attn_forward_kernel(where_ref, q_ref, kv_ref, own_ref, o_ref, lse_ref, peak_ref, sum_ref, acc_ref):
    block = own_ref.shape[-1]
    columns = PER_KEY * block
    shard_pos = where_ref[0]
    branch = where_ref[1]

    def advance(query, key, value, mask):
        scores = dot(jnp.concatenate([key, key], axis=0), query, (0, 0))
        if mask is not None:
            scores = jnp.where(mask, scores, NEGATIVE)
        old = peak_ref[...]
        new = jnp.maximum(old, jnp.max(scores, axis=0, keepdims=True))
        probs = jnp.exp2(scores - new).astype(BF16)
        shrink = jnp.exp2(old - new)
        ones = jnp.ones((16, block), BF16)
        part = dot(jnp.concatenate([value, ones], axis=0), probs, (1, 0))
        peak_ref[...] = new
        sum_ref[...] = sum_ref[...] * shrink + part[HEAD_SIZE : HEAD_SIZE + 1]
        acc_ref[...] = acc_ref[...] * shrink + part[:HEAD_SIZE]

    def begin(start):
        _, high, low = augment_query(q_ref, start, block)
        peak_ref[...] = jnp.full_like(peak_ref, NEGATIVE)
        sum_ref[...] = jnp.zeros_like(sum_ref)
        acc_ref[...] = jnp.zeros_like(acc_ref)
        return jnp.concatenate([high, low], axis=0)

    def finish(start):
        total = sum_ref[...]
        result = acc_ref[...] / total
        lse = peak_ref[...] + jnp.log2(total)
        for g in range(PER_KEY):
            o_ref[g, :, start : start + block] = result[:, g * block : (g + 1) * block]
            lse_ref[0, g : g + 1, start : start + block] = lse[:, g * block : (g + 1) * block]

    def full(query):
        def body(index, carry):
            advance(query, *block_of(kv_ref, index, block), None)
            return carry

        return body

    query = begin(0)
    lax.fori_loop(0, shard_pos, full(query), 0)
    advance(query, *block_of(kv_ref, shard_pos, block), causal(block, columns))
    finish(0)

    query = begin(block)
    whole = branch // block
    lax.fori_loop(0, whole, full(query), 0)

    @pl.when(branch % block != 0)
    def _():
        key_pos = lax.broadcasted_iota(jnp.int32, (block, columns), 0)
        advance(query, *block_of(kv_ref, whole, block), key_pos < branch % block)

    advance(query, own_ref[0, 0], own_ref[1, 0], causal(block, columns))
    finish(block)


def attn_forward(where, query, prompt_kv, own_kv):
    tokens = query.shape[-1]
    block = own_kv.shape[-1]
    columns = PER_KEY * block
    keys = prompt_kv.shape[-1]
    return pl.pallas_call(
        attn_forward_kernel,
        grid=(query.shape[0] // PER_KEY,),
        in_specs=[
            pl.BlockSpec(memory_space=pltpu.SMEM),
            pl.BlockSpec((PER_KEY, HEAD_SIZE, tokens), lambda h: (h, 0, 0)),
            pl.BlockSpec((2, 1, HEAD_SIZE, keys), lambda h: (0, h, 0, 0)),
            pl.BlockSpec((2, 1, HEAD_SIZE, block), lambda h: (0, h, 0, 0)),
        ],
        out_specs=[
            pl.BlockSpec((PER_KEY, HEAD_SIZE, tokens), lambda h: (h, 0, 0)),
            pl.BlockSpec((1, PER_KEY, tokens), lambda h: (h, 0, 0)),
        ],
        out_shape=[
            jax.ShapeDtypeStruct(query.shape, F32),
            jax.ShapeDtypeStruct((query.shape[0] // PER_KEY, PER_KEY, tokens), F32),
        ],
        scratch_shapes=[
            pltpu.VMEM((1, columns), F32),
            pltpu.VMEM((1, columns), F32),
            pltpu.VMEM((HEAD_SIZE, columns), F32),
        ],
        compiler_params=pltpu.CompilerParams(vmem_limit_bytes=48 * MIB),
        cost_estimate=pl.CostEstimate(
            flops=4 * tokens * keys * query.shape[0] * HEAD_SIZE,
            bytes_accessed=16 * MIB,
            transcendentals=query.shape[0] * tokens * keys,
        ),
        name="attn_forward",
    )(where, query, prompt_kv, own_kv)


def attn_backward_kernel(
    where_ref, q_ref, kv_ref, own_ref, go_ref, lse_ref, delta_ref, dq_ref, dkv_ref, down_ref, dkv_acc, dq_acc
):
    block = own_ref.shape[-1]
    columns = PER_KEY * block
    shard_pos = where_ref[0]
    branch = where_ref[1]
    ones = jnp.ones((16, block), BF16)
    pad = jnp.zeros((16 - 3, columns), BF16)

    def begin(start):
        rows, high, low = augment_query(q_ref, start, block)

        def lanes(ref):
            return jnp.concatenate([ref[0, g : g + 1, start : start + block] for g in range(PER_KEY)], axis=1)

        lse = split_three(-lanes(lse_ref))
        delta = split_three(-lanes(delta_ref))
        grad = jnp.concatenate([go_ref[g, :, start : start + block] for g in range(PER_KEY)], axis=1)
        query = jnp.concatenate([high, low, *lse, pad], axis=0)
        grad_plus = jnp.concatenate([grad, *delta, pad], axis=0)
        dq_acc[...] = jnp.zeros_like(dq_acc)
        scaled = (rows.astype(F32) * HEAD_SIZE**-0.5).astype(BF16)
        return query, scaled, grad_plus, grad

    def terms(state, key, value, mask):
        query, scaled, grad_plus, grad = state
        scores = dot(jnp.concatenate([key, key, ones], axis=0), query, (0, 0))
        if mask is not None:
            scores = jnp.where(mask, scores, NEGATIVE)
        probs = jnp.exp2(scores)
        grad_probs = dot(jnp.concatenate([value, ones], axis=0), grad_plus, (0, 0))
        grad_scores = (probs * grad_probs).astype(BF16)
        dq_acc[...] += dot(key, grad_scores, (1, 0))
        return dot(scaled, grad_scores, (1, 1)), dot(grad, probs.astype(BF16), (1, 1))

    def add(index, state, mask):
        dk, dv = terms(state, *block_of(kv_ref, index, block), mask)
        span = pl.ds(pl.multiple_of(index * block, block), block)
        dkv_acc[0, :, span] += dk
        dkv_acc[1, :, span] += dv

    def finish(start):
        total = dq_acc[...] * HEAD_SIZE**-0.5
        for g in range(PER_KEY):
            dq_ref[g, :, start : start + block] = total[:, g * block : (g + 1) * block]

    def full(state):
        def body(index, carry):
            add(index, state, None)
            return carry

        return body

    dkv_acc[...] = jnp.zeros_like(dkv_acc)
    state = begin(0)
    lax.fori_loop(0, shard_pos, full(state), 0)
    add(shard_pos, state, causal(block, columns))
    finish(0)

    state = begin(block)
    whole = branch // block
    lax.fori_loop(0, whole, full(state), 0)

    @pl.when(branch % block != 0)
    def _():
        key_pos = lax.broadcasted_iota(jnp.int32, (block, columns), 0)
        add(whole, state, key_pos < branch % block)

    dk, dv = terms(state, own_ref[0, 0], own_ref[1, 0], causal(block, columns))
    down_ref[0, 0] = dk
    down_ref[1, 0] = dv
    finish(block)
    dkv_ref[:, 0] = dkv_acc[...].astype(BF16)


def attn_backward(where, query, prompt_kv, own_kv, grad_out, lse, delta):
    tokens = query.shape[-1]
    block = own_kv.shape[-1]
    columns = PER_KEY * block
    keys = prompt_kv.shape[-1]
    by_head = pl.BlockSpec((PER_KEY, HEAD_SIZE, tokens), lambda h: (h, 0, 0))
    by_keys = pl.BlockSpec((2, 1, HEAD_SIZE, keys), lambda h: (0, h, 0, 0))
    by_own = pl.BlockSpec((2, 1, HEAD_SIZE, block), lambda h: (0, h, 0, 0))
    by_row = pl.BlockSpec((1, PER_KEY, tokens), lambda h: (h, 0, 0))
    return pl.pallas_call(
        attn_backward_kernel,
        grid=(query.shape[0] // PER_KEY,),
        in_specs=[pl.BlockSpec(memory_space=pltpu.SMEM), by_head, by_keys, by_own, by_head, by_row, by_row],
        out_specs=[by_head, by_keys, by_own],
        out_shape=[
            jax.ShapeDtypeStruct(query.shape, F32),
            jax.ShapeDtypeStruct(prompt_kv.shape, BF16),
            jax.ShapeDtypeStruct(own_kv.shape, F32),
        ],
        scratch_shapes=[
            pltpu.VMEM((2, HEAD_SIZE, keys), F32),
            pltpu.VMEM((HEAD_SIZE, columns), F32),
        ],
        compiler_params=pltpu.CompilerParams(vmem_limit_bytes=56 * MIB),
        cost_estimate=pl.CostEstimate(
            flops=10 * tokens * keys * query.shape[0] * HEAD_SIZE,
            bytes_accessed=32 * MIB,
            transcendentals=query.shape[0] * tokens * keys,
        ),
        name="attn_backward",
    )(where, query, prompt_kv, own_kv, grad_out, lse, delta)


MESH = pl.DeviceIdType.MESH
LINE = 4
TOKEN_PARTS = 4


def start_kernel(
    x_ref,
    w_ref,
    top_ref,
    tok_all,
    w_all,
    top_all,
    own_sem,
    line_recv,
    right_send,
    left_send,
    y_send,
    y_recv,
    x_send,
    x_recv,
    core_send,
    core_recv,
    top_send,
    top_recv,
):
    part = tok_all.shape[1] // TOKEN_PARTS
    quarter = w_all.shape[2]
    half = top_ref.shape[0] // 2
    me = lax.axis_index("shard")
    place, column = me // 2, lax.rem(me, 2)
    rep = lax.axis_index("rep")
    far, core = lax.rem(rep + 2, 4), rep + 1 - 2 * lax.rem(rep, 2)
    to_right, to_left, to_y = {"shard": me + 2}, {"shard": me - 2}, {"shard": me + 1 - 2 * column}
    to_far, to_core = {"rep": far}, {"rep": core}
    weights, mirrored = 0, TOKEN_PARTS + 1
    last = TOKEN_PARTS
    streams = TOKEN_PARTS + 2

    def piece(i, origin, side):
        if i == weights:
            return w_all.at[2 * origin + side, rep]
        k = (i if i != mirrored else last) - 1
        return tok_all.at[2 * origin + side, pl.ds(k * part, part)]

    def side_of(i):
        return 1 - column if i == mirrored else column

    def own(i):
        if i == weights:
            return w_ref.at[pl.ds(pl.multiple_of(rep * quarter, quarter), quarter)]
        if i == mirrored:
            return piece(i, place, 1 - column)
        return x_ref.at[pl.ds((i - 1) * part, part)]

    def remote(source, target, send, receive, device):
        return pltpu.make_async_remote_copy(
            src_ref=source, dst_ref=target, send_sem=send, recv_sem=receive, device_id=device, device_id_type=MESH
        )

    def source(i, origin, at_home):
        return own(i) if at_home else piece(i, origin, side_of(i))

    def right(i, origin, at_home=False):
        return remote(
            source(i, origin, at_home),
            piece(i, origin, side_of(i)),
            right_send.at[i, origin],
            line_recv.at[i, origin],
            to_right,
        )

    def left(i, origin, at_home=False):
        return remote(
            source(i, origin, at_home),
            piece(i, origin, side_of(i)),
            left_send.at[i, origin],
            line_recv.at[i, origin],
            to_left,
        )

    def abreast(i, origin, at_home=False):
        return remote(
            source(i, origin, at_home), piece(i, origin, column), y_send.at[i, origin], y_recv.at[i, origin], to_y
        )

    def over_x(origin, side, at_home=False):
        target = piece(weights, origin, side)
        source_ref = own(weights) if at_home else target
        return remote(source_ref, target, x_send.at[origin, side], x_recv.at[origin, side], to_far)

    def over_core(group, origin, side, at_home=False):
        target = w_all.at[2 * origin + side, rep if group == 0 else far]
        source_ref = own(weights) if at_home else target
        return remote(
            source_ref, target, core_send.at[group, origin, side], core_recv.at[group, origin, side], to_core
        )

    def top_far(h):
        return remote(
            top_ref.at[pl.ds(h * half, half)],
            top_all.at[2, pl.ds(h * half, half)],
            top_send.at[0, h],
            top_recv.at[0, h],
            to_far,
        )

    def top_core(h):
        return remote(
            top_ref.at[pl.ds(h * half, half)],
            top_all.at[1, pl.ds(h * half, half)],
            top_send.at[1, h],
            top_recv.at[1, h],
            to_core,
        )

    def top_diagonal(h):
        return remote(
            top_all.at[2, pl.ds(h * half, half)],
            top_all.at[3, pl.ds(h * half, half)],
            top_send.at[2, h],
            top_recv.at[2, h],
            to_core,
        )

    has_right, has_left = place < LINE - 1, place > 0
    barrier = pltpu.get_barrier_semaphore()

    def greet(device):
        pl.semaphore_signal(barrier, inc=1, device_id=device, device_id_type=MESH)

    for device in (to_y, to_far, to_core):
        greet(device)

    @pl.when(has_right)
    def _():
        greet(to_right)

    @pl.when(has_left)
    def _():
        greet(to_left)

    pl.semaphore_wait(barrier, 3 + has_right.astype(jnp.int32) + has_left.astype(jnp.int32))

    def along(i, origin, at_home=False):
        @pl.when(has_right)
        def _():
            right(i, origin, at_home).start()

        @pl.when(has_left)
        def _():
            left(i, origin, at_home).start()

    order = [weights, last] + list(range(1, last))
    for i in order:
        along(i, place, True)
        abreast(i, place, True).start()
        if i == weights:
            over_x(place, column, True).start()
            over_core(0, place, column, True).start()
            for h in (0, 1):
                top_far(h).start()
    for h in (0, 1):
        top_core(h).start()
    own_copies = [
        pltpu.make_async_copy(own(i), piece(i, place, column), own_sem.at[i]) for i in range(streams - 1)
    ]
    own_copies.append(pltpu.make_async_copy(top_ref, top_all.at[0], own_sem.at[streams - 1]))
    for copy in own_copies:
        copy.start()
    abreast(last, place).wait_recv()
    along(mirrored, place, True)

    def weights_across(origin):
        abreast(weights, origin).wait_recv()
        over_x(origin, 1 - column).start()
        over_core(0, origin, 1 - column).start()

    weights_across(place)
    for d in range(1, LINE):
        before, after = place - d, place + d
        from_left, from_right = before >= 0, after < LINE
        for i in [weights, last, mirrored] + list(range(1, last)):

            @pl.when(from_left)
            def _(i=i):
                right(i, before).wait_recv()

                @pl.when(has_right)
                def _():
                    right(i, before).start()

                if i != last and i != mirrored:
                    abreast(i, before).start()
                if i == weights:
                    over_x(before, column).start()
                    over_core(0, before, column).start()

            @pl.when(from_right)
            def _(i=i):
                left(i, after).wait_recv()

                @pl.when(has_left)
                def _():
                    left(i, after).start()

                if i != last and i != mirrored:
                    abreast(i, after).start()
                if i == weights:
                    over_x(after, column).start()
                    over_core(0, after, column).start()

        @pl.when(from_left)
        def _():
            weights_across(before)

        @pl.when(from_right)
        def _():
            weights_across(after)

        if d >= 2:
            h = d - 2
            top_far(h).wait_recv()
            top_diagonal(h).start()

    for origin in range(LINE):
        for side in (0, 1):
            remote(
                w_all.at[2 * origin + side, far],
                w_all.at[2 * origin + side, far],
                x_send.at[origin, side],
                x_recv.at[origin, side],
                to_far,
            ).wait_recv()
            over_core(1, origin, side).start()

    for origin in range(LINE):
        for i in range(1, last):
            abreast(i, origin).wait_recv()
        for side in (0, 1):
            for group in (0, 1):
                over_core(group, origin, side).wait_recv()
    for h in (0, 1):
        top_core(h).wait_recv()
        top_diagonal(h).wait_recv()
        for copy in (top_far(h), top_core(h), top_diagonal(h)):
            copy.wait_send()
    for copy in own_copies:
        copy.wait()
    for origin in range(LINE):
        for i in range(streams):

            @pl.when(has_right & (origin <= place))
            def _(i=i, origin=origin):
                right(i, origin).wait_send()

            @pl.when(has_left & (origin >= place))
            def _(i=i, origin=origin):
                left(i, origin).wait_send()

            if i != last and i != mirrored:
                abreast(i, origin).wait_send()
        for side in (0, 1):
            over_x(origin, side).wait_send()
            for group in (0, 1):
                over_core(group, origin, side).wait_send()
    abreast(last, place).wait_send()


def start_gather(x, small, top):
    rows, width = x.shape
    prompt = rows - CONTINUATION_LEN
    own_rows, columns = small.shape
    dma = pltpu.SemaphoreType.DMA
    streams = TOKEN_PARTS + 2
    anywhere = pl.BlockSpec(memory_space=pl.ANY)
    return pl.pallas_call(
        start_kernel,
        in_specs=[anywhere] * 3,
        out_specs=[anywhere] * 3,
        out_shape=[
            jax.ShapeDtypeStruct((2 * LINE, prompt, width), BF16),
            jax.ShapeDtypeStruct((2 * LINE, 4, own_rows // 4, columns), BF16),
            jax.ShapeDtypeStruct((4, rows, width), BF16),
        ],
        scratch_shapes=[
            dma((streams,)),
            dma((streams, LINE)),
            dma((streams, LINE)),
            dma((streams, LINE)),
            dma((streams, LINE)),
            dma((streams, LINE)),
            dma((LINE, 2)),
            dma((LINE, 2)),
            dma((2, LINE, 2)),
            dma((2, LINE, 2)),
            dma((3, 2)),
            dma((3, 2)),
        ],
        compiler_params=pltpu.CompilerParams(collective_id=2, has_side_effects=True),
        cost_estimate=pl.CostEstimate(flops=0, bytes_accessed=64 * MIB, transcendentals=0),
        name="start_gather",
    )(x, small, top)


ORDER = ((0, 0), (0, 1), (1, 0), (3, 0), (2, 0), (3, 1), (2, 1), (1, 1))
Y_PLACE = (0, 2, 1, 3)


def experts_kernel(
    x_hbm,
    top_hbm,
    gates_ref,
    w_ref,
    all_x,
    dx_own,
    dx_core,
    dx_far,
    y_all,
    dgu_all,
    gh_all,
    dg_all,
    x_buf,
    top_buf,
    y_buf,
    dx_buf,
    dgu_buf,
    gh_buf,
    relay,
    y_acc,
    dx_acc,
    gates_all,
    gates_now,
    dg_now,
    dg_mine,
    in_sem,
    out_sem,
    copy_sem,
    send_sem,
    recv_sem,
    small_send,
    small_recv,
):
    tile = x_buf.shape[1]
    count = w_ref.shape[1] // (3 * F)
    step = pl.program_id(0)
    steps = len(ORDER)
    slot = lax.rem(step, 2)
    me = lax.axis_index("rep")
    home = [me, me + 1 - 2 * lax.rem(me, 2), lax.rem(me + 2, 4), 3 - me]

    def remote(source, target, send, receive, relation):
        return pltpu.make_async_remote_copy(
            src_ref=source,
            dst_ref=target,
            send_sem=send,
            recv_sem=receive,
            device_id={"rep": home[relation]},
            device_id_type=MESH,
        )

    def half(ref, half_index, *lead):
        return ref.at[(*lead, pl.ds(half_index * tile, tile))]

    def to_core(h):
        return remote(half(x_hbm, h), half(all_x, h, me), send_sem.at[0, h], recv_sem.at[0, h], 1)

    def to_far(h):
        return remote(half(x_hbm, h), half(all_x, h, me), send_sem.at[1, h], recv_sem.at[1, h], 2)

    def forward(h):
        part = half(all_x, h, home[2])
        return remote(part, part, send_sem.at[2, h], recv_sem.at[2, h], 1)

    def give(kind, h, buffer):
        if kind == 3:
            return remote(buffer, relay.at[h], send_sem.at[3, h], recv_sem.at[3, h], 1)
        if kind == 2:
            return remote(buffer, half(dx_far, h), send_sem.at[4, h], recv_sem.at[4, h], 2)
        return remote(buffer, half(dx_core, h), send_sem.at[5, h], recv_sem.at[5, h], 1)

    def small_gates(k):
        return remote(gates_ref.at[home[k]], gates_all.at[me], small_send.at[0, k], small_recv.at[0, k], k)

    def small_back(k):
        return remote(dg_mine.at[home[k]], dg_all.at[me], small_send.at[1, k], small_recv.at[1, k], k)

    def load_x(i):
        kind, h = ORDER[i]
        source = half(x_hbm, h) if kind == 0 else half(all_x, h, home[kind])
        return pltpu.make_async_copy(source, x_buf.at[i % 2], in_sem.at[i % 2, 0])

    def load_top(i):
        kind, h = ORDER[i]
        return pltpu.make_async_copy(half(top_hbm, h, kind), top_buf.at[i % 2], in_sem.at[i % 2, 1])

    def stores(i):
        kind, h = ORDER[i]
        out = []
        places = (y_buf, y_all, Y_PLACE[kind]), (dgu_buf, dgu_all, home[kind]), (gh_buf, gh_all, kind)
        for n, (buffer, target, place) in enumerate(places):
            out.append(pltpu.make_async_copy(buffer.at[i % 2], half(target, h, place), out_sem.at[i % 2, n]))
        return out

    def store_dx(i):
        kind, h = ORDER[i]
        if kind == 0:
            return pltpu.make_async_copy(dx_buf.at[i % 2], half(dx_own, h), out_sem.at[i % 2, 3])
        return give(kind, h, dx_buf.at[i % 2])

    def finish(i):
        for copy in stores(i):
            copy.wait()
        if ORDER[i][0] == 0:
            store_dx(i).wait()
        else:
            store_dx(i).wait_send()

    own_copy = pltpu.make_async_copy(x_hbm, all_x.at[me], copy_sem)
    for i in range(steps):
        kind, h = ORDER[i]

        @pl.when(step == i)
        def _(i=i, kind=kind, h=h):
            if i == 0:
                barrier = pltpu.get_barrier_semaphore()
                for k in (1, 2, 3):
                    pl.semaphore_signal(
                        barrier, inc=1, device_id={"rep": home[k]}, device_id_type=MESH
                    )
                pl.semaphore_wait(barrier, 3)
                to_far(0).start()
                for n in (0, 1):
                    to_core(n).start()
                for k in (1, 2, 3):
                    small_gates(k).start()
                own_copy.start()
                load_top(0).start()
                load_x(0).start()
                gates_all[me] = gates_ref[me]
            if i == 1:
                to_far(1).start()
                for n in (0, 1):
                    to_core(n).wait_recv()
            if i == 2:
                for k in (1, 2, 3):
                    small_gates(k).wait_recv()
                to_far(0).wait_recv()
                forward(0).start()
            if i == 3:
                to_far(1).wait_recv()
                forward(1).start()
            if i == 4:
                forward(1).wait_recv()
            load_x(i).wait()
            load_top(i).wait()
            if i + 1 < steps:
                load_top(i + 1).start()
                if i + 1 != 3:
                    load_x(i + 1).start()
            if i >= 2:
                finish(i - 2)
            gates_now[...] = jnp.transpose(gates_all[home[kind]][:, h * tile : (h + 1) * tile])

    x = x_buf[slot]
    top = top_buf[slot]
    columns = []
    for e in range(count):
        w_in = w_ref[:, e * 2 * F : (e + 1) * 2 * F]
        w_out = w_ref[:, (count * 2 + e) * F : (count * 2 + e + 1) * F]
        gate_up = dot(x, w_in, (1, 0))
        g = gate_up[:, :F]
        u = gate_up[:, F:]
        sig = jax.nn.sigmoid(g)
        act = g * sig
        hidden = (act * u).astype(BF16).astype(F32)
        raw = dot(top, w_out, (1, 0))
        columns.append(jnp.sum(hidden * raw, axis=1, keepdims=True))
        gate = gates_now[:, e : e + 1]
        gated = (hidden * gate).astype(BF16)
        gh_buf[slot, :, e * F : (e + 1) * F] = gated
        grad_hidden = raw * gate
        dg = (grad_hidden * u * sig * (1.0 + g * (1.0 - sig))).astype(BF16)
        du = (grad_hidden * act).astype(BF16)
        dgu = jnp.concatenate([dg, du], axis=1)
        dgu_buf[slot, :, e * 2 * F : (e + 1) * 2 * F] = dgu
        y = dot(gated, w_out, (1, 1))
        dx = dot(dgu, w_in, (1, 1))
        if e == 0:
            y_acc[...] = y
            dx_acc[...] = dx
        elif e < count - 1:
            y_acc[...] += y
            dx_acc[...] += dx
        else:
            y_buf[slot] = (y_acc[...] + y).astype(BF16)
            dx_acc[...] += dx
    columns.append(jnp.zeros((tile, 8 - count), F32))
    dg_now[...] = jnp.transpose(jnp.concatenate(columns, axis=1))

    for i in range(steps):
        kind, h = ORDER[i]

        @pl.when(step == i)
        def _(i=i, kind=kind, h=h):
            dg_mine[home[kind], :, h * tile : (h + 1) * tile] = dg_now[...]
            if kind == 2:
                give(3, h, dx_buf.at[0]).wait_recv()
                dx_buf[i % 2] = (dx_acc[...] + relay[h].astype(F32)).astype(BF16)
            else:
                dx_buf[i % 2] = dx_acc[...].astype(BF16)
            store_dx(i).start()
            for copy in stores(i):
                copy.start()
            if i == 2:
                forward(0).wait_recv()
                load_x(3).start()
            if i == steps - 1:
                own_back = pltpu.make_async_copy(dg_mine.at[me], dg_all.at[me], small_send.at[1, 0])
                own_back.start()
                for k in (1, 2, 3):
                    small_back(k).start()
                finish(i - 1)
                finish(i)
                own_copy.wait()
                own_back.wait()
                for n in (0, 1):
                    to_far(n).wait_send()
                    to_core(n).wait_send()
                    forward(n).wait_send()
                    give(2, n, dx_buf.at[0]).wait_recv()
                    give(1, n, dx_buf.at[0]).wait_recv()
                for k in (1, 2, 3):
                    small_gates(k).wait_send()
                    small_back(k).wait()


def experts(x, all_top, gates, weights):
    rows, width = x.shape
    reps = all_top.shape[0]
    count = weights.shape[1] // (3 * F)
    tile = rows // 2
    anywhere = pl.BlockSpec(memory_space=pl.ANY)
    fixed = pl.BlockSpec(weights.shape, lambda i: (0, 0), pipeline_mode=pl.Buffered(1))
    small = pl.BlockSpec((reps, 8, rows), lambda i: (0, 0, 0))
    dma = pltpu.SemaphoreType.DMA
    return pl.pallas_call(
        experts_kernel,
        grid=(len(ORDER),),
        in_specs=[anywhere, anywhere, small, fixed],
        out_specs=[anywhere] * 8,
        out_shape=[
            jax.ShapeDtypeStruct((reps, rows, width), BF16),
            jax.ShapeDtypeStruct((rows, width), BF16),
            jax.ShapeDtypeStruct((rows, width), BF16),
            jax.ShapeDtypeStruct((rows, width), BF16),
            jax.ShapeDtypeStruct((reps, rows, width), BF16),
            jax.ShapeDtypeStruct((reps, rows, count * 2 * F), BF16),
            jax.ShapeDtypeStruct((reps, rows, count * F), BF16),
            jax.ShapeDtypeStruct((reps, 8, rows), F32),
        ],
        scratch_shapes=[
            pltpu.VMEM((2, tile, width), BF16),
            pltpu.VMEM((2, tile, width), BF16),
            pltpu.VMEM((2, tile, width), BF16),
            pltpu.VMEM((2, tile, width), BF16),
            pltpu.VMEM((2, tile, count * 2 * F), BF16),
            pltpu.VMEM((2, tile, count * F), BF16),
            pltpu.VMEM((2, tile, width), BF16),
            pltpu.VMEM((tile, width), F32),
            pltpu.VMEM((tile, width), F32),
            pltpu.VMEM((reps, 8, rows), F32),
            pltpu.VMEM((tile, 8), F32),
            pltpu.VMEM((8, tile), F32),
            pltpu.VMEM((reps, 8, rows), F32),
            dma((2, 2)),
            dma((2, 4)),
            dma,
            dma((6, 2)),
            dma((6, 2)),
            dma((2, 4)),
            dma((2, 4)),
        ],
        compiler_params=pltpu.CompilerParams(
            vmem_limit_bytes=58 * MIB, collective_id=1, has_side_effects=True
        ),
        cost_estimate=pl.CostEstimate(
            flops=12 * reps * rows * width * count * F,
            bytes_accessed=80 * MIB,
            transcendentals=reps * rows * count * F,
        ),
        name="experts",
    )(x, all_top, gates, weights)


def send_to(source, target, send, receive, device):
    return pltpu.make_async_remote_copy(
        src_ref=source, dst_ref=target, send_sem=send, recv_sem=receive, device_id=device, device_id_type=MESH
    )


def line_reduce(parts, y_buf, right_buf, left_buf, y_sems, right_sems, left_sems):
    me = lax.axis_index("shard")
    place, side = me // 2, lax.rem(me, 2)
    to_y, to_right, to_left = {"shard": me + 1 - 2 * side}, {"shard": me + 2}, {"shard": me - 2}

    def across(c):
        return send_to(parts.at[c, 1 - side], y_buf.at[c], y_sems.at[0, c], y_sems.at[1, c], to_y)

    def add_across(c):
        across(c).wait_recv()
        for p in range(LINE):
            parts[c, side, p] = (parts[c, side, p].astype(F32) + y_buf[c, p].astype(F32)).astype(BF16)

    def hop(c, p, buf, sems, device, first):
        source = parts.at[c, side, p] if first else buf.at[c, p]
        return send_to(source, buf.at[c, p], sems.at[0, c, p], sems.at[1, c, p], device)

    def run(c, p, buf, sems, device, is_first, passes):
        @pl.when(passes & is_first)
        def _():
            hop(c, p, buf, sems, device, True).start()

        @pl.when(passes & jnp.logical_not(is_first))
        def _():
            hop(c, p, buf, sems, device, False).wait_recv()
            buf[c, p] = (parts[c, side, p].astype(F32) + buf[c, p].astype(F32)).astype(BF16)
            hop(c, p, buf, sems, device, False).start()

    def step_right(c):
        for p in range(1, LINE):
            run(c, p, right_buf, right_sems, to_right, place == 0, place < p)

    def step_left(c):
        for p in range(LINE - 1):
            run(c, p, left_buf, left_sems, to_left, place == LINE - 1, place > p)

    def collect(c, total):
        total[...] = parts[c, side, place].astype(F32)

        @pl.when(place > 0)
        def _():
            hop(c, place, right_buf, right_sems, to_right, False).wait_recv()
            total[...] += right_buf[c, place].astype(F32)

        @pl.when(place < LINE - 1)
        def _():
            hop(c, place, left_buf, left_sems, to_left, False).wait_recv()
            total[...] += left_buf[c, place].astype(F32)

    def drain(c):
        across(c).wait_send()
        for p in range(1, LINE):

            @pl.when(place < p)
            def _(p=p):
                hop(c, p, right_buf, right_sems, to_right, False).wait_send()

        for p in range(LINE - 1):

            @pl.when(place > p)
            def _(p=p):
                hop(c, p, left_buf, left_sems, to_left, False).wait_send()

    def greet(extra):
        barrier = pltpu.get_barrier_semaphore()
        for device in [to_y] + extra:
            pl.semaphore_signal(barrier, inc=1, device_id=device, device_id_type=MESH)
        has_right, has_left = place < LINE - 1, place > 0

        @pl.when(has_right)
        def _():
            pl.semaphore_signal(barrier, inc=1, device_id=to_right, device_id_type=MESH)

        @pl.when(has_left)
        def _():
            pl.semaphore_signal(barrier, inc=1, device_id=to_left, device_id_type=MESH)

        count = 1 + len(extra) + has_right.astype(jnp.int32) + has_left.astype(jnp.int32)
        pl.semaphore_wait(barrier, count)

    return place, across, add_across, step_right, step_left, collect, drain, greet


def between(step, low, high, body):
    @pl.when((step >= low) & (step < high))
    def _():
        body()


def expert_grads_kernel(
    xt_ref,
    tt_ref,
    dgu_ref,
    gh_ref,
    out_ref,
    left_op,
    right_op,
    parts,
    y_buf,
    right_buf,
    left_buf,
    total,
    mine,
    load_sem,
    lhs_sem,
    y_sems,
    right_sems,
    left_sems,
    own_sem,
    far_sems,
    near_sems,
    pass_sems,
):
    n = parts.shape[0]
    columns = right_op.shape[2]
    first = dgu_ref.shape[1] // columns
    rows = parts.shape[3]
    rep = lax.axis_index("rep")
    far = lax.rem(rep + 2, 4)
    to_core, to_far = {"rep": rep + 1 - 2 * lax.rem(rep, 2)}, {"rep": far}
    place, across, add_across, step_right, step_left, collect, drain, greet = line_reduce(
        parts, y_buf, right_buf, left_buf, y_sems, right_sems, left_sems
    )

    def load(c, act):
        slot = lax.rem(c, 2)

        @pl.when(c < first)
        def _():
            here = pl.ds(pl.multiple_of(c * columns, columns), columns)
            act(pltpu.make_async_copy(dgu_ref.at[:, here], right_op.at[slot], load_sem.at[slot]))

        @pl.when(c >= first)
        def _():
            here = pl.ds(pl.multiple_of((c - first) * columns, columns), columns)
            act(pltpu.make_async_copy(gh_ref.at[:, here], right_op.at[slot], load_sem.at[slot]))

    def start(copy):
        copy.start()

    def wait(copy):
        copy.wait()

    def place_of(owner, c):
        return out_ref.at[owner, :, pl.ds(pl.multiple_of(c * columns, columns), columns)]

    def over_x(c):
        return send_to(mine.at[c], place_of(rep, c), far_sems.at[0, c], far_sems.at[1, c], to_far)

    def over_core(c):
        return send_to(mine.at[c], place_of(rep, c), near_sems.at[0, c], near_sems.at[1, c], to_core)

    def keep(c):
        return pltpu.make_async_copy(mine.at[c], place_of(rep, c), own_sem.at[c])

    def pass_on(c):
        return send_to(place_of(far, c), place_of(far, c), pass_sems.at[0, c], pass_sems.at[1, c], to_core)

    lhs = pltpu.make_async_copy(xt_ref, left_op, lhs_sem)
    lhs.start()
    load(0, start)
    greet([to_core, to_far])
    lhs.wait()

    def produce(c):
        @pl.when(c == first)
        def _():
            swap = pltpu.make_async_copy(tt_ref, left_op, lhs_sem)
            swap.start()
            swap.wait()

        load(c, wait)

        @pl.when(c + 1 < n)
        def _():
            load(c + 1, start)

        result = dot(left_op[...], right_op[lax.rem(c, 2)], (1, 0)).astype(BF16)
        for t in range(2 * LINE):
            parts[c, t % 2, t // 2] = result[t * rows : (t + 1) * rows]
        across(c).start()

    def finish(c):
        collect(c, total)
        mine[c] = total[...].astype(BF16)
        over_x(c).start()
        over_core(c).start()
        keep(c).start()

    def forward(c):
        over_x(c).wait_recv()
        pass_on(c).start()

    def step(i, carry):
        between(i, 0, n, lambda: produce(i))
        between(i, 1, n + 1, lambda: add_across(i - 1))
        to_right_chunk, to_left_chunk = i - 1 - place, i - LINE + place
        between(to_right_chunk, 0, n, lambda: step_right(to_right_chunk))
        between(to_left_chunk, 0, n, lambda: step_left(to_left_chunk))
        between(i, 5, n + 5, lambda: finish(i - 5))
        between(i, 7, n + 7, lambda: forward(i - 7))
        return carry

    lax.fori_loop(0, n + 7, step, 0)

    def end(c, carry):
        drain(c)
        over_x(c).wait_send()
        over_core(c).wait()
        keep(c).wait()
        pass_on(c).wait()
        return carry

    lax.fori_loop(0, n, end, 0)


def expert_grads(x_t, top_t, dgu, gated, columns=256):
    width, tokens = x_t.shape
    wide = dgu.shape[1] + gated.shape[1]
    n = wide // columns
    rows = width // (2 * LINE)
    dma = pltpu.SemaphoreType.DMA
    anywhere = pl.BlockSpec(memory_space=pl.ANY)
    return pl.pallas_call(
        expert_grads_kernel,
        in_specs=[anywhere] * 4,
        out_specs=anywhere,
        out_shape=jax.ShapeDtypeStruct((4, rows, wide), BF16),
        scratch_shapes=[
            pltpu.VMEM((width, tokens), BF16),
            pltpu.VMEM((2, tokens, columns), BF16),
            pltpu.VMEM((n, 2, LINE, rows, columns), BF16),
            pltpu.VMEM((n, LINE, rows, columns), BF16),
            pltpu.VMEM((n, LINE, rows, columns), BF16),
            pltpu.VMEM((n, LINE, rows, columns), BF16),
            pltpu.VMEM((rows, columns), F32),
            pltpu.VMEM((n, rows, columns), BF16),
            dma((2,)),
            dma,
            dma((2, n)),
            dma((2, n, LINE)),
            dma((2, n, LINE)),
            dma((n,)),
            dma((2, n)),
            dma((2, n)),
            dma((2, n)),
        ],
        compiler_params=pltpu.CompilerParams(vmem_limit_bytes=60 * MIB, collective_id=4, has_side_effects=True),
        cost_estimate=pl.CostEstimate(
            flops=2 * width * tokens * wide, bytes_accessed=80 * MIB, transcendentals=0
        ),
        name="expert_grads",
    )(x_t, top_t, dgu, gated)


def late_reduce_kernel(
    in_ref,
    out_ref,
    own_buf,
    core_buf,
    parts,
    y_buf,
    right_buf,
    left_buf,
    total,
    mine,
    far_buf,
    whole,
    load_sem,
    core_sems,
    y_sems,
    right_sems,
    left_sems,
    own_sem,
    far_sems,
    near_sems,
):
    n = parts.shape[0]
    rows, columns = parts.shape[3:]
    rep = lax.axis_index("rep")
    half = lax.rem(rep, 2)
    to_core, to_far = {"rep": rep + 1 - 2 * half}, {"rep": lax.rem(rep + 2, 4)}
    place, across, add_across, step_right, step_left, collect, drain, greet = line_reduce(
        parts, y_buf, right_buf, left_buf, y_sems, right_sems, left_sems
    )

    def span(which, c):
        return pl.ds(pl.multiple_of((which * n + c) * columns, columns), columns)

    def load(c):
        return pltpu.make_async_copy(in_ref.at[:, span(half, c)], own_buf.at[c], load_sem.at[c])

    def from_core(c):
        return send_to(
            in_ref.at[:, span(1 - half, c)], core_buf.at[c], core_sems.at[0, c], core_sems.at[1, c], to_core
        )

    def over_x(c):
        return send_to(mine.at[c], far_buf.at[c], far_sems.at[0, c], far_sems.at[1, c], to_far)

    def over_core(c):
        return send_to(
            whole.at[c], out_ref.at[:, span(half, c)], near_sems.at[0, c], near_sems.at[1, c], to_core
        )

    def keep(c):
        return pltpu.make_async_copy(whole.at[c], out_ref.at[:, span(half, c)], own_sem.at[c])

    for c in range(n):
        load(c).start()
    greet([to_core, to_far])
    for c in range(n):
        from_core(c).start()

    def produce(c):
        load(c).wait()
        from_core(c).wait_recv()
        for t in range(2 * LINE):
            here = pl.ds(t * rows, rows)
            parts[c, t % 2, t // 2] = (own_buf[c, here].astype(F32) + core_buf[c, here].astype(F32)).astype(BF16)
        across(c).start()

    def finish(c):
        collect(c, total)
        mine[c] = total[...].astype(BF16)
        over_x(c).start()

    def complete(c):
        over_x(c).wait_recv()
        whole[c] = (mine[c].astype(F32) + far_buf[c].astype(F32)).astype(BF16)
        over_core(c).start()
        keep(c).start()

    def step(i, carry):
        between(i, 0, n, lambda: produce(i))
        between(i, 1, n + 1, lambda: add_across(i - 1))
        to_right_chunk, to_left_chunk = i - 1 - place, i - LINE + place
        between(to_right_chunk, 0, n, lambda: step_right(to_right_chunk))
        between(to_left_chunk, 0, n, lambda: step_left(to_left_chunk))
        between(i, LINE, n + LINE, lambda: finish(i - LINE))
        between(i, LINE + 1, n + LINE + 1, lambda: complete(i - LINE - 1))
        return carry

    lax.fori_loop(0, n + LINE + 1, step, 0)

    def end(c, carry):
        drain(c)
        from_core(c).wait_send()
        over_x(c).wait_send()
        over_core(c).wait_send()
        keep(c).wait()
        send_to(
            whole.at[c], out_ref.at[:, span(1 - half, c)], near_sems.at[0, c], near_sems.at[1, c], to_core
        ).wait_recv()
        return carry

    lax.fori_loop(0, n, end, 0)


def late_reduce(values, columns=256):
    width, wide = values.shape
    n = wide // 2 // columns
    rows = width // (2 * LINE)
    dma = pltpu.SemaphoreType.DMA
    anywhere = pl.BlockSpec(memory_space=pl.ANY)
    return pl.pallas_call(
        late_reduce_kernel,
        in_specs=[anywhere],
        out_specs=anywhere,
        out_shape=jax.ShapeDtypeStruct((rows, wide), BF16),
        scratch_shapes=[
            pltpu.VMEM((n, width, columns), BF16),
            pltpu.VMEM((n, width, columns), BF16),
            pltpu.VMEM((n, 2, LINE, rows, columns), BF16),
            pltpu.VMEM((n, LINE, rows, columns), BF16),
            pltpu.VMEM((n, LINE, rows, columns), BF16),
            pltpu.VMEM((n, LINE, rows, columns), BF16),
            pltpu.VMEM((rows, columns), F32),
            pltpu.VMEM((n, rows, columns), BF16),
            pltpu.VMEM((n, rows, columns), BF16),
            pltpu.VMEM((n, rows, columns), BF16),
            dma((n,)),
            dma((2, n)),
            dma((2, n)),
            dma((2, n, LINE)),
            dma((2, n, LINE)),
            dma((n,)),
            dma((2, n)),
            dma((2, n)),
        ],
        compiler_params=pltpu.CompilerParams(vmem_limit_bytes=48 * MIB, collective_id=5, has_side_effects=True),
        cost_estimate=pl.CostEstimate(flops=0, bytes_accessed=16 * MIB, transcendentals=0),
        name="late_reduce",
    )(values)


def flatten_kernel(starts, lead_ref, *refs):
    parts, flat_ref, square_ref = refs[: len(starts)], refs[len(starts)], refs[len(starts) + 1]
    scratch, sems = refs[len(starts) + 2 : -1], refs[-1]
    step = pl.program_id(0)
    steps = pl.num_programs(0)
    slot = lax.rem(step, 2)
    flat = flat_ref.reshape(flat_ref.shape[1] // LANES, LANES)
    lead_places = ((0, 0, 1), (1, starts[2] - 17 , 1), (2, starts[2] - 16, 16))

    def copies(index, where):
        out = []
        for n, (start, buffer) in enumerate(zip(starts, scratch)):
            size = buffer.shape[1]
            out.append(pltpu.make_async_copy(buffer.at[where], flat.at[pl.ds(start + index * size, size)], sems.at[where, n]))
        return out

    @pl.when(step == 0)
    def _():
        square_ref[...] = jnp.sum(lead_ref[...] * lead_ref[...], keepdims=True).reshape(1, 1) + jnp.zeros_like(square_ref)
        for n, (source, target, size) in enumerate(lead_places):
            copy = pltpu.make_async_copy(lead_ref.at[pl.ds(source, size)], flat.at[pl.ds(target, size)], sems.at[2, n])
            copy.start()
            copy.wait()

    @pl.when(step >= 2)
    def _():
        for copy in copies(step - 2, slot):
            copy.wait()

    total = jnp.zeros((8, LANES), F32)
    for part, buffer in zip(parts, scratch):
        rows = part.shape[-2]
        wide = buffer.shape[1] // rows
        reps = part.shape[0] if len(part.shape) == 3 else 1
        each = wide // reps
        for r in range(reps):
            for c in range(each):
                lanes = slice(c * LANES, (c + 1) * LANES)
                value = (part[r, :, lanes] if len(part.shape) == 3 else part[:, lanes]).astype(F32)
                buffer[slot, pl.ds(r * each + c, rows, stride=wide), :] = value
                square = value * value
                for k in range(0, rows, 8):
                    total += square[k : k + 8]
    square_ref[...] += jnp.sum(total, keepdims=True).reshape(1, 1)
    for copy in copies(step, slot):
        copy.start()

    @pl.when(step == steps - 1)
    def _():
        for copy in copies(step - 1, 1 - slot):
            copy.wait()
        for copy in copies(step, slot):
            copy.wait()

def flatten(size, lead, parts, tile=16):
    rows = parts[0][0].shape[-2]
    widths = [columns * (p.shape[0] if p.ndim == 3 else 1) // LANES for p, columns, _ in parts]
    starts, at = [], 1
    for n, w in enumerate(widths):
        if n == 2: at += 1 + 16
        starts.append(at); at += rows * w
    specs = []
    for p, columns, place in parts:
        if p.ndim == 3:
            specs.append(pl.BlockSpec((p.shape[0], tile, columns), lambda i, place=place: (0, i, place)))
        else:
            specs.append(pl.BlockSpec((tile, columns), lambda i, place=place: (i, place)))
    return pl.pallas_call(
        functools.partial(flatten_kernel, starts),
        grid=(rows // tile,),
        in_specs=[pl.BlockSpec(lead.shape, lambda i: (0, 0))] + specs,
        out_specs=[pl.BlockSpec(memory_space=pl.ANY), pl.BlockSpec((1, 1), lambda i: (0, 0))],
        out_shape=[jax.ShapeDtypeStruct((1, size), F32), jax.ShapeDtypeStruct((1, 1), F32)],
        scratch_shapes=[pltpu.VMEM((2, tile * w, LANES), F32) for w in widths] + [pltpu.SemaphoreType.DMA((3, 4))],
        compiler_params=pltpu.CompilerParams(vmem_limit_bytes=48 * MIB),
        name="flatten",
    )(lead, *[p for p, _, _ in parts])

HALF_ROWS = 1056


def moments(grad, first, second, scale):
    clipped = grad * scale
    new_first = BETA_ONE * first + (1.0 - BETA_ONE) * clipped
    new_second = BETA_TWO * second + (1.0 - BETA_TWO) * clipped * clipped
    return new_first, new_second


def inner_step(new_first, new_second, weight):
    root = jnp.sqrt(new_second * (1.0 / (1.0 - BETA_TWO**STEP))) + ADAM_EPS
    return -INNER_RATE * (new_first * (1.0 / (1.0 - BETA_ONE**STEP)) / root + DECAY_RATE * weight)


def flat_chunks(rows):
    chunks, at, half_at = [], 0, 0
    while at < rows:
        size = min(2 * HALF_ROWS, rows - at)
        half = -(-size // 32) * 16
        chunks.append((at, size, half_at, half))
        at, half_at = at + size, half_at + half
    return chunks


def step_kernel(
    square_ref,
    g_ref,
    f_ref,
    s_ref,
    w_ref,
    norm_ref,
    total,
    g_buf,
    f_buf,
    s_buf,
    w_buf,
    step_buf,
    near_buf,
    far_buf,
    sum_buf,
    square_mine,
    square_all,
    in_sem,
    near_send,
    near_recv,
    far_send,
    far_recv,
    back_send,
    back_recv,
    own_sem,
    square_send,
    square_recv,
):
    rows = g_ref.shape[-1] // LANES
    chunks = flat_chunks(rows)
    count = len(chunks)
    shards = lax.axis_size("shard")
    shard, rep = lax.axis_index("shard"), lax.axis_index("rep")
    side = lax.rem(rep, 2)
    to_core, to_far = {"rep": rep + 1 - 2 * side}, {"rep": lax.rem(rep + 2, 4)}

    def other(k):
        return {"shard": lax.rem(shard + k, shards)}

    barrier = pltpu.get_barrier_semaphore()
    greeted = [to_core, to_far] + [other(k) for k in range(1, shards)]
    for device in greeted:
        pl.semaphore_signal(barrier, inc=1, device_id=device, device_id_type=MESH)

    def loads(i):
        at, size, _, _ = chunks[i]
        pairs = (g_ref, g_buf), (f_ref.at[0], f_buf), (s_ref.at[0], s_buf), (w_ref, w_buf)
        return [
            pltpu.make_async_copy(
                ref.at[:, pl.ds(at * LANES, size * LANES)],
                buf.at[i % 2, :, pl.ds(0, size * LANES)],
                in_sem.at[i % 2, n],
            )
            for n, (ref, buf) in enumerate(pairs)
        ]

    def remote(source, target, send, receive, device):
        return pltpu.make_async_remote_copy(
            src_ref=source, dst_ref=target, send_sem=send, recv_sem=receive, device_id=device, device_id_type=MESH
        )

    def near(i):
        _, _, at, half = chunks[i]
        span = pl.ds(at, half)
        return remote(step_buf.at[1 - side, span], near_buf.at[span], near_send.at[i], near_recv.at[i], to_core)

    def far(i):
        _, _, at, half = chunks[i]
        span = pl.ds(at, half)
        return remote(step_buf.at[side, span], far_buf.at[span], far_send.at[i], far_recv.at[i], to_far)

    def back(i):
        _, _, at, half = chunks[i]
        span = pl.ds(at, half)
        return remote(sum_buf.at[span], total.at[side, span], back_send.at[i], back_recv.at[i], to_core)

    def keep(i):
        _, _, at, half = chunks[i]
        span = pl.ds(at, half)
        return pltpu.make_async_copy(sum_buf.at[span], total.at[side, span], own_sem.at[i])

    for copy in loads(0):
        copy.start()
    pl.semaphore_wait(barrier, len(greeted))

    def square_copy(k):
        return remote(square_mine, square_all.at[shard], square_send.at[k], square_recv.at[shard], other(k))

    square_mine[...] = jnp.broadcast_to(square_ref[...], square_mine.shape)
    square_all[shard] = square_mine[...]
    for k in range(1, shards):
        square_copy(k).start()
    for k in range(1, shards):
        source = lax.rem(shard + k, shards)
        remote(
            square_mine, square_all.at[source], square_send.at[k], square_recv.at[source], other(k)
        ).wait_recv()
    norm = jnp.sqrt(jnp.sum(square_all[...], axis=0))
    norm_ref[...] = norm[:1, :1]
    scale = (CLIP_NORM / jnp.maximum(norm, CLIP_NORM))[:1]

    def blocks(size):
        return 48 if size % 48 == 0 else 16

    def compute(i):
        _, _, at, half = chunks[i]
        block = blocks(half)
        for h in (0, 1):

            def body(j, carry):
                here = pl.multiple_of(j * block, 16)
                span = pl.ds(pl.multiple_of((h * half + here) * LANES, LANES), block * LANES)
                grad, first, second, weight = (
                    buf[i % 2, :, span].reshape(block, LANES) for buf in (g_buf, f_buf, s_buf, w_buf)
                )
                new_first, new_second = moments(grad, first, second, scale)
                step = inner_step(new_first, new_second, weight)
                step_buf[h, pl.ds(at + here, block)] = step.astype(BF16)
                return carry

            lax.fori_loop(0, half // block, body, 0)

    def add(i, left, right, target):
        _, _, at, half = chunks[i]
        block = blocks(half)

        def body(j, carry):
            span = pl.ds(pl.multiple_of(at + j * block, 16), block)
            target[span] = (left[span].astype(F32) + right[span].astype(F32)).astype(BF16)
            return carry

        lax.fori_loop(0, half // block, body, 0)

    for i in range(count + 2):
        if i < count:
            for copy in loads(i):
                copy.wait()
            if i + 1 < count:
                for copy in loads(i + 1):
                    copy.start()
            compute(i)
            near(i).start()
        if 1 <= i <= count:
            near(i - 1).wait_recv()
            add(i - 1, step_buf.at[side], near_buf, step_buf.at[side])
            far(i - 1).start()
        if i >= 2:
            far(i - 2).wait_recv()
            add(i - 2, step_buf.at[side], far_buf, sum_buf)
            back(i - 2).start()
            keep(i - 2).start()
    for k in range(1, shards):
        square_copy(k).wait_send()
    for i in range(count):
        near(i).wait_send()
        far(i).wait_send()
        back(i).wait_send()
        keep(i).wait()
        _, _, at, half = chunks[i]
        span = pl.ds(at, half)
        remote(
            sum_buf.at[span], total.at[1 - side, span], back_send.at[i], back_recv.at[i], to_core
        ).wait_recv()


def summed_step(square, grad, first, second, weight):
    rows = grad.shape[-1] // LANES
    chunks = flat_chunks(rows)
    count = len(chunks)
    halves = sum(chunk[3] for chunk in chunks)
    size = chunks[0][3] * 2
    shards = lax.axis_size("shard")
    dma = pltpu.SemaphoreType.DMA
    anywhere = pl.BlockSpec(memory_space=pl.ANY)
    return pl.pallas_call(
        step_kernel,
        in_specs=[pl.BlockSpec(memory_space=pltpu.VMEM)] + [anywhere] * 4,
        out_specs=[pl.BlockSpec(memory_space=pltpu.VMEM), anywhere],
        out_shape=[jax.ShapeDtypeStruct((1, 1), F32), jax.ShapeDtypeStruct((2, halves, LANES), BF16)],
        scratch_shapes=[pltpu.VMEM((2, 1, size * LANES), F32)] * 4
        + [
            pltpu.VMEM((2, halves, LANES), BF16),
            pltpu.VMEM((halves, LANES), BF16),
            pltpu.VMEM((halves, LANES), BF16),
            pltpu.VMEM((halves, LANES), BF16),
            pltpu.VMEM((8, LANES), F32),
            pltpu.VMEM((shards, 8, LANES), F32),
            dma((2, 4)),
        ]
        + [dma((count,))] * 7
        + [dma((shards,))] * 2,
        compiler_params=pltpu.CompilerParams(
            vmem_limit_bytes=48 * MIB, collective_id=3, has_side_effects=True
        ),
        cost_estimate=pl.CostEstimate(flops=0, bytes_accessed=64 * MIB, transcendentals=0),
        name="summed_step",
    )(square, grad, first, second, weight)


def update_kernel(
    reps, norm_ref, g, f, s, total, mom, nf, ns, nm, up, tg, tf, ts, tm, tt, tnf, tns, tnm, tup, sems
):
    rows = g.shape[-1] // LANES
    chunks = flat_chunks(rows)
    whole = [c for c in chunks if c[1] == 2 * HALF_ROWS]
    scale = CLIP_NORM / jnp.maximum(norm_ref[...], CLIP_NORM)

    def body(g_ref, f_ref, s_ref, t_ref, m_ref, nf_ref, ns_ref, nm_ref, up_ref):
        half = t_ref.shape[1]
        size = g_ref.shape[0]
        nf_ref[...], ns_ref[...] = moments(g_ref[...], f_ref[...], s_ref[...], scale)
        for h in (0, 1):
            span = slice(h * half, min((h + 1) * half, size))
            pseudo = t_ref[h, : span.stop - span.start].astype(F32) * (-1.0 / reps)
            new = OUTER_MOMENTUM * m_ref[span] + pseudo
            nm_ref[span] = new
            up_ref[span] = -OUTER_RATE * (pseudo + OUTER_MOMENTUM * new)

    def view(ref):
        return ref.reshape(rows, LANES)

    ins, outs = [view(g), view(f), view(s), total, view(mom)], [view(r) for r in (nf, ns, nm, up)]
    wide = pl.BlockSpec((2 * HALF_ROWS, LANES), lambda i: (i, 0))
    halves = pl.BlockSpec((2, HALF_ROWS, LANES), lambda i: (0, i, 0))
    if whole:
        pltpu.emit_pipeline(
            body, grid=(len(whole),), in_specs=[wide, wide, wide, halves, wide], out_specs=[wide] * 4
        )(*ins, *outs)
    for at, size, half_at, half in chunks[len(whole) :]:

        def part(n, ref):
            return ref.at[:, pl.ds(half_at, half)] if n == 3 else ref.at[pl.ds(at, size)]

        copies = [
            pltpu.make_async_copy(part(n, ref), buf, sems.at[n]) for n, (ref, buf) in enumerate(zip(ins, (tg, tf, ts, tt, tm)))
        ]
        for copy in copies:
            copy.start()
        for copy in copies:
            copy.wait()
        body(tg, tf, ts, tt, tm, tnf, tns, tnm, tup)
        copies = [
            pltpu.make_async_copy(buf, ref.at[pl.ds(at, size)], sems.at[n])
            for n, (buf, ref) in enumerate(zip((tnf, tns, tnm, tup), outs))
        ]
        for copy in copies:
            copy.start()
        for copy in copies:
            copy.wait()


def update(reps, norm, grad, first, second, total, mom):
    _, size, _, half = flat_chunks(grad.shape[-1] // LANES)[-1]
    anywhere = pl.BlockSpec(memory_space=pl.ANY)
    tail = pltpu.VMEM((size, LANES), F32)
    return pl.pallas_call(
        functools.partial(update_kernel, reps),
        in_specs=[pl.BlockSpec(memory_space=pltpu.VMEM)] + [anywhere] * 5,
        out_specs=[anywhere] * 4,
        out_shape=[jax.ShapeDtypeStruct(ref.shape, F32) for ref in (first, second, mom, mom)],
        scratch_shapes=[tail] * 4
        + [pltpu.VMEM((2, half, LANES), BF16)]
        + [tail] * 4
        + [pltpu.SemaphoreType.DMA((5,))],
        compiler_params=pltpu.CompilerParams(vmem_limit_bytes=48 * MIB),
        cost_estimate=pl.CostEstimate(flops=0, bytes_accessed=120 * MIB, transcendentals=0),
        name="update",
    )(norm, grad, first, second, total, mom)


def rms_scale(rows):
    return lax.rsqrt(jnp.mean(rows * rows, axis=-1, keepdims=True) + EPSILON)


def rms_backward(rows, scale, gain, grad_out):
    grad_gain = jnp.sum(grad_out * rows * scale, axis=0)
    inner = jnp.sum(grad_out * gain * rows, axis=-1, keepdims=True)
    grad_in = scale * gain * grad_out - rows * scale * scale * scale * inner / rows.shape[-1]
    return grad_in, grad_gain


def rotate(rows, cosine, sine):
    half = HEAD_SIZE // 2
    front, back = rows[:, :half], rows[:, half:]
    return jnp.concatenate([front * cosine - back * sine, back * cosine + front * sine], axis=1)


def per_device(
    tokens,
    cotangent,
    routes,
    branch,
    attn_gain,
    query_key_value_weight,
    w_attn_out,
    ffn_gain,
    w_router,
    w_in,
    w_out,
    adam_first,
    adam_second,
    outer_mom,
):
    shards = lax.axis_size("shard")
    reps = lax.axis_size("rep")
    count = tokens.shape[2]
    width = tokens.shape[3]
    prompt = count - CONTINUATION_LEN
    local = EXPERTS // reps
    groups = None
    if shards > GROUP_SIZE:
        groups = [list(range(i, i + GROUP_SIZE)) for i in range(0, shards, GROUP_SIZE)]
    shard_pos = lax.axis_index("shard") % GROUP_SIZE
    rep_pos = lax.axis_index("rep")
    branch_len = branch.reshape(())
    x_in = tokens.reshape(count, width).astype(F32)
    top_low = cotangent.reshape(count, width)
    grad_top = top_low.astype(F32)
    route_ids = routes.reshape(count, TOP)
    gather = functools.partial(lax.all_gather, axis_name="shard", axis=0, tiled=True)
    rows = width // shards
    qkv_columns = Q_WIDTH + 2 * KV_WIDTH
    fast = shards == 2 * LINE and reps == 4 and rows == LANES
    flat_path = fast and outer_mom.shape[-1] % LANES == 0

    small = jnp.concatenate(
        [query_key_value_weight, w_attn_out, w_router, attn_gain[:, None], ffn_gain[:, None]], axis=1
    )
    small = jnp.pad(small, ((0, 0), (0, -small.shape[1] % LANES)))
    tokens_low = tokens.reshape(count, width)
    if fast:
        prompt_low, small_full, all_top = start_gather(tokens_low, small, top_low)
        small_full = small_full.reshape(width, small.shape[1])
    else:
        prompt_low = lax.all_gather(tokens_low[:prompt], "shard", axis=0, tiled=False, axis_index_groups=groups)
        small_full = gather(small)
        by_rep = lax.all_gather(top_low, "rep", axis=0, tiled=False)
        core_pos = rep_pos + 1 - 2 * (rep_pos % 2)
        all_top = jnp.stack([top_low] + [by_rep[i] for i in (core_pos, (rep_pos + 2) % 4, 3 - rep_pos)])
    prompt_low = prompt_low.reshape(GROUP_SIZE * prompt, width)
    qkv_full = small_full[:, :qkv_columns]
    attn_out_full = small_full[:, qkv_columns : qkv_columns + Q_WIDTH]
    router_full = small_full[:, qkv_columns + Q_WIDTH : qkv_columns + Q_WIDTH + EXPERTS]
    gains = small_full[:, qkv_columns + Q_WIDTH + EXPERTS :].astype(F32)
    attn_gain_full, ffn_gain_full = gains[:, 0], gains[:, 1]
    w_both = jnp.concatenate(
        [
            lax.dynamic_slice_in_dim(w_in, rep_pos * local * 2 * F, local * 2 * F, 1),
            lax.dynamic_slice_in_dim(w_out, rep_pos * local * F, local * F, 1),
        ],
        axis=1,
    )
    w_both, prompt_low = lax.optimization_barrier((w_both, prompt_low))
    w_both = gather(w_both)

    def normed(values):
        scale = rms_scale(values)
        return (values * scale * attn_gain_full).astype(BF16), scale

    def angles_of(positions):
        half = HEAD_SIZE // 2
        inverse_freq = ROPE_BASE ** (-(jnp.arange(half, dtype=F32) * 2.0) / HEAD_SIZE)
        angles = inverse_freq[:, None] * positions.astype(F32)[None, :]
        return jnp.cos(angles)[None], jnp.sin(angles)[None]

    def project(source, start, size, turn):
        rows = dot(qkv_full[:, start : start + size], source, (0, 1))
        rows = rows.reshape(size // HEAD_SIZE, HEAD_SIZE, source.shape[0])
        return (rotate(rows, *turn) if turn is not None else rows).astype(BF16)

    def keys_values(source, turn):
        return jnp.stack([project(source, Q_WIDTH, KV_WIDTH, turn), project(source, Q_WIDTH + KV_WIDTH, KV_WIDTH, None)])

    normed_attn, attn_scale = normed(x_in)
    normed_prompt, _ = normed(prompt_low.astype(F32))
    prompt_turn = angles_of(jnp.arange(GROUP_SIZE * prompt, dtype=jnp.int32))
    own_turn = angles_of(
        jnp.concatenate(
            [
                shard_pos * prompt + jnp.arange(prompt, dtype=jnp.int32),
                branch_len + jnp.arange(CONTINUATION_LEN, dtype=jnp.int32),
            ]
        )
    )
    continued_turn = tuple(part[..., prompt:] for part in own_turn)
    prompt_kv = keys_values(normed_prompt, prompt_turn)
    own_kv = keys_values(normed_attn[prompt:], continued_turn)
    query = project(normed_attn, 0, Q_WIDTH, own_turn)
    where = jnp.stack([shard_pos.astype(jnp.int32), branch_len])
    attn, lse = attn_forward(where, query, prompt_kv, own_kv)
    attn_low = attn.astype(BF16).reshape(Q_WIDTH, count)
    x_mid = x_in + dot(attn_low, attn_out_full, (0, 1))

    ffn_scale = rms_scale(x_mid)
    normed_ffn = (x_mid * ffn_scale * ffn_gain_full).astype(BF16)
    logits = dot(normed_ffn, router_full, (1, 0))
    chosen = jnp.any(route_ids[:, :, None] == jnp.arange(EXPERTS, dtype=jnp.int32), axis=1)
    gates = jax.nn.softmax(jnp.where(chosen, logits, NEGATIVE), axis=-1)
    gates = jnp.where(chosen, gates, 0.0)

    gates_out = jnp.pad(gates.T.reshape(reps, local, count), ((0, 0), (0, 8 - local), (0, 0)))
    all_normed, dx_own, dx_core, dx_far, y_part, dgu, gated, dgate_part = experts(
        normed_ffn, all_top, gates_out, w_both
    )
    grad_from_experts = dx_own.astype(F32) + dx_core.astype(F32) + dx_far.astype(F32)
    grad_gates = dgate_part[:, :local].reshape(EXPERTS, count).T
    to_core = [(i, i + 1 - 2 * (i % 2)) for i in range(reps)]
    to_far = [(i, (i + 2) % reps) for i in range(reps)]
    y_near = y_part[:2].astype(F32) + lax.ppermute(y_part[2:], "rep", to_core).astype(F32)
    y_sum = y_near[0] + lax.ppermute(y_near[1].astype(BF16), "rep", to_far).astype(F32)
    block_out = (x_mid + y_sum).astype(BF16)

    def rep_sum(values):
        for pairs in (to_core, to_far):
            values = (values.astype(F32) + lax.ppermute(values, "rep", pairs).astype(F32)).astype(BF16)
        return values

    def expert_term(left, right):
        return dot(left.reshape(reps * count, width), right.reshape(reps * count, -1), (0, 0)).astype(BF16)

    grad_logits = (gates * (grad_gates - jnp.sum(gates * grad_gates, axis=-1, keepdims=True))).astype(BF16)
    grad_router_w = dot(normed_ffn, grad_logits, (0, 0))
    grad_normed_ffn = grad_from_experts + dot(grad_logits, router_full, (1, 1))
    grad_mid_norm, grad_ffn_gain = rms_backward(x_mid, ffn_scale, ffn_gain_full, grad_normed_ffn)
    grad_mid = grad_top + grad_mid_norm
    grad_branch = grad_mid.astype(BF16)
    grad_attn_w = dot(grad_branch, attn_low, (0, 1))
    grad_attn = dot(attn_out_full, grad_branch, (0, 1)).astype(BF16).reshape(QUERY_HEADS, HEAD_SIZE, count)
    expert_columns = local * 3 * F
    if fast:
        expert_rows = expert_grads(
            all_normed.reshape(reps * count, width).T,
            all_top.reshape(reps * count, width).T,
            dgu.reshape(reps * count, -1),
            gated.reshape(reps * count, -1),
        )
    else:
        terms = jnp.concatenate([expert_term(all_normed, dgu), expert_term(all_top, gated)], axis=1)
        terms = lax.psum_scatter(terms, "shard", scatter_dimension=0, tiled=True)
        expert_rows = lax.all_gather(terms, "rep", axis=0, tiled=False)
    early = jnp.concatenate(
        [grad_attn_w.astype(BF16), grad_router_w.astype(BF16), grad_ffn_gain[:, None].astype(BF16)], axis=1
    )
    early = jnp.pad(early, ((0, 0), (0, -early.shape[1] % LANES)))
    grad_attn, early, expert_rows = lax.optimization_barrier((grad_attn, early, expert_rows))
    early = rep_sum(lax.psum_scatter(early, "shard", scatter_dimension=0, tiled=True))
    attn_rows, router_rows = early[:, :Q_WIDTH], early[:, Q_WIDTH : Q_WIDTH + EXPERTS]
    ffn_gain_rows = early[:, Q_WIDTH + EXPERTS]

    delta = jnp.sum(grad_attn.astype(F32) * attn, axis=1).reshape(KEY_VALUE_HEADS, PER_KEY, count)
    grad_query, grad_prompt_kv, grad_own_kv = attn_backward(
        where, query, prompt_kv, own_kv, grad_attn, lse, delta
    )

    def turn_back(values, turn):
        spun = rotate(values, turn[0], -turn[1])
        return spun.astype(BF16).reshape(-1, values.shape[-1])

    grad_query = turn_back(grad_query, own_turn)
    grad_prompt_kv = jnp.concatenate(
        [
            turn_back(grad_prompt_kv[0].astype(F32), prompt_turn),
            grad_prompt_kv[1].reshape(KV_WIDTH, GROUP_SIZE * prompt),
        ],
        axis=0,
    )
    grad_own_kv = jnp.concatenate(
        [turn_back(grad_own_kv[0], continued_turn), grad_own_kv[1].astype(BF16).reshape(KV_WIDTH, -1)], axis=0
    )
    late = jnp.concatenate(
        [
            dot(normed_attn, grad_query, (0, 1)).astype(BF16),
            (dot(normed_prompt, grad_prompt_kv, (0, 1)) + dot(normed_attn[prompt:], grad_own_kv, (0, 1))).astype(BF16),
        ],
        axis=1,
    )
    if fast:
        qkv_rows = late_reduce(late)
    else:
        qkv_rows = rep_sum(lax.psum_scatter(late, "shard", scatter_dimension=0, tiled=True))
    qkv_rows, grad_prompt_kv = lax.optimization_barrier((qkv_rows, grad_prompt_kv))
    attn_gain_rows = jnp.sum(
        qkv_rows.astype(F32) * query_key_value_weight.astype(F32), axis=1
    ) / attn_gain.astype(F32)

    grad_prompt_kv = lax.psum_scatter(
        grad_prompt_kv, "shard", scatter_dimension=1, tiled=True, axis_index_groups=groups
    )
    grad_projected = jnp.concatenate(
        [grad_query, jnp.concatenate([grad_prompt_kv, grad_own_kv], axis=1)], axis=0
    )
    grad_normed_attn = dot(grad_projected, qkv_full, (0, 1))
    grad_x_norm, _ = rms_backward(x_in, attn_scale, attn_gain_full, grad_normed_attn)
    grad_input = grad_mid + grad_x_norm

    in_columns = local * 2 * F
    if flat_path:
        size = outer_mom.shape[-1]

        def lead(first, second, rest):
            parts = [first[None].astype(F32), second[None].astype(F32), rest.reshape(-1, LANES).astype(F32)]
            return jnp.concatenate(parts, axis=0)

        def whole(values):
            return values, values.shape[-1], 0

        weight_flat, _ = flatten(
            size,
            lead(attn_gain, ffn_gain, w_router),
            [whole(query_key_value_weight), whole(w_attn_out), whole(w_in), whole(w_out)],
        )
        total_grad, square = flatten(
            size,
            lead(attn_gain_rows, ffn_gain_rows, router_rows),
            [
                whole(qkv_rows),
                whole(attn_rows),
                (expert_rows, in_columns, 0),
                (expert_rows, expert_columns - in_columns, in_columns // (expert_columns - in_columns)),
            ],
        )
        grad_norm, step_sum = summed_step(square, total_grad, adam_first, adam_second, weight_flat)
        new_first, new_second, new_mom, weight_update = update(
            reps, grad_norm, total_grad, adam_first, adam_second, step_sum, outer_mom
        )
        grad_norm = grad_norm.reshape(())
    else:
        weight_flat = jnp.concatenate(
            [
                portion.astype(F32).reshape(-1)
                for portion in (attn_gain, query_key_value_weight, w_attn_out, ffn_gain, w_router, w_in, w_out)
            ]
        )
        total_grad = jnp.concatenate(
            [
                portion.astype(F32).reshape(-1)
                for portion in (
                    attn_gain_rows,
                    qkv_rows,
                    attn_rows,
                    ffn_gain_rows,
                    router_rows,
                    expert_rows[:, :, :in_columns].transpose(1, 0, 2),
                    expert_rows[:, :, in_columns:].transpose(1, 0, 2),
                )
            ]
        )
        grad_norm = jnp.sqrt(lax.psum(jnp.sum(total_grad * total_grad), "shard"))
        new_first, new_second = moments(
            total_grad,
            adam_first.reshape(-1),
            adam_second.reshape(-1),
            CLIP_NORM / jnp.maximum(grad_norm, CLIP_NORM),
        )
        step = inner_step(new_first, new_second, weight_flat)
        pseudo = -(lax.psum(step.astype(BF16), "rep").astype(F32) / reps)
        new_mom = OUTER_MOMENTUM * outer_mom.reshape(-1) + pseudo
        weight_update = -OUTER_RATE * (pseudo + OUTER_MOMENTUM * new_mom)
    return (
        block_out.reshape(tokens.shape),
        grad_input.reshape(tokens.shape),
        total_grad.reshape(outer_mom.shape),
        grad_norm,
        new_first.reshape(adam_first.shape),
        new_second.reshape(adam_second.shape),
        new_mom.reshape(outer_mom.shape),
        weight_update.reshape(outer_mom.shape),
    )


def solution(mesh):
    by_token = P("rep", "shard", None, None)
    by_state = P("rep", "shard", None)
    by_row = P("shard", None)
    placed = (
        by_token,
        by_token,
        by_token,
        P("rep", "shard"),
        P("shard"),
        by_row,
        by_row,
        P("shard"),
        by_row,
        by_row,
        by_row,
        by_state,
        by_state,
        by_row,
    )
    return jax.shard_map(
        per_device,
        mesh=mesh,
        in_specs=placed,
        out_specs=(by_token, by_token, by_row, P(), by_state, by_state, by_row, by_row),
        check_vma=False,
    )
```

```python
import functools

import jax
import jax.numpy as jnp
from jax import lax
from jax.experimental import pallas as pl
from jax.experimental.pallas import tpu as pltpu
from jax.sharding import PartitionSpec as P

QUERY_HEADS = 16
KEY_VALUE_HEADS = 8
HEAD_SIZE = 64
F = 512
EXPERTS = 16
TOP = 8
GROUP_SIZE = 8
CONTINUATION_LEN = 512
STEP = 10

EPSILON = 1e-06
NEGATIVE = -1e30
ROPE_BASE = 10000.0
BETA_ONE = 0.9
BETA_TWO = 0.95
ADAM_EPS = 1e-08
INNER_RATE = 0.01
DECAY_RATE = 0.1
OUTER_RATE = 0.7
OUTER_MOMENTUM = 0.9
CLIP_NORM = 1.0

LOG2E = 1.4426950408889634
LANES = 128
MIB = 1 << 20
BF16 = jnp.bfloat16
F32 = jnp.float32
PER_KEY = QUERY_HEADS // KEY_VALUE_HEADS
Q_WIDTH = QUERY_HEADS * HEAD_SIZE
KV_WIDTH = KEY_VALUE_HEADS * HEAD_SIZE


def dot(left, right, dims):
    return lax.dot_general(left, right, ((dims[:1], dims[1:]), ((), ())), preferred_element_type=F32)


def split_three(value):
    high = value.astype(BF16)
    rest = value - high.astype(F32)
    middle = rest.astype(BF16)
    low = (rest - middle.astype(F32)).astype(BF16)
    return high, middle, low


def augment_query(q_ref, start, width):
    rows = jnp.concatenate([q_ref[g, :, start : start + width] for g in range(PER_KEY)], axis=1)
    scaled = rows.astype(F32) * (HEAD_SIZE**-0.5 * LOG2E)
    high = scaled.astype(BF16)
    low = (scaled - high.astype(F32)).astype(BF16)
    return rows, high, low


def block_of(ref, index, block):
    span = pl.ds(pl.multiple_of(index * block, block), block)
    return ref[0, 0, :, span], ref[1, 0, :, span]


def causal(width, columns):
    key_pos = lax.broadcasted_iota(jnp.int32, (width, columns), 0)
    query_pos = lax.broadcasted_iota(jnp.int32, (width, columns), 1) % width
    return key_pos <= query_pos


SAFE_BOUND = 48.0


def attn_forward_kernel(where_ref, q_ref, kv_ref, own_ref, o_ref, lse_ref, peak_ref, acc_ref):
    block = own_ref.shape[-1]
    columns = PER_KEY * block
    shard_pos = where_ref[0]
    branch = where_ref[1]
    ones = jnp.ones((16, block), BF16)
    pad = jnp.zeros((16 - 3, columns), BF16)
    whole = branch // block

    def longest(key):
        squares = key.astype(F32)
        return jnp.max(jnp.sum(squares * squares, axis=0, keepdims=True), axis=1, keepdims=True)

    longest_key = jnp.sqrt(jnp.maximum(longest(kv_ref[0, 0]), longest(own_ref[0, 0])))

    def emit(start, result, lse):
        for g in range(PER_KEY):
            o_ref[g, :, start : start + block] = result[:, g * block : (g + 1) * block]
            lse_ref[0, g : g + 1, start : start + block] = lse[:, g * block : (g + 1) * block]

    def sweep(advance, start):
        def body(index, carry):
            advance(*block_of(kv_ref, index, block), None)
            return carry

        if start == 0:
            lax.fori_loop(0, shard_pos, body, 0)
            advance(*block_of(kv_ref, shard_pos, block), causal(block, columns))
        else:
            lax.fori_loop(0, whole, body, 0)

            @pl.when(branch % block != 0)
            def _():
                key_pos = lax.broadcasted_iota(jnp.int32, (block, columns), 0)
                advance(*block_of(kv_ref, whole, block), key_pos < branch % block)

            advance(own_ref[0, 0], own_ref[1, 0], causal(block, columns))

    def bounded(start, high, low, bound):
        query = jnp.concatenate([high, low, *split_three(-bound), pad], axis=0)

        def advance(key, value, mask):
            scores = dot(jnp.concatenate([key, key, ones], axis=0), query, (0, 0))
            if mask is not None:
                scores = jnp.where(mask, scores, NEGATIVE)
            probs = jnp.exp2(scores).astype(BF16)
            acc_ref[...] += dot(jnp.concatenate([value, ones], axis=0), probs, (1, 0))

        acc_ref[...] = jnp.zeros_like(acc_ref)
        sweep(advance, start)
        total = acc_ref[HEAD_SIZE : HEAD_SIZE + 1]
        emit(start, acc_ref[:HEAD_SIZE] / total, bound + jnp.log2(total))

    def running(start, high, low):
        query = jnp.concatenate([high, low], axis=0)

        def advance(key, value, mask):
            scores = dot(jnp.concatenate([key, key], axis=0), query, (0, 0))
            if mask is not None:
                scores = jnp.where(mask, scores, NEGATIVE)
            old = peak_ref[...]
            new = jnp.maximum(old, jnp.max(scores, axis=0, keepdims=True))
            probs = jnp.exp2(scores - new).astype(BF16)
            shrink = jnp.exp2(old - new)
            part = dot(jnp.concatenate([value, ones], axis=0), probs, (1, 0))
            peak_ref[...] = new
            acc_ref[...] = acc_ref[...] * shrink + part

        peak_ref[...] = jnp.full_like(peak_ref, NEGATIVE)
        acc_ref[...] = jnp.zeros_like(acc_ref)
        sweep(advance, start)
        total = acc_ref[HEAD_SIZE : HEAD_SIZE + 1]
        emit(start, acc_ref[:HEAD_SIZE] / total, peak_ref[...] + jnp.log2(total))

    for start in (0, block):
        rows, high, low = augment_query(q_ref, start, block)
        wide = rows.astype(F32)
        length = jnp.sqrt(jnp.sum(wide * wide, axis=0, keepdims=True))
        bound = length * longest_key * (1.02 * HEAD_SIZE**-0.5 * LOG2E)
        safe = jnp.max(bound) < SAFE_BOUND

        @pl.when(safe)
        def _(start=start, high=high, low=low, bound=bound):
            bounded(start, high, low, bound)

        @pl.when(jnp.logical_not(safe))
        def _(start=start, high=high, low=low):
            running(start, high, low)


def attn_forward(where, query, prompt_kv, own_kv):
    tokens = query.shape[-1]
    block = own_kv.shape[-1]
    columns = PER_KEY * block
    keys = prompt_kv.shape[-1]
    return pl.pallas_call(
        attn_forward_kernel,
        grid=(query.shape[0] // PER_KEY,),
        in_specs=[
            pl.BlockSpec(memory_space=pltpu.SMEM),
            pl.BlockSpec((PER_KEY, HEAD_SIZE, tokens), lambda h: (h, 0, 0)),
            pl.BlockSpec((2, 1, HEAD_SIZE, keys), lambda h: (0, h, 0, 0)),
            pl.BlockSpec((2, 1, HEAD_SIZE, block), lambda h: (0, h, 0, 0)),
        ],
        out_specs=[
            pl.BlockSpec((PER_KEY, HEAD_SIZE, tokens), lambda h: (h, 0, 0)),
            pl.BlockSpec((1, PER_KEY, tokens), lambda h: (h, 0, 0)),
        ],
        out_shape=[
            jax.ShapeDtypeStruct(query.shape, F32),
            jax.ShapeDtypeStruct((query.shape[0] // PER_KEY, PER_KEY, tokens), F32),
        ],
        scratch_shapes=[
            pltpu.VMEM((1, columns), F32),
            pltpu.VMEM((HEAD_SIZE + 16, columns), F32),
        ],
        compiler_params=pltpu.CompilerParams(vmem_limit_bytes=48 * MIB),
        cost_estimate=pl.CostEstimate(
            flops=4 * tokens * keys * query.shape[0] * HEAD_SIZE,
            bytes_accessed=16 * MIB,
            transcendentals=query.shape[0] * tokens * keys,
        ),
        name="attn_forward",
    )(where, query, prompt_kv, own_kv)


def attn_backward_kernel(
    where_ref, q_ref, kv_ref, own_ref, go_ref, lse_ref, delta_ref, dq_ref, dkv_ref, down_ref, dkv_acc, dq_acc
):
    block = own_ref.shape[-1]
    columns = PER_KEY * block
    shard_pos = where_ref[0]
    branch = where_ref[1]
    ones = jnp.ones((16, block), BF16)
    pad = jnp.zeros((16 - 3, columns), BF16)

    def begin(start):
        rows, high, low = augment_query(q_ref, start, block)

        def lanes(ref):
            return jnp.concatenate([ref[0, g : g + 1, start : start + block] for g in range(PER_KEY)], axis=1)

        lse = split_three(-lanes(lse_ref))
        delta = split_three(-lanes(delta_ref))
        grad = jnp.concatenate([go_ref[g, :, start : start + block] for g in range(PER_KEY)], axis=1)
        query = jnp.concatenate([high, low, *lse, pad], axis=0)
        grad_plus = jnp.concatenate([grad, *delta, pad], axis=0)
        dq_acc[...] = jnp.zeros_like(dq_acc)
        scaled = (rows.astype(F32) * HEAD_SIZE**-0.5).astype(BF16)
        return query, scaled, grad_plus, grad

    def terms(state, key, value, mask):
        query, scaled, grad_plus, grad = state
        scores = dot(jnp.concatenate([key, key, ones], axis=0), query, (0, 0))
        if mask is not None:
            scores = jnp.where(mask, scores, NEGATIVE)
        probs = jnp.exp2(scores)
        dv = dot(grad, probs.astype(BF16), (1, 1))
        grad_probs = dot(jnp.concatenate([value, ones], axis=0), grad_plus, (0, 0))
        grad_scores = (probs * grad_probs).astype(BF16)
        dq_acc[...] += dot(key, grad_scores, (1, 0))
        return dot(scaled, grad_scores, (1, 1)), dv

    def add(index, state, mask):
        dk, dv = terms(state, *block_of(kv_ref, index, block), mask)
        span = pl.ds(pl.multiple_of(index * block, block), block)
        dkv_acc[0, :, span] += dk
        dkv_acc[1, :, span] += dv

    def finish(start):
        total = dq_acc[...] * HEAD_SIZE**-0.5
        for g in range(PER_KEY):
            dq_ref[g, :, start : start + block] = total[:, g * block : (g + 1) * block]

    def run(state, count):
        def body(index, carry):
            add(2 * index, state, None)
            add(2 * index + 1, state, None)
            return carry

        lax.fori_loop(0, count // 2, body, 0)

        @pl.when(count % 2 == 1)
        def _():
            add(count - 1, state, None)

    dkv_acc[...] = jnp.zeros_like(dkv_acc)
    state = begin(0)
    run(state, shard_pos)
    add(shard_pos, state, causal(block, columns))
    finish(0)

    state = begin(block)
    whole = branch // block
    run(state, whole)

    @pl.when(branch % block != 0)
    def _():
        key_pos = lax.broadcasted_iota(jnp.int32, (block, columns), 0)
        add(whole, state, key_pos < branch % block)

    dk, dv = terms(state, own_ref[0, 0], own_ref[1, 0], causal(block, columns))
    down_ref[0, 0] = dk
    down_ref[1, 0] = dv
    finish(block)
    dkv_ref[:, 0] = dkv_acc[...].astype(BF16)


def attn_backward(where, query, prompt_kv, own_kv, grad_out, lse, delta):
    tokens = query.shape[-1]
    block = own_kv.shape[-1]
    columns = PER_KEY * block
    keys = prompt_kv.shape[-1]
    by_head = pl.BlockSpec((PER_KEY, HEAD_SIZE, tokens), lambda h: (h, 0, 0))
    by_keys = pl.BlockSpec((2, 1, HEAD_SIZE, keys), lambda h: (0, h, 0, 0))
    by_own = pl.BlockSpec((2, 1, HEAD_SIZE, block), lambda h: (0, h, 0, 0))
    by_row = pl.BlockSpec((1, PER_KEY, tokens), lambda h: (h, 0, 0))
    return pl.pallas_call(
        attn_backward_kernel,
        grid=(query.shape[0] // PER_KEY,),
        in_specs=[pl.BlockSpec(memory_space=pltpu.SMEM), by_head, by_keys, by_own, by_head, by_row, by_row],
        out_specs=[by_head, by_keys, by_own],
        out_shape=[
            jax.ShapeDtypeStruct(query.shape, F32),
            jax.ShapeDtypeStruct(prompt_kv.shape, BF16),
            jax.ShapeDtypeStruct(own_kv.shape, F32),
        ],
        scratch_shapes=[
            pltpu.VMEM((2, HEAD_SIZE, keys), F32),
            pltpu.VMEM((HEAD_SIZE, columns), F32),
        ],
        compiler_params=pltpu.CompilerParams(vmem_limit_bytes=56 * MIB),
        cost_estimate=pl.CostEstimate(
            flops=10 * tokens * keys * query.shape[0] * HEAD_SIZE,
            bytes_accessed=32 * MIB,
            transcendentals=query.shape[0] * tokens * keys,
        ),
        name="attn_backward",
    )(where, query, prompt_kv, own_kv, grad_out, lse, delta)


MESH = pl.DeviceIdType.MESH
LINE = 4
TOKEN_PARTS = 4


def start_kernel(
    x_ref,
    w_ref,
    top_ref,
    tok_all,
    w_all,
    top_all,
    own_sem,
    line_recv,
    right_send,
    left_send,
    y_send,
    y_recv,
    x_send,
    x_recv,
    core_send,
    core_recv,
    top_send,
    top_recv,
):
    part = tok_all.shape[1] // TOKEN_PARTS
    quarter = w_all.shape[2]
    half = top_ref.shape[0] // 2
    me = lax.axis_index("shard")
    place, column = me // 2, lax.rem(me, 2)
    rep = lax.axis_index("rep")
    far, core = lax.rem(rep + 2, 4), rep + 1 - 2 * lax.rem(rep, 2)
    to_right, to_left, to_y = {"shard": me + 2}, {"shard": me - 2}, {"shard": me + 1 - 2 * column}
    to_far, to_core = {"rep": far}, {"rep": core}
    weights, mirrored = 0, TOKEN_PARTS + 1
    last = TOKEN_PARTS
    streams = TOKEN_PARTS + 2

    def piece(i, origin, side):
        if i == weights:
            return w_all.at[2 * origin + side, rep]
        k = (i if i != mirrored else last) - 1
        return tok_all.at[2 * origin + side, pl.ds(k * part, part)]

    def side_of(i):
        return 1 - column if i == mirrored else column

    def own(i):
        if i == weights:
            return w_ref.at[pl.ds(pl.multiple_of(rep * quarter, quarter), quarter)]
        if i == mirrored:
            return piece(i, place, 1 - column)
        return x_ref.at[pl.ds((i - 1) * part, part)]

    def remote(source, target, send, receive, device):
        return pltpu.make_async_remote_copy(
            src_ref=source, dst_ref=target, send_sem=send, recv_sem=receive, device_id=device, device_id_type=MESH
        )

    def source(i, origin, at_home):
        return own(i) if at_home else piece(i, origin, side_of(i))

    def right(i, origin, at_home=False):
        return remote(
            source(i, origin, at_home),
            piece(i, origin, side_of(i)),
            right_send.at[i, origin],
            line_recv.at[i, origin],
            to_right,
        )

    def left(i, origin, at_home=False):
        return remote(
            source(i, origin, at_home),
            piece(i, origin, side_of(i)),
            left_send.at[i, origin],
            line_recv.at[i, origin],
            to_left,
        )

    def abreast(i, origin, at_home=False):
        return remote(
            source(i, origin, at_home), piece(i, origin, column), y_send.at[i, origin], y_recv.at[i, origin], to_y
        )

    def over_x(origin, side, at_home=False):
        target = piece(weights, origin, side)
        source_ref = own(weights) if at_home else target
        return remote(source_ref, target, x_send.at[origin, side], x_recv.at[origin, side], to_far)

    def over_core(group, origin, side, at_home=False):
        target = w_all.at[2 * origin + side, rep if group == 0 else far]
        source_ref = own(weights) if at_home else target
        return remote(
            source_ref, target, core_send.at[group, origin, side], core_recv.at[group, origin, side], to_core
        )

    def top_far(h):
        return remote(
            top_ref.at[pl.ds(h * half, half)],
            top_all.at[2, pl.ds(h * half, half)],
            top_send.at[0, h],
            top_recv.at[0, h],
            to_far,
        )

    def top_core(h):
        return remote(
            top_ref.at[pl.ds(h * half, half)],
            top_all.at[1, pl.ds(h * half, half)],
            top_send.at[1, h],
            top_recv.at[1, h],
            to_core,
        )

    def top_diagonal(h):
        return remote(
            top_all.at[2, pl.ds(h * half, half)],
            top_all.at[3, pl.ds(h * half, half)],
            top_send.at[2, h],
            top_recv.at[2, h],
            to_core,
        )

    has_right, has_left = place < LINE - 1, place > 0
    barrier = pltpu.get_barrier_semaphore()

    def greet(device):
        pl.semaphore_signal(barrier, inc=1, device_id=device, device_id_type=MESH)

    for device in (to_y, to_far, to_core):
        greet(device)

    @pl.when(has_right)
    def _():
        greet(to_right)

    @pl.when(has_left)
    def _():
        greet(to_left)

    pl.semaphore_wait(barrier, 3 + has_right.astype(jnp.int32) + has_left.astype(jnp.int32))

    def along(i, origin, at_home=False):
        @pl.when(has_right)
        def _():
            right(i, origin, at_home).start()

        @pl.when(has_left)
        def _():
            left(i, origin, at_home).start()

    order = [weights, last] + list(range(1, last))
    for i in order:
        along(i, place, True)
        abreast(i, place, True).start()
        if i == weights:
            over_x(place, column, True).start()
            over_core(0, place, column, True).start()
            for h in (0, 1):
                top_far(h).start()
    for h in (0, 1):
        top_core(h).start()
    own_copies = [
        pltpu.make_async_copy(own(i), piece(i, place, column), own_sem.at[i]) for i in range(streams - 1)
    ]
    own_copies.append(pltpu.make_async_copy(top_ref, top_all.at[0], own_sem.at[streams - 1]))
    for copy in own_copies:
        copy.start()
    abreast(last, place).wait_recv()
    along(mirrored, place, True)

    def weights_across(origin):
        abreast(weights, origin).wait_recv()
        over_x(origin, 1 - column).start()
        over_core(0, origin, 1 - column).start()

    weights_across(place)
    for d in range(1, LINE):
        before, after = place - d, place + d
        from_left, from_right = before >= 0, after < LINE
        for i in [weights, last, mirrored] + list(range(1, last)):

            @pl.when(from_left)
            def _(i=i):
                right(i, before).wait_recv()

                @pl.when(has_right)
                def _():
                    right(i, before).start()

                if i != last and i != mirrored:
                    abreast(i, before).start()
                if i == weights:
                    over_x(before, column).start()
                    over_core(0, before, column).start()

            @pl.when(from_right)
            def _(i=i):
                left(i, after).wait_recv()

                @pl.when(has_left)
                def _():
                    left(i, after).start()

                if i != last and i != mirrored:
                    abreast(i, after).start()
                if i == weights:
                    over_x(after, column).start()
                    over_core(0, after, column).start()

        @pl.when(from_left)
        def _():
            weights_across(before)

        @pl.when(from_right)
        def _():
            weights_across(after)

        if d >= 2:
            h = d - 2
            top_far(h).wait_recv()
            top_diagonal(h).start()

    for origin in range(LINE):
        for side in (0, 1):
            remote(
                w_all.at[2 * origin + side, far],
                w_all.at[2 * origin + side, far],
                x_send.at[origin, side],
                x_recv.at[origin, side],
                to_far,
            ).wait_recv()
            over_core(1, origin, side).start()

    for origin in range(LINE):
        for i in range(1, last):
            abreast(i, origin).wait_recv()
        for side in (0, 1):
            for group in (0, 1):
                over_core(group, origin, side).wait_recv()
    for h in (0, 1):
        top_core(h).wait_recv()
        top_diagonal(h).wait_recv()
        for copy in (top_far(h), top_core(h), top_diagonal(h)):
            copy.wait_send()
    for copy in own_copies:
        copy.wait()
    for origin in range(LINE):
        for i in range(streams):

            @pl.when(has_right & (origin <= place))
            def _(i=i, origin=origin):
                right(i, origin).wait_send()

            @pl.when(has_left & (origin >= place))
            def _(i=i, origin=origin):
                left(i, origin).wait_send()

            if i != last and i != mirrored:
                abreast(i, origin).wait_send()
        for side in (0, 1):
            over_x(origin, side).wait_send()
            for group in (0, 1):
                over_core(group, origin, side).wait_send()
    abreast(last, place).wait_send()


def start_gather(x, small, top):
    rows, width = x.shape
    prompt = rows - CONTINUATION_LEN
    own_rows, columns = small.shape
    dma = pltpu.SemaphoreType.DMA
    streams = TOKEN_PARTS + 2
    anywhere = pl.BlockSpec(memory_space=pl.ANY)
    return pl.pallas_call(
        start_kernel,
        in_specs=[anywhere] * 3,
        out_specs=[anywhere] * 3,
        out_shape=[
            jax.ShapeDtypeStruct((2 * LINE, prompt, width), BF16),
            jax.ShapeDtypeStruct((2 * LINE, 4, own_rows // 4, columns), BF16),
            jax.ShapeDtypeStruct((4, rows, width), BF16),
        ],
        scratch_shapes=[
            dma((streams,)),
            dma((streams, LINE)),
            dma((streams, LINE)),
            dma((streams, LINE)),
            dma((streams, LINE)),
            dma((streams, LINE)),
            dma((LINE, 2)),
            dma((LINE, 2)),
            dma((2, LINE, 2)),
            dma((2, LINE, 2)),
            dma((3, 2)),
            dma((3, 2)),
        ],
        compiler_params=pltpu.CompilerParams(collective_id=2, has_side_effects=True),
        cost_estimate=pl.CostEstimate(flops=0, bytes_accessed=64 * MIB, transcendentals=0),
        name="start_gather",
    )(x, small, top)


ORDER = ((0, 0), (0, 1), (1, 0), (3, 0), (2, 0), (3, 1), (2, 1), (1, 1))


def experts_kernel(
    x_hbm,
    top_hbm,
    gates_ref,
    w_ref,
    all_x,
    dx_own,
    dx_core,
    dx_far,
    y_keep,
    y_give,
    xt_all,
    tt_all,
    dgu_all,
    gh_all,
    dg_all,
    x_buf,
    top_buf,
    y_buf,
    dx_buf,
    xt_buf,
    tt_buf,
    dgu_buf,
    gh_buf,
    relay,
    y_acc,
    dx_acc,
    gates_all,
    gates_now,
    dg_now,
    dg_mine,
    in_sem,
    out_sem,
    copy_sem,
    send_sem,
    recv_sem,
    small_send,
    small_recv,
):
    tile = x_buf.shape[1]
    count = w_ref.shape[1] // (3 * F)
    step = pl.program_id(0)
    steps = len(ORDER)
    slot = lax.rem(step, 2)
    me = lax.axis_index("rep")
    home = [me, me + 1 - 2 * lax.rem(me, 2), lax.rem(me + 2, 4), 3 - me]

    def remote(source, target, send, receive, relation):
        return pltpu.make_async_remote_copy(
            src_ref=source,
            dst_ref=target,
            send_sem=send,
            recv_sem=receive,
            device_id={"rep": home[relation]},
            device_id_type=MESH,
        )

    def half(ref, half_index, *lead):
        return ref.at[(*lead, pl.ds(half_index * tile, tile))]

    def to_core(h):
        return remote(half(x_hbm, h), half(all_x, h, me), send_sem.at[0, h], recv_sem.at[0, h], 1)

    def to_far(h):
        return remote(half(x_hbm, h), half(all_x, h, me), send_sem.at[1, h], recv_sem.at[1, h], 2)

    def forward(h):
        part = half(all_x, h, home[2])
        return remote(part, part, send_sem.at[2, h], recv_sem.at[2, h], 1)

    def give(kind, h, buffer):
        if kind == 3:
            return remote(buffer, relay.at[h], send_sem.at[3, h], recv_sem.at[3, h], 1)
        if kind == 2:
            return remote(buffer, half(dx_far, h), send_sem.at[4, h], recv_sem.at[4, h], 2)
        return remote(buffer, half(dx_core, h), send_sem.at[5, h], recv_sem.at[5, h], 1)

    def small_gates(k):
        return remote(gates_ref.at[home[k]], gates_all.at[me], small_send.at[0, k], small_recv.at[0, k], k)

    def small_back(k):
        return remote(dg_mine.at[home[k]], dg_all.at[me], small_send.at[1, k], small_recv.at[1, k], k)

    def load_x(i):
        kind, h = ORDER[i]
        source = half(x_hbm, h) if kind == 0 else half(all_x, h, home[kind])
        return pltpu.make_async_copy(source, x_buf.at[i % 2], in_sem.at[i % 2, 0])

    def load_top(i):
        kind, h = ORDER[i]
        return pltpu.make_async_copy(half(top_hbm, h, kind), top_buf.at[i % 2], in_sem.at[i % 2, 1])

    def stores(i):
        kind, h = ORDER[i]
        out = []
        rows = 2 * tile

        def turned(ref, place):
            here = pl.multiple_of(place * rows + h * tile, LANES)
            return ref.at[:, pl.ds(here, tile)]

        targets = (
            (y_buf, half((y_keep, y_give, y_keep, y_give)[kind], h, (0, 0, 1, 1)[kind])),
            (dgu_buf, half(dgu_all, h, home[kind])),
            (gh_buf, half(gh_all, h, kind)),
            (xt_buf, turned(xt_all, home[kind])),
            (tt_buf, turned(tt_all, kind)),
        )
        for n, (buffer, target) in enumerate(targets):
            out.append(pltpu.make_async_copy(buffer.at[i % 2], target, out_sem.at[i % 2, n]))
        return out

    def store_dx(i):
        kind, h = ORDER[i]
        if kind == 0:
            return pltpu.make_async_copy(dx_buf.at[i % 2], half(dx_own, h), out_sem.at[i % 2, 5])
        return give(kind, h, dx_buf.at[i % 2])

    def finish(i):
        for copy in stores(i):
            copy.wait()
        if ORDER[i][0] == 0:
            store_dx(i).wait()
        else:
            store_dx(i).wait_send()

    own_copy = pltpu.make_async_copy(x_hbm, all_x.at[me], copy_sem)
    for i in range(steps):
        kind, h = ORDER[i]

        @pl.when(step == i)
        def _(i=i, kind=kind, h=h):
            if i == 0:
                barrier = pltpu.get_barrier_semaphore()
                for k in (1, 2, 3):
                    pl.semaphore_signal(
                        barrier, inc=1, device_id={"rep": home[k]}, device_id_type=MESH
                    )
                pl.semaphore_wait(barrier, 3)
                to_far(0).start()
                for n in (0, 1):
                    to_core(n).start()
                for k in (1, 2, 3):
                    small_gates(k).start()
                own_copy.start()
                load_top(0).start()
                load_x(0).start()
                gates_all[me] = gates_ref[me]
            if i == 1:
                to_far(1).start()
                for n in (0, 1):
                    to_core(n).wait_recv()
            if i == 2:
                for k in (1, 2, 3):
                    small_gates(k).wait_recv()
                to_far(0).wait_recv()
                forward(0).start()
            if i == 3:
                to_far(1).wait_recv()
                forward(1).start()
            if i == 4:
                forward(1).wait_recv()
            load_x(i).wait()
            load_top(i).wait()
            if i + 1 < steps:
                load_top(i + 1).start()
                if i + 1 != 3:
                    load_x(i + 1).start()
            if i >= 2:
                finish(i - 2)
            gates_now[...] = jnp.transpose(gates_all[home[kind]][:, h * tile : (h + 1) * tile])

    x = x_buf[slot]
    top = top_buf[slot]
    xt_buf[slot] = x.T
    tt_buf[slot] = top.T
    columns = []
    for e in range(count):
        w_in = w_ref[:, e * 2 * F : (e + 1) * 2 * F]
        w_out = w_ref[:, (count * 2 + e) * F : (count * 2 + e + 1) * F]
        gate_up = dot(x, w_in, (1, 0))
        g = gate_up[:, :F]
        u = gate_up[:, F:]
        sig = jax.nn.sigmoid(g)
        act = g * sig
        hidden = (act * u).astype(BF16).astype(F32)
        raw = dot(top, w_out, (1, 0))
        columns.append(jnp.sum(hidden * raw, axis=1, keepdims=True))
        gate = gates_now[:, e : e + 1]
        gated = (hidden * gate).astype(BF16)
        gh_buf[slot, :, e * F : (e + 1) * F] = gated
        grad_hidden = raw * gate
        dg = (grad_hidden * u * sig * (1.0 + g * (1.0 - sig))).astype(BF16)
        du = (grad_hidden * act).astype(BF16)
        dgu = jnp.concatenate([dg, du], axis=1)
        dgu_buf[slot, :, e * 2 * F : (e + 1) * 2 * F] = dgu
        y = dot(gated, w_out, (1, 1))
        dx = dot(dgu, w_in, (1, 1))
        if e == 0:
            y_acc[...] = y
            dx_acc[...] = dx
        elif e < count - 1:
            y_acc[...] += y
            dx_acc[...] += dx
        else:
            y_buf[slot] = (y_acc[...] + y).astype(BF16)
            dx_acc[...] += dx
    columns.append(jnp.zeros((tile, 8 - count), F32))
    dg_now[...] = jnp.transpose(jnp.concatenate(columns, axis=1))

    for i in range(steps):
        kind, h = ORDER[i]

        @pl.when(step == i)
        def _(i=i, kind=kind, h=h):
            dg_mine[home[kind], :, h * tile : (h + 1) * tile] = dg_now[...]
            if kind == 2:
                give(3, h, dx_buf.at[0]).wait_recv()
                dx_buf[i % 2] = (dx_acc[...] + relay[h].astype(F32)).astype(BF16)
            else:
                dx_buf[i % 2] = dx_acc[...].astype(BF16)
            store_dx(i).start()
            for copy in stores(i):
                copy.start()
            if i == 2:
                forward(0).wait_recv()
                load_x(3).start()
            if i == steps - 1:
                own_back = pltpu.make_async_copy(dg_mine.at[me], dg_all.at[me], small_send.at[1, 0])
                own_back.start()
                for k in (1, 2, 3):
                    small_back(k).start()
                finish(i - 1)
                finish(i)
                own_copy.wait()
                own_back.wait()
                for n in (0, 1):
                    to_far(n).wait_send()
                    to_core(n).wait_send()
                    forward(n).wait_send()
                    give(2, n, dx_buf.at[0]).wait_recv()
                    give(1, n, dx_buf.at[0]).wait_recv()
                for k in (1, 2, 3):
                    small_gates(k).wait_send()
                    small_back(k).wait()


def experts(x, all_top, gates, weights):
    rows, width = x.shape
    reps = all_top.shape[0]
    count = weights.shape[1] // (3 * F)
    tile = rows // 2
    anywhere = pl.BlockSpec(memory_space=pl.ANY)
    fixed = pl.BlockSpec(weights.shape, lambda i: (0, 0), pipeline_mode=pl.Buffered(1))
    small = pl.BlockSpec((reps, 8, rows), lambda i: (0, 0, 0))
    dma = pltpu.SemaphoreType.DMA
    return pl.pallas_call(
        experts_kernel,
        grid=(len(ORDER),),
        in_specs=[anywhere, anywhere, small, fixed],
        out_specs=[anywhere] * 11,
        out_shape=[
            jax.ShapeDtypeStruct((reps, rows, width), BF16),
            jax.ShapeDtypeStruct((rows, width), BF16),
            jax.ShapeDtypeStruct((rows, width), BF16),
            jax.ShapeDtypeStruct((rows, width), BF16),
            jax.ShapeDtypeStruct((2, rows, width), BF16),
            jax.ShapeDtypeStruct((2, rows, width), BF16),
            jax.ShapeDtypeStruct((width, reps * rows), BF16),
            jax.ShapeDtypeStruct((width, reps * rows), BF16),
            jax.ShapeDtypeStruct((reps, rows, count * 2 * F), BF16),
            jax.ShapeDtypeStruct((reps, rows, count * F), BF16),
            jax.ShapeDtypeStruct((reps, 8, rows), F32),
        ],
        scratch_shapes=[
            pltpu.VMEM((2, tile, width), BF16),
            pltpu.VMEM((2, tile, width), BF16),
            pltpu.VMEM((2, tile, width), BF16),
            pltpu.VMEM((2, tile, width), BF16),
            pltpu.VMEM((2, width, tile), BF16),
            pltpu.VMEM((2, width, tile), BF16),
            pltpu.VMEM((2, tile, count * 2 * F), BF16),
            pltpu.VMEM((2, tile, count * F), BF16),
            pltpu.VMEM((2, tile, width), BF16),
            pltpu.VMEM((tile, width), F32),
            pltpu.VMEM((tile, width), F32),
            pltpu.VMEM((reps, 8, rows), F32),
            pltpu.VMEM((tile, 8), F32),
            pltpu.VMEM((8, tile), F32),
            pltpu.VMEM((reps, 8, rows), F32),
            dma((2, 2)),
            dma((2, 6)),
            dma,
            dma((6, 2)),
            dma((6, 2)),
            dma((2, 4)),
            dma((2, 4)),
        ],
        compiler_params=pltpu.CompilerParams(
            vmem_limit_bytes=58 * MIB, collective_id=1, has_side_effects=True
        ),
        cost_estimate=pl.CostEstimate(
            flops=12 * reps * rows * width * count * F,
            bytes_accessed=80 * MIB,
            transcendentals=reps * rows * count * F,
        ),
        name="experts",
    )(x, all_top, gates, weights)


def send_to(source, target, send, receive, device):
    return pltpu.make_async_remote_copy(
        src_ref=source, dst_ref=target, send_sem=send, recv_sem=receive, device_id=device, device_id_type=MESH
    )


def line_reduce(parts, y_buf, right_buf, left_buf, y_sems, right_sems, left_sems):
    me = lax.axis_index("shard")
    place, side = me // 2, lax.rem(me, 2)
    to_y, to_right, to_left = {"shard": me + 1 - 2 * side}, {"shard": me + 2}, {"shard": me - 2}

    def across(c):
        return send_to(parts.at[c, 1 - side], y_buf.at[c], y_sems.at[0, c], y_sems.at[1, c], to_y)

    def add_across(c):
        across(c).wait_recv()
        for p in range(LINE):
            parts[c, side, p] = (parts[c, side, p].astype(F32) + y_buf[c, p].astype(F32)).astype(BF16)

    def hop(c, p, buf, sems, device, first):
        source = parts.at[c, side, p] if first else buf.at[c, p]
        return send_to(source, buf.at[c, p], sems.at[0, c, p], sems.at[1, c, p], device)

    def run(c, p, buf, sems, device, is_first, passes):
        @pl.when(passes & is_first)
        def _():
            hop(c, p, buf, sems, device, True).start()

        @pl.when(passes & jnp.logical_not(is_first))
        def _():
            hop(c, p, buf, sems, device, False).wait_recv()
            buf[c, p] = (parts[c, side, p].astype(F32) + buf[c, p].astype(F32)).astype(BF16)
            hop(c, p, buf, sems, device, False).start()

    def step_right(c):
        for p in range(1, LINE):
            run(c, p, right_buf, right_sems, to_right, place == 0, place < p)

    def step_left(c):
        for p in range(LINE - 1):
            run(c, p, left_buf, left_sems, to_left, place == LINE - 1, place > p)

    def collect(c, total):
        total[...] = parts[c, side, place].astype(F32)

        @pl.when(place > 0)
        def _():
            hop(c, place, right_buf, right_sems, to_right, False).wait_recv()
            total[...] += right_buf[c, place].astype(F32)

        @pl.when(place < LINE - 1)
        def _():
            hop(c, place, left_buf, left_sems, to_left, False).wait_recv()
            total[...] += left_buf[c, place].astype(F32)

    def drain(c):
        across(c).wait_send()
        for p in range(1, LINE):

            @pl.when(place < p)
            def _(p=p):
                hop(c, p, right_buf, right_sems, to_right, False).wait_send()

        for p in range(LINE - 1):

            @pl.when(place > p)
            def _(p=p):
                hop(c, p, left_buf, left_sems, to_left, False).wait_send()

    def greet(extra):
        barrier = pltpu.get_barrier_semaphore()
        for device in [to_y] + extra:
            pl.semaphore_signal(barrier, inc=1, device_id=device, device_id_type=MESH)
        has_right, has_left = place < LINE - 1, place > 0

        @pl.when(has_right)
        def _():
            pl.semaphore_signal(barrier, inc=1, device_id=to_right, device_id_type=MESH)

        @pl.when(has_left)
        def _():
            pl.semaphore_signal(barrier, inc=1, device_id=to_left, device_id_type=MESH)

        count = 1 + len(extra) + has_right.astype(jnp.int32) + has_left.astype(jnp.int32)
        pl.semaphore_wait(barrier, count)

    return place, across, add_across, step_right, step_left, collect, drain, greet


def between(step, low, high, body):
    @pl.when((step >= low) & (step < high))
    def _():
        body()


def expert_grads_kernel(
    xt_ref,
    tt_ref,
    dgu_ref,
    gh_ref,
    out_ref,
    left_op,
    right_op,
    parts,
    y_buf,
    right_buf,
    left_buf,
    total,
    mine,
    load_sem,
    lhs_sem,
    y_sems,
    right_sems,
    left_sems,
    own_sem,
    far_sems,
    near_sems,
    pass_sems,
):
    n = parts.shape[0]
    columns = right_op.shape[2]
    first = dgu_ref.shape[1] // columns
    rows = parts.shape[3]
    rep = lax.axis_index("rep")
    far = lax.rem(rep + 2, 4)
    to_core, to_far = {"rep": rep + 1 - 2 * lax.rem(rep, 2)}, {"rep": far}
    place, across, add_across, step_right, step_left, collect, drain, greet = line_reduce(
        parts, y_buf, right_buf, left_buf, y_sems, right_sems, left_sems
    )

    def load(c, act):
        slot = lax.rem(c, 2)

        @pl.when(c < first)
        def _():
            here = pl.ds(pl.multiple_of(c * columns, columns), columns)
            act(pltpu.make_async_copy(dgu_ref.at[:, here], right_op.at[slot], load_sem.at[slot]))

        @pl.when(c >= first)
        def _():
            here = pl.ds(pl.multiple_of((c - first) * columns, columns), columns)
            act(pltpu.make_async_copy(gh_ref.at[:, here], right_op.at[slot], load_sem.at[slot]))

    def start(copy):
        copy.start()

    def wait(copy):
        copy.wait()

    def place_of(owner, c):
        return out_ref.at[owner, :, pl.ds(pl.multiple_of(c * columns, columns), columns)]

    def over_x(c):
        return send_to(mine.at[c], place_of(rep, c), far_sems.at[0, c], far_sems.at[1, c], to_far)

    def over_core(c):
        return send_to(mine.at[c], place_of(rep, c), near_sems.at[0, c], near_sems.at[1, c], to_core)

    def keep(c):
        return pltpu.make_async_copy(mine.at[c], place_of(rep, c), own_sem.at[c])

    def pass_on(c):
        return send_to(place_of(far, c), place_of(far, c), pass_sems.at[0, c], pass_sems.at[1, c], to_core)

    lhs = pltpu.make_async_copy(xt_ref, left_op, lhs_sem)
    lhs.start()
    load(0, start)
    greet([to_core, to_far])
    lhs.wait()

    def produce(c):
        @pl.when(c == first)
        def _():
            swap = pltpu.make_async_copy(tt_ref, left_op, lhs_sem)
            swap.start()
            swap.wait()

        load(c, wait)

        @pl.when(c + 1 < n)
        def _():
            load(c + 1, start)

        result = dot(left_op[...], right_op[lax.rem(c, 2)], (1, 0)).astype(BF16)
        for t in range(2 * LINE):
            parts[c, t % 2, t // 2] = result[t * rows : (t + 1) * rows]
        across(c).start()

    def finish(c):
        collect(c, total)
        mine[c] = total[...].astype(BF16)
        over_x(c).start()
        over_core(c).start()
        keep(c).start()

    def forward(c):
        over_x(c).wait_recv()
        pass_on(c).start()

    def step(i, carry):
        between(i, 0, n, lambda: produce(i))
        between(i, 1, n + 1, lambda: add_across(i - 1))
        to_right_chunk, to_left_chunk = i - 1 - place, i - LINE + place
        between(to_right_chunk, 0, n, lambda: step_right(to_right_chunk))
        between(to_left_chunk, 0, n, lambda: step_left(to_left_chunk))
        between(i, 5, n + 5, lambda: finish(i - 5))
        between(i, 7, n + 7, lambda: forward(i - 7))
        return carry

    lax.fori_loop(0, n + 7, step, 0)

    def end(c, carry):
        drain(c)
        over_x(c).wait_send()
        over_core(c).wait()
        keep(c).wait()
        pass_on(c).wait()
        return carry

    lax.fori_loop(0, n, end, 0)


def expert_grads(x_t, top_t, dgu, gated, columns=256):
    width, tokens = x_t.shape
    wide = dgu.shape[1] + gated.shape[1]
    n = wide // columns
    rows = width // (2 * LINE)
    dma = pltpu.SemaphoreType.DMA
    anywhere = pl.BlockSpec(memory_space=pl.ANY)
    return pl.pallas_call(
        expert_grads_kernel,
        in_specs=[anywhere] * 4,
        out_specs=anywhere,
        out_shape=jax.ShapeDtypeStruct((4, rows, wide), BF16),
        scratch_shapes=[
            pltpu.VMEM((width, tokens), BF16),
            pltpu.VMEM((2, tokens, columns), BF16),
            pltpu.VMEM((n, 2, LINE, rows, columns), BF16),
            pltpu.VMEM((n, LINE, rows, columns), BF16),
            pltpu.VMEM((n, LINE, rows, columns), BF16),
            pltpu.VMEM((n, LINE, rows, columns), BF16),
            pltpu.VMEM((rows, columns), F32),
            pltpu.VMEM((n, rows, columns), BF16),
            dma((2,)),
            dma,
            dma((2, n)),
            dma((2, n, LINE)),
            dma((2, n, LINE)),
            dma((n,)),
            dma((2, n)),
            dma((2, n)),
            dma((2, n)),
        ],
        compiler_params=pltpu.CompilerParams(vmem_limit_bytes=60 * MIB, collective_id=4, has_side_effects=True),
        cost_estimate=pl.CostEstimate(
            flops=2 * width * tokens * wide, bytes_accessed=80 * MIB, transcendentals=0
        ),
        name="expert_grads",
    )(x_t, top_t, dgu, gated)


def late_reduce_kernel(
    in_ref,
    out_ref,
    own_buf,
    core_buf,
    parts,
    y_buf,
    right_buf,
    left_buf,
    total,
    mine,
    far_buf,
    whole,
    load_sem,
    core_sems,
    y_sems,
    right_sems,
    left_sems,
    own_sem,
    far_sems,
    near_sems,
):
    n = parts.shape[0]
    rows, columns = parts.shape[3:]
    rep = lax.axis_index("rep")
    half = lax.rem(rep, 2)
    to_core, to_far = {"rep": rep + 1 - 2 * half}, {"rep": lax.rem(rep + 2, 4)}
    place, across, add_across, step_right, step_left, collect, drain, greet = line_reduce(
        parts, y_buf, right_buf, left_buf, y_sems, right_sems, left_sems
    )

    def span(which, c):
        return pl.ds(pl.multiple_of((which * n + c) * columns, columns), columns)

    def load(c):
        return pltpu.make_async_copy(in_ref.at[:, span(half, c)], own_buf.at[c], load_sem.at[c])

    def from_core(c):
        return send_to(
            in_ref.at[:, span(1 - half, c)], core_buf.at[c], core_sems.at[0, c], core_sems.at[1, c], to_core
        )

    def over_x(c):
        return send_to(mine.at[c], far_buf.at[c], far_sems.at[0, c], far_sems.at[1, c], to_far)

    def over_core(c):
        return send_to(
            whole.at[c], out_ref.at[:, span(half, c)], near_sems.at[0, c], near_sems.at[1, c], to_core
        )

    def keep(c):
        return pltpu.make_async_copy(whole.at[c], out_ref.at[:, span(half, c)], own_sem.at[c])

    for c in range(n):
        load(c).start()
    greet([to_core, to_far])
    for c in range(n):
        from_core(c).start()

    def produce(c):
        load(c).wait()
        from_core(c).wait_recv()
        for t in range(2 * LINE):
            here = pl.ds(t * rows, rows)
            parts[c, t % 2, t // 2] = (own_buf[c, here].astype(F32) + core_buf[c, here].astype(F32)).astype(BF16)
        across(c).start()

    def finish(c):
        collect(c, total)
        mine[c] = total[...].astype(BF16)
        over_x(c).start()

    def complete(c):
        over_x(c).wait_recv()
        whole[c] = (mine[c].astype(F32) + far_buf[c].astype(F32)).astype(BF16)
        over_core(c).start()
        keep(c).start()

    def step(i, carry):
        between(i, 0, n, lambda: produce(i))
        between(i, 1, n + 1, lambda: add_across(i - 1))
        to_right_chunk, to_left_chunk = i - 1 - place, i - LINE + place
        between(to_right_chunk, 0, n, lambda: step_right(to_right_chunk))
        between(to_left_chunk, 0, n, lambda: step_left(to_left_chunk))
        between(i, LINE, n + LINE, lambda: finish(i - LINE))
        between(i, LINE + 1, n + LINE + 1, lambda: complete(i - LINE - 1))
        return carry

    lax.fori_loop(0, n + LINE + 1, step, 0)

    def end(c, carry):
        drain(c)
        from_core(c).wait_send()
        over_x(c).wait_send()
        over_core(c).wait_send()
        keep(c).wait()
        send_to(
            whole.at[c], out_ref.at[:, span(1 - half, c)], near_sems.at[0, c], near_sems.at[1, c], to_core
        ).wait_recv()
        return carry

    lax.fori_loop(0, n, end, 0)


def late_reduce(values, columns=256):
    width, wide = values.shape
    n = wide // 2 // columns
    rows = width // (2 * LINE)
    dma = pltpu.SemaphoreType.DMA
    anywhere = pl.BlockSpec(memory_space=pl.ANY)
    return pl.pallas_call(
        late_reduce_kernel,
        in_specs=[anywhere],
        out_specs=anywhere,
        out_shape=jax.ShapeDtypeStruct((rows, wide), BF16),
        scratch_shapes=[
            pltpu.VMEM((n, width, columns), BF16),
            pltpu.VMEM((n, width, columns), BF16),
            pltpu.VMEM((n, 2, LINE, rows, columns), BF16),
            pltpu.VMEM((n, LINE, rows, columns), BF16),
            pltpu.VMEM((n, LINE, rows, columns), BF16),
            pltpu.VMEM((n, LINE, rows, columns), BF16),
            pltpu.VMEM((rows, columns), F32),
            pltpu.VMEM((n, rows, columns), BF16),
            pltpu.VMEM((n, rows, columns), BF16),
            pltpu.VMEM((n, rows, columns), BF16),
            dma((n,)),
            dma((2, n)),
            dma((2, n)),
            dma((2, n, LINE)),
            dma((2, n, LINE)),
            dma((n,)),
            dma((2, n)),
            dma((2, n)),
        ],
        compiler_params=pltpu.CompilerParams(vmem_limit_bytes=48 * MIB, collective_id=5, has_side_effects=True),
        cost_estimate=pl.CostEstimate(flops=0, bytes_accessed=16 * MIB, transcendentals=0),
        name="late_reduce",
    )(values)


def flatten_kernel(starts, lead_ref, *refs):
    parts, flat_ref, square_ref = refs[: len(starts)], refs[len(starts)], refs[len(starts) + 1]
    scratch, sems = refs[len(starts) + 2 : -1], refs[-1]
    step = pl.program_id(0)
    steps = pl.num_programs(0)
    slot = lax.rem(step, 2)
    flat = flat_ref.reshape(flat_ref.shape[1] // LANES, LANES)
    lead_places = ((0, 0, 1), (1, starts[2] - 17 , 1), (2, starts[2] - 16, 16))

    def copies(index, where):
        out = []
        for n, (start, buffer) in enumerate(zip(starts, scratch)):
            size = buffer.shape[1]
            out.append(pltpu.make_async_copy(buffer.at[where], flat.at[pl.ds(start + index * size, size)], sems.at[where, n]))
        return out

    @pl.when(step == 0)
    def _():
        square_ref[...] = jnp.sum(lead_ref[...] * lead_ref[...], keepdims=True).reshape(1, 1) + jnp.zeros_like(square_ref)
        for n, (source, target, size) in enumerate(lead_places):
            copy = pltpu.make_async_copy(lead_ref.at[pl.ds(source, size)], flat.at[pl.ds(target, size)], sems.at[2, n])
            copy.start()
            copy.wait()

    @pl.when(step >= 2)
    def _():
        for copy in copies(step - 2, slot):
            copy.wait()

    total = jnp.zeros((8, LANES), F32)
    for part, buffer in zip(parts, scratch):
        rows = part.shape[-2]
        wide = buffer.shape[1] // rows
        reps = part.shape[0] if len(part.shape) == 3 else 1
        each = wide // reps
        for r in range(reps):
            for c in range(each):
                lanes = slice(c * LANES, (c + 1) * LANES)
                value = (part[r, :, lanes] if len(part.shape) == 3 else part[:, lanes]).astype(F32)
                buffer[slot, pl.ds(r * each + c, rows, stride=wide), :] = value
                square = value * value
                for k in range(0, rows, 8):
                    total += square[k : k + 8]
    square_ref[...] += jnp.sum(total, keepdims=True).reshape(1, 1)
    for copy in copies(step, slot):
        copy.start()

    @pl.when(step == steps - 1)
    def _():
        for copy in copies(step - 1, 1 - slot):
            copy.wait()
        for copy in copies(step, slot):
            copy.wait()

def flatten(size, lead, parts, tile=16):
    rows = parts[0][0].shape[-2]
    widths = [columns * (p.shape[0] if p.ndim == 3 else 1) // LANES for p, columns, _ in parts]
    starts, at = [], 1
    for n, w in enumerate(widths):
        if n == 2: at += 1 + 16
        starts.append(at); at += rows * w
    specs = []
    for p, columns, place in parts:
        if p.ndim == 3:
            specs.append(pl.BlockSpec((p.shape[0], tile, columns), lambda i, place=place: (0, i, place)))
        else:
            specs.append(pl.BlockSpec((tile, columns), lambda i, place=place: (i, place)))
    return pl.pallas_call(
        functools.partial(flatten_kernel, starts),
        grid=(rows // tile,),
        in_specs=[pl.BlockSpec(lead.shape, lambda i: (0, 0))] + specs,
        out_specs=[pl.BlockSpec(memory_space=pl.ANY), pl.BlockSpec((1, 1), lambda i: (0, 0))],
        out_shape=[jax.ShapeDtypeStruct((1, size), F32), jax.ShapeDtypeStruct((1, 1), F32)],
        scratch_shapes=[pltpu.VMEM((2, tile * w, LANES), F32) for w in widths] + [pltpu.SemaphoreType.DMA((3, 4))],
        compiler_params=pltpu.CompilerParams(vmem_limit_bytes=48 * MIB),
        name="flatten",
    )(lead, *[p for p, _, _ in parts])

HALF_ROWS = 1056


def moments(grad, first, second, scale):
    clipped = grad * scale
    new_first = BETA_ONE * first + (1.0 - BETA_ONE) * clipped
    new_second = BETA_TWO * second + (1.0 - BETA_TWO) * clipped * clipped
    return new_first, new_second


def inner_step(new_first, new_second, weight):
    root = jnp.sqrt(new_second * (1.0 / (1.0 - BETA_TWO**STEP))) + ADAM_EPS
    return -INNER_RATE * (new_first * (1.0 / (1.0 - BETA_ONE**STEP)) / root + DECAY_RATE * weight)


def flat_chunks(rows):
    chunks, at, half_at = [], 0, 0
    while at < rows:
        size = min(2 * HALF_ROWS, rows - at)
        half = -(-size // 32) * 16
        chunks.append((at, size, half_at, half))
        at, half_at = at + size, half_at + half
    return chunks


def step_kernel(
    square_ref,
    g_ref,
    f_ref,
    s_ref,
    w_ref,
    norm_ref,
    total,
    g_buf,
    f_buf,
    s_buf,
    w_buf,
    step_buf,
    near_buf,
    far_buf,
    sum_buf,
    square_mine,
    square_all,
    in_sem,
    near_send,
    near_recv,
    far_send,
    far_recv,
    back_send,
    back_recv,
    own_sem,
    square_send,
    square_recv,
):
    rows = g_ref.shape[-1] // LANES
    chunks = flat_chunks(rows)
    count = len(chunks)
    shards = lax.axis_size("shard")
    shard, rep = lax.axis_index("shard"), lax.axis_index("rep")
    side = lax.rem(rep, 2)
    to_core, to_far = {"rep": rep + 1 - 2 * side}, {"rep": lax.rem(rep + 2, 4)}

    def other(k):
        return {"shard": lax.rem(shard + k, shards)}

    barrier = pltpu.get_barrier_semaphore()
    greeted = [to_core, to_far] + [other(k) for k in range(1, shards)]
    for device in greeted:
        pl.semaphore_signal(barrier, inc=1, device_id=device, device_id_type=MESH)

    def loads(i):
        at, size, _, _ = chunks[i]
        pairs = (g_ref, g_buf), (f_ref.at[0], f_buf), (s_ref.at[0], s_buf), (w_ref, w_buf)
        return [
            pltpu.make_async_copy(
                ref.at[:, pl.ds(at * LANES, size * LANES)],
                buf.at[i % 2, :, pl.ds(0, size * LANES)],
                in_sem.at[i % 2, n],
            )
            for n, (ref, buf) in enumerate(pairs)
        ]

    def remote(source, target, send, receive, device):
        return pltpu.make_async_remote_copy(
            src_ref=source, dst_ref=target, send_sem=send, recv_sem=receive, device_id=device, device_id_type=MESH
        )

    def near(i):
        _, _, at, half = chunks[i]
        span = pl.ds(at, half)
        return remote(step_buf.at[1 - side, span], near_buf.at[span], near_send.at[i], near_recv.at[i], to_core)

    def far(i):
        _, _, at, half = chunks[i]
        span = pl.ds(at, half)
        return remote(step_buf.at[side, span], far_buf.at[span], far_send.at[i], far_recv.at[i], to_far)

    def back(i):
        _, _, at, half = chunks[i]
        span = pl.ds(at, half)
        return remote(sum_buf.at[span], total.at[side, span], back_send.at[i], back_recv.at[i], to_core)

    def keep(i):
        _, _, at, half = chunks[i]
        span = pl.ds(at, half)
        return pltpu.make_async_copy(sum_buf.at[span], total.at[side, span], own_sem.at[i])

    for copy in loads(0):
        copy.start()
    pl.semaphore_wait(barrier, len(greeted))

    def square_copy(k):
        return remote(square_mine, square_all.at[shard], square_send.at[k], square_recv.at[shard], other(k))

    square_mine[...] = jnp.broadcast_to(square_ref[...], square_mine.shape)
    square_all[shard] = square_mine[...]
    for k in range(1, shards):
        square_copy(k).start()
    for k in range(1, shards):
        source = lax.rem(shard + k, shards)
        remote(
            square_mine, square_all.at[source], square_send.at[k], square_recv.at[source], other(k)
        ).wait_recv()
    norm = jnp.sqrt(jnp.sum(square_all[...], axis=0))
    norm_ref[...] = norm[:1, :1]
    scale = (CLIP_NORM / jnp.maximum(norm, CLIP_NORM))[:1]

    def blocks(size):
        return 48 if size % 48 == 0 else 16

    def compute(i):
        _, _, at, half = chunks[i]
        block = blocks(half)
        for h in (0, 1):

            def body(j, carry):
                here = pl.multiple_of(j * block, 16)
                span = pl.ds(pl.multiple_of((h * half + here) * LANES, LANES), block * LANES)
                grad, first, second, weight = (
                    buf[i % 2, :, span].reshape(block, LANES) for buf in (g_buf, f_buf, s_buf, w_buf)
                )
                new_first, new_second = moments(grad, first, second, scale)
                step = inner_step(new_first, new_second, weight)
                step_buf[h, pl.ds(at + here, block)] = step.astype(BF16)
                return carry

            lax.fori_loop(0, half // block, body, 0)

    def add(i, left, right, target):
        _, _, at, half = chunks[i]
        block = blocks(half)

        def body(j, carry):
            span = pl.ds(pl.multiple_of(at + j * block, 16), block)
            target[span] = (left[span].astype(F32) + right[span].astype(F32)).astype(BF16)
            return carry

        lax.fori_loop(0, half // block, body, 0)

    for i in range(count + 2):
        if i < count:
            for copy in loads(i):
                copy.wait()
            if i + 1 < count:
                for copy in loads(i + 1):
                    copy.start()
            compute(i)
            near(i).start()
        if 1 <= i <= count:
            near(i - 1).wait_recv()
            add(i - 1, step_buf.at[side], near_buf, step_buf.at[side])
            far(i - 1).start()
        if i >= 2:
            far(i - 2).wait_recv()
            add(i - 2, step_buf.at[side], far_buf, sum_buf)
            back(i - 2).start()
            keep(i - 2).start()
    for k in range(1, shards):
        square_copy(k).wait_send()
    for i in range(count):
        near(i).wait_send()
        far(i).wait_send()
        back(i).wait_send()
        keep(i).wait()
        _, _, at, half = chunks[i]
        span = pl.ds(at, half)
        remote(
            sum_buf.at[span], total.at[1 - side, span], back_send.at[i], back_recv.at[i], to_core
        ).wait_recv()


def summed_step(square, grad, first, second, weight):
    rows = grad.shape[-1] // LANES
    chunks = flat_chunks(rows)
    count = len(chunks)
    halves = sum(chunk[3] for chunk in chunks)
    size = chunks[0][3] * 2
    shards = lax.axis_size("shard")
    dma = pltpu.SemaphoreType.DMA
    anywhere = pl.BlockSpec(memory_space=pl.ANY)
    return pl.pallas_call(
        step_kernel,
        in_specs=[pl.BlockSpec(memory_space=pltpu.VMEM)] + [anywhere] * 4,
        out_specs=[pl.BlockSpec(memory_space=pltpu.VMEM), anywhere],
        out_shape=[jax.ShapeDtypeStruct((1, 1), F32), jax.ShapeDtypeStruct((2, halves, LANES), BF16)],
        scratch_shapes=[pltpu.VMEM((2, 1, size * LANES), F32)] * 4
        + [
            pltpu.VMEM((2, halves, LANES), BF16),
            pltpu.VMEM((halves, LANES), BF16),
            pltpu.VMEM((halves, LANES), BF16),
            pltpu.VMEM((halves, LANES), BF16),
            pltpu.VMEM((8, LANES), F32),
            pltpu.VMEM((shards, 8, LANES), F32),
            dma((2, 4)),
        ]
        + [dma((count,))] * 7
        + [dma((shards,))] * 2,
        compiler_params=pltpu.CompilerParams(
            vmem_limit_bytes=48 * MIB, collective_id=3, has_side_effects=True
        ),
        cost_estimate=pl.CostEstimate(flops=0, bytes_accessed=64 * MIB, transcendentals=0),
        name="summed_step",
    )(square, grad, first, second, weight)


def update_kernel(
    reps, norm_ref, g, f, s, total, mom, nf, ns, nm, up, tg, tf, ts, tm, tt, tnf, tns, tnm, tup, sems
):
    rows = g.shape[-1] // LANES
    chunks = flat_chunks(rows)
    whole = [c for c in chunks if c[1] == 2 * HALF_ROWS]
    scale = CLIP_NORM / jnp.maximum(norm_ref[...], CLIP_NORM)

    def body(g_ref, f_ref, s_ref, t_ref, m_ref, nf_ref, ns_ref, nm_ref, up_ref):
        half = t_ref.shape[1]
        size = g_ref.shape[0]
        nf_ref[...], ns_ref[...] = moments(g_ref[...], f_ref[...], s_ref[...], scale)
        for h in (0, 1):
            span = slice(h * half, min((h + 1) * half, size))
            pseudo = t_ref[h, : span.stop - span.start].astype(F32) * (-1.0 / reps)
            new = OUTER_MOMENTUM * m_ref[span] + pseudo
            nm_ref[span] = new
            up_ref[span] = -OUTER_RATE * (pseudo + OUTER_MOMENTUM * new)

    def view(ref):
        return ref.reshape(rows, LANES)

    ins, outs = [view(g), view(f), view(s), total, view(mom)], [view(r) for r in (nf, ns, nm, up)]
    wide = pl.BlockSpec((2 * HALF_ROWS, LANES), lambda i: (i, 0))
    halves = pl.BlockSpec((2, HALF_ROWS, LANES), lambda i: (0, i, 0))
    if whole:
        pltpu.emit_pipeline(
            body, grid=(len(whole),), in_specs=[wide, wide, wide, halves, wide], out_specs=[wide] * 4
        )(*ins, *outs)
    for at, size, half_at, half in chunks[len(whole) :]:

        def part(n, ref):
            return ref.at[:, pl.ds(half_at, half)] if n == 3 else ref.at[pl.ds(at, size)]

        copies = [
            pltpu.make_async_copy(part(n, ref), buf, sems.at[n]) for n, (ref, buf) in enumerate(zip(ins, (tg, tf, ts, tt, tm)))
        ]
        for copy in copies:
            copy.start()
        for copy in copies:
            copy.wait()
        body(tg, tf, ts, tt, tm, tnf, tns, tnm, tup)
        copies = [
            pltpu.make_async_copy(buf, ref.at[pl.ds(at, size)], sems.at[n])
            for n, (buf, ref) in enumerate(zip((tnf, tns, tnm, tup), outs))
        ]
        for copy in copies:
            copy.start()
        for copy in copies:
            copy.wait()


def update(reps, norm, grad, first, second, total, mom):
    _, size, _, half = flat_chunks(grad.shape[-1] // LANES)[-1]
    anywhere = pl.BlockSpec(memory_space=pl.ANY)
    tail = pltpu.VMEM((size, LANES), F32)
    return pl.pallas_call(
        functools.partial(update_kernel, reps),
        in_specs=[pl.BlockSpec(memory_space=pltpu.VMEM)] + [anywhere] * 5,
        out_specs=[anywhere] * 4,
        out_shape=[jax.ShapeDtypeStruct(ref.shape, F32) for ref in (first, second, mom, mom)],
        scratch_shapes=[tail] * 4
        + [pltpu.VMEM((2, half, LANES), BF16)]
        + [tail] * 4
        + [pltpu.SemaphoreType.DMA((5,))],
        compiler_params=pltpu.CompilerParams(vmem_limit_bytes=48 * MIB),
        cost_estimate=pl.CostEstimate(flops=0, bytes_accessed=120 * MIB, transcendentals=0),
        name="update",
    )(norm, grad, first, second, total, mom)


def rms_scale(rows):
    return lax.rsqrt(jnp.mean(rows * rows, axis=-1, keepdims=True) + EPSILON)


def rms_backward(rows, scale, gain, grad_out):
    grad_gain = jnp.sum(grad_out * rows * scale, axis=0)
    inner = jnp.sum(grad_out * gain * rows, axis=-1, keepdims=True)
    grad_in = scale * gain * grad_out - rows * scale * scale * scale * inner / rows.shape[-1]
    return grad_in, grad_gain


def rotate(rows, cosine, sine):
    half = HEAD_SIZE // 2
    front, back = rows[:, :half], rows[:, half:]
    return jnp.concatenate([front * cosine - back * sine, back * cosine + front * sine], axis=1)


def per_device(
    tokens,
    cotangent,
    routes,
    branch,
    attn_gain,
    query_key_value_weight,
    w_attn_out,
    ffn_gain,
    w_router,
    w_in,
    w_out,
    adam_first,
    adam_second,
    outer_mom,
):
    shards = lax.axis_size("shard")
    reps = lax.axis_size("rep")
    count = tokens.shape[2]
    width = tokens.shape[3]
    prompt = count - CONTINUATION_LEN
    local = EXPERTS // reps
    groups = None
    if shards > GROUP_SIZE:
        groups = [list(range(i, i + GROUP_SIZE)) for i in range(0, shards, GROUP_SIZE)]
    shard_pos = lax.axis_index("shard") % GROUP_SIZE
    rep_pos = lax.axis_index("rep")
    branch_len = branch.reshape(())
    x_in = tokens.reshape(count, width).astype(F32)
    top_low = cotangent.reshape(count, width)
    grad_top = top_low.astype(F32)
    route_ids = routes.reshape(count, TOP)
    gather = functools.partial(lax.all_gather, axis_name="shard", axis=0, tiled=True)
    rows = width // shards
    qkv_columns = Q_WIDTH + 2 * KV_WIDTH
    fast = shards == 2 * LINE and reps == 4 and rows == LANES
    flat_path = fast and outer_mom.shape[-1] % LANES == 0

    small = jnp.concatenate(
        [query_key_value_weight, w_attn_out, w_router, attn_gain[:, None], ffn_gain[:, None]], axis=1
    )
    small = jnp.pad(small, ((0, 0), (0, -small.shape[1] % LANES)))
    tokens_low = tokens.reshape(count, width)
    if fast:
        prompt_low, small_full, all_top = start_gather(tokens_low, small, top_low)
        small_full = small_full.reshape(width, small.shape[1])
    else:
        prompt_low = lax.all_gather(tokens_low[:prompt], "shard", axis=0, tiled=False, axis_index_groups=groups)
        small_full = gather(small)
        by_rep = lax.all_gather(top_low, "rep", axis=0, tiled=False)
        core_pos = rep_pos + 1 - 2 * (rep_pos % 2)
        all_top = jnp.stack([top_low] + [by_rep[i] for i in (core_pos, (rep_pos + 2) % 4, 3 - rep_pos)])
    prompt_low = prompt_low.reshape(GROUP_SIZE * prompt, width)
    qkv_full = small_full[:, :qkv_columns]
    attn_out_full = small_full[:, qkv_columns : qkv_columns + Q_WIDTH]
    router_full = small_full[:, qkv_columns + Q_WIDTH : qkv_columns + Q_WIDTH + EXPERTS]
    gains = small_full[:, qkv_columns + Q_WIDTH + EXPERTS :].astype(F32)
    attn_gain_full, ffn_gain_full = gains[:, 0], gains[:, 1]
    w_both = jnp.concatenate(
        [
            lax.dynamic_slice_in_dim(w_in, rep_pos * local * 2 * F, local * 2 * F, 1),
            lax.dynamic_slice_in_dim(w_out, rep_pos * local * F, local * F, 1),
        ],
        axis=1,
    )
    w_both, prompt_low = lax.optimization_barrier((w_both, prompt_low))
    w_both = gather(w_both)

    def normed(values):
        scale = rms_scale(values)
        return (values * scale * attn_gain_full).astype(BF16), scale

    def angles_of(positions):
        half = HEAD_SIZE // 2
        inverse_freq = ROPE_BASE ** (-(jnp.arange(half, dtype=F32) * 2.0) / HEAD_SIZE)
        angles = inverse_freq[:, None] * positions.astype(F32)[None, :]
        return jnp.cos(angles)[None], jnp.sin(angles)[None]

    def project(source, start, size, turn):
        rows = dot(qkv_full[:, start : start + size], source, (0, 1))
        rows = rows.reshape(size // HEAD_SIZE, HEAD_SIZE, source.shape[0])
        return (rotate(rows, *turn) if turn is not None else rows).astype(BF16)

    def keys_values(source, turn):
        return jnp.stack([project(source, Q_WIDTH, KV_WIDTH, turn), project(source, Q_WIDTH + KV_WIDTH, KV_WIDTH, None)])

    normed_attn, attn_scale = normed(x_in)
    normed_prompt, _ = normed(prompt_low.astype(F32))
    prompt_turn = angles_of(jnp.arange(GROUP_SIZE * prompt, dtype=jnp.int32))
    own_turn = angles_of(
        jnp.concatenate(
            [
                shard_pos * prompt + jnp.arange(prompt, dtype=jnp.int32),
                branch_len + jnp.arange(CONTINUATION_LEN, dtype=jnp.int32),
            ]
        )
    )
    continued_turn = tuple(part[..., prompt:] for part in own_turn)
    prompt_kv = keys_values(normed_prompt, prompt_turn)
    own_kv = keys_values(normed_attn[prompt:], continued_turn)
    query = project(normed_attn, 0, Q_WIDTH, own_turn)
    where = jnp.stack([shard_pos.astype(jnp.int32), branch_len])
    attn, lse = attn_forward(where, query, prompt_kv, own_kv)
    attn_low = attn.astype(BF16).reshape(Q_WIDTH, count)
    x_mid = x_in + dot(attn_low, attn_out_full, (0, 1))

    ffn_scale = rms_scale(x_mid)
    normed_ffn = (x_mid * ffn_scale * ffn_gain_full).astype(BF16)
    logits = dot(normed_ffn, router_full, (1, 0))
    chosen = jnp.any(route_ids[:, :, None] == jnp.arange(EXPERTS, dtype=jnp.int32), axis=1)
    gates = jax.nn.softmax(jnp.where(chosen, logits, NEGATIVE), axis=-1)
    gates = jnp.where(chosen, gates, 0.0)

    gates_out = jnp.pad(gates.T.reshape(reps, local, count), ((0, 0), (0, 8 - local), (0, 0)))
    _, dx_own, dx_core, dx_far, y_keep, y_give, normed_t, top_t, dgu, gated, dgate_part = experts(
        normed_ffn, all_top, gates_out, w_both
    )
    grad_from_experts = dx_own.astype(F32) + dx_core.astype(F32) + dx_far.astype(F32)
    grad_gates = dgate_part[:, :local].reshape(EXPERTS, count).T
    to_core = [(i, i + 1 - 2 * (i % 2)) for i in range(reps)]
    to_far = [(i, (i + 2) % reps) for i in range(reps)]
    y_near = y_keep.astype(F32) + lax.ppermute(y_give, "rep", to_core).astype(F32)
    y_sum = y_near[0] + lax.ppermute(y_near[1].astype(BF16), "rep", to_far).astype(F32)
    block_out = (x_mid + y_sum).astype(BF16)

    def rep_sum(values):
        for pairs in (to_core, to_far):
            values = (values.astype(F32) + lax.ppermute(values, "rep", pairs).astype(F32)).astype(BF16)
        return values

    def expert_term(left, right):
        return dot(left, right.reshape(reps * count, -1), (1, 0)).astype(BF16)

    grad_logits = (gates * (grad_gates - jnp.sum(gates * grad_gates, axis=-1, keepdims=True))).astype(BF16)
    grad_router_w = dot(normed_ffn, grad_logits, (0, 0))
    grad_normed_ffn = grad_from_experts + dot(grad_logits, router_full, (1, 1))
    grad_mid_norm, grad_ffn_gain = rms_backward(x_mid, ffn_scale, ffn_gain_full, grad_normed_ffn)
    grad_mid = grad_top + grad_mid_norm
    grad_branch = grad_mid.astype(BF16)
    grad_attn_w = dot(grad_branch, attn_low, (0, 1))
    grad_attn = dot(attn_out_full, grad_branch, (0, 1)).astype(BF16).reshape(QUERY_HEADS, HEAD_SIZE, count)
    expert_columns = local * 3 * F
    if fast:
        expert_rows = expert_grads(
            normed_t,
            top_t,
            dgu.reshape(reps * count, -1),
            gated.reshape(reps * count, -1),
        )
    else:
        terms = jnp.concatenate([expert_term(normed_t, dgu), expert_term(top_t, gated)], axis=1)
        terms = lax.psum_scatter(terms, "shard", scatter_dimension=0, tiled=True)
        expert_rows = lax.all_gather(terms, "rep", axis=0, tiled=False)
    early = jnp.concatenate(
        [grad_attn_w.astype(BF16), grad_router_w.astype(BF16), grad_ffn_gain[:, None].astype(BF16)], axis=1
    )
    early = jnp.pad(early, ((0, 0), (0, -early.shape[1] % LANES)))
    grad_attn, early, expert_rows = lax.optimization_barrier((grad_attn, early, expert_rows))
    early = lax.psum_scatter(early, "shard", scatter_dimension=0, tiled=True)

    delta = jnp.sum(grad_attn.astype(F32) * attn, axis=1).reshape(KEY_VALUE_HEADS, PER_KEY, count)
    grad_query, grad_prompt_kv, grad_own_kv = attn_backward(
        where, query, prompt_kv, own_kv, grad_attn, lse, delta
    )

    early, grad_query, grad_prompt_kv, grad_own_kv = lax.optimization_barrier(
        (early, grad_query, grad_prompt_kv, grad_own_kv)
    )
    early = rep_sum(early)
    attn_rows, router_rows = early[:, :Q_WIDTH], early[:, Q_WIDTH : Q_WIDTH + EXPERTS]
    ffn_gain_rows = early[:, Q_WIDTH + EXPERTS]

    def turn_back(values, turn):
        spun = rotate(values, turn[0], -turn[1])
        return spun.astype(BF16).reshape(-1, values.shape[-1])

    grad_query = turn_back(grad_query, own_turn)
    grad_prompt_kv = (
        turn_back(grad_prompt_kv[0].astype(F32), prompt_turn),
        grad_prompt_kv[1].reshape(KV_WIDTH, GROUP_SIZE * prompt),
    )
    grad_own_kv = (turn_back(grad_own_kv[0], continued_turn), grad_own_kv[1].astype(BF16).reshape(KV_WIDTH, -1))
    late = [dot(normed_attn, grad_query, (0, 1)).astype(BF16)]
    for shared, own in zip(grad_prompt_kv, grad_own_kv):
        late.append((dot(normed_prompt, shared, (0, 1)) + dot(normed_attn[prompt:], own, (0, 1))).astype(BF16))
    late = jnp.concatenate(late, axis=1)
    if fast:
        qkv_rows = late_reduce(late)
    else:
        qkv_rows = rep_sum(lax.psum_scatter(late, "shard", scatter_dimension=0, tiled=True))
    qkv_rows, grad_prompt_kv = lax.optimization_barrier((qkv_rows, grad_prompt_kv))
    attn_gain_rows = jnp.sum(
        qkv_rows.astype(F32) * query_key_value_weight.astype(F32), axis=1
    ) / attn_gain.astype(F32)

    grad_projected = [grad_query]
    for shared, own in zip(grad_prompt_kv, grad_own_kv):
        shared = lax.psum_scatter(shared, "shard", scatter_dimension=1, tiled=True, axis_index_groups=groups)
        grad_projected.append(jnp.concatenate([shared, own], axis=1))
    grad_projected = jnp.concatenate(grad_projected, axis=0)
    grad_normed_attn = dot(grad_projected, qkv_full, (0, 1))
    grad_x_norm, _ = rms_backward(x_in, attn_scale, attn_gain_full, grad_normed_attn)
    grad_input = grad_mid + grad_x_norm

    in_columns = local * 2 * F
    if flat_path:
        size = outer_mom.shape[-1]

        def lead(first, second, rest):
            parts = [first[None].astype(F32), second[None].astype(F32), rest.reshape(-1, LANES).astype(F32)]
            return jnp.concatenate(parts, axis=0)

        def whole(values):
            return values, values.shape[-1], 0

        weight_flat, _ = flatten(
            size,
            lead(attn_gain, ffn_gain, w_router),
            [whole(query_key_value_weight), whole(w_attn_out), whole(w_in), whole(w_out)],
        )
        total_grad, square = flatten(
            size,
            lead(attn_gain_rows, ffn_gain_rows, router_rows),
            [
                whole(qkv_rows),
                whole(attn_rows),
                (expert_rows, in_columns, 0),
                (expert_rows, expert_columns - in_columns, in_columns // (expert_columns - in_columns)),
            ],
        )
        grad_norm, step_sum = summed_step(square, total_grad, adam_first, adam_second, weight_flat)
        new_first, new_second, new_mom, weight_update = update(
            reps, grad_norm, total_grad, adam_first, adam_second, step_sum, outer_mom
        )
        grad_norm = grad_norm.reshape(())
    else:
        weight_flat = jnp.concatenate(
            [
                portion.astype(F32).reshape(-1)
                for portion in (attn_gain, query_key_value_weight, w_attn_out, ffn_gain, w_router, w_in, w_out)
            ]
        )
        total_grad = jnp.concatenate(
            [
                portion.astype(F32).reshape(-1)
                for portion in (
                    attn_gain_rows,
                    qkv_rows,
                    attn_rows,
                    ffn_gain_rows,
                    router_rows,
                    expert_rows[:, :, :in_columns].transpose(1, 0, 2),
                    expert_rows[:, :, in_columns:].transpose(1, 0, 2),
                )
            ]
        )
        grad_norm = jnp.sqrt(lax.psum(jnp.sum(total_grad * total_grad), "shard"))
        new_first, new_second = moments(
            total_grad,
            adam_first.reshape(-1),
            adam_second.reshape(-1),
            CLIP_NORM / jnp.maximum(grad_norm, CLIP_NORM),
        )
        step = inner_step(new_first, new_second, weight_flat)
        pseudo = -(lax.psum(step.astype(BF16), "rep").astype(F32) / reps)
        new_mom = OUTER_MOMENTUM * outer_mom.reshape(-1) + pseudo
        weight_update = -OUTER_RATE * (pseudo + OUTER_MOMENTUM * new_mom)
    return (
        block_out.reshape(tokens.shape),
        grad_input.reshape(tokens.shape),
        total_grad.reshape(outer_mom.shape),
        grad_norm,
        new_first.reshape(adam_first.shape),
        new_second.reshape(adam_second.shape),
        new_mom.reshape(outer_mom.shape),
        weight_update.reshape(outer_mom.shape),
    )


def solution(mesh):
    by_token = P("rep", "shard", None, None)
    by_state = P("rep", "shard", None)
    by_row = P("shard", None)
    placed = (
        by_token,
        by_token,
        by_token,
        P("rep", "shard"),
        P("shard"),
        by_row,
        by_row,
        P("shard"),
        by_row,
        by_row,
        by_row,
        by_state,
        by_state,
        by_row,
    )
    return jax.shard_map(
        per_device,
        mesh=mesh,
        in_specs=placed,
        out_specs=(by_token, by_token, by_row, P(), by_state, by_state, by_row, by_row),
        check_vma=False,
    )
```

```python
import functools

import jax
import jax.numpy as jnp
from jax import lax
from jax.experimental import pallas as pl
from jax.experimental.pallas import tpu as pltpu
from jax.sharding import PartitionSpec as P

QUERY_HEADS = 16
KEY_VALUE_HEADS = 8
HEAD_SIZE = 64
F = 512
EXPERTS = 16
TOP = 8
GROUP_SIZE = 8
CONTINUATION_LEN = 512
STEP = 10

EPSILON = 1e-06
NEGATIVE = -1e30
ROPE_BASE = 10000.0
BETA_ONE = 0.9
BETA_TWO = 0.95
ADAM_EPS = 1e-08
INNER_RATE = 0.01
DECAY_RATE = 0.1
OUTER_RATE = 0.7
OUTER_MOMENTUM = 0.9
CLIP_NORM = 1.0

LOG2E = 1.4426950408889634
LANES = 128
MIB = 1 << 20
BF16 = jnp.bfloat16
F32 = jnp.float32
PER_KEY = QUERY_HEADS // KEY_VALUE_HEADS
Q_WIDTH = QUERY_HEADS * HEAD_SIZE
KV_WIDTH = KEY_VALUE_HEADS * HEAD_SIZE


def dot(left, right, dims):
    return lax.dot_general(left, right, ((dims[:1], dims[1:]), ((), ())), preferred_element_type=F32)


def split_three(value):
    high = value.astype(BF16)
    rest = value - high.astype(F32)
    middle = rest.astype(BF16)
    low = (rest - middle.astype(F32)).astype(BF16)
    return high, middle, low


def augment_query(q_ref, start, width):
    rows = jnp.concatenate([q_ref[g, :, start : start + width] for g in range(PER_KEY)], axis=1)
    scaled = rows.astype(F32) * (HEAD_SIZE**-0.5 * LOG2E)
    high = scaled.astype(BF16)
    low = (scaled - high.astype(F32)).astype(BF16)
    return rows, high, low


def block_of(ref, index, block):
    span = pl.ds(pl.multiple_of(index * block, block), block)
    return ref[0, 0, :, span], ref[1, 0, :, span]


def causal(width, columns):
    key_pos = lax.broadcasted_iota(jnp.int32, (width, columns), 0)
    query_pos = lax.broadcasted_iota(jnp.int32, (width, columns), 1) % width
    return key_pos <= query_pos


SAFE_BOUND = 48.0


def attn_forward_kernel(where_ref, q_ref, kv_ref, own_ref, o_ref, lse_ref, peak_ref, acc_ref):
    block = own_ref.shape[-1]
    columns = PER_KEY * block
    shard_pos = where_ref[0]
    branch = where_ref[1]
    ones = jnp.ones((16, block), BF16)
    pad = jnp.zeros((16 - 3, columns), BF16)
    whole = branch // block

    def longest(key):
        squares = key.astype(F32)
        return jnp.max(jnp.sum(squares * squares, axis=0, keepdims=True), axis=1, keepdims=True)

    longest_key = jnp.sqrt(jnp.maximum(longest(kv_ref[0, 0]), longest(own_ref[0, 0])))

    def emit(start, result, lse):
        for g in range(PER_KEY):
            o_ref[g, :, start : start + block] = result[:, g * block : (g + 1) * block].astype(BF16)
            lse_ref[0, g : g + 1, start : start + block] = lse[:, g * block : (g + 1) * block]

    def sweep(advance, start):
        def body(index, carry):
            advance(*block_of(kv_ref, index, block), None)
            return carry

        if start == 0:
            lax.fori_loop(0, shard_pos, body, 0)
            advance(*block_of(kv_ref, shard_pos, block), causal(block, columns))
        else:
            lax.fori_loop(0, whole, body, 0)

            @pl.when(branch % block != 0)
            def _():
                key_pos = lax.broadcasted_iota(jnp.int32, (block, columns), 0)
                advance(*block_of(kv_ref, whole, block), key_pos < branch % block)

            advance(own_ref[0, 0], own_ref[1, 0], causal(block, columns))

    def bounded(start, high, low, bound):
        query = jnp.concatenate([high, low, *split_three(-bound), pad], axis=0)

        def advance(key, value, mask):
            scores = dot(jnp.concatenate([key, key, ones], axis=0), query, (0, 0))
            if mask is not None:
                scores = jnp.where(mask, scores, NEGATIVE)
            probs = jnp.exp2(scores).astype(BF16)
            acc_ref[...] += dot(jnp.concatenate([value, ones], axis=0), probs, (1, 0))

        acc_ref[...] = jnp.zeros_like(acc_ref)
        sweep(advance, start)
        total = acc_ref[HEAD_SIZE : HEAD_SIZE + 1]
        emit(start, acc_ref[:HEAD_SIZE] / total, bound + jnp.log2(total))

    def running(start, high, low):
        query = jnp.concatenate([high, low], axis=0)

        def advance(key, value, mask):
            scores = dot(jnp.concatenate([key, key], axis=0), query, (0, 0))
            if mask is not None:
                scores = jnp.where(mask, scores, NEGATIVE)
            old = peak_ref[...]
            new = jnp.maximum(old, jnp.max(scores, axis=0, keepdims=True))
            probs = jnp.exp2(scores - new).astype(BF16)
            shrink = jnp.exp2(old - new)
            part = dot(jnp.concatenate([value, ones], axis=0), probs, (1, 0))
            peak_ref[...] = new
            acc_ref[...] = acc_ref[...] * shrink + part

        peak_ref[...] = jnp.full_like(peak_ref, NEGATIVE)
        acc_ref[...] = jnp.zeros_like(acc_ref)
        sweep(advance, start)
        total = acc_ref[HEAD_SIZE : HEAD_SIZE + 1]
        emit(start, acc_ref[:HEAD_SIZE] / total, peak_ref[...] + jnp.log2(total))

    for start in (0, block):
        rows, high, low = augment_query(q_ref, start, block)
        wide = rows.astype(F32)
        length = jnp.sqrt(jnp.sum(wide * wide, axis=0, keepdims=True))
        bound = length * longest_key * (1.02 * HEAD_SIZE**-0.5 * LOG2E)
        safe = jnp.max(bound) < SAFE_BOUND

        @pl.when(safe)
        def _(start=start, high=high, low=low, bound=bound):
            bounded(start, high, low, bound)

        @pl.when(jnp.logical_not(safe))
        def _(start=start, high=high, low=low):
            running(start, high, low)


def attn_forward(where, query, prompt_kv, own_kv):
    tokens = query.shape[-1]
    block = own_kv.shape[-1]
    columns = PER_KEY * block
    keys = prompt_kv.shape[-1]
    return pl.pallas_call(
        attn_forward_kernel,
        grid=(query.shape[0] // PER_KEY,),
        in_specs=[
            pl.BlockSpec(memory_space=pltpu.SMEM),
            pl.BlockSpec((PER_KEY, HEAD_SIZE, tokens), lambda h: (h, 0, 0)),
            pl.BlockSpec((2, 1, HEAD_SIZE, keys), lambda h: (0, h, 0, 0)),
            pl.BlockSpec((2, 1, HEAD_SIZE, block), lambda h: (0, h, 0, 0)),
        ],
        out_specs=[
            pl.BlockSpec((PER_KEY, HEAD_SIZE, tokens), lambda h: (h, 0, 0)),
            pl.BlockSpec((1, PER_KEY, tokens), lambda h: (h, 0, 0)),
        ],
        out_shape=[
            jax.ShapeDtypeStruct(query.shape, BF16),
            jax.ShapeDtypeStruct((query.shape[0] // PER_KEY, PER_KEY, tokens), F32),
        ],
        scratch_shapes=[
            pltpu.VMEM((1, columns), F32),
            pltpu.VMEM((HEAD_SIZE + 16, columns), F32),
        ],
        compiler_params=pltpu.CompilerParams(vmem_limit_bytes=48 * MIB),
        cost_estimate=pl.CostEstimate(
            flops=4 * tokens * keys * query.shape[0] * HEAD_SIZE,
            bytes_accessed=16 * MIB,
            transcendentals=query.shape[0] * tokens * keys,
        ),
        name="attn_forward",
    )(where, query, prompt_kv, own_kv)


def attn_backward_kernel(
    where_ref, q_ref, kv_ref, own_ref, go_ref, o_ref, lse_ref, dq_ref, dkv_ref, down_ref, dkv_acc, dq_acc
):
    block = own_ref.shape[-1]
    columns = PER_KEY * block
    shard_pos = where_ref[0]
    branch = where_ref[1]
    ones = jnp.ones((16, block), BF16)
    pad = jnp.zeros((16 - 3, columns), BF16)

    def begin(start):
        rows, high, low = augment_query(q_ref, start, block)

        def lanes(ref):
            return jnp.concatenate([ref[0, g : g + 1, start : start + block] for g in range(PER_KEY)], axis=1)

        lse = split_three(-lanes(lse_ref))
        grad, out = (
            jnp.concatenate([ref[g, :, start : start + block] for g in range(PER_KEY)], axis=1)
            for ref in (go_ref, o_ref)
        )
        delta = split_three(-jnp.sum(grad.astype(F32) * out.astype(F32), axis=0, keepdims=True))
        query = jnp.concatenate([high, low, *lse, pad], axis=0)
        grad_plus = jnp.concatenate([grad, *delta, pad], axis=0)
        dq_acc[...] = jnp.zeros_like(dq_acc)
        scaled = (rows.astype(F32) * HEAD_SIZE**-0.5).astype(BF16)
        return query, scaled, grad_plus, grad

    def terms(state, key, value, mask):
        query, scaled, grad_plus, grad = state
        scores = dot(jnp.concatenate([key, key, ones], axis=0), query, (0, 0))
        if mask is not None:
            scores = jnp.where(mask, scores, NEGATIVE)
        probs = jnp.exp2(scores)
        dv = dot(grad, probs.astype(BF16), (1, 1))
        grad_probs = dot(jnp.concatenate([value, ones], axis=0), grad_plus, (0, 0))
        grad_scores = (probs * grad_probs).astype(BF16)
        dq_acc[...] += dot(key, grad_scores, (1, 0))
        return dot(scaled, grad_scores, (1, 1)), dv

    def add(index, state, mask):
        dk, dv = terms(state, *block_of(kv_ref, index, block), mask)
        span = pl.ds(pl.multiple_of(index * block, block), block)
        dkv_acc[0, :, span] += dk
        dkv_acc[1, :, span] += dv

    def finish(start):
        total = dq_acc[...] * HEAD_SIZE**-0.5
        for g in range(PER_KEY):
            dq_ref[g, :, start : start + block] = total[:, g * block : (g + 1) * block]

    def run(state, count):
        def body(index, carry):
            add(2 * index, state, None)
            add(2 * index + 1, state, None)
            return carry

        lax.fori_loop(0, count // 2, body, 0)

        @pl.when(count % 2 == 1)
        def _():
            add(count - 1, state, None)

    dkv_acc[...] = jnp.zeros_like(dkv_acc)
    state = begin(0)
    run(state, shard_pos)
    add(shard_pos, state, causal(block, columns))
    finish(0)

    state = begin(block)
    whole = branch // block
    run(state, whole)

    @pl.when(branch % block != 0)
    def _():
        key_pos = lax.broadcasted_iota(jnp.int32, (block, columns), 0)
        add(whole, state, key_pos < branch % block)

    dk, dv = terms(state, own_ref[0, 0], own_ref[1, 0], causal(block, columns))
    down_ref[0, 0] = dk
    down_ref[1, 0] = dv
    finish(block)
    dkv_ref[:, 0] = dkv_acc[...].astype(BF16)


def attn_backward(where, query, prompt_kv, own_kv, grad_out, out, lse):
    tokens = query.shape[-1]
    block = own_kv.shape[-1]
    columns = PER_KEY * block
    keys = prompt_kv.shape[-1]
    by_head = pl.BlockSpec((PER_KEY, HEAD_SIZE, tokens), lambda h: (h, 0, 0))
    by_keys = pl.BlockSpec((2, 1, HEAD_SIZE, keys), lambda h: (0, h, 0, 0))
    by_own = pl.BlockSpec((2, 1, HEAD_SIZE, block), lambda h: (0, h, 0, 0))
    by_row = pl.BlockSpec((1, PER_KEY, tokens), lambda h: (h, 0, 0))
    return pl.pallas_call(
        attn_backward_kernel,
        grid=(query.shape[0] // PER_KEY,),
        in_specs=[pl.BlockSpec(memory_space=pltpu.SMEM), by_head, by_keys, by_own, by_head, by_head, by_row],
        out_specs=[by_head, by_keys, by_own],
        out_shape=[
            jax.ShapeDtypeStruct(query.shape, F32),
            jax.ShapeDtypeStruct(prompt_kv.shape, BF16),
            jax.ShapeDtypeStruct(own_kv.shape, F32),
        ],
        scratch_shapes=[
            pltpu.VMEM((2, HEAD_SIZE, keys), F32),
            pltpu.VMEM((HEAD_SIZE, columns), F32),
        ],
        compiler_params=pltpu.CompilerParams(vmem_limit_bytes=56 * MIB),
        cost_estimate=pl.CostEstimate(
            flops=10 * tokens * keys * query.shape[0] * HEAD_SIZE,
            bytes_accessed=32 * MIB,
            transcendentals=query.shape[0] * tokens * keys,
        ),
        name="attn_backward",
    )(where, query, prompt_kv, own_kv, grad_out, out, lse)


MESH = pl.DeviceIdType.MESH
LINE = 4
TOKEN_PARTS = 4


def start_kernel(
    x_ref,
    w_ref,
    top_ref,
    tok_all,
    w_all,
    top_all,
    own_sem,
    line_recv,
    right_send,
    left_send,
    y_send,
    y_recv,
    x_send,
    x_recv,
    core_send,
    core_recv,
    top_send,
    top_recv,
):
    part = tok_all.shape[1] // TOKEN_PARTS
    quarter = w_all.shape[2]
    half = top_ref.shape[0] // 2
    me = lax.axis_index("shard")
    place, column = me // 2, lax.rem(me, 2)
    rep = lax.axis_index("rep")
    far, core = lax.rem(rep + 2, 4), rep + 1 - 2 * lax.rem(rep, 2)
    to_right, to_left, to_y = {"shard": me + 2}, {"shard": me - 2}, {"shard": me + 1 - 2 * column}
    to_far, to_core = {"rep": far}, {"rep": core}
    weights, mirrored = 0, TOKEN_PARTS + 1
    last = TOKEN_PARTS
    streams = TOKEN_PARTS + 2

    def piece(i, origin, side):
        if i == weights:
            return w_all.at[2 * origin + side, rep]
        k = (i if i != mirrored else last) - 1
        return tok_all.at[2 * origin + side, pl.ds(k * part, part)]

    def side_of(i):
        return 1 - column if i == mirrored else column

    def own(i):
        if i == weights:
            return w_ref.at[pl.ds(pl.multiple_of(rep * quarter, quarter), quarter)]
        if i == mirrored:
            return piece(i, place, 1 - column)
        return x_ref.at[pl.ds((i - 1) * part, part)]

    def remote(source, target, send, receive, device):
        return pltpu.make_async_remote_copy(
            src_ref=source, dst_ref=target, send_sem=send, recv_sem=receive, device_id=device, device_id_type=MESH
        )

    def source(i, origin, at_home):
        return own(i) if at_home else piece(i, origin, side_of(i))

    def right(i, origin, at_home=False):
        return remote(
            source(i, origin, at_home),
            piece(i, origin, side_of(i)),
            right_send.at[i, origin],
            line_recv.at[i, origin],
            to_right,
        )

    def left(i, origin, at_home=False):
        return remote(
            source(i, origin, at_home),
            piece(i, origin, side_of(i)),
            left_send.at[i, origin],
            line_recv.at[i, origin],
            to_left,
        )

    def abreast(i, origin, at_home=False):
        return remote(
            source(i, origin, at_home), piece(i, origin, column), y_send.at[i, origin], y_recv.at[i, origin], to_y
        )

    def over_x(origin, side, at_home=False):
        target = piece(weights, origin, side)
        source_ref = own(weights) if at_home else target
        return remote(source_ref, target, x_send.at[origin, side], x_recv.at[origin, side], to_far)

    def over_core(group, origin, side, at_home=False):
        target = w_all.at[2 * origin + side, rep if group == 0 else far]
        source_ref = own(weights) if at_home else target
        return remote(
            source_ref, target, core_send.at[group, origin, side], core_recv.at[group, origin, side], to_core
        )

    def top_far(h):
        return remote(
            top_ref.at[pl.ds(h * half, half)],
            top_all.at[2, pl.ds(h * half, half)],
            top_send.at[0, h],
            top_recv.at[0, h],
            to_far,
        )

    def top_core(h):
        return remote(
            top_ref.at[pl.ds(h * half, half)],
            top_all.at[1, pl.ds(h * half, half)],
            top_send.at[1, h],
            top_recv.at[1, h],
            to_core,
        )

    def top_diagonal(h):
        return remote(
            top_all.at[2, pl.ds(h * half, half)],
            top_all.at[3, pl.ds(h * half, half)],
            top_send.at[2, h],
            top_recv.at[2, h],
            to_core,
        )

    has_right, has_left = place < LINE - 1, place > 0
    barrier = pltpu.get_barrier_semaphore()

    def greet(device):
        pl.semaphore_signal(barrier, inc=1, device_id=device, device_id_type=MESH)

    for device in (to_y, to_far, to_core):
        greet(device)

    @pl.when(has_right)
    def _():
        greet(to_right)

    @pl.when(has_left)
    def _():
        greet(to_left)

    pl.semaphore_wait(barrier, 3 + has_right.astype(jnp.int32) + has_left.astype(jnp.int32))

    def along(i, origin, at_home=False):
        @pl.when(has_right)
        def _():
            right(i, origin, at_home).start()

        @pl.when(has_left)
        def _():
            left(i, origin, at_home).start()

    order = [weights, last] + list(range(1, last))
    for i in order:
        along(i, place, True)
        abreast(i, place, True).start()
        if i == weights:
            over_x(place, column, True).start()
            over_core(0, place, column, True).start()
            for h in (0, 1):
                top_far(h).start()
    for h in (0, 1):
        top_core(h).start()
    own_copies = [
        pltpu.make_async_copy(own(i), piece(i, place, column), own_sem.at[i]) for i in range(streams - 1)
    ]
    own_copies.append(pltpu.make_async_copy(top_ref, top_all.at[0], own_sem.at[streams - 1]))
    for copy in own_copies:
        copy.start()
    abreast(last, place).wait_recv()
    along(mirrored, place, True)

    def weights_across(origin):
        abreast(weights, origin).wait_recv()
        over_x(origin, 1 - column).start()
        over_core(0, origin, 1 - column).start()

    weights_across(place)
    for d in range(1, LINE):
        before, after = place - d, place + d
        from_left, from_right = before >= 0, after < LINE
        for i in [weights, last, mirrored] + list(range(1, last)):

            @pl.when(from_left)
            def _(i=i):
                right(i, before).wait_recv()

                @pl.when(has_right)
                def _():
                    right(i, before).start()

                if i != last and i != mirrored:
                    abreast(i, before).start()
                if i == weights:
                    over_x(before, column).start()
                    over_core(0, before, column).start()

            @pl.when(from_right)
            def _(i=i):
                left(i, after).wait_recv()

                @pl.when(has_left)
                def _():
                    left(i, after).start()

                if i != last and i != mirrored:
                    abreast(i, after).start()
                if i == weights:
                    over_x(after, column).start()
                    over_core(0, after, column).start()

        @pl.when(from_left)
        def _():
            weights_across(before)

        @pl.when(from_right)
        def _():
            weights_across(after)

        if d >= 2:
            h = d - 2
            top_far(h).wait_recv()
            top_diagonal(h).start()

    for origin in range(LINE):
        for side in (0, 1):
            remote(
                w_all.at[2 * origin + side, far],
                w_all.at[2 * origin + side, far],
                x_send.at[origin, side],
                x_recv.at[origin, side],
                to_far,
            ).wait_recv()
            over_core(1, origin, side).start()

    for origin in range(LINE):
        for i in range(1, last):
            abreast(i, origin).wait_recv()
        for side in (0, 1):
            for group in (0, 1):
                over_core(group, origin, side).wait_recv()
    for h in (0, 1):
        top_core(h).wait_recv()
        top_diagonal(h).wait_recv()
        for copy in (top_far(h), top_core(h), top_diagonal(h)):
            copy.wait_send()
    for copy in own_copies:
        copy.wait()
    for origin in range(LINE):
        for i in range(streams):

            @pl.when(has_right & (origin <= place))
            def _(i=i, origin=origin):
                right(i, origin).wait_send()

            @pl.when(has_left & (origin >= place))
            def _(i=i, origin=origin):
                left(i, origin).wait_send()

            if i != last and i != mirrored:
                abreast(i, origin).wait_send()
        for side in (0, 1):
            over_x(origin, side).wait_send()
            for group in (0, 1):
                over_core(group, origin, side).wait_send()
    abreast(last, place).wait_send()


def start_gather(x, small, top):
    rows, width = x.shape
    prompt = rows - CONTINUATION_LEN
    own_rows, columns = small.shape
    dma = pltpu.SemaphoreType.DMA
    streams = TOKEN_PARTS + 2
    anywhere = pl.BlockSpec(memory_space=pl.ANY)
    return pl.pallas_call(
        start_kernel,
        in_specs=[anywhere] * 3,
        out_specs=[anywhere] * 3,
        out_shape=[
            jax.ShapeDtypeStruct((2 * LINE, prompt, width), BF16),
            jax.ShapeDtypeStruct((2 * LINE, 4, own_rows // 4, columns), BF16),
            jax.ShapeDtypeStruct((4, rows, width), BF16),
        ],
        scratch_shapes=[
            dma((streams,)),
            dma((streams, LINE)),
            dma((streams, LINE)),
            dma((streams, LINE)),
            dma((streams, LINE)),
            dma((streams, LINE)),
            dma((LINE, 2)),
            dma((LINE, 2)),
            dma((2, LINE, 2)),
            dma((2, LINE, 2)),
            dma((3, 2)),
            dma((3, 2)),
        ],
        compiler_params=pltpu.CompilerParams(collective_id=2, has_side_effects=True),
        cost_estimate=pl.CostEstimate(flops=0, bytes_accessed=64 * MIB, transcendentals=0),
        name="start_gather",
    )(x, small, top)


ORDER = ((0, 0), (0, 1), (1, 0), (3, 0), (2, 0), (3, 1), (2, 1), (1, 1))


def experts_kernel(
    x_hbm,
    top_hbm,
    gates_ref,
    w_ref,
    all_x,
    dx_own,
    dx_core,
    dx_far,
    y_keep,
    y_give,
    xt_all,
    tt_all,
    dgu_all,
    gh_all,
    dg_all,
    x_buf,
    top_buf,
    y_buf,
    dx_buf,
    xt_buf,
    tt_buf,
    dgu_buf,
    gh_buf,
    relay,
    y_acc,
    dx_acc,
    gates_all,
    gates_now,
    dg_now,
    dg_mine,
    in_sem,
    out_sem,
    copy_sem,
    send_sem,
    recv_sem,
    small_send,
    small_recv,
):
    tile = x_buf.shape[1]
    count = w_ref.shape[1] // (3 * F)
    step = pl.program_id(0)
    steps = len(ORDER)
    slot = lax.rem(step, 2)
    me = lax.axis_index("rep")
    home = [me, me + 1 - 2 * lax.rem(me, 2), lax.rem(me + 2, 4), 3 - me]

    def remote(source, target, send, receive, relation):
        return pltpu.make_async_remote_copy(
            src_ref=source,
            dst_ref=target,
            send_sem=send,
            recv_sem=receive,
            device_id={"rep": home[relation]},
            device_id_type=MESH,
        )

    def half(ref, half_index, *lead):
        return ref.at[(*lead, pl.ds(half_index * tile, tile))]

    def to_core(h):
        return remote(half(x_hbm, h), half(all_x, h, me), send_sem.at[0, h], recv_sem.at[0, h], 1)

    def to_far(h):
        return remote(half(x_hbm, h), half(all_x, h, me), send_sem.at[1, h], recv_sem.at[1, h], 2)

    def forward(h):
        part = half(all_x, h, home[2])
        return remote(part, part, send_sem.at[2, h], recv_sem.at[2, h], 1)

    def give(kind, h, buffer):
        if kind == 3:
            return remote(buffer, relay.at[h], send_sem.at[3, h], recv_sem.at[3, h], 1)
        if kind == 2:
            return remote(buffer, half(dx_far, h), send_sem.at[4, h], recv_sem.at[4, h], 2)
        return remote(buffer, half(dx_core, h), send_sem.at[5, h], recv_sem.at[5, h], 1)

    def small_gates(k):
        return remote(gates_ref.at[home[k]], gates_all.at[me], small_send.at[0, k], small_recv.at[0, k], k)

    def small_back(k):
        return remote(dg_mine.at[home[k]], dg_all.at[me], small_send.at[1, k], small_recv.at[1, k], k)

    def load_x(i):
        kind, h = ORDER[i]
        source = half(x_hbm, h) if kind == 0 else half(all_x, h, home[kind])
        return pltpu.make_async_copy(source, x_buf.at[i % 2], in_sem.at[i % 2, 0])

    def load_top(i):
        kind, h = ORDER[i]
        return pltpu.make_async_copy(half(top_hbm, h, kind), top_buf.at[i % 2], in_sem.at[i % 2, 1])

    def stores(i):
        kind, h = ORDER[i]
        out = []
        rows = 2 * tile

        def turned(ref, place):
            here = pl.multiple_of(place * rows + h * tile, LANES)
            return ref.at[:, pl.ds(here, tile)]

        targets = (
            (y_buf, half((y_keep, y_give, y_keep, y_give)[kind], h, (0, 0, 1, 1)[kind])),
            (dgu_buf, half(dgu_all, h, home[kind])),
            (gh_buf, half(gh_all, h, kind)),
            (xt_buf, turned(xt_all, home[kind])),
            (tt_buf, turned(tt_all, kind)),
        )
        for n, (buffer, target) in enumerate(targets):
            out.append(pltpu.make_async_copy(buffer.at[i % 2], target, out_sem.at[i % 2, n]))
        return out

    def store_dx(i):
        kind, h = ORDER[i]
        if kind == 0:
            return pltpu.make_async_copy(dx_buf.at[i % 2], half(dx_own, h), out_sem.at[i % 2, 5])
        return give(kind, h, dx_buf.at[i % 2])

    def finish(i):
        for copy in stores(i):
            copy.wait()
        if ORDER[i][0] == 0:
            store_dx(i).wait()
        else:
            store_dx(i).wait_send()

    own_copy = pltpu.make_async_copy(x_hbm, all_x.at[me], copy_sem)
    for i in range(steps):
        kind, h = ORDER[i]

        @pl.when(step == i)
        def _(i=i, kind=kind, h=h):
            if i == 0:
                barrier = pltpu.get_barrier_semaphore()
                for k in (1, 2, 3):
                    pl.semaphore_signal(
                        barrier, inc=1, device_id={"rep": home[k]}, device_id_type=MESH
                    )
                pl.semaphore_wait(barrier, 3)
                to_far(0).start()
                for n in (0, 1):
                    to_core(n).start()
                for k in (1, 2, 3):
                    small_gates(k).start()
                own_copy.start()
                load_top(0).start()
                load_x(0).start()
                gates_all[me] = gates_ref[me]
            if i == 1:
                to_far(1).start()
                for n in (0, 1):
                    to_core(n).wait_recv()
            if i == 2:
                for k in (1, 2, 3):
                    small_gates(k).wait_recv()
                to_far(0).wait_recv()
                forward(0).start()
            if i == 3:
                to_far(1).wait_recv()
                forward(1).start()
            if i == 4:
                forward(1).wait_recv()
            load_x(i).wait()
            load_top(i).wait()
            if i + 1 < steps:
                load_top(i + 1).start()
                if i + 1 != 3:
                    load_x(i + 1).start()
            if i >= 2:
                finish(i - 2)
            gates_now[...] = jnp.transpose(gates_all[home[kind]][:, h * tile : (h + 1) * tile])

    x = x_buf[slot]
    top = top_buf[slot]
    xt_buf[slot] = x.T
    tt_buf[slot] = top.T
    columns = []
    for e in range(count):
        w_in = w_ref[:, e * 2 * F : (e + 1) * 2 * F]
        w_out = w_ref[:, (count * 2 + e) * F : (count * 2 + e + 1) * F]
        gate_up = dot(x, w_in, (1, 0))
        g = gate_up[:, :F]
        u = gate_up[:, F:]
        sig = jax.nn.sigmoid(g)
        act = g * sig
        hidden = (act * u).astype(BF16).astype(F32)
        raw = dot(top, w_out, (1, 0))
        columns.append(jnp.sum(hidden * raw, axis=1, keepdims=True))
        gate = gates_now[:, e : e + 1]
        gated = (hidden * gate).astype(BF16)
        gh_buf[slot, :, e * F : (e + 1) * F] = gated
        grad_hidden = raw * gate
        dg = (grad_hidden * u * sig * (1.0 + g * (1.0 - sig))).astype(BF16)
        du = (grad_hidden * act).astype(BF16)
        dgu = jnp.concatenate([dg, du], axis=1)
        dgu_buf[slot, :, e * 2 * F : (e + 1) * 2 * F] = dgu
        y = dot(gated, w_out, (1, 1))
        dx = dot(dgu, w_in, (1, 1))
        if e == 0:
            y_acc[...] = y
            dx_acc[...] = dx
        elif e < count - 1:
            y_acc[...] += y
            dx_acc[...] += dx
        else:
            y_buf[slot] = (y_acc[...] + y).astype(BF16)
            dx_acc[...] += dx
    columns.append(jnp.zeros((tile, 8 - count), F32))
    dg_now[...] = jnp.transpose(jnp.concatenate(columns, axis=1))

    for i in range(steps):
        kind, h = ORDER[i]

        @pl.when(step == i)
        def _(i=i, kind=kind, h=h):
            dg_mine[home[kind], :, h * tile : (h + 1) * tile] = dg_now[...]
            if kind == 2:
                give(3, h, dx_buf.at[0]).wait_recv()
                dx_buf[i % 2] = (dx_acc[...] + relay[h].astype(F32)).astype(BF16)
            else:
                dx_buf[i % 2] = dx_acc[...].astype(BF16)
            store_dx(i).start()
            for copy in stores(i):
                copy.start()
            if i == 2:
                forward(0).wait_recv()
                load_x(3).start()
            if i == steps - 1:
                own_back = pltpu.make_async_copy(dg_mine.at[me], dg_all.at[me], small_send.at[1, 0])
                own_back.start()
                for k in (1, 2, 3):
                    small_back(k).start()
                finish(i - 1)
                finish(i)
                own_copy.wait()
                own_back.wait()
                for n in (0, 1):
                    to_far(n).wait_send()
                    to_core(n).wait_send()
                    forward(n).wait_send()
                    give(2, n, dx_buf.at[0]).wait_recv()
                    give(1, n, dx_buf.at[0]).wait_recv()
                for k in (1, 2, 3):
                    small_gates(k).wait_send()
                    small_back(k).wait()


def experts(x, all_top, gates, weights):
    rows, width = x.shape
    reps = all_top.shape[0]
    count = weights.shape[1] // (3 * F)
    tile = rows // 2
    anywhere = pl.BlockSpec(memory_space=pl.ANY)
    fixed = pl.BlockSpec(weights.shape, lambda i: (0, 0), pipeline_mode=pl.Buffered(1))
    small = pl.BlockSpec((reps, 8, rows), lambda i: (0, 0, 0))
    dma = pltpu.SemaphoreType.DMA
    return pl.pallas_call(
        experts_kernel,
        grid=(len(ORDER),),
        in_specs=[anywhere, anywhere, small, fixed],
        out_specs=[anywhere] * 11,
        out_shape=[
            jax.ShapeDtypeStruct((reps, rows, width), BF16),
            jax.ShapeDtypeStruct((rows, width), BF16),
            jax.ShapeDtypeStruct((rows, width), BF16),
            jax.ShapeDtypeStruct((rows, width), BF16),
            jax.ShapeDtypeStruct((2, rows, width), BF16),
            jax.ShapeDtypeStruct((2, rows, width), BF16),
            jax.ShapeDtypeStruct((width, reps * rows), BF16),
            jax.ShapeDtypeStruct((width, reps * rows), BF16),
            jax.ShapeDtypeStruct((reps, rows, count * 2 * F), BF16),
            jax.ShapeDtypeStruct((reps, rows, count * F), BF16),
            jax.ShapeDtypeStruct((reps, 8, rows), F32),
        ],
        scratch_shapes=[
            pltpu.VMEM((2, tile, width), BF16),
            pltpu.VMEM((2, tile, width), BF16),
            pltpu.VMEM((2, tile, width), BF16),
            pltpu.VMEM((2, tile, width), BF16),
            pltpu.VMEM((2, width, tile), BF16),
            pltpu.VMEM((2, width, tile), BF16),
            pltpu.VMEM((2, tile, count * 2 * F), BF16),
            pltpu.VMEM((2, tile, count * F), BF16),
            pltpu.VMEM((2, tile, width), BF16),
            pltpu.VMEM((tile, width), F32),
            pltpu.VMEM((tile, width), F32),
            pltpu.VMEM((reps, 8, rows), F32),
            pltpu.VMEM((tile, 8), F32),
            pltpu.VMEM((8, tile), F32),
            pltpu.VMEM((reps, 8, rows), F32),
            dma((2, 2)),
            dma((2, 6)),
            dma,
            dma((6, 2)),
            dma((6, 2)),
            dma((2, 4)),
            dma((2, 4)),
        ],
        compiler_params=pltpu.CompilerParams(
            vmem_limit_bytes=58 * MIB, collective_id=1, has_side_effects=True
        ),
        cost_estimate=pl.CostEstimate(
            flops=12 * reps * rows * width * count * F,
            bytes_accessed=80 * MIB,
            transcendentals=reps * rows * count * F,
        ),
        name="experts",
    )(x, all_top, gates, weights)


def send_to(source, target, send, receive, device):
    return pltpu.make_async_remote_copy(
        src_ref=source, dst_ref=target, send_sem=send, recv_sem=receive, device_id=device, device_id_type=MESH
    )


def line_reduce(parts, y_buf, right_buf, left_buf, y_sems, right_sems, left_sems):
    me = lax.axis_index("shard")
    place, side = me // 2, lax.rem(me, 2)
    to_y, to_right, to_left = {"shard": me + 1 - 2 * side}, {"shard": me + 2}, {"shard": me - 2}

    def across(c):
        return send_to(parts.at[c, 1 - side], y_buf.at[c], y_sems.at[0, c], y_sems.at[1, c], to_y)

    def add_across(c):
        across(c).wait_recv()
        for p in range(LINE):
            parts[c, side, p] = (parts[c, side, p].astype(F32) + y_buf[c, p].astype(F32)).astype(BF16)

    def hop(c, p, buf, sems, device, first):
        source = parts.at[c, side, p] if first else buf.at[c, p]
        return send_to(source, buf.at[c, p], sems.at[0, c, p], sems.at[1, c, p], device)

    def run(c, p, buf, sems, device, is_first, passes):
        @pl.when(passes & is_first)
        def _():
            hop(c, p, buf, sems, device, True).start()

        @pl.when(passes & jnp.logical_not(is_first))
        def _():
            hop(c, p, buf, sems, device, False).wait_recv()
            buf[c, p] = (parts[c, side, p].astype(F32) + buf[c, p].astype(F32)).astype(BF16)
            hop(c, p, buf, sems, device, False).start()

    def step_right(c):
        for p in range(1, LINE):
            run(c, p, right_buf, right_sems, to_right, place == 0, place < p)

    def step_left(c):
        for p in range(LINE - 1):
            run(c, p, left_buf, left_sems, to_left, place == LINE - 1, place > p)

    def collect(c, total):
        total[...] = parts[c, side, place].astype(F32)

        @pl.when(place > 0)
        def _():
            hop(c, place, right_buf, right_sems, to_right, False).wait_recv()
            total[...] += right_buf[c, place].astype(F32)

        @pl.when(place < LINE - 1)
        def _():
            hop(c, place, left_buf, left_sems, to_left, False).wait_recv()
            total[...] += left_buf[c, place].astype(F32)

    def drain(c):
        across(c).wait_send()
        for p in range(1, LINE):

            @pl.when(place < p)
            def _(p=p):
                hop(c, p, right_buf, right_sems, to_right, False).wait_send()

        for p in range(LINE - 1):

            @pl.when(place > p)
            def _(p=p):
                hop(c, p, left_buf, left_sems, to_left, False).wait_send()

    def greet(extra):
        barrier = pltpu.get_barrier_semaphore()
        for device in [to_y] + extra:
            pl.semaphore_signal(barrier, inc=1, device_id=device, device_id_type=MESH)
        has_right, has_left = place < LINE - 1, place > 0

        @pl.when(has_right)
        def _():
            pl.semaphore_signal(barrier, inc=1, device_id=to_right, device_id_type=MESH)

        @pl.when(has_left)
        def _():
            pl.semaphore_signal(barrier, inc=1, device_id=to_left, device_id_type=MESH)

        count = 1 + len(extra) + has_right.astype(jnp.int32) + has_left.astype(jnp.int32)
        pl.semaphore_wait(barrier, count)

    return place, across, add_across, step_right, step_left, collect, drain, greet


def between(step, low, high, body):
    @pl.when((step >= low) & (step < high))
    def _():
        body()


def expert_grads_kernel(
    xt_ref,
    tt_ref,
    dgu_ref,
    gh_ref,
    out_ref,
    left_op,
    right_op,
    parts,
    y_buf,
    right_buf,
    left_buf,
    total,
    mine,
    load_sem,
    lhs_sem,
    y_sems,
    right_sems,
    left_sems,
    own_sem,
    far_sems,
    near_sems,
    pass_sems,
):
    n = parts.shape[0]
    columns = right_op.shape[2]
    first = dgu_ref.shape[1] // columns
    rows = parts.shape[3]
    rep = lax.axis_index("rep")
    far = lax.rem(rep + 2, 4)
    to_core, to_far = {"rep": rep + 1 - 2 * lax.rem(rep, 2)}, {"rep": far}
    place, across, add_across, step_right, step_left, collect, drain, greet = line_reduce(
        parts, y_buf, right_buf, left_buf, y_sems, right_sems, left_sems
    )

    def load(c, act):
        slot = lax.rem(c, 2)

        @pl.when(c < first)
        def _():
            here = pl.ds(pl.multiple_of(c * columns, columns), columns)
            act(pltpu.make_async_copy(dgu_ref.at[:, here], right_op.at[slot], load_sem.at[slot]))

        @pl.when(c >= first)
        def _():
            here = pl.ds(pl.multiple_of((c - first) * columns, columns), columns)
            act(pltpu.make_async_copy(gh_ref.at[:, here], right_op.at[slot], load_sem.at[slot]))

    def start(copy):
        copy.start()

    def wait(copy):
        copy.wait()

    def place_of(owner, c):
        return out_ref.at[owner, :, pl.ds(pl.multiple_of(c * columns, columns), columns)]

    def over_x(c):
        return send_to(mine.at[c], place_of(rep, c), far_sems.at[0, c], far_sems.at[1, c], to_far)

    def over_core(c):
        return send_to(mine.at[c], place_of(rep, c), near_sems.at[0, c], near_sems.at[1, c], to_core)

    def keep(c):
        return pltpu.make_async_copy(mine.at[c], place_of(rep, c), own_sem.at[c])

    def pass_on(c):
        return send_to(place_of(far, c), place_of(far, c), pass_sems.at[0, c], pass_sems.at[1, c], to_core)

    lhs = pltpu.make_async_copy(xt_ref, left_op, lhs_sem)
    lhs.start()
    load(0, start)
    greet([to_core, to_far])
    lhs.wait()

    def produce(c):
        @pl.when(c == first)
        def _():
            swap = pltpu.make_async_copy(tt_ref, left_op, lhs_sem)
            swap.start()
            swap.wait()

        load(c, wait)

        @pl.when(c + 1 < n)
        def _():
            load(c + 1, start)

        result = dot(left_op[...], right_op[lax.rem(c, 2)], (1, 0)).astype(BF16)
        for t in range(2 * LINE):
            parts[c, t % 2, t // 2] = result[t * rows : (t + 1) * rows]
        across(c).start()

    def finish(c):
        collect(c, total)
        mine[c] = total[...].astype(BF16)
        over_x(c).start()
        over_core(c).start()
        keep(c).start()

    def forward(c):
        over_x(c).wait_recv()
        pass_on(c).start()

    def step(i, carry):
        between(i, 0, n, lambda: produce(i))
        between(i, 1, n + 1, lambda: add_across(i - 1))
        to_right_chunk, to_left_chunk = i - 1 - place, i - LINE + place
        between(to_right_chunk, 0, n, lambda: step_right(to_right_chunk))
        between(to_left_chunk, 0, n, lambda: step_left(to_left_chunk))
        between(i, 5, n + 5, lambda: finish(i - 5))
        between(i, 7, n + 7, lambda: forward(i - 7))
        return carry

    lax.fori_loop(0, n + 7, step, 0)

    def end(c, carry):
        drain(c)
        over_x(c).wait_send()
        over_core(c).wait()
        keep(c).wait()
        pass_on(c).wait()
        return carry

    lax.fori_loop(0, n, end, 0)


def expert_grads(x_t, top_t, dgu, gated, columns=256):
    width, tokens = x_t.shape
    wide = dgu.shape[1] + gated.shape[1]
    n = wide // columns
    rows = width // (2 * LINE)
    dma = pltpu.SemaphoreType.DMA
    anywhere = pl.BlockSpec(memory_space=pl.ANY)
    return pl.pallas_call(
        expert_grads_kernel,
        in_specs=[anywhere] * 4,
        out_specs=anywhere,
        out_shape=jax.ShapeDtypeStruct((4, rows, wide), BF16),
        scratch_shapes=[
            pltpu.VMEM((width, tokens), BF16),
            pltpu.VMEM((2, tokens, columns), BF16),
            pltpu.VMEM((n, 2, LINE, rows, columns), BF16),
            pltpu.VMEM((n, LINE, rows, columns), BF16),
            pltpu.VMEM((n, LINE, rows, columns), BF16),
            pltpu.VMEM((n, LINE, rows, columns), BF16),
            pltpu.VMEM((rows, columns), F32),
            pltpu.VMEM((n, rows, columns), BF16),
            dma((2,)),
            dma,
            dma((2, n)),
            dma((2, n, LINE)),
            dma((2, n, LINE)),
            dma((n,)),
            dma((2, n)),
            dma((2, n)),
            dma((2, n)),
        ],
        compiler_params=pltpu.CompilerParams(vmem_limit_bytes=60 * MIB, collective_id=4, has_side_effects=True),
        cost_estimate=pl.CostEstimate(
            flops=2 * width * tokens * wide, bytes_accessed=80 * MIB, transcendentals=0
        ),
        name="expert_grads",
    )(x_t, top_t, dgu, gated)


def late_reduce_kernel(
    in_ref,
    out_ref,
    own_buf,
    core_buf,
    parts,
    y_buf,
    right_buf,
    left_buf,
    total,
    mine,
    far_buf,
    whole,
    load_sem,
    core_sems,
    y_sems,
    right_sems,
    left_sems,
    own_sem,
    far_sems,
    near_sems,
):
    n = parts.shape[0]
    rows, columns = parts.shape[3:]
    rep = lax.axis_index("rep")
    half = lax.rem(rep, 2)
    to_core, to_far = {"rep": rep + 1 - 2 * half}, {"rep": lax.rem(rep + 2, 4)}
    place, across, add_across, step_right, step_left, collect, drain, greet = line_reduce(
        parts, y_buf, right_buf, left_buf, y_sems, right_sems, left_sems
    )

    def span(which, c):
        return pl.ds(pl.multiple_of((which * n + c) * columns, columns), columns)

    def load(c):
        return pltpu.make_async_copy(in_ref.at[:, span(half, c)], own_buf.at[c], load_sem.at[c])

    def from_core(c):
        return send_to(
            in_ref.at[:, span(1 - half, c)], core_buf.at[c], core_sems.at[0, c], core_sems.at[1, c], to_core
        )

    def over_x(c):
        return send_to(mine.at[c], far_buf.at[c], far_sems.at[0, c], far_sems.at[1, c], to_far)

    def over_core(c):
        return send_to(
            whole.at[c], out_ref.at[:, span(half, c)], near_sems.at[0, c], near_sems.at[1, c], to_core
        )

    def keep(c):
        return pltpu.make_async_copy(whole.at[c], out_ref.at[:, span(half, c)], own_sem.at[c])

    for c in range(n):
        load(c).start()
    greet([to_core, to_far])
    for c in range(n):
        from_core(c).start()

    def produce(c):
        load(c).wait()
        from_core(c).wait_recv()
        for t in range(2 * LINE):
            here = pl.ds(t * rows, rows)
            parts[c, t % 2, t // 2] = (own_buf[c, here].astype(F32) + core_buf[c, here].astype(F32)).astype(BF16)
        across(c).start()

    def finish(c):
        collect(c, total)
        mine[c] = total[...].astype(BF16)
        over_x(c).start()

    def complete(c):
        over_x(c).wait_recv()
        whole[c] = (mine[c].astype(F32) + far_buf[c].astype(F32)).astype(BF16)
        over_core(c).start()
        keep(c).start()

    def step(i, carry):
        between(i, 0, n, lambda: produce(i))
        between(i, 1, n + 1, lambda: add_across(i - 1))
        to_right_chunk, to_left_chunk = i - 1 - place, i - LINE + place
        between(to_right_chunk, 0, n, lambda: step_right(to_right_chunk))
        between(to_left_chunk, 0, n, lambda: step_left(to_left_chunk))
        between(i, LINE, n + LINE, lambda: finish(i - LINE))
        between(i, LINE + 1, n + LINE + 1, lambda: complete(i - LINE - 1))
        return carry

    lax.fori_loop(0, n + LINE + 1, step, 0)

    def end(c, carry):
        drain(c)
        from_core(c).wait_send()
        over_x(c).wait_send()
        over_core(c).wait_send()
        keep(c).wait()
        send_to(
            whole.at[c], out_ref.at[:, span(1 - half, c)], near_sems.at[0, c], near_sems.at[1, c], to_core
        ).wait_recv()
        return carry

    lax.fori_loop(0, n, end, 0)


def late_reduce(values, columns=256):
    width, wide = values.shape
    n = wide // 2 // columns
    rows = width // (2 * LINE)
    dma = pltpu.SemaphoreType.DMA
    anywhere = pl.BlockSpec(memory_space=pl.ANY)
    return pl.pallas_call(
        late_reduce_kernel,
        in_specs=[anywhere],
        out_specs=anywhere,
        out_shape=jax.ShapeDtypeStruct((rows, wide), BF16),
        scratch_shapes=[
            pltpu.VMEM((n, width, columns), BF16),
            pltpu.VMEM((n, width, columns), BF16),
            pltpu.VMEM((n, 2, LINE, rows, columns), BF16),
            pltpu.VMEM((n, LINE, rows, columns), BF16),
            pltpu.VMEM((n, LINE, rows, columns), BF16),
            pltpu.VMEM((n, LINE, rows, columns), BF16),
            pltpu.VMEM((rows, columns), F32),
            pltpu.VMEM((n, rows, columns), BF16),
            pltpu.VMEM((n, rows, columns), BF16),
            pltpu.VMEM((n, rows, columns), BF16),
            dma((n,)),
            dma((2, n)),
            dma((2, n)),
            dma((2, n, LINE)),
            dma((2, n, LINE)),
            dma((n,)),
            dma((2, n)),
            dma((2, n)),
        ],
        compiler_params=pltpu.CompilerParams(vmem_limit_bytes=48 * MIB, collective_id=5, has_side_effects=True),
        cost_estimate=pl.CostEstimate(flops=0, bytes_accessed=16 * MIB, transcendentals=0),
        name="late_reduce",
    )(values)


def flatten_kernel(starts, lead_ref, *refs):
    parts, flat_ref, square_ref = refs[: len(starts)], refs[len(starts)], refs[len(starts) + 1]
    scratch, sems = refs[len(starts) + 2 : -1], refs[-1]
    step = pl.program_id(0)
    steps = pl.num_programs(0)
    slot = lax.rem(step, 2)
    flat = flat_ref.reshape(flat_ref.shape[1] // LANES, LANES)
    lead_places = ((0, 0, 1), (1, starts[2] - 17 , 1), (2, starts[2] - 16, 16))

    def copies(index, where):
        out = []
        for n, (start, buffer) in enumerate(zip(starts, scratch)):
            size = buffer.shape[1]
            out.append(pltpu.make_async_copy(buffer.at[where], flat.at[pl.ds(start + index * size, size)], sems.at[where, n]))
        return out

    @pl.when(step == 0)
    def _():
        square_ref[...] = jnp.sum(lead_ref[...] * lead_ref[...], keepdims=True).reshape(1, 1) + jnp.zeros_like(square_ref)
        for n, (source, target, size) in enumerate(lead_places):
            copy = pltpu.make_async_copy(lead_ref.at[pl.ds(source, size)], flat.at[pl.ds(target, size)], sems.at[2, n])
            copy.start()
            copy.wait()

    @pl.when(step >= 2)
    def _():
        for copy in copies(step - 2, slot):
            copy.wait()

    total = jnp.zeros((8, LANES), F32)
    for part, buffer in zip(parts, scratch):
        rows = part.shape[-2]
        wide = buffer.shape[1] // rows
        reps = part.shape[0] if len(part.shape) == 3 else 1
        each = wide // reps
        for r in range(reps):
            for c in range(each):
                lanes = slice(c * LANES, (c + 1) * LANES)
                value = (part[r, :, lanes] if len(part.shape) == 3 else part[:, lanes]).astype(F32)
                buffer[slot, pl.ds(r * each + c, rows, stride=wide), :] = value
                square = value * value
                for k in range(0, rows, 8):
                    total += square[k : k + 8]
    square_ref[...] += jnp.sum(total, keepdims=True).reshape(1, 1)
    for copy in copies(step, slot):
        copy.start()

    @pl.when(step == steps - 1)
    def _():
        for copy in copies(step - 1, 1 - slot):
            copy.wait()
        for copy in copies(step, slot):
            copy.wait()

def flatten(size, lead, parts, tile=16):
    rows = parts[0][0].shape[-2]
    widths = [columns * (p.shape[0] if p.ndim == 3 else 1) // LANES for p, columns, _ in parts]
    starts, at = [], 1
    for n, w in enumerate(widths):
        if n == 2: at += 1 + 16
        starts.append(at); at += rows * w
    specs = []
    for p, columns, place in parts:
        if p.ndim == 3:
            specs.append(pl.BlockSpec((p.shape[0], tile, columns), lambda i, place=place: (0, i, place)))
        else:
            specs.append(pl.BlockSpec((tile, columns), lambda i, place=place: (i, place)))
    return pl.pallas_call(
        functools.partial(flatten_kernel, starts),
        grid=(rows // tile,),
        in_specs=[pl.BlockSpec(lead.shape, lambda i: (0, 0))] + specs,
        out_specs=[pl.BlockSpec(memory_space=pl.ANY), pl.BlockSpec((1, 1), lambda i: (0, 0))],
        out_shape=[jax.ShapeDtypeStruct((1, size), F32), jax.ShapeDtypeStruct((1, 1), F32)],
        scratch_shapes=[pltpu.VMEM((2, tile * w, LANES), F32) for w in widths] + [pltpu.SemaphoreType.DMA((3, 4))],
        compiler_params=pltpu.CompilerParams(vmem_limit_bytes=48 * MIB),
        name="flatten",
    )(lead, *[p for p, _, _ in parts])

HALF_ROWS = 1056


def moments(grad, first, second, scale):
    clipped = grad * scale
    new_first = BETA_ONE * first + (1.0 - BETA_ONE) * clipped
    new_second = BETA_TWO * second + (1.0 - BETA_TWO) * clipped * clipped
    return new_first, new_second


def inner_step(new_first, new_second, weight):
    root = jnp.sqrt(new_second * (1.0 / (1.0 - BETA_TWO**STEP))) + ADAM_EPS
    return -INNER_RATE * (new_first * (1.0 / (1.0 - BETA_ONE**STEP)) / root + DECAY_RATE * weight)


def flat_chunks(rows):
    chunks, at, half_at = [], 0, 0
    while at < rows:
        size = min(2 * HALF_ROWS, rows - at)
        half = -(-size // 32) * 16
        chunks.append((at, size, half_at, half))
        at, half_at = at + size, half_at + half
    return chunks


def step_kernel(
    square_ref,
    g_ref,
    f_ref,
    s_ref,
    w_ref,
    norm_ref,
    total,
    g_buf,
    f_buf,
    s_buf,
    w_buf,
    step_buf,
    near_buf,
    far_buf,
    sum_buf,
    square_mine,
    square_all,
    in_sem,
    near_send,
    near_recv,
    far_send,
    far_recv,
    back_send,
    back_recv,
    own_sem,
    square_send,
    square_recv,
):
    rows = g_ref.shape[-1] // LANES
    chunks = flat_chunks(rows)
    count = len(chunks)
    shards = lax.axis_size("shard")
    shard, rep = lax.axis_index("shard"), lax.axis_index("rep")
    side = lax.rem(rep, 2)
    to_core, to_far = {"rep": rep + 1 - 2 * side}, {"rep": lax.rem(rep + 2, 4)}

    def other(k):
        return {"shard": lax.rem(shard + k, shards)}

    barrier = pltpu.get_barrier_semaphore()
    greeted = [to_core, to_far] + [other(k) for k in range(1, shards)]
    for device in greeted:
        pl.semaphore_signal(barrier, inc=1, device_id=device, device_id_type=MESH)

    def loads(i):
        at, size, _, _ = chunks[i]
        pairs = (g_ref, g_buf), (f_ref.at[0], f_buf), (s_ref.at[0], s_buf), (w_ref, w_buf)
        return [
            pltpu.make_async_copy(
                ref.at[:, pl.ds(at * LANES, size * LANES)],
                buf.at[i % 2, :, pl.ds(0, size * LANES)],
                in_sem.at[i % 2, n],
            )
            for n, (ref, buf) in enumerate(pairs)
        ]

    def remote(source, target, send, receive, device):
        return pltpu.make_async_remote_copy(
            src_ref=source, dst_ref=target, send_sem=send, recv_sem=receive, device_id=device, device_id_type=MESH
        )

    def near(i):
        _, _, at, half = chunks[i]
        span = pl.ds(at, half)
        return remote(step_buf.at[1 - side, span], near_buf.at[span], near_send.at[i], near_recv.at[i], to_core)

    def far(i):
        _, _, at, half = chunks[i]
        span = pl.ds(at, half)
        return remote(step_buf.at[side, span], far_buf.at[span], far_send.at[i], far_recv.at[i], to_far)

    def back(i):
        _, _, at, half = chunks[i]
        span = pl.ds(at, half)
        return remote(sum_buf.at[span], total.at[side, span], back_send.at[i], back_recv.at[i], to_core)

    def keep(i):
        _, _, at, half = chunks[i]
        span = pl.ds(at, half)
        return pltpu.make_async_copy(sum_buf.at[span], total.at[side, span], own_sem.at[i])

    for copy in loads(0):
        copy.start()
    pl.semaphore_wait(barrier, len(greeted))

    def square_copy(k):
        return remote(square_mine, square_all.at[shard], square_send.at[k], square_recv.at[shard], other(k))

    square_mine[...] = jnp.broadcast_to(square_ref[...], square_mine.shape)
    square_all[shard] = square_mine[...]
    for k in range(1, shards):
        square_copy(k).start()
    for k in range(1, shards):
        source = lax.rem(shard + k, shards)
        remote(
            square_mine, square_all.at[source], square_send.at[k], square_recv.at[source], other(k)
        ).wait_recv()
    norm = jnp.sqrt(jnp.sum(square_all[...], axis=0))
    norm_ref[...] = norm[:1, :1]
    scale = (CLIP_NORM / jnp.maximum(norm, CLIP_NORM))[:1]

    def blocks(size):
        return 48 if size % 48 == 0 else 16

    def compute(i):
        _, _, at, half = chunks[i]
        block = blocks(half)
        for h in (0, 1):

            def body(j, carry):
                here = pl.multiple_of(j * block, 16)
                span = pl.ds(pl.multiple_of((h * half + here) * LANES, LANES), block * LANES)
                grad, first, second, weight = (
                    buf[i % 2, :, span].reshape(block, LANES) for buf in (g_buf, f_buf, s_buf, w_buf)
                )
                new_first, new_second = moments(grad, first, second, scale)
                step = inner_step(new_first, new_second, weight)
                step_buf[h, pl.ds(at + here, block)] = step.astype(BF16)
                return carry

            lax.fori_loop(0, half // block, body, 0)

    def add(i, left, right, target):
        _, _, at, half = chunks[i]
        block = blocks(half)

        def body(j, carry):
            span = pl.ds(pl.multiple_of(at + j * block, 16), block)
            target[span] = (left[span].astype(F32) + right[span].astype(F32)).astype(BF16)
            return carry

        lax.fori_loop(0, half // block, body, 0)

    for i in range(count + 2):
        if i < count:
            for copy in loads(i):
                copy.wait()
            if i + 1 < count:
                for copy in loads(i + 1):
                    copy.start()
            compute(i)
            near(i).start()
        if 1 <= i <= count:
            near(i - 1).wait_recv()
            add(i - 1, step_buf.at[side], near_buf, step_buf.at[side])
            far(i - 1).start()
        if i >= 2:
            far(i - 2).wait_recv()
            add(i - 2, step_buf.at[side], far_buf, sum_buf)
            back(i - 2).start()
            keep(i - 2).start()
    for k in range(1, shards):
        square_copy(k).wait_send()
    for i in range(count):
        near(i).wait_send()
        far(i).wait_send()
        back(i).wait_send()
        keep(i).wait()
        _, _, at, half = chunks[i]
        span = pl.ds(at, half)
        remote(
            sum_buf.at[span], total.at[1 - side, span], back_send.at[i], back_recv.at[i], to_core
        ).wait_recv()


def summed_step(square, grad, first, second, weight):
    rows = grad.shape[-1] // LANES
    chunks = flat_chunks(rows)
    count = len(chunks)
    halves = sum(chunk[3] for chunk in chunks)
    size = chunks[0][3] * 2
    shards = lax.axis_size("shard")
    dma = pltpu.SemaphoreType.DMA
    anywhere = pl.BlockSpec(memory_space=pl.ANY)
    return pl.pallas_call(
        step_kernel,
        in_specs=[pl.BlockSpec(memory_space=pltpu.VMEM)] + [anywhere] * 4,
        out_specs=[pl.BlockSpec(memory_space=pltpu.VMEM), anywhere],
        out_shape=[jax.ShapeDtypeStruct((1, 1), F32), jax.ShapeDtypeStruct((2, halves, LANES), BF16)],
        scratch_shapes=[pltpu.VMEM((2, 1, size * LANES), F32)] * 4
        + [
            pltpu.VMEM((2, halves, LANES), BF16),
            pltpu.VMEM((halves, LANES), BF16),
            pltpu.VMEM((halves, LANES), BF16),
            pltpu.VMEM((halves, LANES), BF16),
            pltpu.VMEM((8, LANES), F32),
            pltpu.VMEM((shards, 8, LANES), F32),
            dma((2, 4)),
        ]
        + [dma((count,))] * 7
        + [dma((shards,))] * 2,
        compiler_params=pltpu.CompilerParams(
            vmem_limit_bytes=48 * MIB, collective_id=3, has_side_effects=True
        ),
        cost_estimate=pl.CostEstimate(flops=0, bytes_accessed=64 * MIB, transcendentals=0),
        name="summed_step",
    )(square, grad, first, second, weight)


def update_kernel(
    reps, norm_ref, g, f, s, total, mom, nf, ns, nm, up, tg, tf, ts, tm, tt, tnf, tns, tnm, tup, sems
):
    rows = g.shape[-1] // LANES
    chunks = flat_chunks(rows)
    whole = [c for c in chunks if c[1] == 2 * HALF_ROWS]
    scale = CLIP_NORM / jnp.maximum(norm_ref[...], CLIP_NORM)

    def body(g_ref, f_ref, s_ref, t_ref, m_ref, nf_ref, ns_ref, nm_ref, up_ref):
        half = t_ref.shape[1]
        size = g_ref.shape[0]
        nf_ref[...], ns_ref[...] = moments(g_ref[...], f_ref[...], s_ref[...], scale)
        for h in (0, 1):
            span = slice(h * half, min((h + 1) * half, size))
            pseudo = t_ref[h, : span.stop - span.start].astype(F32) * (-1.0 / reps)
            new = OUTER_MOMENTUM * m_ref[span] + pseudo
            nm_ref[span] = new
            up_ref[span] = -OUTER_RATE * (pseudo + OUTER_MOMENTUM * new)

    def view(ref):
        return ref.reshape(rows, LANES)

    ins, outs = [view(g), view(f), view(s), total, view(mom)], [view(r) for r in (nf, ns, nm, up)]
    wide = pl.BlockSpec((2 * HALF_ROWS, LANES), lambda i: (i, 0))
    halves = pl.BlockSpec((2, HALF_ROWS, LANES), lambda i: (0, i, 0))
    if whole:
        pltpu.emit_pipeline(
            body, grid=(len(whole),), in_specs=[wide, wide, wide, halves, wide], out_specs=[wide] * 4
        )(*ins, *outs)
    for at, size, half_at, half in chunks[len(whole) :]:

        def part(n, ref):
            return ref.at[:, pl.ds(half_at, half)] if n == 3 else ref.at[pl.ds(at, size)]

        copies = [
            pltpu.make_async_copy(part(n, ref), buf, sems.at[n]) for n, (ref, buf) in enumerate(zip(ins, (tg, tf, ts, tt, tm)))
        ]
        for copy in copies:
            copy.start()
        for copy in copies:
            copy.wait()
        body(tg, tf, ts, tt, tm, tnf, tns, tnm, tup)
        copies = [
            pltpu.make_async_copy(buf, ref.at[pl.ds(at, size)], sems.at[n])
            for n, (buf, ref) in enumerate(zip((tnf, tns, tnm, tup), outs))
        ]
        for copy in copies:
            copy.start()
        for copy in copies:
            copy.wait()


def update(reps, norm, grad, first, second, total, mom):
    _, size, _, half = flat_chunks(grad.shape[-1] // LANES)[-1]
    anywhere = pl.BlockSpec(memory_space=pl.ANY)
    tail = pltpu.VMEM((size, LANES), F32)
    return pl.pallas_call(
        functools.partial(update_kernel, reps),
        in_specs=[pl.BlockSpec(memory_space=pltpu.VMEM)] + [anywhere] * 5,
        out_specs=[anywhere] * 4,
        out_shape=[jax.ShapeDtypeStruct(ref.shape, F32) for ref in (first, second, mom, mom)],
        scratch_shapes=[tail] * 4
        + [pltpu.VMEM((2, half, LANES), BF16)]
        + [tail] * 4
        + [pltpu.SemaphoreType.DMA((5,))],
        compiler_params=pltpu.CompilerParams(vmem_limit_bytes=48 * MIB),
        cost_estimate=pl.CostEstimate(flops=0, bytes_accessed=120 * MIB, transcendentals=0),
        name="update",
    )(norm, grad, first, second, total, mom)


def rms_scale(rows):
    return lax.rsqrt(jnp.mean(rows * rows, axis=-1, keepdims=True) + EPSILON)


def rms_backward(rows, scale, gain, grad_out):
    grad_gain = jnp.sum(grad_out * rows * scale, axis=0)
    inner = jnp.sum(grad_out * gain * rows, axis=-1, keepdims=True)
    grad_in = scale * gain * grad_out - rows * scale * scale * scale * inner / rows.shape[-1]
    return grad_in, grad_gain


def rotate(rows, cosine, sine):
    half = HEAD_SIZE // 2
    front, back = rows[:, :half], rows[:, half:]
    return jnp.concatenate([front * cosine - back * sine, back * cosine + front * sine], axis=1)


def per_device(
    tokens,
    cotangent,
    routes,
    branch,
    attn_gain,
    query_key_value_weight,
    w_attn_out,
    ffn_gain,
    w_router,
    w_in,
    w_out,
    adam_first,
    adam_second,
    outer_mom,
):
    shards = lax.axis_size("shard")
    reps = lax.axis_size("rep")
    count = tokens.shape[2]
    width = tokens.shape[3]
    prompt = count - CONTINUATION_LEN
    local = EXPERTS // reps
    groups = None
    if shards > GROUP_SIZE:
        groups = [list(range(i, i + GROUP_SIZE)) for i in range(0, shards, GROUP_SIZE)]
    shard_pos = lax.axis_index("shard") % GROUP_SIZE
    rep_pos = lax.axis_index("rep")
    branch_len = branch.reshape(())
    x_in = tokens.reshape(count, width).astype(F32)
    top_low = cotangent.reshape(count, width)
    grad_top = top_low.astype(F32)
    route_ids = routes.reshape(count, TOP)
    gather = functools.partial(lax.all_gather, axis_name="shard", axis=0, tiled=True)
    rows = width // shards
    qkv_columns = Q_WIDTH + 2 * KV_WIDTH
    fast = shards == 2 * LINE and reps == 4 and rows == LANES
    flat_path = fast and outer_mom.shape[-1] % LANES == 0

    small = jnp.concatenate(
        [query_key_value_weight, w_attn_out, w_router, attn_gain[:, None], ffn_gain[:, None]], axis=1
    )
    small = jnp.pad(small, ((0, 0), (0, -small.shape[1] % LANES)))
    tokens_low = tokens.reshape(count, width)
    if fast:
        prompt_low, small_full, all_top = start_gather(tokens_low, small, top_low)
        small_full = small_full.reshape(width, small.shape[1])
    else:
        prompt_low = lax.all_gather(tokens_low[:prompt], "shard", axis=0, tiled=False, axis_index_groups=groups)
        small_full = gather(small)
        by_rep = lax.all_gather(top_low, "rep", axis=0, tiled=False)
        core_pos = rep_pos + 1 - 2 * (rep_pos % 2)
        all_top = jnp.stack([top_low] + [by_rep[i] for i in (core_pos, (rep_pos + 2) % 4, 3 - rep_pos)])
    prompt_low = prompt_low.reshape(GROUP_SIZE * prompt, width)
    qkv_full = small_full[:, :qkv_columns]
    attn_out_full = small_full[:, qkv_columns : qkv_columns + Q_WIDTH]
    router_full = small_full[:, qkv_columns + Q_WIDTH : qkv_columns + Q_WIDTH + EXPERTS]
    gains = small_full[:, qkv_columns + Q_WIDTH + EXPERTS :].astype(F32)
    attn_gain_full, ffn_gain_full = gains[:, 0], gains[:, 1]
    w_both = jnp.concatenate(
        [
            lax.dynamic_slice_in_dim(w_in, rep_pos * local * 2 * F, local * 2 * F, 1),
            lax.dynamic_slice_in_dim(w_out, rep_pos * local * F, local * F, 1),
        ],
        axis=1,
    )
    w_both, prompt_low = lax.optimization_barrier((w_both, prompt_low))
    w_both = gather(w_both)

    def normed(values):
        scale = rms_scale(values)
        return (values * scale * attn_gain_full).astype(BF16), scale

    def angles_of(positions):
        half = HEAD_SIZE // 2
        inverse_freq = ROPE_BASE ** (-(jnp.arange(half, dtype=F32) * 2.0) / HEAD_SIZE)
        angles = inverse_freq[:, None] * positions.astype(F32)[None, :]
        return jnp.cos(angles)[None], jnp.sin(angles)[None]

    def project(source, start, size, turn):
        rows = dot(qkv_full[:, start : start + size], source, (0, 1))
        rows = rows.reshape(size // HEAD_SIZE, HEAD_SIZE, source.shape[0])
        return (rotate(rows, *turn) if turn is not None else rows).astype(BF16)

    def keys_values(source, turn):
        return jnp.stack([project(source, Q_WIDTH, KV_WIDTH, turn), project(source, Q_WIDTH + KV_WIDTH, KV_WIDTH, None)])

    normed_attn, attn_scale = normed(x_in)
    normed_prompt, _ = normed(prompt_low.astype(F32))
    prompt_turn = angles_of(jnp.arange(GROUP_SIZE * prompt, dtype=jnp.int32))
    own_turn = angles_of(
        jnp.concatenate(
            [
                shard_pos * prompt + jnp.arange(prompt, dtype=jnp.int32),
                branch_len + jnp.arange(CONTINUATION_LEN, dtype=jnp.int32),
            ]
        )
    )
    continued_turn = tuple(part[..., prompt:] for part in own_turn)
    prompt_kv = keys_values(normed_prompt, prompt_turn)
    own_kv = keys_values(normed_attn[prompt:], continued_turn)
    query = project(normed_attn, 0, Q_WIDTH, own_turn)
    where = jnp.stack([shard_pos.astype(jnp.int32), branch_len])
    if flat_path:
        size = outer_mom.shape[-1]

        def lead(first, second, rest):
            parts = [first[None].astype(F32), second[None].astype(F32), rest.reshape(-1, LANES).astype(F32)]
            return jnp.concatenate(parts, axis=0)

        def whole(values):
            return values, values.shape[-1], 0

        weight_flat, _ = flatten(
            size,
            lead(attn_gain, ffn_gain, w_router),
            [whole(query_key_value_weight), whole(w_attn_out), whole(w_in), whole(w_out)],
        )
        weight_flat, query = lax.optimization_barrier((weight_flat, query))
    attn, lse = attn_forward(where, query, prompt_kv, own_kv)
    attn_low = attn.reshape(Q_WIDTH, count)
    x_mid = x_in + dot(attn_low, attn_out_full, (0, 1))

    ffn_scale = rms_scale(x_mid)
    normed_ffn = (x_mid * ffn_scale * ffn_gain_full).astype(BF16)
    logits = dot(normed_ffn, router_full, (1, 0))
    chosen = jnp.any(route_ids[:, :, None] == jnp.arange(EXPERTS, dtype=jnp.int32), axis=1)
    gates = jax.nn.softmax(jnp.where(chosen, logits, NEGATIVE), axis=-1)
    gates = jnp.where(chosen, gates, 0.0)

    gates_out = jnp.pad(gates.T.reshape(reps, local, count), ((0, 0), (0, 8 - local), (0, 0)))
    _, dx_own, dx_core, dx_far, y_keep, y_give, normed_t, top_t, dgu, gated, dgate_part = experts(
        normed_ffn, all_top, gates_out, w_both
    )
    grad_from_experts = dx_own.astype(F32) + dx_core.astype(F32) + dx_far.astype(F32)
    grad_gates = dgate_part[:, :local].reshape(EXPERTS, count).T
    to_core = [(i, i + 1 - 2 * (i % 2)) for i in range(reps)]
    to_far = [(i, (i + 2) % reps) for i in range(reps)]
    def rep_sum(values):
        for pairs in (to_core, to_far):
            values = (values.astype(F32) + lax.ppermute(values, "rep", pairs).astype(F32)).astype(BF16)
        return values

    def expert_term(left, right):
        return dot(left, right.reshape(reps * count, -1), (1, 0)).astype(BF16)

    grad_logits = (gates * (grad_gates - jnp.sum(gates * grad_gates, axis=-1, keepdims=True))).astype(BF16)
    grad_router_w = dot(normed_ffn, grad_logits, (0, 0))
    grad_normed_ffn = grad_from_experts + dot(grad_logits, router_full, (1, 1))
    grad_mid_norm, grad_ffn_gain = rms_backward(x_mid, ffn_scale, ffn_gain_full, grad_normed_ffn)
    grad_mid = grad_top + grad_mid_norm
    grad_branch = grad_mid.astype(BF16)
    grad_attn_w = dot(grad_branch, attn_low, (0, 1))
    grad_attn = dot(attn_out_full, grad_branch, (0, 1)).astype(BF16).reshape(QUERY_HEADS, HEAD_SIZE, count)
    expert_columns = local * 3 * F
    if fast:
        expert_rows = expert_grads(
            normed_t,
            top_t,
            dgu.reshape(reps * count, -1),
            gated.reshape(reps * count, -1),
        )
    else:
        terms = jnp.concatenate([expert_term(normed_t, dgu), expert_term(top_t, gated)], axis=1)
        terms = lax.psum_scatter(terms, "shard", scatter_dimension=0, tiled=True)
        expert_rows = lax.all_gather(terms, "rep", axis=0, tiled=False)
    y_keep, y_give, expert_rows = lax.optimization_barrier((y_keep, y_give, expert_rows))
    y_near = y_keep.astype(F32) + lax.ppermute(y_give, "rep", to_core).astype(F32)
    y_sum = y_near[0] + lax.ppermute(y_near[1].astype(BF16), "rep", to_far).astype(F32)
    block_out = (x_mid + y_sum).astype(BF16)

    blank = jnp.zeros((width, -(Q_WIDTH + EXPERTS + 1) % LANES), BF16)
    early = jnp.concatenate(
        [grad_attn_w.astype(BF16), grad_router_w.astype(BF16), grad_ffn_gain[:, None].astype(BF16), blank], axis=1
    )
    grad_attn, early, expert_rows = lax.optimization_barrier((grad_attn, early, expert_rows))
    early = lax.psum_scatter(early, "shard", scatter_dimension=0, tiled=True)

    grad_query, grad_prompt_kv, grad_own_kv = attn_backward(
        where, query, prompt_kv, own_kv, grad_attn, attn, lse
    )

    early, grad_query, grad_prompt_kv, grad_own_kv = lax.optimization_barrier(
        (early, grad_query, grad_prompt_kv, grad_own_kv)
    )
    early = rep_sum(early)

    def turn_back(values, turn):
        spun = rotate(values, turn[0], -turn[1])
        return spun.astype(BF16).reshape(-1, values.shape[-1])

    grad_query = turn_back(grad_query, own_turn)
    grad_prompt_kv = (
        turn_back(grad_prompt_kv[0].astype(F32), prompt_turn),
        grad_prompt_kv[1].reshape(KV_WIDTH, GROUP_SIZE * prompt),
    )
    grad_own_kv = (turn_back(grad_own_kv[0], continued_turn), grad_own_kv[1].astype(BF16).reshape(KV_WIDTH, -1))
    late = [dot(normed_attn, grad_query, (0, 1)).astype(BF16)]
    for shared, own in zip(grad_prompt_kv, grad_own_kv):
        late.append((dot(normed_prompt, shared, (0, 1)) + dot(normed_attn[prompt:], own, (0, 1))).astype(BF16))
    late = jnp.concatenate(late, axis=1)
    late, early = lax.optimization_barrier((late, early))
    attn_rows, router_rows = early[:, :Q_WIDTH], early[:, Q_WIDTH : Q_WIDTH + EXPERTS]
    ffn_gain_rows = early[:, Q_WIDTH + EXPERTS]
    if fast:
        qkv_rows = late_reduce(late)
    else:
        qkv_rows = rep_sum(lax.psum_scatter(late, "shard", scatter_dimension=0, tiled=True))
    qkv_rows, grad_prompt_kv = lax.optimization_barrier((qkv_rows, grad_prompt_kv))
    attn_gain_rows = jnp.sum(
        qkv_rows.astype(F32) * query_key_value_weight.astype(F32), axis=1
    ) / attn_gain.astype(F32)

    grad_projected = [grad_query]
    for shared, own in zip(grad_prompt_kv, grad_own_kv):
        shared = lax.psum_scatter(shared, "shard", scatter_dimension=1, tiled=True, axis_index_groups=groups)
        grad_projected.append(jnp.concatenate([shared, own], axis=1))
    grad_projected = jnp.concatenate(grad_projected, axis=0)
    grad_normed_attn = dot(grad_projected, qkv_full, (0, 1))
    grad_x_norm, _ = rms_backward(x_in, attn_scale, attn_gain_full, grad_normed_attn)
    grad_input = grad_mid + grad_x_norm

    in_columns = local * 2 * F
    if flat_path:
        total_grad, square = flatten(
            size,
            lead(attn_gain_rows, ffn_gain_rows, router_rows),
            [
                whole(qkv_rows),
                whole(attn_rows),
                (expert_rows, in_columns, 0),
                (expert_rows, expert_columns - in_columns, in_columns // (expert_columns - in_columns)),
            ],
        )
        grad_norm, step_sum = summed_step(square, total_grad, adam_first, adam_second, weight_flat)
        new_first, new_second, new_mom, weight_update = update(
            reps, grad_norm, total_grad, adam_first, adam_second, step_sum, outer_mom
        )
        grad_norm = grad_norm.reshape(())
    else:
        weight_flat = jnp.concatenate(
            [
                portion.astype(F32).reshape(-1)
                for portion in (attn_gain, query_key_value_weight, w_attn_out, ffn_gain, w_router, w_in, w_out)
            ]
        )
        total_grad = jnp.concatenate(
            [
                portion.astype(F32).reshape(-1)
                for portion in (
                    attn_gain_rows,
                    qkv_rows,
                    attn_rows,
                    ffn_gain_rows,
                    router_rows,
                    expert_rows[:, :, :in_columns].transpose(1, 0, 2),
                    expert_rows[:, :, in_columns:].transpose(1, 0, 2),
                )
            ]
        )
        grad_norm = jnp.sqrt(lax.psum(jnp.sum(total_grad * total_grad), "shard"))
        new_first, new_second = moments(
            total_grad,
            adam_first.reshape(-1),
            adam_second.reshape(-1),
            CLIP_NORM / jnp.maximum(grad_norm, CLIP_NORM),
        )
        step = inner_step(new_first, new_second, weight_flat)
        pseudo = -(lax.psum(step.astype(BF16), "rep").astype(F32) / reps)
        new_mom = OUTER_MOMENTUM * outer_mom.reshape(-1) + pseudo
        weight_update = -OUTER_RATE * (pseudo + OUTER_MOMENTUM * new_mom)
    return (
        block_out.reshape(tokens.shape),
        grad_input.reshape(tokens.shape),
        total_grad.reshape(outer_mom.shape),
        grad_norm,
        new_first.reshape(adam_first.shape),
        new_second.reshape(adam_second.shape),
        new_mom.reshape(outer_mom.shape),
        weight_update.reshape(outer_mom.shape),
    )


def solution(mesh):
    by_token = P("rep", "shard", None, None)
    by_state = P("rep", "shard", None)
    by_row = P("shard", None)
    placed = (
        by_token,
        by_token,
        by_token,
        P("rep", "shard"),
        P("shard"),
        by_row,
        by_row,
        P("shard"),
        by_row,
        by_row,
        by_row,
        by_state,
        by_state,
        by_row,
    )
    return jax.shard_map(
        per_device,
        mesh=mesh,
        in_specs=placed,
        out_specs=(by_token, by_token, by_row, P(), by_state, by_state, by_row, by_row),
        check_vma=False,
    )
```

```python
import functools

import jax
import jax.numpy as jnp
from jax import lax
from jax.experimental import pallas as pl
from jax.experimental.pallas import tpu as pltpu
from jax.sharding import PartitionSpec as P

QUERY_HEADS = 16
KEY_VALUE_HEADS = 8
HEAD_SIZE = 64
F = 512
EXPERTS = 16
TOP = 8
GROUP_SIZE = 8
CONTINUATION_LEN = 512
STEP = 10

EPSILON = 1e-06
NEGATIVE = -1e30
ROPE_BASE = 10000.0
BETA_ONE = 0.9
BETA_TWO = 0.95
ADAM_EPS = 1e-08
INNER_RATE = 0.01
DECAY_RATE = 0.1
OUTER_RATE = 0.7
OUTER_MOMENTUM = 0.9
CLIP_NORM = 1.0

LOG2E = 1.4426950408889634
LANES = 128
MIB = 1 << 20
BF16 = jnp.bfloat16
F32 = jnp.float32
PER_KEY = QUERY_HEADS // KEY_VALUE_HEADS
Q_WIDTH = QUERY_HEADS * HEAD_SIZE
KV_WIDTH = KEY_VALUE_HEADS * HEAD_SIZE


def dot(left, right, dims):
    return lax.dot_general(left, right, ((dims[:1], dims[1:]), ((), ())), preferred_element_type=F32)


def split_three(value):
    high = value.astype(BF16)
    rest = value - high.astype(F32)
    middle = rest.astype(BF16)
    low = (rest - middle.astype(F32)).astype(BF16)
    return high, middle, low


def augment_query(q_ref, start, width):
    rows = jnp.concatenate([q_ref[g, :, start : start + width] for g in range(PER_KEY)], axis=1)
    scaled = rows.astype(F32) * (HEAD_SIZE**-0.5 * LOG2E)
    high = scaled.astype(BF16)
    low = (scaled - high.astype(F32)).astype(BF16)
    return rows, high, low


def block_of(refs, index, block):
    span = pl.ds(pl.multiple_of(index * block, block), block)
    return tuple(ref[0, :, span] for ref in refs)


def causal(width, columns):
    key_pos = lax.broadcasted_iota(jnp.int32, (width, columns), 0)
    query_pos = lax.broadcasted_iota(jnp.int32, (width, columns), 1) % width
    return key_pos <= query_pos


SAFE_BOUND = 48.0


def attn_forward_kernel(where_ref, q_ref, k_ref, v_ref, own_ref, o_ref, lse_ref, peak_ref, acc_ref):
    block = own_ref.shape[-1]
    columns = PER_KEY * block
    shard_pos = where_ref[0]
    branch = where_ref[1]
    ones = jnp.ones((16, block), BF16)
    pad = jnp.zeros((16 - 3, columns), BF16)
    whole = branch // block
    kv_ref = (k_ref, v_ref)

    def longest(key):
        squares = key.astype(F32)
        return jnp.max(jnp.sum(squares * squares, axis=0, keepdims=True), axis=1, keepdims=True)

    longest_key = jnp.sqrt(jnp.maximum(longest(k_ref[0]), longest(own_ref[0, 0])))

    def emit(start, result, lse):
        for g in range(PER_KEY):
            o_ref[g, :, start : start + block] = result[:, g * block : (g + 1) * block].astype(BF16)
            lse_ref[0, g : g + 1, start : start + block] = lse[:, g * block : (g + 1) * block]

    def sweep(advance, start):
        def body(index, carry):
            advance(*block_of(kv_ref, index, block), None)
            return carry

        if start == 0:
            lax.fori_loop(0, shard_pos, body, 0)
            advance(*block_of(kv_ref, shard_pos, block), causal(block, columns))
        else:
            lax.fori_loop(0, whole, body, 0)

            @pl.when(branch % block != 0)
            def _():
                key_pos = lax.broadcasted_iota(jnp.int32, (block, columns), 0)
                advance(*block_of(kv_ref, whole, block), key_pos < branch % block)

            advance(own_ref[0, 0], own_ref[1, 0], causal(block, columns))

    def bounded(start, high, low, bound):
        query = jnp.concatenate([high, low, *split_three(-bound), pad], axis=0)

        def advance(key, value, mask):
            scores = dot(jnp.concatenate([key, key, ones], axis=0), query, (0, 0))
            if mask is not None:
                scores = jnp.where(mask, scores, NEGATIVE)
            probs = jnp.exp2(scores).astype(BF16)
            acc_ref[...] += dot(jnp.concatenate([value, ones], axis=0), probs, (1, 0))

        acc_ref[...] = jnp.zeros_like(acc_ref)
        sweep(advance, start)
        total = acc_ref[HEAD_SIZE : HEAD_SIZE + 1]
        emit(start, acc_ref[:HEAD_SIZE] / total, bound + jnp.log2(total))

    def running(start, high, low):
        query = jnp.concatenate([high, low], axis=0)

        def advance(key, value, mask):
            scores = dot(jnp.concatenate([key, key], axis=0), query, (0, 0))
            if mask is not None:
                scores = jnp.where(mask, scores, NEGATIVE)
            old = peak_ref[...]
            new = jnp.maximum(old, jnp.max(scores, axis=0, keepdims=True))
            probs = jnp.exp2(scores - new).astype(BF16)
            shrink = jnp.exp2(old - new)
            part = dot(jnp.concatenate([value, ones], axis=0), probs, (1, 0))
            peak_ref[...] = new
            acc_ref[...] = acc_ref[...] * shrink + part

        peak_ref[...] = jnp.full_like(peak_ref, NEGATIVE)
        acc_ref[...] = jnp.zeros_like(acc_ref)
        sweep(advance, start)
        total = acc_ref[HEAD_SIZE : HEAD_SIZE + 1]
        emit(start, acc_ref[:HEAD_SIZE] / total, peak_ref[...] + jnp.log2(total))

    for start in (0, block):
        rows, high, low = augment_query(q_ref, start, block)
        wide = rows.astype(F32)
        length = jnp.sqrt(jnp.sum(wide * wide, axis=0, keepdims=True))
        bound = length * longest_key * (1.02 * HEAD_SIZE**-0.5 * LOG2E)
        safe = jnp.max(bound) < SAFE_BOUND

        @pl.when(safe)
        def _(start=start, high=high, low=low, bound=bound):
            bounded(start, high, low, bound)

        @pl.when(jnp.logical_not(safe))
        def _(start=start, high=high, low=low):
            running(start, high, low)


def attn_forward(where, query, prompt_kv, own_kv):
    tokens = query.shape[-1]
    block = own_kv.shape[-1]
    columns = PER_KEY * block
    keys = prompt_kv[0].shape[-1]
    return pl.pallas_call(
        attn_forward_kernel,
        grid=(query.shape[0] // PER_KEY,),
        in_specs=[
            pl.BlockSpec(memory_space=pltpu.SMEM),
            pl.BlockSpec((PER_KEY, HEAD_SIZE, tokens), lambda h: (h, 0, 0)),
            pl.BlockSpec((1, HEAD_SIZE, keys), lambda h: (h, 0, 0)),
            pl.BlockSpec((1, HEAD_SIZE, keys), lambda h: (h, 0, 0)),
            pl.BlockSpec((2, 1, HEAD_SIZE, block), lambda h: (0, h, 0, 0)),
        ],
        out_specs=[
            pl.BlockSpec((PER_KEY, HEAD_SIZE, tokens), lambda h: (h, 0, 0)),
            pl.BlockSpec((1, PER_KEY, tokens), lambda h: (h, 0, 0)),
        ],
        out_shape=[
            jax.ShapeDtypeStruct(query.shape, BF16),
            jax.ShapeDtypeStruct((query.shape[0] // PER_KEY, PER_KEY, tokens), F32),
        ],
        scratch_shapes=[
            pltpu.VMEM((1, columns), F32),
            pltpu.VMEM((HEAD_SIZE + 16, columns), F32),
        ],
        compiler_params=pltpu.CompilerParams(vmem_limit_bytes=48 * MIB),
        cost_estimate=pl.CostEstimate(
            flops=4 * tokens * keys * query.shape[0] * HEAD_SIZE,
            bytes_accessed=16 * MIB,
            transcendentals=query.shape[0] * tokens * keys,
        ),
        name="attn_forward",
    )(where, query, *prompt_kv, own_kv)


def attn_backward_kernel(
    where_ref, q_ref, k_ref, v_ref, own_ref, go_ref, o_ref, lse_ref, turn_ref, own_turn_ref, dq_ref, dkv_ref, down_ref, dkv_acc, dq_acc
):
    block = own_ref.shape[-1]
    columns = PER_KEY * block
    shard_pos = where_ref[0]
    branch = where_ref[1]
    ones = jnp.ones((16, block), BF16)
    pad = jnp.zeros((16 - 3, columns), BF16)
    kv_ref = (k_ref, v_ref)

    def turn_back(values, ref, span):
        half = HEAD_SIZE // 2
        cosine, sine = ref[0, :, span], ref[1, :, span]
        front, back = values[:half], values[half:]
        return jnp.concatenate([front * cosine + back * sine, back * cosine - front * sine], axis=0).astype(BF16)

    def begin(start):
        rows, high, low = augment_query(q_ref, start, block)

        def lanes(ref):
            return jnp.concatenate([ref[0, g : g + 1, start : start + block] for g in range(PER_KEY)], axis=1)

        lse = split_three(-lanes(lse_ref))
        grad, out = (
            jnp.concatenate([ref[g, :, start : start + block] for g in range(PER_KEY)], axis=1)
            for ref in (go_ref, o_ref)
        )
        delta = split_three(-jnp.sum(grad.astype(F32) * out.astype(F32), axis=0, keepdims=True))
        query = jnp.concatenate([high, low, *lse, pad], axis=0)
        grad_plus = jnp.concatenate([grad, *delta, pad], axis=0)
        dq_acc[...] = jnp.zeros_like(dq_acc)
        scaled = (rows.astype(F32) * HEAD_SIZE**-0.5).astype(BF16)
        return query, scaled, grad_plus, grad

    def terms(state, key, value, mask):
        query, scaled, grad_plus, grad = state
        scores = dot(jnp.concatenate([key, key, ones], axis=0), query, (0, 0))
        if mask is not None:
            scores = jnp.where(mask, scores, NEGATIVE)
        probs = jnp.exp2(scores)
        dv = dot(grad, probs.astype(BF16), (1, 1))
        grad_probs = dot(jnp.concatenate([value, ones], axis=0), grad_plus, (0, 0))
        grad_scores = (probs * grad_probs).astype(BF16)
        dq_acc[...] += dot(key, grad_scores, (1, 0))
        return dot(scaled, grad_scores, (1, 1)), dv

    def add(index, state, mask):
        dk, dv = terms(state, *block_of(kv_ref, index, block), mask)
        span = pl.ds(pl.multiple_of(index * block, block), block)
        dkv_acc[0, :, span] += dk
        dkv_acc[1, :, span] += dv

    def finish(start):
        total = dq_acc[...] * HEAD_SIZE**-0.5
        for g in range(PER_KEY):
            span = slice(start, start + block)
            dq_ref[g, :, span] = turn_back(total[:, g * block : (g + 1) * block], own_turn_ref, span)

    def run(state, count):
        def body(index, carry):
            add(2 * index, state, None)
            add(2 * index + 1, state, None)
            return carry

        lax.fori_loop(0, count // 2, body, 0)

        @pl.when(count % 2 == 1)
        def _():
            add(count - 1, state, None)

    dkv_acc[...] = jnp.zeros_like(dkv_acc)
    state = begin(0)
    run(state, shard_pos)
    add(shard_pos, state, causal(block, columns))
    finish(0)

    state = begin(block)
    whole = branch // block
    run(state, whole)

    @pl.when(branch % block != 0)
    def _():
        key_pos = lax.broadcasted_iota(jnp.int32, (block, columns), 0)
        add(whole, state, key_pos < branch % block)

    dk, dv = terms(state, own_ref[0, 0], own_ref[1, 0], causal(block, columns))
    down_ref[0, 0] = turn_back(dk, own_turn_ref, slice(block, 2 * block))
    down_ref[1, 0] = dv.astype(BF16)
    finish(block)
    dkv_ref[0, 0] = turn_back(dkv_acc[0], turn_ref, slice(None))
    dkv_ref[1, 0] = dkv_acc[1].astype(BF16)


def attn_backward(where, query, prompt_kv, own_kv, grad_out, out, lse, turn, own_turn):
    tokens = query.shape[-1]
    block = own_kv.shape[-1]
    columns = PER_KEY * block
    keys = prompt_kv[0].shape[-1]
    by_head = pl.BlockSpec((PER_KEY, HEAD_SIZE, tokens), lambda h: (h, 0, 0))
    by_keys = pl.BlockSpec((2, 1, HEAD_SIZE, keys), lambda h: (0, h, 0, 0))
    by_key = pl.BlockSpec((1, HEAD_SIZE, keys), lambda h: (h, 0, 0))
    by_own = pl.BlockSpec((2, 1, HEAD_SIZE, block), lambda h: (0, h, 0, 0))
    by_row = pl.BlockSpec((1, PER_KEY, tokens), lambda h: (h, 0, 0))
    return pl.pallas_call(
        attn_backward_kernel,
        grid=(query.shape[0] // PER_KEY,),
        in_specs=[pl.BlockSpec(memory_space=pltpu.SMEM), by_head, by_key, by_key, by_own, by_head, by_head, by_row]
        + [pl.BlockSpec(part.shape, lambda h: (0, 0, 0)) for part in (turn, own_turn)],
        out_specs=[by_head, by_keys, by_own],
        out_shape=[
            jax.ShapeDtypeStruct(query.shape, BF16),
            jax.ShapeDtypeStruct((2, *prompt_kv[0].shape), BF16),
            jax.ShapeDtypeStruct(own_kv.shape, BF16),
        ],
        scratch_shapes=[
            pltpu.VMEM((2, HEAD_SIZE, keys), F32),
            pltpu.VMEM((HEAD_SIZE, columns), F32),
        ],
        compiler_params=pltpu.CompilerParams(vmem_limit_bytes=56 * MIB),
        cost_estimate=pl.CostEstimate(
            flops=10 * tokens * keys * query.shape[0] * HEAD_SIZE,
            bytes_accessed=32 * MIB,
            transcendentals=query.shape[0] * tokens * keys,
        ),
        name="attn_backward",
    )(where, query, *prompt_kv, own_kv, grad_out, out, lse, turn, own_turn)


MESH = pl.DeviceIdType.MESH
LINE = 4
TOKEN_PARTS = 4


def start_kernel(
    x_ref,
    w_ref,
    top_ref,
    tok_all,
    w_all,
    top_all,
    own_sem,
    line_recv,
    right_send,
    left_send,
    y_send,
    y_recv,
    x_send,
    x_recv,
    core_send,
    core_recv,
    top_send,
    top_recv,
):
    part = tok_all.shape[1] // TOKEN_PARTS
    quarter = w_all.shape[2]
    half = top_ref.shape[0] // 2
    me = lax.axis_index("shard")
    place, column = me // 2, lax.rem(me, 2)
    rep = lax.axis_index("rep")
    far, core = lax.rem(rep + 2, 4), rep + 1 - 2 * lax.rem(rep, 2)
    to_right, to_left, to_y = {"shard": me + 2}, {"shard": me - 2}, {"shard": me + 1 - 2 * column}
    to_far, to_core = {"rep": far}, {"rep": core}
    weights, mirrored = 0, TOKEN_PARTS + 1
    last = TOKEN_PARTS
    streams = TOKEN_PARTS + 2

    def piece(i, origin, side):
        if i == weights:
            return w_all.at[2 * origin + side, rep]
        k = (i if i != mirrored else last) - 1
        return tok_all.at[2 * origin + side, pl.ds(k * part, part)]

    def side_of(i):
        return 1 - column if i == mirrored else column

    def own(i):
        if i == weights:
            return w_ref.at[pl.ds(pl.multiple_of(rep * quarter, quarter), quarter)]
        if i == mirrored:
            return piece(i, place, 1 - column)
        return x_ref.at[pl.ds((i - 1) * part, part)]

    def remote(source, target, send, receive, device):
        return pltpu.make_async_remote_copy(
            src_ref=source, dst_ref=target, send_sem=send, recv_sem=receive, device_id=device, device_id_type=MESH
        )

    def source(i, origin, at_home):
        return own(i) if at_home else piece(i, origin, side_of(i))

    def right(i, origin, at_home=False):
        return remote(
            source(i, origin, at_home),
            piece(i, origin, side_of(i)),
            right_send.at[i, origin],
            line_recv.at[i, origin],
            to_right,
        )

    def left(i, origin, at_home=False):
        return remote(
            source(i, origin, at_home),
            piece(i, origin, side_of(i)),
            left_send.at[i, origin],
            line_recv.at[i, origin],
            to_left,
        )

    def abreast(i, origin, at_home=False):
        return remote(
            source(i, origin, at_home), piece(i, origin, column), y_send.at[i, origin], y_recv.at[i, origin], to_y
        )

    def over_x(origin, side, at_home=False):
        target = piece(weights, origin, side)
        source_ref = own(weights) if at_home else target
        return remote(source_ref, target, x_send.at[origin, side], x_recv.at[origin, side], to_far)

    def over_core(group, origin, side, at_home=False):
        target = w_all.at[2 * origin + side, rep if group == 0 else far]
        source_ref = own(weights) if at_home else target
        return remote(
            source_ref, target, core_send.at[group, origin, side], core_recv.at[group, origin, side], to_core
        )

    def top_far(h):
        return remote(
            top_ref.at[pl.ds(h * half, half)],
            top_all.at[2, pl.ds(h * half, half)],
            top_send.at[0, h],
            top_recv.at[0, h],
            to_far,
        )

    def top_core(h):
        return remote(
            top_ref.at[pl.ds(h * half, half)],
            top_all.at[1, pl.ds(h * half, half)],
            top_send.at[1, h],
            top_recv.at[1, h],
            to_core,
        )

    def top_diagonal(h):
        return remote(
            top_all.at[2, pl.ds(h * half, half)],
            top_all.at[3, pl.ds(h * half, half)],
            top_send.at[2, h],
            top_recv.at[2, h],
            to_core,
        )

    has_right, has_left = place < LINE - 1, place > 0
    barrier = pltpu.get_barrier_semaphore()

    def greet(device):
        pl.semaphore_signal(barrier, inc=1, device_id=device, device_id_type=MESH)

    for device in (to_y, to_far, to_core):
        greet(device)

    @pl.when(has_right)
    def _():
        greet(to_right)

    @pl.when(has_left)
    def _():
        greet(to_left)

    pl.semaphore_wait(barrier, 3 + has_right.astype(jnp.int32) + has_left.astype(jnp.int32))

    def along(i, origin, at_home=False):
        @pl.when(has_right)
        def _():
            right(i, origin, at_home).start()

        @pl.when(has_left)
        def _():
            left(i, origin, at_home).start()

    order = [weights, last] + list(range(1, last))
    for i in order:
        along(i, place, True)
        abreast(i, place, True).start()
        if i == weights:
            over_x(place, column, True).start()
            over_core(0, place, column, True).start()
            for h in (0, 1):
                top_far(h).start()
    for h in (0, 1):
        top_core(h).start()
    own_copies = [
        pltpu.make_async_copy(own(i), piece(i, place, column), own_sem.at[i]) for i in range(streams - 1)
    ]
    own_copies.append(pltpu.make_async_copy(top_ref, top_all.at[0], own_sem.at[streams - 1]))
    for copy in own_copies:
        copy.start()
    abreast(last, place).wait_recv()
    along(mirrored, place, True)

    def weights_across(origin):
        abreast(weights, origin).wait_recv()
        over_x(origin, 1 - column).start()
        over_core(0, origin, 1 - column).start()

    weights_across(place)
    for d in range(1, LINE):
        before, after = place - d, place + d
        from_left, from_right = before >= 0, after < LINE
        for i in [weights, last, mirrored] + list(range(1, last)):

            @pl.when(from_left)
            def _(i=i):
                right(i, before).wait_recv()

                @pl.when(has_right)
                def _():
                    right(i, before).start()

                if i != last and i != mirrored:
                    abreast(i, before).start()
                if i == weights:
                    over_x(before, column).start()
                    over_core(0, before, column).start()

            @pl.when(from_right)
            def _(i=i):
                left(i, after).wait_recv()

                @pl.when(has_left)
                def _():
                    left(i, after).start()

                if i != last and i != mirrored:
                    abreast(i, after).start()
                if i == weights:
                    over_x(after, column).start()
                    over_core(0, after, column).start()

        @pl.when(from_left)
        def _():
            weights_across(before)

        @pl.when(from_right)
        def _():
            weights_across(after)

        if d >= 2:
            h = d - 2
            top_far(h).wait_recv()
            top_diagonal(h).start()

    for origin in range(LINE):
        for side in (0, 1):
            remote(
                w_all.at[2 * origin + side, far],
                w_all.at[2 * origin + side, far],
                x_send.at[origin, side],
                x_recv.at[origin, side],
                to_far,
            ).wait_recv()
            over_core(1, origin, side).start()

    for origin in range(LINE):
        for i in range(1, last):
            abreast(i, origin).wait_recv()
        for side in (0, 1):
            for group in (0, 1):
                over_core(group, origin, side).wait_recv()
    for h in (0, 1):
        top_core(h).wait_recv()
        top_diagonal(h).wait_recv()
        for copy in (top_far(h), top_core(h), top_diagonal(h)):
            copy.wait_send()
    for copy in own_copies:
        copy.wait()
    for origin in range(LINE):
        for i in range(streams):

            @pl.when(has_right & (origin <= place))
            def _(i=i, origin=origin):
                right(i, origin).wait_send()

            @pl.when(has_left & (origin >= place))
            def _(i=i, origin=origin):
                left(i, origin).wait_send()

            if i != last and i != mirrored:
                abreast(i, origin).wait_send()
        for side in (0, 1):
            over_x(origin, side).wait_send()
            for group in (0, 1):
                over_core(group, origin, side).wait_send()
    abreast(last, place).wait_send()


def start_gather(x, small, top):
    rows, width = x.shape
    prompt = rows - CONTINUATION_LEN
    own_rows, columns = small.shape
    dma = pltpu.SemaphoreType.DMA
    streams = TOKEN_PARTS + 2
    anywhere = pl.BlockSpec(memory_space=pl.ANY)
    return pl.pallas_call(
        start_kernel,
        in_specs=[anywhere] * 3,
        out_specs=[anywhere] * 3,
        out_shape=[
            jax.ShapeDtypeStruct((2 * LINE, prompt, width), BF16),
            jax.ShapeDtypeStruct((2 * LINE, 4, own_rows // 4, columns), BF16),
            jax.ShapeDtypeStruct((4, rows, width), BF16),
        ],
        scratch_shapes=[
            dma((streams,)),
            dma((streams, LINE)),
            dma((streams, LINE)),
            dma((streams, LINE)),
            dma((streams, LINE)),
            dma((streams, LINE)),
            dma((LINE, 2)),
            dma((LINE, 2)),
            dma((2, LINE, 2)),
            dma((2, LINE, 2)),
            dma((3, 2)),
            dma((3, 2)),
        ],
        compiler_params=pltpu.CompilerParams(collective_id=2, has_side_effects=True),
        cost_estimate=pl.CostEstimate(flops=0, bytes_accessed=64 * MIB, transcendentals=0),
        name="start_gather",
    )(x, small, top)


ORDER = ((0, 0), (0, 1), (1, 0), (3, 0), (2, 0), (3, 1), (2, 1), (1, 1))


def experts_kernel(
    x_hbm,
    top_hbm,
    gates_ref,
    w_ref,
    all_x,
    dx_own,
    dx_core,
    dx_far,
    y_keep,
    y_give,
    xt_all,
    tt_all,
    dgu_all,
    gh_all,
    dg_all,
    x_buf,
    top_buf,
    y_buf,
    dx_buf,
    xt_buf,
    tt_buf,
    dgu_buf,
    gh_buf,
    relay,
    y_acc,
    dx_acc,
    gates_all,
    gates_now,
    dg_now,
    dg_mine,
    in_sem,
    out_sem,
    copy_sem,
    send_sem,
    recv_sem,
    small_send,
    small_recv,
):
    tile = x_buf.shape[1]
    count = w_ref.shape[1] // (3 * F)
    step = pl.program_id(0)
    steps = len(ORDER)
    slot = lax.rem(step, 2)
    me = lax.axis_index("rep")
    home = [me, me + 1 - 2 * lax.rem(me, 2), lax.rem(me + 2, 4), 3 - me]

    def remote(source, target, send, receive, relation):
        return pltpu.make_async_remote_copy(
            src_ref=source,
            dst_ref=target,
            send_sem=send,
            recv_sem=receive,
            device_id={"rep": home[relation]},
            device_id_type=MESH,
        )

    def half(ref, half_index, *lead):
        return ref.at[(*lead, pl.ds(half_index * tile, tile))]

    def to_core(h):
        return remote(half(x_hbm, h), half(all_x, h, me), send_sem.at[0, h], recv_sem.at[0, h], 1)

    def to_far(h):
        return remote(half(x_hbm, h), half(all_x, h, me), send_sem.at[1, h], recv_sem.at[1, h], 2)

    def forward(h):
        part = half(all_x, h, home[2])
        return remote(part, part, send_sem.at[2, h], recv_sem.at[2, h], 1)

    def give(kind, h, buffer):
        if kind == 3:
            return remote(buffer, relay.at[h], send_sem.at[3, h], recv_sem.at[3, h], 1)
        if kind == 2:
            return remote(buffer, half(dx_far, h), send_sem.at[4, h], recv_sem.at[4, h], 2)
        return remote(buffer, half(dx_core, h), send_sem.at[5, h], recv_sem.at[5, h], 1)

    def small_gates(k):
        return remote(gates_ref.at[home[k]], gates_all.at[me], small_send.at[0, k], small_recv.at[0, k], k)

    def small_back(k):
        return remote(dg_mine.at[home[k]], dg_all.at[me], small_send.at[1, k], small_recv.at[1, k], k)

    def load_x(i):
        kind, h = ORDER[i]
        source = half(x_hbm, h) if kind == 0 else half(all_x, h, home[kind])
        return pltpu.make_async_copy(source, x_buf.at[i % 2], in_sem.at[i % 2, 0])

    def load_top(i):
        kind, h = ORDER[i]
        return pltpu.make_async_copy(half(top_hbm, h, kind), top_buf.at[i % 2], in_sem.at[i % 2, 1])

    def stores(i):
        kind, h = ORDER[i]
        out = []
        rows = 2 * tile

        def turned(ref, place):
            here = pl.multiple_of(place * rows + h * tile, LANES)
            return ref.at[:, pl.ds(here, tile)]

        targets = (
            (y_buf, half((y_keep, y_give, y_keep, y_give)[kind], h, (0, 0, 1, 1)[kind])),
            (dgu_buf, half(dgu_all, h, home[kind])),
            (gh_buf, half(gh_all, h, kind)),
            (xt_buf, turned(xt_all, home[kind])),
            (tt_buf, turned(tt_all, kind)),
        )
        for n, (buffer, target) in enumerate(targets):
            out.append(pltpu.make_async_copy(buffer.at[i % 2], target, out_sem.at[i % 2, n]))
        return out

    def store_dx(i):
        kind, h = ORDER[i]
        if kind == 0:
            return pltpu.make_async_copy(dx_buf.at[i % 2], half(dx_own, h), out_sem.at[i % 2, 5])
        return give(kind, h, dx_buf.at[i % 2])

    def finish(i):
        for copy in stores(i):
            copy.wait()
        if ORDER[i][0] == 0:
            store_dx(i).wait()
        else:
            store_dx(i).wait_send()

    own_copy = pltpu.make_async_copy(x_hbm, all_x.at[me], copy_sem)
    for i in range(steps):
        kind, h = ORDER[i]

        @pl.when(step == i)
        def _(i=i, kind=kind, h=h):
            if i == 0:
                barrier = pltpu.get_barrier_semaphore()
                for k in (1, 2, 3):
                    pl.semaphore_signal(
                        barrier, inc=1, device_id={"rep": home[k]}, device_id_type=MESH
                    )
                pl.semaphore_wait(barrier, 3)
                to_far(0).start()
                for n in (0, 1):
                    to_core(n).start()
                for k in (1, 2, 3):
                    small_gates(k).start()
                own_copy.start()
                load_top(0).start()
                load_x(0).start()
                gates_all[me] = gates_ref[me]
            if i == 1:
                to_far(1).start()
                for n in (0, 1):
                    to_core(n).wait_recv()
            if i == 2:
                for k in (1, 2, 3):
                    small_gates(k).wait_recv()
                to_far(0).wait_recv()
                forward(0).start()
            if i == 3:
                to_far(1).wait_recv()
                forward(1).start()
            if i == 4:
                forward(1).wait_recv()
            load_x(i).wait()
            load_top(i).wait()
            if i + 1 < steps:
                load_top(i + 1).start()
                if i + 1 != 3:
                    load_x(i + 1).start()
            if i >= 2:
                finish(i - 2)
            gates_now[...] = jnp.transpose(gates_all[home[kind]][:, h * tile : (h + 1) * tile])

    x = x_buf[slot]
    top = top_buf[slot]
    xt_buf[slot] = x.T
    tt_buf[slot] = top.T
    columns = []
    for e in range(count):
        w_in = w_ref[:, e * 2 * F : (e + 1) * 2 * F]
        w_out = w_ref[:, (count * 2 + e) * F : (count * 2 + e + 1) * F]
        gate_up = dot(x, w_in, (1, 0))
        g = gate_up[:, :F]
        u = gate_up[:, F:]
        sig = jax.nn.sigmoid(g)
        act = g * sig
        hidden = (act * u).astype(BF16).astype(F32)
        raw = dot(top, w_out, (1, 0))
        columns.append(jnp.sum(hidden * raw, axis=1, keepdims=True))
        gate = gates_now[:, e : e + 1]
        gated = (hidden * gate).astype(BF16)
        gh_buf[slot, :, e * F : (e + 1) * F] = gated
        grad_hidden = raw * gate
        dg = (grad_hidden * u * sig * (1.0 + g * (1.0 - sig))).astype(BF16)
        du = (grad_hidden * act).astype(BF16)
        dgu = jnp.concatenate([dg, du], axis=1)
        dgu_buf[slot, :, e * 2 * F : (e + 1) * 2 * F] = dgu
        y = dot(gated, w_out, (1, 1))
        dx = dot(dgu, w_in, (1, 1))
        if e == 0:
            y_acc[...] = y
            dx_acc[...] = dx
        elif e < count - 1:
            y_acc[...] += y
            dx_acc[...] += dx
        else:
            y_buf[slot] = (y_acc[...] + y).astype(BF16)
            dx_acc[...] += dx
    columns.append(jnp.zeros((tile, 8 - count), F32))
    dg_now[...] = jnp.transpose(jnp.concatenate(columns, axis=1))

    for i in range(steps):
        kind, h = ORDER[i]

        @pl.when(step == i)
        def _(i=i, kind=kind, h=h):
            dg_mine[home[kind], :, h * tile : (h + 1) * tile] = dg_now[...]
            if kind == 2:
                give(3, h, dx_buf.at[0]).wait_recv()
                dx_buf[i % 2] = (dx_acc[...] + relay[h].astype(F32)).astype(BF16)
            else:
                dx_buf[i % 2] = dx_acc[...].astype(BF16)
            store_dx(i).start()
            for copy in stores(i):
                copy.start()
            if i == 2:
                forward(0).wait_recv()
                load_x(3).start()
            if i == steps - 1:
                own_back = pltpu.make_async_copy(dg_mine.at[me], dg_all.at[me], small_send.at[1, 0])
                own_back.start()
                for k in (1, 2, 3):
                    small_back(k).start()
                finish(i - 1)
                finish(i)
                own_copy.wait()
                own_back.wait()
                for n in (0, 1):
                    to_far(n).wait_send()
                    to_core(n).wait_send()
                    forward(n).wait_send()
                    give(2, n, dx_buf.at[0]).wait_recv()
                    give(1, n, dx_buf.at[0]).wait_recv()
                for k in (1, 2, 3):
                    small_gates(k).wait_send()
                    small_back(k).wait()


def experts(x, all_top, gates, weights):
    rows, width = x.shape
    reps = all_top.shape[0]
    count = weights.shape[1] // (3 * F)
    tile = rows // 2
    anywhere = pl.BlockSpec(memory_space=pl.ANY)
    fixed = pl.BlockSpec(weights.shape, lambda i: (0, 0), pipeline_mode=pl.Buffered(1))
    small = pl.BlockSpec((reps, 8, rows), lambda i: (0, 0, 0))
    dma = pltpu.SemaphoreType.DMA
    return pl.pallas_call(
        experts_kernel,
        grid=(len(ORDER),),
        in_specs=[anywhere, anywhere, small, fixed],
        out_specs=[anywhere] * 11,
        out_shape=[
            jax.ShapeDtypeStruct((reps, rows, width), BF16),
            jax.ShapeDtypeStruct((rows, width), BF16),
            jax.ShapeDtypeStruct((rows, width), BF16),
            jax.ShapeDtypeStruct((rows, width), BF16),
            jax.ShapeDtypeStruct((2, rows, width), BF16),
            jax.ShapeDtypeStruct((2, rows, width), BF16),
            jax.ShapeDtypeStruct((width, reps * rows), BF16),
            jax.ShapeDtypeStruct((width, reps * rows), BF16),
            jax.ShapeDtypeStruct((reps, rows, count * 2 * F), BF16),
            jax.ShapeDtypeStruct((reps, rows, count * F), BF16),
            jax.ShapeDtypeStruct((reps, 8, rows), F32),
        ],
        scratch_shapes=[
            pltpu.VMEM((2, tile, width), BF16),
            pltpu.VMEM((2, tile, width), BF16),
            pltpu.VMEM((2, tile, width), BF16),
            pltpu.VMEM((2, tile, width), BF16),
            pltpu.VMEM((2, width, tile), BF16),
            pltpu.VMEM((2, width, tile), BF16),
            pltpu.VMEM((2, tile, count * 2 * F), BF16),
            pltpu.VMEM((2, tile, count * F), BF16),
            pltpu.VMEM((2, tile, width), BF16),
            pltpu.VMEM((tile, width), F32),
            pltpu.VMEM((tile, width), F32),
            pltpu.VMEM((reps, 8, rows), F32),
            pltpu.VMEM((tile, 8), F32),
            pltpu.VMEM((8, tile), F32),
            pltpu.VMEM((reps, 8, rows), F32),
            dma((2, 2)),
            dma((2, 6)),
            dma,
            dma((6, 2)),
            dma((6, 2)),
            dma((2, 4)),
            dma((2, 4)),
        ],
        compiler_params=pltpu.CompilerParams(
            vmem_limit_bytes=58 * MIB, collective_id=1, has_side_effects=True
        ),
        cost_estimate=pl.CostEstimate(
            flops=12 * reps * rows * width * count * F,
            bytes_accessed=80 * MIB,
            transcendentals=reps * rows * count * F,
        ),
        name="experts",
    )(x, all_top, gates, weights)


def send_to(source, target, send, receive, device):
    return pltpu.make_async_remote_copy(
        src_ref=source, dst_ref=target, send_sem=send, recv_sem=receive, device_id=device, device_id_type=MESH
    )


def line_reduce(parts, y_buf, right_buf, left_buf, y_sems, right_sems, left_sems):
    me = lax.axis_index("shard")
    place, side = me // 2, lax.rem(me, 2)
    to_y, to_right, to_left = {"shard": me + 1 - 2 * side}, {"shard": me + 2}, {"shard": me - 2}

    def across(c):
        return send_to(parts.at[c, 1 - side], y_buf.at[c], y_sems.at[0, c], y_sems.at[1, c], to_y)

    def add_across(c):
        across(c).wait_recv()
        for p in range(LINE):
            parts[c, side, p] = (parts[c, side, p].astype(F32) + y_buf[c, p].astype(F32)).astype(BF16)

    def hop(c, p, buf, sems, device, first):
        source = parts.at[c, side, p] if first else buf.at[c, p]
        return send_to(source, buf.at[c, p], sems.at[0, c, p], sems.at[1, c, p], device)

    def run(c, p, buf, sems, device, is_first, passes):
        @pl.when(passes & is_first)
        def _():
            hop(c, p, buf, sems, device, True).start()

        @pl.when(passes & jnp.logical_not(is_first))
        def _():
            hop(c, p, buf, sems, device, False).wait_recv()
            buf[c, p] = (parts[c, side, p].astype(F32) + buf[c, p].astype(F32)).astype(BF16)
            hop(c, p, buf, sems, device, False).start()

    def step_right(c):
        for p in range(1, LINE):
            run(c, p, right_buf, right_sems, to_right, place == 0, place < p)

    def step_left(c):
        for p in range(LINE - 1):
            run(c, p, left_buf, left_sems, to_left, place == LINE - 1, place > p)

    def collect(c, total):
        total[...] = parts[c, side, place].astype(F32)

        @pl.when(place > 0)
        def _():
            hop(c, place, right_buf, right_sems, to_right, False).wait_recv()
            total[...] += right_buf[c, place].astype(F32)

        @pl.when(place < LINE - 1)
        def _():
            hop(c, place, left_buf, left_sems, to_left, False).wait_recv()
            total[...] += left_buf[c, place].astype(F32)

    def drain(c):
        across(c).wait_send()
        for p in range(1, LINE):

            @pl.when(place < p)
            def _(p=p):
                hop(c, p, right_buf, right_sems, to_right, False).wait_send()

        for p in range(LINE - 1):

            @pl.when(place > p)
            def _(p=p):
                hop(c, p, left_buf, left_sems, to_left, False).wait_send()

    def greet(extra):
        barrier = pltpu.get_barrier_semaphore()
        for device in [to_y] + extra:
            pl.semaphore_signal(barrier, inc=1, device_id=device, device_id_type=MESH)
        has_right, has_left = place < LINE - 1, place > 0

        @pl.when(has_right)
        def _():
            pl.semaphore_signal(barrier, inc=1, device_id=to_right, device_id_type=MESH)

        @pl.when(has_left)
        def _():
            pl.semaphore_signal(barrier, inc=1, device_id=to_left, device_id_type=MESH)

        count = 1 + len(extra) + has_right.astype(jnp.int32) + has_left.astype(jnp.int32)
        pl.semaphore_wait(barrier, count)

    return place, across, add_across, step_right, step_left, collect, drain, greet


def between(step, low, high, body):
    @pl.when((step >= low) & (step < high))
    def _():
        body()


def expert_grads_kernel(
    xt_ref,
    tt_ref,
    dgu_ref,
    gh_ref,
    out_ref,
    left_op,
    right_op,
    parts,
    y_buf,
    right_buf,
    left_buf,
    total,
    mine,
    load_sem,
    lhs_sem,
    y_sems,
    right_sems,
    left_sems,
    own_sem,
    far_sems,
    near_sems,
    pass_sems,
):
    n = parts.shape[0]
    columns = right_op.shape[2]
    first = dgu_ref.shape[1] // columns
    rows = parts.shape[3]
    rep = lax.axis_index("rep")
    far = lax.rem(rep + 2, 4)
    to_core, to_far = {"rep": rep + 1 - 2 * lax.rem(rep, 2)}, {"rep": far}
    place, across, add_across, step_right, step_left, collect, drain, greet = line_reduce(
        parts, y_buf, right_buf, left_buf, y_sems, right_sems, left_sems
    )

    def load(c, act):
        slot = lax.rem(c, 2)

        @pl.when(c < first)
        def _():
            here = pl.ds(pl.multiple_of(c * columns, columns), columns)
            act(pltpu.make_async_copy(dgu_ref.at[:, here], right_op.at[slot], load_sem.at[slot]))

        @pl.when(c >= first)
        def _():
            here = pl.ds(pl.multiple_of((c - first) * columns, columns), columns)
            act(pltpu.make_async_copy(gh_ref.at[:, here], right_op.at[slot], load_sem.at[slot]))

    def start(copy):
        copy.start()

    def wait(copy):
        copy.wait()

    def place_of(owner, c):
        return out_ref.at[owner, :, pl.ds(pl.multiple_of(c * columns, columns), columns)]

    def over_x(c):
        return send_to(mine.at[c], place_of(rep, c), far_sems.at[0, c], far_sems.at[1, c], to_far)

    def over_core(c):
        return send_to(mine.at[c], place_of(rep, c), near_sems.at[0, c], near_sems.at[1, c], to_core)

    def keep(c):
        return pltpu.make_async_copy(mine.at[c], place_of(rep, c), own_sem.at[c])

    def pass_on(c):
        return send_to(place_of(far, c), place_of(far, c), pass_sems.at[0, c], pass_sems.at[1, c], to_core)

    lhs = pltpu.make_async_copy(xt_ref, left_op, lhs_sem)
    lhs.start()
    load(0, start)
    greet([to_core, to_far])
    lhs.wait()

    def produce(c):
        @pl.when(c == first)
        def _():
            swap = pltpu.make_async_copy(tt_ref, left_op, lhs_sem)
            swap.start()
            swap.wait()

        load(c, wait)

        @pl.when(c + 1 < n)
        def _():
            load(c + 1, start)

        result = dot(left_op[...], right_op[lax.rem(c, 2)], (1, 0)).astype(BF16)
        for t in range(2 * LINE):
            parts[c, t % 2, t // 2] = result[t * rows : (t + 1) * rows]
        across(c).start()

    def finish(c):
        collect(c, total)
        mine[c] = total[...].astype(BF16)
        over_x(c).start()
        over_core(c).start()
        keep(c).start()

    def forward(c):
        over_x(c).wait_recv()
        pass_on(c).start()

    def step(i, carry):
        between(i, 0, n, lambda: produce(i))
        between(i, 1, n + 1, lambda: add_across(i - 1))
        to_right_chunk, to_left_chunk = i - 1 - place, i - LINE + place
        between(to_right_chunk, 0, n, lambda: step_right(to_right_chunk))
        between(to_left_chunk, 0, n, lambda: step_left(to_left_chunk))
        between(i, 5, n + 5, lambda: finish(i - 5))
        between(i, 7, n + 7, lambda: forward(i - 7))
        return carry

    lax.fori_loop(0, n + 7, step, 0)

    def end(c, carry):
        drain(c)
        over_x(c).wait_send()
        over_core(c).wait()
        keep(c).wait()
        pass_on(c).wait()
        return carry

    lax.fori_loop(0, n, end, 0)


def expert_grads(x_t, top_t, dgu, gated, columns=256):
    width, tokens = x_t.shape
    wide = dgu.shape[1] + gated.shape[1]
    n = wide // columns
    rows = width // (2 * LINE)
    dma = pltpu.SemaphoreType.DMA
    anywhere = pl.BlockSpec(memory_space=pl.ANY)
    return pl.pallas_call(
        expert_grads_kernel,
        in_specs=[anywhere] * 4,
        out_specs=anywhere,
        out_shape=jax.ShapeDtypeStruct((4, rows, wide), BF16),
        scratch_shapes=[
            pltpu.VMEM((width, tokens), BF16),
            pltpu.VMEM((2, tokens, columns), BF16),
            pltpu.VMEM((n, 2, LINE, rows, columns), BF16),
            pltpu.VMEM((n, LINE, rows, columns), BF16),
            pltpu.VMEM((n, LINE, rows, columns), BF16),
            pltpu.VMEM((n, LINE, rows, columns), BF16),
            pltpu.VMEM((rows, columns), F32),
            pltpu.VMEM((n, rows, columns), BF16),
            dma((2,)),
            dma,
            dma((2, n)),
            dma((2, n, LINE)),
            dma((2, n, LINE)),
            dma((n,)),
            dma((2, n)),
            dma((2, n)),
            dma((2, n)),
        ],
        compiler_params=pltpu.CompilerParams(vmem_limit_bytes=60 * MIB, collective_id=4, has_side_effects=True),
        cost_estimate=pl.CostEstimate(
            flops=2 * width * tokens * wide, bytes_accessed=80 * MIB, transcendentals=0
        ),
        name="expert_grads",
    )(x_t, top_t, dgu, gated)


def late_reduce_kernel(
    in_ref,
    early_ref,
    out_ref,
    early_out,
    early_core,
    early_mid,
    early_far,
    early_sems,
    own_buf,
    core_buf,
    parts,
    y_buf,
    right_buf,
    left_buf,
    total,
    mine,
    far_buf,
    whole,
    load_sem,
    core_sems,
    y_sems,
    right_sems,
    left_sems,
    own_sem,
    far_sems,
    near_sems,
):
    n = parts.shape[0]
    rows, columns = parts.shape[3:]
    rep = lax.axis_index("rep")
    half = lax.rem(rep, 2)
    to_core, to_far = {"rep": rep + 1 - 2 * half}, {"rep": lax.rem(rep + 2, 4)}
    place, across, add_across, step_right, step_left, collect, drain, greet = line_reduce(
        parts, y_buf, right_buf, left_buf, y_sems, right_sems, left_sems
    )

    def span(which, c):
        return pl.ds(pl.multiple_of((which * n + c) * columns, columns), columns)

    def load(c):
        return pltpu.make_async_copy(in_ref.at[:, span(half, c)], own_buf.at[c], load_sem.at[c])

    def from_core(c):
        return send_to(
            in_ref.at[:, span(1 - half, c)], core_buf.at[c], core_sems.at[0, c], core_sems.at[1, c], to_core
        )

    def over_x(c):
        return send_to(mine.at[c], far_buf.at[c], far_sems.at[0, c], far_sems.at[1, c], to_far)

    def over_core(c):
        return send_to(
            whole.at[c], out_ref.at[:, span(half, c)], near_sems.at[0, c], near_sems.at[1, c], to_core
        )

    def keep(c):
        return pltpu.make_async_copy(whole.at[c], out_ref.at[:, span(half, c)], own_sem.at[c])

    for c in range(n):
        load(c).start()
    greet([to_core, to_far])
    early_near = send_to(early_ref, early_core, early_sems.at[0, 0], early_sems.at[1, 0], to_core)
    early_over = send_to(early_mid, early_far, early_sems.at[0, 1], early_sems.at[1, 1], to_far)
    early_near.start()
    for c in range(n):
        from_core(c).start()
    early_near.wait_recv()
    early_mid[...] = (early_ref[...].astype(F32) + early_core[...].astype(F32)).astype(BF16)
    early_over.start()

    def produce(c):
        load(c).wait()
        from_core(c).wait_recv()
        for t in range(2 * LINE):
            here = pl.ds(t * rows, rows)
            parts[c, t % 2, t // 2] = (own_buf[c, here].astype(F32) + core_buf[c, here].astype(F32)).astype(BF16)
        across(c).start()

    def finish(c):
        collect(c, total)
        mine[c] = total[...].astype(BF16)
        over_x(c).start()

    def complete(c):
        over_x(c).wait_recv()
        whole[c] = (mine[c].astype(F32) + far_buf[c].astype(F32)).astype(BF16)
        over_core(c).start()
        keep(c).start()

    def step(i, carry):
        between(i, 0, n, lambda: produce(i))
        between(i, 1, n + 1, lambda: add_across(i - 1))
        to_right_chunk, to_left_chunk = i - 1 - place, i - LINE + place
        between(to_right_chunk, 0, n, lambda: step_right(to_right_chunk))
        between(to_left_chunk, 0, n, lambda: step_left(to_left_chunk))
        between(i, LINE, n + LINE, lambda: finish(i - LINE))
        between(i, LINE + 1, n + LINE + 1, lambda: complete(i - LINE - 1))
        return carry

    lax.fori_loop(0, n + LINE + 1, step, 0)
    early_over.wait_recv()
    early_out[...] = (early_mid[...].astype(F32) + early_far[...].astype(F32)).astype(BF16)
    early_near.wait_send()
    early_over.wait_send()

    def end(c, carry):
        drain(c)
        from_core(c).wait_send()
        over_x(c).wait_send()
        over_core(c).wait_send()
        keep(c).wait()
        send_to(
            whole.at[c], out_ref.at[:, span(1 - half, c)], near_sems.at[0, c], near_sems.at[1, c], to_core
        ).wait_recv()
        return carry

    lax.fori_loop(0, n, end, 0)


def late_reduce(values, early, columns=256):
    width, wide = values.shape
    n = wide // 2 // columns
    rows = width // (2 * LINE)
    dma = pltpu.SemaphoreType.DMA
    anywhere = pl.BlockSpec(memory_space=pl.ANY)
    return pl.pallas_call(
        late_reduce_kernel,
        in_specs=[anywhere, pl.BlockSpec(memory_space=pltpu.VMEM)],
        out_specs=[anywhere, pl.BlockSpec(memory_space=pltpu.VMEM)],
        out_shape=[jax.ShapeDtypeStruct((rows, wide), BF16), jax.ShapeDtypeStruct(early.shape, BF16)],
        scratch_shapes=[
            pltpu.VMEM(early.shape, BF16),
            pltpu.VMEM(early.shape, BF16),
            pltpu.VMEM(early.shape, BF16),
            dma((2, 2)),
            pltpu.VMEM((n, width, columns), BF16),
            pltpu.VMEM((n, width, columns), BF16),
            pltpu.VMEM((n, 2, LINE, rows, columns), BF16),
            pltpu.VMEM((n, LINE, rows, columns), BF16),
            pltpu.VMEM((n, LINE, rows, columns), BF16),
            pltpu.VMEM((n, LINE, rows, columns), BF16),
            pltpu.VMEM((rows, columns), F32),
            pltpu.VMEM((n, rows, columns), BF16),
            pltpu.VMEM((n, rows, columns), BF16),
            pltpu.VMEM((n, rows, columns), BF16),
            dma((n,)),
            dma((2, n)),
            dma((2, n)),
            dma((2, n, LINE)),
            dma((2, n, LINE)),
            dma((n,)),
            dma((2, n)),
            dma((2, n)),
        ],
        compiler_params=pltpu.CompilerParams(vmem_limit_bytes=48 * MIB, collective_id=5, has_side_effects=True),
        cost_estimate=pl.CostEstimate(flops=0, bytes_accessed=4 * MIB, transcendentals=0),
        name="late_reduce",
    )(values, early)


def flatten_kernel(starts, lead_ref, *refs):
    parts, flat_ref, square_ref = refs[: len(starts)], refs[len(starts)], refs[len(starts) + 1]
    scratch, sems = refs[len(starts) + 2 : -1], refs[-1]
    step = pl.program_id(0)
    steps = pl.num_programs(0)
    slot = lax.rem(step, 2)
    flat = flat_ref.reshape(flat_ref.shape[1] // LANES, LANES)
    lead_places = ((0, 0, 1), (1, starts[2] - 17 , 1), (2, starts[2] - 16, 16))

    def copies(index, where):
        out = []
        for n, (start, buffer) in enumerate(zip(starts, scratch)):
            size = buffer.shape[1]
            out.append(pltpu.make_async_copy(buffer.at[where], flat.at[pl.ds(start + index * size, size)], sems.at[where, n]))
        return out

    @pl.when(step == 0)
    def _():
        square_ref[...] = jnp.sum(lead_ref[...] * lead_ref[...], keepdims=True).reshape(1, 1) + jnp.zeros_like(square_ref)
        for n, (source, target, size) in enumerate(lead_places):
            copy = pltpu.make_async_copy(lead_ref.at[pl.ds(source, size)], flat.at[pl.ds(target, size)], sems.at[2, n])
            copy.start()
            copy.wait()

    @pl.when(step >= 2)
    def _():
        for copy in copies(step - 2, slot):
            copy.wait()

    total = jnp.zeros((8, LANES), F32)
    for part, buffer in zip(parts, scratch):
        rows = part.shape[-2]
        wide = buffer.shape[1] // rows
        reps = part.shape[0] if len(part.shape) == 3 else 1
        each = wide // reps
        for r in range(reps):
            for c in range(each):
                lanes = slice(c * LANES, (c + 1) * LANES)
                value = (part[r, :, lanes] if len(part.shape) == 3 else part[:, lanes]).astype(F32)
                buffer[slot, pl.ds(r * each + c, rows, stride=wide), :] = value
                square = value * value
                for k in range(0, rows, 8):
                    total += square[k : k + 8]
    square_ref[...] += jnp.sum(total, keepdims=True).reshape(1, 1)
    for copy in copies(step, slot):
        copy.start()

    @pl.when(step == steps - 1)
    def _():
        for copy in copies(step - 1, 1 - slot):
            copy.wait()
        for copy in copies(step, slot):
            copy.wait()

def flatten(size, lead, parts, tile=16):
    rows = parts[0][0].shape[-2]
    widths = [columns * (p.shape[0] if p.ndim == 3 else 1) // LANES for p, columns, _ in parts]
    starts, at = [], 1
    for n, w in enumerate(widths):
        if n == 2: at += 1 + 16
        starts.append(at); at += rows * w
    specs = []
    for p, columns, place in parts:
        if p.ndim == 3:
            specs.append(pl.BlockSpec((p.shape[0], tile, columns), lambda i, place=place: (0, i, place)))
        else:
            specs.append(pl.BlockSpec((tile, columns), lambda i, place=place: (i, place)))
    return pl.pallas_call(
        functools.partial(flatten_kernel, starts),
        grid=(rows // tile,),
        in_specs=[pl.BlockSpec(lead.shape, lambda i: (0, 0))] + specs,
        out_specs=[pl.BlockSpec(memory_space=pl.ANY), pl.BlockSpec((1, 1), lambda i: (0, 0))],
        out_shape=[jax.ShapeDtypeStruct((1, size), F32), jax.ShapeDtypeStruct((1, 1), F32)],
        scratch_shapes=[pltpu.VMEM((2, tile * w, LANES), F32) for w in widths] + [pltpu.SemaphoreType.DMA((3, 4))],
        compiler_params=pltpu.CompilerParams(vmem_limit_bytes=48 * MIB),
        name="flatten",
    )(lead, *[p for p, _, _ in parts])

HALF_ROWS = 1056


def moments(grad, first, second, scale):
    clipped = grad * scale
    new_first = BETA_ONE * first + (1.0 - BETA_ONE) * clipped
    new_second = BETA_TWO * second + (1.0 - BETA_TWO) * clipped * clipped
    return new_first, new_second


def inner_step(new_first, new_second, weight):
    root = jnp.sqrt(new_second * (1.0 / (1.0 - BETA_TWO**STEP))) + ADAM_EPS
    return -INNER_RATE * (new_first * (1.0 / (1.0 - BETA_ONE**STEP)) / root + DECAY_RATE * weight)


def flat_chunks(rows):
    chunks, at, half_at = [], 0, 0
    while at < rows:
        size = min(2 * HALF_ROWS, rows - at)
        half = -(-size // 32) * 16
        chunks.append((at, size, half_at, half))
        at, half_at = at + size, half_at + half
    return chunks


def step_kernel(
    square_ref,
    g_ref,
    f_ref,
    s_ref,
    w_ref,
    norm_ref,
    total,
    g_buf,
    f_buf,
    s_buf,
    w_buf,
    step_buf,
    near_buf,
    far_buf,
    sum_buf,
    square_mine,
    square_all,
    in_sem,
    near_send,
    near_recv,
    far_send,
    far_recv,
    back_send,
    back_recv,
    own_sem,
    square_send,
    square_recv,
):
    rows = g_ref.shape[-1] // LANES
    chunks = flat_chunks(rows)
    count = len(chunks)
    shards = lax.axis_size("shard")
    shard, rep = lax.axis_index("shard"), lax.axis_index("rep")
    side = lax.rem(rep, 2)
    to_core, to_far = {"rep": rep + 1 - 2 * side}, {"rep": lax.rem(rep + 2, 4)}

    def other(k):
        return {"shard": lax.rem(shard + k, shards)}

    barrier = pltpu.get_barrier_semaphore()
    greeted = [to_core, to_far] + [other(k) for k in range(1, shards)]
    for device in greeted:
        pl.semaphore_signal(barrier, inc=1, device_id=device, device_id_type=MESH)

    def loads(i):
        at, size, _, _ = chunks[i]
        pairs = (g_ref, g_buf), (f_ref.at[0], f_buf), (s_ref.at[0], s_buf), (w_ref, w_buf)
        return [
            pltpu.make_async_copy(
                ref.at[:, pl.ds(at * LANES, size * LANES)],
                buf.at[i % 2, :, pl.ds(0, size * LANES)],
                in_sem.at[i % 2, n],
            )
            for n, (ref, buf) in enumerate(pairs)
        ]

    def remote(source, target, send, receive, device):
        return pltpu.make_async_remote_copy(
            src_ref=source, dst_ref=target, send_sem=send, recv_sem=receive, device_id=device, device_id_type=MESH
        )

    def near(i):
        _, _, at, half = chunks[i]
        span = pl.ds(at, half)
        return remote(step_buf.at[1 - side, span], near_buf.at[span], near_send.at[i], near_recv.at[i], to_core)

    def far(i):
        _, _, at, half = chunks[i]
        span = pl.ds(at, half)
        return remote(step_buf.at[side, span], far_buf.at[span], far_send.at[i], far_recv.at[i], to_far)

    def back(i):
        _, _, at, half = chunks[i]
        span = pl.ds(at, half)
        return remote(sum_buf.at[span], total.at[side, span], back_send.at[i], back_recv.at[i], to_core)

    def keep(i):
        _, _, at, half = chunks[i]
        span = pl.ds(at, half)
        return pltpu.make_async_copy(sum_buf.at[span], total.at[side, span], own_sem.at[i])

    for copy in loads(0):
        copy.start()
    pl.semaphore_wait(barrier, len(greeted))

    def square_copy(k):
        return remote(square_mine, square_all.at[shard], square_send.at[k], square_recv.at[shard], other(k))

    square_mine[...] = jnp.broadcast_to(square_ref[...], square_mine.shape)
    square_all[shard] = square_mine[...]
    for k in range(1, shards):
        square_copy(k).start()
    for k in range(1, shards):
        source = lax.rem(shard + k, shards)
        remote(
            square_mine, square_all.at[source], square_send.at[k], square_recv.at[source], other(k)
        ).wait_recv()
    norm = jnp.sqrt(jnp.sum(square_all[...], axis=0))
    norm_ref[...] = norm[:1, :1]
    scale = (CLIP_NORM / jnp.maximum(norm, CLIP_NORM))[:1]

    def blocks(size):
        return 48 if size % 48 == 0 else 16

    def compute(i):
        _, _, at, half = chunks[i]
        block = blocks(half)
        for h in (0, 1):

            def body(j, carry):
                here = pl.multiple_of(j * block, 16)
                span = pl.ds(pl.multiple_of((h * half + here) * LANES, LANES), block * LANES)
                grad, first, second, weight = (
                    buf[i % 2, :, span].reshape(block, LANES) for buf in (g_buf, f_buf, s_buf, w_buf)
                )
                new_first, new_second = moments(grad, first, second, scale)
                step = inner_step(new_first, new_second, weight)
                step_buf[h, pl.ds(at + here, block)] = step.astype(BF16)
                return carry

            lax.fori_loop(0, half // block, body, 0)

    def add(i, left, right, target):
        _, _, at, half = chunks[i]
        block = blocks(half)

        def body(j, carry):
            span = pl.ds(pl.multiple_of(at + j * block, 16), block)
            target[span] = (left[span].astype(F32) + right[span].astype(F32)).astype(BF16)
            return carry

        lax.fori_loop(0, half // block, body, 0)

    for i in range(count + 2):
        if i < count:
            for copy in loads(i):
                copy.wait()
            if i + 1 < count:
                for copy in loads(i + 1):
                    copy.start()
            compute(i)
            near(i).start()
        if 1 <= i <= count:
            near(i - 1).wait_recv()
            add(i - 1, step_buf.at[side], near_buf, step_buf.at[side])
            far(i - 1).start()
        if i >= 2:
            far(i - 2).wait_recv()
            add(i - 2, step_buf.at[side], far_buf, sum_buf)
            back(i - 2).start()
            keep(i - 2).start()
    for k in range(1, shards):
        square_copy(k).wait_send()
    for i in range(count):
        near(i).wait_send()
        far(i).wait_send()
        back(i).wait_send()
        keep(i).wait()
        _, _, at, half = chunks[i]
        span = pl.ds(at, half)
        remote(
            sum_buf.at[span], total.at[1 - side, span], back_send.at[i], back_recv.at[i], to_core
        ).wait_recv()


def summed_step(square, grad, first, second, weight):
    rows = grad.shape[-1] // LANES
    chunks = flat_chunks(rows)
    count = len(chunks)
    halves = sum(chunk[3] for chunk in chunks)
    size = chunks[0][3] * 2
    shards = lax.axis_size("shard")
    dma = pltpu.SemaphoreType.DMA
    anywhere = pl.BlockSpec(memory_space=pl.ANY)
    return pl.pallas_call(
        step_kernel,
        in_specs=[pl.BlockSpec(memory_space=pltpu.VMEM)] + [anywhere] * 4,
        out_specs=[pl.BlockSpec(memory_space=pltpu.VMEM), anywhere],
        out_shape=[jax.ShapeDtypeStruct((1, 1), F32), jax.ShapeDtypeStruct((2, halves, LANES), BF16)],
        scratch_shapes=[pltpu.VMEM((2, 1, size * LANES), F32)] * 4
        + [
            pltpu.VMEM((2, halves, LANES), BF16),
            pltpu.VMEM((halves, LANES), BF16),
            pltpu.VMEM((halves, LANES), BF16),
            pltpu.VMEM((halves, LANES), BF16),
            pltpu.VMEM((8, LANES), F32),
            pltpu.VMEM((shards, 8, LANES), F32),
            dma((2, 4)),
        ]
        + [dma((count,))] * 7
        + [dma((shards,))] * 2,
        compiler_params=pltpu.CompilerParams(
            vmem_limit_bytes=48 * MIB, collective_id=3, has_side_effects=True
        ),
        cost_estimate=pl.CostEstimate(flops=0, bytes_accessed=4 * MIB, transcendentals=0),
        name="summed_step",
    )(square, grad, first, second, weight)


def update_kernel(
    reps, norm_ref, g, f, s, total, mom, nf, ns, nm, up, tg, tf, ts, tm, tt, tnf, tns, tnm, tup, sems
):
    rows = g.shape[-1] // LANES
    chunks = flat_chunks(rows)
    whole = [c for c in chunks if c[1] == 2 * HALF_ROWS]
    scale = CLIP_NORM / jnp.maximum(norm_ref[...], CLIP_NORM)

    def body(g_ref, f_ref, s_ref, t_ref, m_ref, nf_ref, ns_ref, nm_ref, up_ref):
        half = t_ref.shape[1]
        size = g_ref.shape[0]
        nf_ref[...], ns_ref[...] = moments(g_ref[...], f_ref[...], s_ref[...], scale)
        for h in (0, 1):
            span = slice(h * half, min((h + 1) * half, size))
            pseudo = t_ref[h, : span.stop - span.start].astype(F32) * (-1.0 / reps)
            new = OUTER_MOMENTUM * m_ref[span] + pseudo
            nm_ref[span] = new
            up_ref[span] = -OUTER_RATE * (pseudo + OUTER_MOMENTUM * new)

    def view(ref):
        return ref.reshape(rows, LANES)

    ins, outs = [view(g), view(f), view(s), total, view(mom)], [view(r) for r in (nf, ns, nm, up)]
    wide = pl.BlockSpec((2 * HALF_ROWS, LANES), lambda i: (i, 0))
    halves = pl.BlockSpec((2, HALF_ROWS, LANES), lambda i: (0, i, 0))
    if whole:
        pltpu.emit_pipeline(
            body, grid=(len(whole),), in_specs=[wide, wide, wide, halves, wide], out_specs=[wide] * 4
        )(*ins, *outs)
    for at, size, half_at, half in chunks[len(whole) :]:

        def part(n, ref):
            return ref.at[:, pl.ds(half_at, half)] if n == 3 else ref.at[pl.ds(at, size)]

        copies = [
            pltpu.make_async_copy(part(n, ref), buf, sems.at[n]) for n, (ref, buf) in enumerate(zip(ins, (tg, tf, ts, tt, tm)))
        ]
        for copy in copies:
            copy.start()
        for copy in copies:
            copy.wait()
        body(tg, tf, ts, tt, tm, tnf, tns, tnm, tup)
        copies = [
            pltpu.make_async_copy(buf, ref.at[pl.ds(at, size)], sems.at[n])
            for n, (buf, ref) in enumerate(zip((tnf, tns, tnm, tup), outs))
        ]
        for copy in copies:
            copy.start()
        for copy in copies:
            copy.wait()


def update(reps, norm, grad, first, second, total, mom):
    _, size, _, half = flat_chunks(grad.shape[-1] // LANES)[-1]
    anywhere = pl.BlockSpec(memory_space=pl.ANY)
    tail = pltpu.VMEM((size, LANES), F32)
    return pl.pallas_call(
        functools.partial(update_kernel, reps),
        in_specs=[pl.BlockSpec(memory_space=pltpu.VMEM)] + [anywhere] * 5,
        out_specs=[anywhere] * 4,
        out_shape=[jax.ShapeDtypeStruct(ref.shape, F32) for ref in (first, second, mom, mom)],
        scratch_shapes=[tail] * 4
        + [pltpu.VMEM((2, half, LANES), BF16)]
        + [tail] * 4
        + [pltpu.SemaphoreType.DMA((5,))],
        compiler_params=pltpu.CompilerParams(vmem_limit_bytes=48 * MIB),
        cost_estimate=pl.CostEstimate(flops=0, bytes_accessed=120 * MIB, transcendentals=0),
        name="update",
    )(norm, grad, first, second, total, mom)


def rms_scale(rows):
    return lax.rsqrt(jnp.mean(rows * rows, axis=-1, keepdims=True) + EPSILON)


def rms_backward(rows, scale, gain, grad_out):
    grad_gain = jnp.sum(grad_out * rows * scale, axis=0)
    inner = jnp.sum(grad_out * gain * rows, axis=-1, keepdims=True)
    grad_in = scale * gain * grad_out - rows * scale * scale * scale * inner / rows.shape[-1]
    return grad_in, grad_gain


def rotate(rows, cosine, sine):
    half = HEAD_SIZE // 2
    front, back = rows[:, :half], rows[:, half:]
    return jnp.concatenate([front * cosine - back * sine, back * cosine + front * sine], axis=1)


def per_device(
    tokens,
    cotangent,
    routes,
    branch,
    attn_gain,
    query_key_value_weight,
    w_attn_out,
    ffn_gain,
    w_router,
    w_in,
    w_out,
    adam_first,
    adam_second,
    outer_mom,
):
    shards = lax.axis_size("shard")
    reps = lax.axis_size("rep")
    count = tokens.shape[2]
    width = tokens.shape[3]
    prompt = count - CONTINUATION_LEN
    local = EXPERTS // reps
    groups = None
    if shards > GROUP_SIZE:
        groups = [list(range(i, i + GROUP_SIZE)) for i in range(0, shards, GROUP_SIZE)]
    shard_pos = lax.axis_index("shard") % GROUP_SIZE
    rep_pos = lax.axis_index("rep")
    branch_len = branch.reshape(())
    x_in = tokens.reshape(count, width).astype(F32)
    top_low = cotangent.reshape(count, width)
    grad_top = top_low.astype(F32)
    route_ids = routes.reshape(count, TOP)
    gather = functools.partial(lax.all_gather, axis_name="shard", axis=0, tiled=True)
    rows = width // shards
    qkv_columns = Q_WIDTH + 2 * KV_WIDTH
    fast = shards == 2 * LINE and reps == 4 and rows == LANES
    flat_path = fast and outer_mom.shape[-1] % LANES == 0

    small = jnp.concatenate(
        [query_key_value_weight, w_attn_out, w_router, attn_gain[:, None], ffn_gain[:, None]], axis=1
    )
    small = jnp.pad(small, ((0, 0), (0, -small.shape[1] % LANES)))
    tokens_low = tokens.reshape(count, width)
    if fast:
        prompt_low, small_full, all_top = start_gather(tokens_low, small, top_low)
        small_full = small_full.reshape(width, small.shape[1])
    else:
        prompt_low = lax.all_gather(tokens_low[:prompt], "shard", axis=0, tiled=False, axis_index_groups=groups)
        small_full = gather(small)
        by_rep = lax.all_gather(top_low, "rep", axis=0, tiled=False)
        core_pos = rep_pos + 1 - 2 * (rep_pos % 2)
        all_top = jnp.stack([top_low] + [by_rep[i] for i in (core_pos, (rep_pos + 2) % 4, 3 - rep_pos)])
    prompt_low = prompt_low.reshape(GROUP_SIZE * prompt, width)
    qkv_full = small_full[:, :qkv_columns]
    attn_out_full = small_full[:, qkv_columns : qkv_columns + Q_WIDTH]
    router_full = small_full[:, qkv_columns + Q_WIDTH : qkv_columns + Q_WIDTH + EXPERTS]
    gains = small_full[:, qkv_columns + Q_WIDTH + EXPERTS :].astype(F32)
    attn_gain_full, ffn_gain_full = gains[:, 0], gains[:, 1]
    w_both = jnp.concatenate(
        [
            lax.dynamic_slice_in_dim(w_in, rep_pos * local * 2 * F, local * 2 * F, 1),
            lax.dynamic_slice_in_dim(w_out, rep_pos * local * F, local * F, 1),
        ],
        axis=1,
    )
    w_both, prompt_low = lax.optimization_barrier((w_both, prompt_low))
    w_both = gather(w_both)

    def normed(values):
        scale = rms_scale(values)
        return (values * scale * attn_gain_full).astype(BF16), scale

    def angles_of(positions):
        half = HEAD_SIZE // 2
        inverse_freq = ROPE_BASE ** (-(jnp.arange(half, dtype=F32) * 2.0) / HEAD_SIZE)
        angles = inverse_freq[:, None] * positions.astype(F32)[None, :]
        return jnp.cos(angles)[None], jnp.sin(angles)[None]

    def project(source, start, size, turn):
        rows = dot(qkv_full[:, start : start + size], source, (0, 1))
        rows = rows.reshape(size // HEAD_SIZE, HEAD_SIZE, source.shape[0])
        return (rotate(rows, *turn) if turn is not None else rows).astype(BF16)

    def keys_values(source, turn):
        return project(source, Q_WIDTH, KV_WIDTH, turn), project(source, Q_WIDTH + KV_WIDTH, KV_WIDTH, None)

    normed_attn, attn_scale = normed(x_in)
    normed_prompt, _ = normed(prompt_low.astype(F32))
    prompt_turn = angles_of(jnp.arange(GROUP_SIZE * prompt, dtype=jnp.int32))
    own_turn = angles_of(
        jnp.concatenate(
            [
                shard_pos * prompt + jnp.arange(prompt, dtype=jnp.int32),
                branch_len + jnp.arange(CONTINUATION_LEN, dtype=jnp.int32),
            ]
        )
    )
    continued_turn = tuple(part[..., prompt:] for part in own_turn)
    prompt_kv = keys_values(normed_prompt, prompt_turn)
    own_kv = jnp.stack(keys_values(normed_attn[prompt:], continued_turn))
    query = project(normed_attn, 0, Q_WIDTH, own_turn)
    where = jnp.stack([shard_pos.astype(jnp.int32), branch_len])
    if flat_path:
        size = outer_mom.shape[-1]

        def lead(first, second, rest):
            parts = [first[None].astype(F32), second[None].astype(F32), rest.reshape(-1, LANES).astype(F32)]
            return jnp.concatenate(parts, axis=0)

        def whole(values):
            return values, values.shape[-1], 0

        weight_flat, _ = flatten(
            size,
            lead(attn_gain, ffn_gain, w_router),
            [whole(query_key_value_weight), whole(w_attn_out), whole(w_in), whole(w_out)],
        )
        weight_flat, query = lax.optimization_barrier((weight_flat, query))
    attn, lse = attn_forward(where, query, prompt_kv, own_kv)
    attn_low = attn.reshape(Q_WIDTH, count)
    x_mid = x_in + dot(attn_low, attn_out_full, (0, 1))

    ffn_scale = rms_scale(x_mid)
    normed_ffn = (x_mid * ffn_scale * ffn_gain_full).astype(BF16)
    logits = dot(normed_ffn, router_full, (1, 0))
    chosen = jnp.any(route_ids[:, :, None] == jnp.arange(EXPERTS, dtype=jnp.int32), axis=1)
    gates = jax.nn.softmax(jnp.where(chosen, logits, NEGATIVE), axis=-1)
    gates = jnp.where(chosen, gates, 0.0)

    gates_out = jnp.pad(gates.T.reshape(reps, local, count), ((0, 0), (0, 8 - local), (0, 0)))
    _, dx_own, dx_core, dx_far, y_keep, y_give, normed_t, top_t, dgu, gated, dgate_part = experts(
        normed_ffn, all_top, gates_out, w_both
    )
    grad_from_experts = dx_own.astype(F32) + dx_core.astype(F32) + dx_far.astype(F32)
    grad_gates = dgate_part[:, :local].reshape(EXPERTS, count).T
    to_core = [(i, i + 1 - 2 * (i % 2)) for i in range(reps)]
    to_far = [(i, (i + 2) % reps) for i in range(reps)]
    y_near = y_keep.astype(F32) + lax.ppermute(y_give, "rep", to_core).astype(F32)
    y_sum = y_near[0] + lax.ppermute(y_near[1].astype(BF16), "rep", to_far).astype(F32)
    block_out = (x_mid + y_sum).astype(BF16)

    def rep_sum(values):
        for pairs in (to_core, to_far):
            values = (values.astype(F32) + lax.ppermute(values, "rep", pairs).astype(F32)).astype(BF16)
        return values

    def expert_term(left, right):
        return dot(left, right.reshape(reps * count, -1), (1, 0)).astype(BF16)

    grad_logits = (gates * (grad_gates - jnp.sum(gates * grad_gates, axis=-1, keepdims=True))).astype(BF16)
    grad_router_w = dot(normed_ffn, grad_logits, (0, 0))
    grad_normed_ffn = grad_from_experts + dot(grad_logits, router_full, (1, 1))
    grad_mid_norm, grad_ffn_gain = rms_backward(x_mid, ffn_scale, ffn_gain_full, grad_normed_ffn)
    grad_mid = grad_top + grad_mid_norm
    grad_branch = grad_mid.astype(BF16)
    grad_attn_w = dot(grad_branch, attn_low, (0, 1))
    grad_attn = dot(attn_out_full, grad_branch, (0, 1)).astype(BF16).reshape(QUERY_HEADS, HEAD_SIZE, count)
    expert_columns = local * 3 * F
    if fast:
        expert_rows = expert_grads(
            normed_t,
            top_t,
            dgu.reshape(reps * count, -1),
            gated.reshape(reps * count, -1),
        )
    else:
        terms = jnp.concatenate([expert_term(normed_t, dgu), expert_term(top_t, gated)], axis=1)
        terms = lax.psum_scatter(terms, "shard", scatter_dimension=0, tiled=True)
        expert_rows = lax.all_gather(terms, "rep", axis=0, tiled=False)
    blank = jnp.zeros((width, -(Q_WIDTH + EXPERTS + 1) % LANES), BF16)
    early = jnp.concatenate(
        [grad_attn_w.astype(BF16), grad_router_w.astype(BF16), grad_ffn_gain[:, None].astype(BF16), blank], axis=1
    )
    grad_attn, early, expert_rows = lax.optimization_barrier((grad_attn, early, expert_rows))
    early = lax.psum_scatter(early, "shard", scatter_dimension=0, tiled=True)

    grad_query, grad_prompt_kv, grad_own_kv = attn_backward(
        where, query, prompt_kv, own_kv, grad_attn, attn, lse, jnp.concatenate(prompt_turn), jnp.concatenate(own_turn)
    )

    early, grad_query, grad_prompt_kv, grad_own_kv = lax.optimization_barrier(
        (early, grad_query, grad_prompt_kv, grad_own_kv)
    )
    grad_query = grad_query.reshape(Q_WIDTH, count)
    grad_prompt_kv = grad_prompt_kv.reshape(2 * KV_WIDTH, GROUP_SIZE * prompt)
    grad_own_kv = grad_own_kv.reshape(2 * KV_WIDTH, CONTINUATION_LEN)
    late_kv = dot(normed_prompt, grad_prompt_kv, (0, 1)) + dot(normed_attn[prompt:], grad_own_kv, (0, 1))
    late = jnp.concatenate([dot(normed_attn, grad_query, (0, 1)).astype(BF16), late_kv.astype(BF16)], axis=1)
    if fast:
        qkv_rows, early = late_reduce(late, early)
    else:
        qkv_rows = rep_sum(lax.psum_scatter(late, "shard", scatter_dimension=0, tiled=True))
        early = rep_sum(early)
    attn_rows, router_rows = early[:, :Q_WIDTH], early[:, Q_WIDTH : Q_WIDTH + EXPERTS]
    ffn_gain_rows = early[:, Q_WIDTH + EXPERTS]
    attn_gain_rows = jnp.sum(
        qkv_rows.astype(F32) * query_key_value_weight.astype(F32), axis=1
    ) / attn_gain.astype(F32)

    in_columns = local * 2 * F
    if flat_path:
        total_grad, square = flatten(
            size,
            lead(attn_gain_rows, ffn_gain_rows, router_rows),
            [
                whole(qkv_rows),
                whole(attn_rows),
                (expert_rows, in_columns, 0),
                (expert_rows, expert_columns - in_columns, in_columns // (expert_columns - in_columns)),
            ],
        )
    else:
        weight_flat = jnp.concatenate(
            [
                portion.astype(F32).reshape(-1)
                for portion in (attn_gain, query_key_value_weight, w_attn_out, ffn_gain, w_router, w_in, w_out)
            ]
        )
        total_grad = jnp.concatenate(
            [
                portion.astype(F32).reshape(-1)
                for portion in (
                    attn_gain_rows,
                    qkv_rows,
                    attn_rows,
                    ffn_gain_rows,
                    router_rows,
                    expert_rows[:, :, :in_columns].transpose(1, 0, 2),
                    expert_rows[:, :, in_columns:].transpose(1, 0, 2),
                )
            ]
        )

    def scatter(shared):
        return lax.psum_scatter(shared, "shard", scatter_dimension=1, tiled=True, axis_index_groups=groups)

    reduced_kv = scatter(grad_prompt_kv)
    if flat_path:
        grad_norm, step_sum = summed_step(square, total_grad, adam_first, adam_second, weight_flat)
        step_sum, reduced_kv = lax.optimization_barrier((step_sum, reduced_kv))
    grad_projected = jnp.concatenate([grad_query, jnp.concatenate([reduced_kv, grad_own_kv], axis=1)], axis=0)
    grad_normed_attn = dot(grad_projected, qkv_full, (0, 1))
    grad_x_norm, _ = rms_backward(x_in, attn_scale, attn_gain_full, grad_normed_attn)
    grad_input = grad_mid + grad_x_norm

    if flat_path:
        new_first, new_second, new_mom, weight_update = update(
            reps, grad_norm, total_grad, adam_first, adam_second, step_sum, outer_mom
        )
        grad_norm = grad_norm.reshape(())
    else:
        grad_norm = jnp.sqrt(lax.psum(jnp.sum(total_grad * total_grad), "shard"))
        new_first, new_second = moments(
            total_grad,
            adam_first.reshape(-1),
            adam_second.reshape(-1),
            CLIP_NORM / jnp.maximum(grad_norm, CLIP_NORM),
        )
        step = inner_step(new_first, new_second, weight_flat)
        pseudo = -(lax.psum(step.astype(BF16), "rep").astype(F32) / reps)
        new_mom = OUTER_MOMENTUM * outer_mom.reshape(-1) + pseudo
        weight_update = -OUTER_RATE * (pseudo + OUTER_MOMENTUM * new_mom)
    return (
        block_out.reshape(tokens.shape),
        grad_input.reshape(tokens.shape),
        total_grad.reshape(outer_mom.shape),
        grad_norm,
        new_first.reshape(adam_first.shape),
        new_second.reshape(adam_second.shape),
        new_mom.reshape(outer_mom.shape),
        weight_update.reshape(outer_mom.shape),
    )


def solution(mesh):
    by_token = P("rep", "shard", None, None)
    by_state = P("rep", "shard", None)
    by_row = P("shard", None)
    placed = (
        by_token,
        by_token,
        by_token,
        P("rep", "shard"),
        P("shard"),
        by_row,
        by_row,
        P("shard"),
        by_row,
        by_row,
        by_row,
        by_state,
        by_state,
        by_row,
    )
    return jax.shard_map(
        per_device,
        mesh=mesh,
        in_specs=placed,
        out_specs=(by_token, by_token, by_row, P(), by_state, by_state, by_row, by_row),
        check_vma=False,
    )
```

```python
import functools

import jax
import jax.numpy as jnp
from jax import lax
from jax.experimental import pallas as pl
from jax.experimental.pallas import tpu as pltpu
from jax.sharding import PartitionSpec as P

QUERY_HEADS = 16
KEY_VALUE_HEADS = 8
HEAD_SIZE = 64
F = 512
EXPERTS = 16
TOP = 8
GROUP_SIZE = 8
CONTINUATION_LEN = 512
STEP = 10

EPSILON = 1e-06
NEGATIVE = -1e30
ROPE_BASE = 10000.0
BETA_ONE = 0.9
BETA_TWO = 0.95
ADAM_EPS = 1e-08
INNER_RATE = 0.01
DECAY_RATE = 0.1
OUTER_RATE = 0.7
OUTER_MOMENTUM = 0.9
CLIP_NORM = 1.0

LOG2E = 1.4426950408889634
LANES = 128
MIB = 1 << 20
BF16 = jnp.bfloat16
F32 = jnp.float32
PER_KEY = QUERY_HEADS // KEY_VALUE_HEADS
Q_WIDTH = QUERY_HEADS * HEAD_SIZE
KV_WIDTH = KEY_VALUE_HEADS * HEAD_SIZE


def dot(left, right, dims):
    return lax.dot_general(left, right, ((dims[:1], dims[1:]), ((), ())), preferred_element_type=F32)


def split_three(value):
    high = value.astype(BF16)
    rest = value - high.astype(F32)
    middle = rest.astype(BF16)
    low = (rest - middle.astype(F32)).astype(BF16)
    return high, middle, low


def augment_query(q_ref, start, width):
    rows = jnp.concatenate([q_ref[g, :, start : start + width] for g in range(PER_KEY)], axis=1)
    scaled = rows.astype(F32) * (HEAD_SIZE**-0.5 * LOG2E)
    high = scaled.astype(BF16)
    low = (scaled - high.astype(F32)).astype(BF16)
    return rows, high, low


def block_of(refs, index, block):
    span = pl.ds(pl.multiple_of(index * block, block), block)
    return tuple(ref[0, :, span] for ref in refs)


def causal(width, columns):
    key_pos = lax.broadcasted_iota(jnp.int32, (width, columns), 0)
    query_pos = lax.broadcasted_iota(jnp.int32, (width, columns), 1) % width
    return key_pos <= query_pos


SAFE_BOUND = 48.0


def attn_forward_kernel(where_ref, q_ref, k_ref, v_ref, own_ref, o_ref, lse_ref, peak_ref, acc_ref):
    block = own_ref.shape[-1]
    columns = PER_KEY * block
    shard_pos = where_ref[0]
    branch = where_ref[1]
    ones = jnp.ones((16, block), BF16)
    pad = jnp.zeros((16 - 3, columns), BF16)
    whole = branch // block
    kv_ref = (k_ref, v_ref)

    def longest(key):
        squares = key.astype(F32)
        return jnp.max(jnp.sum(squares * squares, axis=0, keepdims=True), axis=1, keepdims=True)

    longest_key = jnp.sqrt(jnp.maximum(longest(k_ref[0]), longest(own_ref[0, 0])))

    def emit(start, result, lse):
        for g in range(PER_KEY):
            o_ref[g, :, start : start + block] = result[:, g * block : (g + 1) * block].astype(BF16)
            lse_ref[0, g : g + 1, start : start + block] = lse[:, g * block : (g + 1) * block]

    def sweep(advance, start):
        def body(index, carry):
            advance(*block_of(kv_ref, index, block), None)
            return carry

        if start == 0:
            lax.fori_loop(0, shard_pos, body, 0)
            advance(*block_of(kv_ref, shard_pos, block), causal(block, columns))
        else:
            lax.fori_loop(0, whole, body, 0)

            @pl.when(branch % block != 0)
            def _():
                key_pos = lax.broadcasted_iota(jnp.int32, (block, columns), 0)
                advance(*block_of(kv_ref, whole, block), key_pos < branch % block)

            advance(own_ref[0, 0], own_ref[1, 0], causal(block, columns))

    def bounded(start, high, low, bound):
        query = jnp.concatenate([high, low, *split_three(-bound), pad], axis=0)

        def advance(key, value, mask):
            scores = dot(jnp.concatenate([key, key, ones], axis=0), query, (0, 0))
            if mask is not None:
                scores = jnp.where(mask, scores, NEGATIVE)
            probs = jnp.exp2(scores).astype(BF16)
            acc_ref[...] += dot(jnp.concatenate([value, ones], axis=0), probs, (1, 0))

        acc_ref[...] = jnp.zeros_like(acc_ref)
        sweep(advance, start)
        total = acc_ref[HEAD_SIZE : HEAD_SIZE + 1]
        emit(start, acc_ref[:HEAD_SIZE] / total, bound + jnp.log2(total))

    def running(start, high, low):
        query = jnp.concatenate([high, low], axis=0)

        def advance(key, value, mask):
            scores = dot(jnp.concatenate([key, key], axis=0), query, (0, 0))
            if mask is not None:
                scores = jnp.where(mask, scores, NEGATIVE)
            old = peak_ref[...]
            new = jnp.maximum(old, jnp.max(scores, axis=0, keepdims=True))
            probs = jnp.exp2(scores - new).astype(BF16)
            shrink = jnp.exp2(old - new)
            part = dot(jnp.concatenate([value, ones], axis=0), probs, (1, 0))
            peak_ref[...] = new
            acc_ref[...] = acc_ref[...] * shrink + part

        peak_ref[...] = jnp.full_like(peak_ref, NEGATIVE)
        acc_ref[...] = jnp.zeros_like(acc_ref)
        sweep(advance, start)
        total = acc_ref[HEAD_SIZE : HEAD_SIZE + 1]
        emit(start, acc_ref[:HEAD_SIZE] / total, peak_ref[...] + jnp.log2(total))

    for start in (0, block):
        rows, high, low = augment_query(q_ref, start, block)
        wide = rows.astype(F32)
        length = jnp.sqrt(jnp.sum(wide * wide, axis=0, keepdims=True))
        bound = length * longest_key * (1.02 * HEAD_SIZE**-0.5 * LOG2E)
        safe = jnp.max(bound) < SAFE_BOUND

        @pl.when(safe)
        def _(start=start, high=high, low=low, bound=bound):
            bounded(start, high, low, bound)

        @pl.when(jnp.logical_not(safe))
        def _(start=start, high=high, low=low):
            running(start, high, low)


def attn_forward(where, query, prompt_kv, own_kv):
    tokens = query.shape[-1]
    block = own_kv.shape[-1]
    columns = PER_KEY * block
    keys = prompt_kv[0].shape[-1]
    return pl.pallas_call(
        attn_forward_kernel,
        grid=(query.shape[0] // PER_KEY,),
        in_specs=[
            pl.BlockSpec(memory_space=pltpu.SMEM),
            pl.BlockSpec((PER_KEY, HEAD_SIZE, tokens), lambda h: (h, 0, 0)),
            pl.BlockSpec((1, HEAD_SIZE, keys), lambda h: (h, 0, 0)),
            pl.BlockSpec((1, HEAD_SIZE, keys), lambda h: (h, 0, 0)),
            pl.BlockSpec((2, 1, HEAD_SIZE, block), lambda h: (0, h, 0, 0)),
        ],
        out_specs=[
            pl.BlockSpec((PER_KEY, HEAD_SIZE, tokens), lambda h: (h, 0, 0)),
            pl.BlockSpec((1, PER_KEY, tokens), lambda h: (h, 0, 0)),
        ],
        out_shape=[
            jax.ShapeDtypeStruct(query.shape, BF16),
            jax.ShapeDtypeStruct((query.shape[0] // PER_KEY, PER_KEY, tokens), F32),
        ],
        scratch_shapes=[
            pltpu.VMEM((1, columns), F32),
            pltpu.VMEM((HEAD_SIZE + 16, columns), F32),
        ],
        compiler_params=pltpu.CompilerParams(vmem_limit_bytes=48 * MIB),
        cost_estimate=pl.CostEstimate(
            flops=4 * tokens * keys * query.shape[0] * HEAD_SIZE,
            bytes_accessed=16 * MIB,
            transcendentals=query.shape[0] * tokens * keys,
        ),
        name="attn_forward",
    )(where, query, *prompt_kv, own_kv)


def attn_backward_kernel(
    where_ref, q_ref, k_ref, v_ref, own_ref, go_ref, o_ref, lse_ref, turn_ref, own_turn_ref, dq_ref, dkv_ref, down_ref, dkv_acc, dq_acc
):
    block = own_ref.shape[-1]
    columns = PER_KEY * block
    shard_pos = where_ref[0]
    branch = where_ref[1]
    ones = jnp.ones((16, block), BF16)
    pad = jnp.zeros((16 - 3, columns), BF16)
    kv_ref = (k_ref, v_ref)

    def turn_back(values, ref, span):
        half = HEAD_SIZE // 2
        cosine, sine = ref[0, :, span], ref[1, :, span]
        front, back = values[:half], values[half:]
        return jnp.concatenate([front * cosine + back * sine, back * cosine - front * sine], axis=0).astype(BF16)

    def begin(start):
        rows, high, low = augment_query(q_ref, start, block)

        def lanes(ref):
            return jnp.concatenate([ref[0, g : g + 1, start : start + block] for g in range(PER_KEY)], axis=1)

        lse = split_three(-lanes(lse_ref))
        grad, out = (
            jnp.concatenate([ref[g, :, start : start + block] for g in range(PER_KEY)], axis=1)
            for ref in (go_ref, o_ref)
        )
        delta = split_three(-jnp.sum(grad.astype(F32) * out.astype(F32), axis=0, keepdims=True))
        query = jnp.concatenate([high, low, *lse, pad], axis=0)
        grad_plus = jnp.concatenate([grad, *delta, pad], axis=0)
        dq_acc[...] = jnp.zeros_like(dq_acc)
        scaled = (rows.astype(F32) * HEAD_SIZE**-0.5).astype(BF16)
        return query, scaled, grad_plus, grad

    def terms(state, key, value, mask):
        query, scaled, grad_plus, grad = state
        scores = dot(jnp.concatenate([key, key, ones], axis=0), query, (0, 0))
        if mask is not None:
            scores = jnp.where(mask, scores, NEGATIVE)
        probs = jnp.exp2(scores)
        dv = dot(grad, probs.astype(BF16), (1, 1))
        grad_probs = dot(jnp.concatenate([value, ones], axis=0), grad_plus, (0, 0))
        grad_scores = (probs * grad_probs).astype(BF16)
        dq_acc[...] += dot(key, grad_scores, (1, 0))
        return dot(scaled, grad_scores, (1, 1)), dv

    def add(index, state, mask):
        dk, dv = terms(state, *block_of(kv_ref, index, block), mask)
        span = pl.ds(pl.multiple_of(index * block, block), block)
        dkv_acc[0, :, span] += dk
        dkv_acc[1, :, span] += dv

    def finish(start):
        total = dq_acc[...] * HEAD_SIZE**-0.5
        for g in range(PER_KEY):
            span = slice(start, start + block)
            dq_ref[g, :, span] = turn_back(total[:, g * block : (g + 1) * block], own_turn_ref, span)

    def run(state, count):
        def body(index, carry):
            add(2 * index, state, None)
            add(2 * index + 1, state, None)
            return carry

        lax.fori_loop(0, count // 2, body, 0)

        @pl.when(count % 2 == 1)
        def _():
            add(count - 1, state, None)

    dkv_acc[...] = jnp.zeros_like(dkv_acc)
    state = begin(0)
    run(state, shard_pos)
    add(shard_pos, state, causal(block, columns))
    finish(0)

    state = begin(block)
    whole = branch // block
    run(state, whole)

    @pl.when(branch % block != 0)
    def _():
        key_pos = lax.broadcasted_iota(jnp.int32, (block, columns), 0)
        add(whole, state, key_pos < branch % block)

    dk, dv = terms(state, own_ref[0, 0], own_ref[1, 0], causal(block, columns))
    down_ref[0, 0] = turn_back(dk, own_turn_ref, slice(block, 2 * block))
    down_ref[1, 0] = dv.astype(BF16)
    finish(block)
    dkv_ref[0, 0] = turn_back(dkv_acc[0], turn_ref, slice(None))
    dkv_ref[1, 0] = dkv_acc[1].astype(BF16)


def attn_backward(where, query, prompt_kv, own_kv, grad_out, out, lse, turn, own_turn):
    tokens = query.shape[-1]
    block = own_kv.shape[-1]
    columns = PER_KEY * block
    keys = prompt_kv[0].shape[-1]
    by_head = pl.BlockSpec((PER_KEY, HEAD_SIZE, tokens), lambda h: (h, 0, 0))
    by_keys = pl.BlockSpec((2, 1, HEAD_SIZE, keys), lambda h: (0, h, 0, 0))
    by_key = pl.BlockSpec((1, HEAD_SIZE, keys), lambda h: (h, 0, 0))
    by_own = pl.BlockSpec((2, 1, HEAD_SIZE, block), lambda h: (0, h, 0, 0))
    by_row = pl.BlockSpec((1, PER_KEY, tokens), lambda h: (h, 0, 0))
    return pl.pallas_call(
        attn_backward_kernel,
        grid=(query.shape[0] // PER_KEY,),
        in_specs=[pl.BlockSpec(memory_space=pltpu.SMEM), by_head, by_key, by_key, by_own, by_head, by_head, by_row]
        + [pl.BlockSpec(part.shape, lambda h: (0, 0, 0)) for part in (turn, own_turn)],
        out_specs=[by_head, by_keys, by_own],
        out_shape=[
            jax.ShapeDtypeStruct(query.shape, BF16),
            jax.ShapeDtypeStruct((2, *prompt_kv[0].shape), BF16),
            jax.ShapeDtypeStruct(own_kv.shape, BF16),
        ],
        scratch_shapes=[
            pltpu.VMEM((2, HEAD_SIZE, keys), F32),
            pltpu.VMEM((HEAD_SIZE, columns), F32),
        ],
        compiler_params=pltpu.CompilerParams(vmem_limit_bytes=56 * MIB),
        cost_estimate=pl.CostEstimate(
            flops=10 * tokens * keys * query.shape[0] * HEAD_SIZE,
            bytes_accessed=32 * MIB,
            transcendentals=query.shape[0] * tokens * keys,
        ),
        name="attn_backward",
    )(where, query, *prompt_kv, own_kv, grad_out, out, lse, turn, own_turn)


MESH = pl.DeviceIdType.MESH
LINE = 4
TOKEN_PARTS = 4


def start_kernel(
    x_ref,
    w_ref,
    top_ref,
    tok_all,
    w_all,
    top_all,
    own_sem,
    line_recv,
    right_send,
    left_send,
    y_send,
    y_recv,
    x_send,
    x_recv,
    core_send,
    core_recv,
    top_send,
    top_recv,
):
    part = tok_all.shape[1] // TOKEN_PARTS
    quarter = w_all.shape[2]
    half = top_ref.shape[0] // 2
    me = lax.axis_index("shard")
    place, column = me // 2, lax.rem(me, 2)
    rep = lax.axis_index("rep")
    far, core = lax.rem(rep + 2, 4), rep + 1 - 2 * lax.rem(rep, 2)
    to_right, to_left, to_y = {"shard": me + 2}, {"shard": me - 2}, {"shard": me + 1 - 2 * column}
    to_far, to_core = {"rep": far}, {"rep": core}
    weights, mirrored = 0, TOKEN_PARTS + 1
    last = TOKEN_PARTS
    streams = TOKEN_PARTS + 2

    def piece(i, origin, side):
        if i == weights:
            return w_all.at[2 * origin + side, rep]
        k = (i if i != mirrored else last) - 1
        return tok_all.at[2 * origin + side, pl.ds(k * part, part)]

    def side_of(i):
        return 1 - column if i == mirrored else column

    def own(i):
        if i == weights:
            return w_ref.at[pl.ds(pl.multiple_of(rep * quarter, quarter), quarter)]
        if i == mirrored:
            return piece(i, place, 1 - column)
        return x_ref.at[pl.ds((i - 1) * part, part)]

    def remote(source, target, send, receive, device):
        return pltpu.make_async_remote_copy(
            src_ref=source, dst_ref=target, send_sem=send, recv_sem=receive, device_id=device, device_id_type=MESH
        )

    def source(i, origin, at_home):
        return own(i) if at_home else piece(i, origin, side_of(i))

    def right(i, origin, at_home=False):
        return remote(
            source(i, origin, at_home),
            piece(i, origin, side_of(i)),
            right_send.at[i, origin],
            line_recv.at[i, origin],
            to_right,
        )

    def left(i, origin, at_home=False):
        return remote(
            source(i, origin, at_home),
            piece(i, origin, side_of(i)),
            left_send.at[i, origin],
            line_recv.at[i, origin],
            to_left,
        )

    def abreast(i, origin, at_home=False):
        return remote(
            source(i, origin, at_home), piece(i, origin, column), y_send.at[i, origin], y_recv.at[i, origin], to_y
        )

    def over_x(origin, side, at_home=False):
        target = piece(weights, origin, side)
        source_ref = own(weights) if at_home else target
        return remote(source_ref, target, x_send.at[origin, side], x_recv.at[origin, side], to_far)

    def over_core(group, origin, side, at_home=False):
        target = w_all.at[2 * origin + side, rep if group == 0 else far]
        source_ref = own(weights) if at_home else target
        return remote(
            source_ref, target, core_send.at[group, origin, side], core_recv.at[group, origin, side], to_core
        )

    def top_far(h):
        return remote(
            top_ref.at[pl.ds(h * half, half)],
            top_all.at[2, pl.ds(h * half, half)],
            top_send.at[0, h],
            top_recv.at[0, h],
            to_far,
        )

    def top_core(h):
        return remote(
            top_ref.at[pl.ds(h * half, half)],
            top_all.at[1, pl.ds(h * half, half)],
            top_send.at[1, h],
            top_recv.at[1, h],
            to_core,
        )

    def top_diagonal(h):
        return remote(
            top_all.at[2, pl.ds(h * half, half)],
            top_all.at[3, pl.ds(h * half, half)],
            top_send.at[2, h],
            top_recv.at[2, h],
            to_core,
        )

    has_right, has_left = place < LINE - 1, place > 0
    barrier = pltpu.get_barrier_semaphore()

    def greet(device):
        pl.semaphore_signal(barrier, inc=1, device_id=device, device_id_type=MESH)

    for device in (to_y, to_far, to_core):
        greet(device)

    @pl.when(has_right)
    def _():
        greet(to_right)

    @pl.when(has_left)
    def _():
        greet(to_left)

    pl.semaphore_wait(barrier, 3 + has_right.astype(jnp.int32) + has_left.astype(jnp.int32))

    def along(i, origin, at_home=False):
        @pl.when(has_right)
        def _():
            right(i, origin, at_home).start()

        @pl.when(has_left)
        def _():
            left(i, origin, at_home).start()

    order = [weights, last] + list(range(1, last))
    for i in order:
        along(i, place, True)
        abreast(i, place, True).start()
        if i == weights:
            over_x(place, column, True).start()
            over_core(0, place, column, True).start()
            for h in (0, 1):
                top_far(h).start()
    for h in (0, 1):
        top_core(h).start()
    own_copies = [
        pltpu.make_async_copy(own(i), piece(i, place, column), own_sem.at[i]) for i in range(streams - 1)
    ]
    own_copies.append(pltpu.make_async_copy(top_ref, top_all.at[0], own_sem.at[streams - 1]))
    for copy in own_copies:
        copy.start()
    abreast(last, place).wait_recv()
    along(mirrored, place, True)

    def weights_across(origin):
        abreast(weights, origin).wait_recv()
        over_x(origin, 1 - column).start()
        over_core(0, origin, 1 - column).start()

    weights_across(place)
    for d in range(1, LINE):
        before, after = place - d, place + d
        from_left, from_right = before >= 0, after < LINE
        for i in [weights, last, mirrored] + list(range(1, last)):

            @pl.when(from_left)
            def _(i=i):
                right(i, before).wait_recv()

                @pl.when(has_right)
                def _():
                    right(i, before).start()

                if i != last and i != mirrored:
                    abreast(i, before).start()
                if i == weights:
                    over_x(before, column).start()
                    over_core(0, before, column).start()

            @pl.when(from_right)
            def _(i=i):
                left(i, after).wait_recv()

                @pl.when(has_left)
                def _():
                    left(i, after).start()

                if i != last and i != mirrored:
                    abreast(i, after).start()
                if i == weights:
                    over_x(after, column).start()
                    over_core(0, after, column).start()

        @pl.when(from_left)
        def _():
            weights_across(before)

        @pl.when(from_right)
        def _():
            weights_across(after)

        if d >= 2:
            h = d - 2
            top_far(h).wait_recv()
            top_diagonal(h).start()

    for origin in range(LINE):
        for side in (0, 1):
            remote(
                w_all.at[2 * origin + side, far],
                w_all.at[2 * origin + side, far],
                x_send.at[origin, side],
                x_recv.at[origin, side],
                to_far,
            ).wait_recv()
            over_core(1, origin, side).start()

    for origin in range(LINE):
        for i in range(1, last):
            abreast(i, origin).wait_recv()
        for side in (0, 1):
            for group in (0, 1):
                over_core(group, origin, side).wait_recv()
    for h in (0, 1):
        top_core(h).wait_recv()
        top_diagonal(h).wait_recv()
        for copy in (top_far(h), top_core(h), top_diagonal(h)):
            copy.wait_send()
    for copy in own_copies:
        copy.wait()
    for origin in range(LINE):
        for i in range(streams):

            @pl.when(has_right & (origin <= place))
            def _(i=i, origin=origin):
                right(i, origin).wait_send()

            @pl.when(has_left & (origin >= place))
            def _(i=i, origin=origin):
                left(i, origin).wait_send()

            if i != last and i != mirrored:
                abreast(i, origin).wait_send()
        for side in (0, 1):
            over_x(origin, side).wait_send()
            for group in (0, 1):
                over_core(group, origin, side).wait_send()
    abreast(last, place).wait_send()


def start_gather(x, small, top):
    rows, width = x.shape
    prompt = rows - CONTINUATION_LEN
    own_rows, columns = small.shape
    dma = pltpu.SemaphoreType.DMA
    streams = TOKEN_PARTS + 2
    anywhere = pl.BlockSpec(memory_space=pl.ANY)
    return pl.pallas_call(
        start_kernel,
        in_specs=[anywhere] * 3,
        out_specs=[anywhere] * 3,
        out_shape=[
            jax.ShapeDtypeStruct((2 * LINE, prompt, width), BF16),
            jax.ShapeDtypeStruct((2 * LINE, 4, own_rows // 4, columns), BF16),
            jax.ShapeDtypeStruct((4, rows, width), BF16),
        ],
        scratch_shapes=[
            dma((streams,)),
            dma((streams, LINE)),
            dma((streams, LINE)),
            dma((streams, LINE)),
            dma((streams, LINE)),
            dma((streams, LINE)),
            dma((LINE, 2)),
            dma((LINE, 2)),
            dma((2, LINE, 2)),
            dma((2, LINE, 2)),
            dma((3, 2)),
            dma((3, 2)),
        ],
        compiler_params=pltpu.CompilerParams(collective_id=2, has_side_effects=True),
        cost_estimate=pl.CostEstimate(flops=0, bytes_accessed=64 * MIB, transcendentals=0),
        name="start_gather",
    )(x, small, top)


ORDER = ((0, 0), (0, 1), (1, 0), (3, 0), (2, 0), (3, 1), (2, 1), (1, 1))


def experts_kernel(
    x_hbm,
    top_hbm,
    gates_ref,
    w_ref,
    all_x,
    dx_own,
    dx_core,
    dx_far,
    y_keep,
    y_give,
    xt_all,
    tt_all,
    dgu_all,
    gh_all,
    dg_all,
    x_buf,
    top_buf,
    y_buf,
    dx_buf,
    xt_buf,
    tt_buf,
    dgu_buf,
    gh_buf,
    relay,
    y_acc,
    dx_acc,
    gates_all,
    gates_now,
    dg_now,
    dg_mine,
    in_sem,
    out_sem,
    copy_sem,
    send_sem,
    recv_sem,
    small_send,
    small_recv,
):
    tile = x_buf.shape[1]
    count = w_ref.shape[1] // (3 * F)
    step = pl.program_id(0)
    steps = len(ORDER)
    slot = lax.rem(step, 2)
    me = lax.axis_index("rep")
    home = [me, me + 1 - 2 * lax.rem(me, 2), lax.rem(me + 2, 4), 3 - me]

    def remote(source, target, send, receive, relation):
        return pltpu.make_async_remote_copy(
            src_ref=source,
            dst_ref=target,
            send_sem=send,
            recv_sem=receive,
            device_id={"rep": home[relation]},
            device_id_type=MESH,
        )

    def half(ref, half_index, *lead):
        return ref.at[(*lead, pl.ds(half_index * tile, tile))]

    def to_core(h):
        return remote(half(x_hbm, h), half(all_x, h, me), send_sem.at[0, h], recv_sem.at[0, h], 1)

    def to_far(h):
        return remote(half(x_hbm, h), half(all_x, h, me), send_sem.at[1, h], recv_sem.at[1, h], 2)

    def forward(h):
        part = half(all_x, h, home[2])
        return remote(part, part, send_sem.at[2, h], recv_sem.at[2, h], 1)

    def give(kind, h, buffer):
        if kind == 3:
            return remote(buffer, relay.at[h], send_sem.at[3, h], recv_sem.at[3, h], 1)
        if kind == 2:
            return remote(buffer, half(dx_far, h), send_sem.at[4, h], recv_sem.at[4, h], 2)
        return remote(buffer, half(dx_core, h), send_sem.at[5, h], recv_sem.at[5, h], 1)

    def small_gates(k):
        return remote(gates_ref.at[home[k]], gates_all.at[me], small_send.at[0, k], small_recv.at[0, k], k)

    def small_back(k):
        return remote(dg_mine.at[home[k]], dg_all.at[me], small_send.at[1, k], small_recv.at[1, k], k)

    def load_x(i):
        kind, h = ORDER[i]
        source = half(x_hbm, h) if kind == 0 else half(all_x, h, home[kind])
        return pltpu.make_async_copy(source, x_buf.at[i % 2], in_sem.at[i % 2, 0])

    def load_top(i):
        kind, h = ORDER[i]
        return pltpu.make_async_copy(half(top_hbm, h, kind), top_buf.at[i % 2], in_sem.at[i % 2, 1])

    def stores(i):
        kind, h = ORDER[i]
        out = []
        rows = 2 * tile

        def turned(ref, place):
            here = pl.multiple_of(place * rows + h * tile, LANES)
            return ref.at[:, pl.ds(here, tile)]

        targets = (
            (y_buf, half((y_keep, y_give, y_keep, y_give)[kind], h, (0, 0, 1, 1)[kind])),
            (dgu_buf, half(dgu_all, h, home[kind])),
            (gh_buf, half(gh_all, h, kind)),
            (xt_buf, turned(xt_all, home[kind])),
            (tt_buf, turned(tt_all, kind)),
        )
        for n, (buffer, target) in enumerate(targets):
            out.append(pltpu.make_async_copy(buffer.at[i % 2], target, out_sem.at[i % 2, n]))
        return out

    def store_dx(i):
        kind, h = ORDER[i]
        if kind == 0:
            return pltpu.make_async_copy(dx_buf.at[i % 2], half(dx_own, h), out_sem.at[i % 2, 5])
        return give(kind, h, dx_buf.at[i % 2])

    def finish(i):
        for copy in stores(i):
            copy.wait()
        if ORDER[i][0] == 0:
            store_dx(i).wait()
        else:
            store_dx(i).wait_send()

    own_copy = pltpu.make_async_copy(x_hbm, all_x.at[me], copy_sem)
    for i in range(steps):
        kind, h = ORDER[i]

        @pl.when(step == i)
        def _(i=i, kind=kind, h=h):
            if i == 0:
                barrier = pltpu.get_barrier_semaphore()
                for k in (1, 2, 3):
                    pl.semaphore_signal(
                        barrier, inc=1, device_id={"rep": home[k]}, device_id_type=MESH
                    )
                pl.semaphore_wait(barrier, 3)
                to_far(0).start()
                for n in (0, 1):
                    to_core(n).start()
                for k in (1, 2, 3):
                    small_gates(k).start()
                own_copy.start()
                load_top(0).start()
                load_x(0).start()
                gates_all[me] = gates_ref[me]
            if i == 1:
                to_far(1).start()
                for n in (0, 1):
                    to_core(n).wait_recv()
            if i == 2:
                for k in (1, 2, 3):
                    small_gates(k).wait_recv()
                to_far(0).wait_recv()
                forward(0).start()
            if i == 3:
                to_far(1).wait_recv()
                forward(1).start()
            if i == 4:
                forward(1).wait_recv()
            load_x(i).wait()
            load_top(i).wait()
            if i + 1 < steps:
                load_top(i + 1).start()
                if i + 1 != 3:
                    load_x(i + 1).start()
            if i >= 2:
                finish(i - 2)
            gates_now[...] = jnp.transpose(gates_all[home[kind]][:, h * tile : (h + 1) * tile])

    x = x_buf[slot]
    top = top_buf[slot]
    xt_buf[slot] = x.T
    tt_buf[slot] = top.T
    columns = []
    for e in range(count):
        w_in = w_ref[:, e * 2 * F : (e + 1) * 2 * F]
        w_out = w_ref[:, (count * 2 + e) * F : (count * 2 + e + 1) * F]
        gate_up = dot(x, w_in, (1, 0))
        g = gate_up[:, :F]
        u = gate_up[:, F:]
        sig = jax.nn.sigmoid(g)
        act = g * sig
        hidden = (act * u).astype(BF16).astype(F32)
        raw = dot(top, w_out, (1, 0))
        columns.append(jnp.sum(hidden * raw, axis=1, keepdims=True))
        gate = gates_now[:, e : e + 1]
        gated = (hidden * gate).astype(BF16)
        gh_buf[slot, :, e * F : (e + 1) * F] = gated
        grad_hidden = raw * gate
        dg = (grad_hidden * u * sig * (1.0 + g * (1.0 - sig))).astype(BF16)
        du = (grad_hidden * act).astype(BF16)
        dgu = jnp.concatenate([dg, du], axis=1)
        dgu_buf[slot, :, e * 2 * F : (e + 1) * 2 * F] = dgu
        y = dot(gated, w_out, (1, 1))
        dx = dot(dgu, w_in, (1, 1))
        if e == 0:
            y_acc[...] = y
            dx_acc[...] = dx
        elif e < count - 1:
            y_acc[...] += y
            dx_acc[...] += dx
        else:
            y_buf[slot] = (y_acc[...] + y).astype(BF16)
            dx_acc[...] += dx
    columns.append(jnp.zeros((tile, 8 - count), F32))
    dg_now[...] = jnp.transpose(jnp.concatenate(columns, axis=1))

    for i in range(steps):
        kind, h = ORDER[i]

        @pl.when(step == i)
        def _(i=i, kind=kind, h=h):
            dg_mine[home[kind], :, h * tile : (h + 1) * tile] = dg_now[...]
            if kind == 2:
                give(3, h, dx_buf.at[0]).wait_recv()
                dx_buf[i % 2] = (dx_acc[...] + relay[h].astype(F32)).astype(BF16)
            else:
                dx_buf[i % 2] = dx_acc[...].astype(BF16)
            store_dx(i).start()
            for copy in stores(i):
                copy.start()
            if i == 2:
                forward(0).wait_recv()
                load_x(3).start()
            if i == steps - 1:
                own_back = pltpu.make_async_copy(dg_mine.at[me], dg_all.at[me], small_send.at[1, 0])
                own_back.start()
                for k in (1, 2, 3):
                    small_back(k).start()
                finish(i - 1)
                finish(i)
                own_copy.wait()
                own_back.wait()
                for n in (0, 1):
                    to_far(n).wait_send()
                    to_core(n).wait_send()
                    forward(n).wait_send()
                    give(2, n, dx_buf.at[0]).wait_recv()
                    give(1, n, dx_buf.at[0]).wait_recv()
                for k in (1, 2, 3):
                    small_gates(k).wait_send()
                    small_back(k).wait()


def experts(x, all_top, gates, weights):
    rows, width = x.shape
    reps = all_top.shape[0]
    count = weights.shape[1] // (3 * F)
    tile = rows // 2
    anywhere = pl.BlockSpec(memory_space=pl.ANY)
    fixed = pl.BlockSpec(weights.shape, lambda i: (0, 0), pipeline_mode=pl.Buffered(1))
    small = pl.BlockSpec((reps, 8, rows), lambda i: (0, 0, 0))
    dma = pltpu.SemaphoreType.DMA
    return pl.pallas_call(
        experts_kernel,
        grid=(len(ORDER),),
        in_specs=[anywhere, anywhere, small, fixed],
        out_specs=[anywhere] * 11,
        out_shape=[
            jax.ShapeDtypeStruct((reps, rows, width), BF16),
            jax.ShapeDtypeStruct((rows, width), BF16),
            jax.ShapeDtypeStruct((rows, width), BF16),
            jax.ShapeDtypeStruct((rows, width), BF16),
            jax.ShapeDtypeStruct((2, rows, width), BF16),
            jax.ShapeDtypeStruct((2, rows, width), BF16),
            jax.ShapeDtypeStruct((width, reps * rows), BF16),
            jax.ShapeDtypeStruct((width, reps * rows), BF16),
            jax.ShapeDtypeStruct((reps, rows, count * 2 * F), BF16),
            jax.ShapeDtypeStruct((reps, rows, count * F), BF16),
            jax.ShapeDtypeStruct((reps, 8, rows), F32),
        ],
        scratch_shapes=[
            pltpu.VMEM((2, tile, width), BF16),
            pltpu.VMEM((2, tile, width), BF16),
            pltpu.VMEM((2, tile, width), BF16),
            pltpu.VMEM((2, tile, width), BF16),
            pltpu.VMEM((2, width, tile), BF16),
            pltpu.VMEM((2, width, tile), BF16),
            pltpu.VMEM((2, tile, count * 2 * F), BF16),
            pltpu.VMEM((2, tile, count * F), BF16),
            pltpu.VMEM((2, tile, width), BF16),
            pltpu.VMEM((tile, width), F32),
            pltpu.VMEM((tile, width), F32),
            pltpu.VMEM((reps, 8, rows), F32),
            pltpu.VMEM((tile, 8), F32),
            pltpu.VMEM((8, tile), F32),
            pltpu.VMEM((reps, 8, rows), F32),
            dma((2, 2)),
            dma((2, 6)),
            dma,
            dma((6, 2)),
            dma((6, 2)),
            dma((2, 4)),
            dma((2, 4)),
        ],
        compiler_params=pltpu.CompilerParams(
            vmem_limit_bytes=58 * MIB, collective_id=1, has_side_effects=True
        ),
        cost_estimate=pl.CostEstimate(
            flops=12 * reps * rows * width * count * F,
            bytes_accessed=80 * MIB,
            transcendentals=reps * rows * count * F,
        ),
        name="experts",
    )(x, all_top, gates, weights)


def send_to(source, target, send, receive, device):
    return pltpu.make_async_remote_copy(
        src_ref=source, dst_ref=target, send_sem=send, recv_sem=receive, device_id=device, device_id_type=MESH
    )


def line_reduce(parts, y_buf, right_buf, left_buf, y_sems, right_sems, left_sems):
    me = lax.axis_index("shard")
    place, side = me // 2, lax.rem(me, 2)
    to_y, to_right, to_left = {"shard": me + 1 - 2 * side}, {"shard": me + 2}, {"shard": me - 2}

    def across(c):
        return send_to(parts.at[c, 1 - side], y_buf.at[c], y_sems.at[0, c], y_sems.at[1, c], to_y)

    def add_across(c):
        across(c).wait_recv()
        for p in range(LINE):
            parts[c, side, p] = (parts[c, side, p].astype(F32) + y_buf[c, p].astype(F32)).astype(BF16)

    def hop(c, p, buf, sems, device, first):
        source = parts.at[c, side, p] if first else buf.at[c, p]
        return send_to(source, buf.at[c, p], sems.at[0, c, p], sems.at[1, c, p], device)

    def run(c, p, buf, sems, device, is_first, passes):
        @pl.when(passes & is_first)
        def _():
            hop(c, p, buf, sems, device, True).start()

        @pl.when(passes & jnp.logical_not(is_first))
        def _():
            hop(c, p, buf, sems, device, False).wait_recv()
            buf[c, p] = (parts[c, side, p].astype(F32) + buf[c, p].astype(F32)).astype(BF16)
            hop(c, p, buf, sems, device, False).start()

    def step_right(c):
        for p in range(1, LINE):
            run(c, p, right_buf, right_sems, to_right, place == 0, place < p)

    def step_left(c):
        for p in range(LINE - 1):
            run(c, p, left_buf, left_sems, to_left, place == LINE - 1, place > p)

    def collect(c, total):
        total[...] = parts[c, side, place].astype(F32)

        @pl.when(place > 0)
        def _():
            hop(c, place, right_buf, right_sems, to_right, False).wait_recv()
            total[...] += right_buf[c, place].astype(F32)

        @pl.when(place < LINE - 1)
        def _():
            hop(c, place, left_buf, left_sems, to_left, False).wait_recv()
            total[...] += left_buf[c, place].astype(F32)

    def drain(c):
        across(c).wait_send()
        for p in range(1, LINE):

            @pl.when(place < p)
            def _(p=p):
                hop(c, p, right_buf, right_sems, to_right, False).wait_send()

        for p in range(LINE - 1):

            @pl.when(place > p)
            def _(p=p):
                hop(c, p, left_buf, left_sems, to_left, False).wait_send()

    def greet(extra):
        barrier = pltpu.get_barrier_semaphore()
        for device in [to_y] + extra:
            pl.semaphore_signal(barrier, inc=1, device_id=device, device_id_type=MESH)
        has_right, has_left = place < LINE - 1, place > 0

        @pl.when(has_right)
        def _():
            pl.semaphore_signal(barrier, inc=1, device_id=to_right, device_id_type=MESH)

        @pl.when(has_left)
        def _():
            pl.semaphore_signal(barrier, inc=1, device_id=to_left, device_id_type=MESH)

        count = 1 + len(extra) + has_right.astype(jnp.int32) + has_left.astype(jnp.int32)
        pl.semaphore_wait(barrier, count)

    return place, across, add_across, step_right, step_left, collect, drain, greet


def between(step, low, high, body):
    @pl.when((step >= low) & (step < high))
    def _():
        body()


def expert_grads_kernel(
    xt_ref,
    tt_ref,
    dgu_ref,
    gh_ref,
    out_ref,
    left_op,
    right_op,
    parts,
    y_buf,
    right_buf,
    left_buf,
    total,
    mine,
    load_sem,
    lhs_sem,
    y_sems,
    right_sems,
    left_sems,
    own_sem,
    far_sems,
    near_sems,
    pass_sems,
):
    n = parts.shape[0]
    columns = right_op.shape[2]
    first = dgu_ref.shape[1] // columns
    rows = parts.shape[3]
    rep = lax.axis_index("rep")
    far = lax.rem(rep + 2, 4)
    to_core, to_far = {"rep": rep + 1 - 2 * lax.rem(rep, 2)}, {"rep": far}
    place, across, add_across, step_right, step_left, collect, drain, greet = line_reduce(
        parts, y_buf, right_buf, left_buf, y_sems, right_sems, left_sems
    )

    def load(c, act):
        slot = lax.rem(c, 2)

        @pl.when(c < first)
        def _():
            here = pl.ds(pl.multiple_of(c * columns, columns), columns)
            act(pltpu.make_async_copy(dgu_ref.at[:, here], right_op.at[slot], load_sem.at[slot]))

        @pl.when(c >= first)
        def _():
            here = pl.ds(pl.multiple_of((c - first) * columns, columns), columns)
            act(pltpu.make_async_copy(gh_ref.at[:, here], right_op.at[slot], load_sem.at[slot]))

    def start(copy):
        copy.start()

    def wait(copy):
        copy.wait()

    def place_of(owner, c):
        return out_ref.at[owner, :, pl.ds(pl.multiple_of(c * columns, columns), columns)]

    def over_x(c):
        return send_to(mine.at[c], place_of(rep, c), far_sems.at[0, c], far_sems.at[1, c], to_far)

    def over_core(c):
        return send_to(mine.at[c], place_of(rep, c), near_sems.at[0, c], near_sems.at[1, c], to_core)

    def keep(c):
        return pltpu.make_async_copy(mine.at[c], place_of(rep, c), own_sem.at[c])

    def pass_on(c):
        return send_to(place_of(far, c), place_of(far, c), pass_sems.at[0, c], pass_sems.at[1, c], to_core)

    lhs = pltpu.make_async_copy(xt_ref, left_op, lhs_sem)
    lhs.start()
    load(0, start)
    greet([to_core, to_far])
    lhs.wait()

    def produce(c):
        @pl.when(c == first)
        def _():
            swap = pltpu.make_async_copy(tt_ref, left_op, lhs_sem)
            swap.start()
            swap.wait()

        load(c, wait)

        @pl.when(c + 1 < n)
        def _():
            load(c + 1, start)

        result = dot(left_op[...], right_op[lax.rem(c, 2)], (1, 0)).astype(BF16)
        for t in range(2 * LINE):
            parts[c, t % 2, t // 2] = result[t * rows : (t + 1) * rows]
        across(c).start()

    def finish(c):
        collect(c, total)
        mine[c] = total[...].astype(BF16)
        over_x(c).start()
        over_core(c).start()
        keep(c).start()

    def forward(c):
        over_x(c).wait_recv()
        pass_on(c).start()

    def step(i, carry):
        between(i, 0, n, lambda: produce(i))
        between(i, 1, n + 1, lambda: add_across(i - 1))
        to_right_chunk, to_left_chunk = i - 1 - place, i - LINE + place
        between(to_right_chunk, 0, n, lambda: step_right(to_right_chunk))
        between(to_left_chunk, 0, n, lambda: step_left(to_left_chunk))
        between(i, 5, n + 5, lambda: finish(i - 5))
        between(i, 7, n + 7, lambda: forward(i - 7))
        return carry

    lax.fori_loop(0, n + 7, step, 0)

    def end(c, carry):
        drain(c)
        over_x(c).wait_send()
        over_core(c).wait()
        keep(c).wait()
        pass_on(c).wait()
        return carry

    lax.fori_loop(0, n, end, 0)


def expert_grads(x_t, top_t, dgu, gated, columns=256):
    width, tokens = x_t.shape
    wide = dgu.shape[1] + gated.shape[1]
    n = wide // columns
    rows = width // (2 * LINE)
    dma = pltpu.SemaphoreType.DMA
    anywhere = pl.BlockSpec(memory_space=pl.ANY)
    return pl.pallas_call(
        expert_grads_kernel,
        in_specs=[anywhere] * 4,
        out_specs=anywhere,
        out_shape=jax.ShapeDtypeStruct((4, rows, wide), BF16),
        scratch_shapes=[
            pltpu.VMEM((width, tokens), BF16),
            pltpu.VMEM((2, tokens, columns), BF16),
            pltpu.VMEM((n, 2, LINE, rows, columns), BF16),
            pltpu.VMEM((n, LINE, rows, columns), BF16),
            pltpu.VMEM((n, LINE, rows, columns), BF16),
            pltpu.VMEM((n, LINE, rows, columns), BF16),
            pltpu.VMEM((rows, columns), F32),
            pltpu.VMEM((n, rows, columns), BF16),
            dma((2,)),
            dma,
            dma((2, n)),
            dma((2, n, LINE)),
            dma((2, n, LINE)),
            dma((n,)),
            dma((2, n)),
            dma((2, n)),
            dma((2, n)),
        ],
        compiler_params=pltpu.CompilerParams(vmem_limit_bytes=60 * MIB, collective_id=4, has_side_effects=True),
        cost_estimate=pl.CostEstimate(
            flops=2 * width * tokens * wide, bytes_accessed=80 * MIB, transcendentals=0
        ),
        name="expert_grads",
    )(x_t, top_t, dgu, gated)


def late_reduce_kernel(
    in_ref,
    early_ref,
    out_ref,
    early_out,
    early_core,
    early_mid,
    early_far,
    early_sems,
    own_buf,
    core_buf,
    parts,
    y_buf,
    right_buf,
    left_buf,
    total,
    mine,
    far_buf,
    whole,
    load_sem,
    core_sems,
    y_sems,
    right_sems,
    left_sems,
    own_sem,
    far_sems,
    near_sems,
):
    n = parts.shape[0]
    rows, columns = parts.shape[3:]
    rep = lax.axis_index("rep")
    half = lax.rem(rep, 2)
    to_core, to_far = {"rep": rep + 1 - 2 * half}, {"rep": lax.rem(rep + 2, 4)}
    place, across, add_across, step_right, step_left, collect, drain, greet = line_reduce(
        parts, y_buf, right_buf, left_buf, y_sems, right_sems, left_sems
    )

    def span(which, c):
        return pl.ds(pl.multiple_of((which * n + c) * columns, columns), columns)

    def load(c):
        return pltpu.make_async_copy(in_ref.at[:, span(half, c)], own_buf.at[c], load_sem.at[c])

    def from_core(c):
        return send_to(
            in_ref.at[:, span(1 - half, c)], core_buf.at[c], core_sems.at[0, c], core_sems.at[1, c], to_core
        )

    def over_x(c):
        return send_to(mine.at[c], far_buf.at[c], far_sems.at[0, c], far_sems.at[1, c], to_far)

    def over_core(c):
        return send_to(
            whole.at[c], out_ref.at[:, span(half, c)], near_sems.at[0, c], near_sems.at[1, c], to_core
        )

    def keep(c):
        return pltpu.make_async_copy(whole.at[c], out_ref.at[:, span(half, c)], own_sem.at[c])

    for c in range(n):
        load(c).start()
    greet([to_core, to_far])
    early_near = send_to(early_ref, early_core, early_sems.at[0, 0], early_sems.at[1, 0], to_core)
    early_over = send_to(early_mid, early_far, early_sems.at[0, 1], early_sems.at[1, 1], to_far)
    early_near.start()
    for c in range(n):
        from_core(c).start()
    early_near.wait_recv()
    early_mid[...] = (early_ref[...].astype(F32) + early_core[...].astype(F32)).astype(BF16)
    early_over.start()

    def produce(c):
        load(c).wait()
        from_core(c).wait_recv()
        for t in range(2 * LINE):
            here = pl.ds(t * rows, rows)
            parts[c, t % 2, t // 2] = (own_buf[c, here].astype(F32) + core_buf[c, here].astype(F32)).astype(BF16)
        across(c).start()

    def finish(c):
        collect(c, total)
        mine[c] = total[...].astype(BF16)
        over_x(c).start()

    def complete(c):
        over_x(c).wait_recv()
        whole[c] = (mine[c].astype(F32) + far_buf[c].astype(F32)).astype(BF16)
        over_core(c).start()
        keep(c).start()

    def step(i, carry):
        between(i, 0, n, lambda: produce(i))
        between(i, 1, n + 1, lambda: add_across(i - 1))
        to_right_chunk, to_left_chunk = i - 1 - place, i - LINE + place
        between(to_right_chunk, 0, n, lambda: step_right(to_right_chunk))
        between(to_left_chunk, 0, n, lambda: step_left(to_left_chunk))
        between(i, LINE, n + LINE, lambda: finish(i - LINE))
        between(i, LINE + 1, n + LINE + 1, lambda: complete(i - LINE - 1))
        return carry

    lax.fori_loop(0, n + LINE + 1, step, 0)
    early_over.wait_recv()
    early_out[...] = (early_mid[...].astype(F32) + early_far[...].astype(F32)).astype(BF16)
    early_near.wait_send()
    early_over.wait_send()

    def end(c, carry):
        drain(c)
        from_core(c).wait_send()
        over_x(c).wait_send()
        over_core(c).wait_send()
        keep(c).wait()
        send_to(
            whole.at[c], out_ref.at[:, span(1 - half, c)], near_sems.at[0, c], near_sems.at[1, c], to_core
        ).wait_recv()
        return carry

    lax.fori_loop(0, n, end, 0)


def late_reduce(values, early, columns=256):
    width, wide = values.shape
    n = wide // 2 // columns
    rows = width // (2 * LINE)
    dma = pltpu.SemaphoreType.DMA
    anywhere = pl.BlockSpec(memory_space=pl.ANY)
    return pl.pallas_call(
        late_reduce_kernel,
        in_specs=[anywhere, pl.BlockSpec(memory_space=pltpu.VMEM)],
        out_specs=[anywhere, pl.BlockSpec(memory_space=pltpu.VMEM)],
        out_shape=[jax.ShapeDtypeStruct((rows, wide), BF16), jax.ShapeDtypeStruct(early.shape, BF16)],
        scratch_shapes=[
            pltpu.VMEM(early.shape, BF16),
            pltpu.VMEM(early.shape, BF16),
            pltpu.VMEM(early.shape, BF16),
            dma((2, 2)),
            pltpu.VMEM((n, width, columns), BF16),
            pltpu.VMEM((n, width, columns), BF16),
            pltpu.VMEM((n, 2, LINE, rows, columns), BF16),
            pltpu.VMEM((n, LINE, rows, columns), BF16),
            pltpu.VMEM((n, LINE, rows, columns), BF16),
            pltpu.VMEM((n, LINE, rows, columns), BF16),
            pltpu.VMEM((rows, columns), F32),
            pltpu.VMEM((n, rows, columns), BF16),
            pltpu.VMEM((n, rows, columns), BF16),
            pltpu.VMEM((n, rows, columns), BF16),
            dma((n,)),
            dma((2, n)),
            dma((2, n)),
            dma((2, n, LINE)),
            dma((2, n, LINE)),
            dma((n,)),
            dma((2, n)),
            dma((2, n)),
        ],
        compiler_params=pltpu.CompilerParams(vmem_limit_bytes=48 * MIB, collective_id=5, has_side_effects=True),
        cost_estimate=pl.CostEstimate(flops=0, bytes_accessed=4 * MIB, transcendentals=0),
        name="late_reduce",
    )(values, early)


def flatten_kernel(starts, lead_ref, *refs):
    parts, flat_ref, square_ref = refs[: len(starts)], refs[len(starts)], refs[len(starts) + 1]
    scratch, sems = refs[len(starts) + 2 : -1], refs[-1]
    step = pl.program_id(0)
    steps = pl.num_programs(0)
    slot = lax.rem(step, 2)
    flat = flat_ref.reshape(flat_ref.shape[1] // LANES, LANES)
    lead_places = ((0, 0, 1), (1, starts[2] - 17 , 1), (2, starts[2] - 16, 16))

    def copies(index, where):
        out = []
        for n, (start, buffer) in enumerate(zip(starts, scratch)):
            size = buffer.shape[1]
            out.append(pltpu.make_async_copy(buffer.at[where], flat.at[pl.ds(start + index * size, size)], sems.at[where, n]))
        return out

    @pl.when(step == 0)
    def _():
        square_ref[...] = jnp.sum(lead_ref[...] * lead_ref[...], keepdims=True).reshape(1, 1) + jnp.zeros_like(square_ref)
        for n, (source, target, size) in enumerate(lead_places):
            copy = pltpu.make_async_copy(lead_ref.at[pl.ds(source, size)], flat.at[pl.ds(target, size)], sems.at[2, n])
            copy.start()
            copy.wait()

    @pl.when(step >= 2)
    def _():
        for copy in copies(step - 2, slot):
            copy.wait()

    total = jnp.zeros((8, LANES), F32)
    for part, buffer in zip(parts, scratch):
        rows = part.shape[-2]
        wide = buffer.shape[1] // rows
        reps = part.shape[0] if len(part.shape) == 3 else 1
        each = wide // reps
        for r in range(reps):
            for c in range(each):
                lanes = slice(c * LANES, (c + 1) * LANES)
                value = (part[r, :, lanes] if len(part.shape) == 3 else part[:, lanes]).astype(F32)
                buffer[slot, pl.ds(r * each + c, rows, stride=wide), :] = value
                square = value * value
                for k in range(0, rows, 8):
                    total += square[k : k + 8]
    square_ref[...] += jnp.sum(total, keepdims=True).reshape(1, 1)
    for copy in copies(step, slot):
        copy.start()

    @pl.when(step == steps - 1)
    def _():
        for copy in copies(step - 1, 1 - slot):
            copy.wait()
        for copy in copies(step, slot):
            copy.wait()

def flatten(size, lead, parts, tile=16):
    rows = parts[0][0].shape[-2]
    widths = [columns * (p.shape[0] if p.ndim == 3 else 1) // LANES for p, columns, _ in parts]
    starts, at = [], 1
    for n, w in enumerate(widths):
        if n == 2: at += 1 + 16
        starts.append(at); at += rows * w
    specs = []
    for p, columns, place in parts:
        if p.ndim == 3:
            specs.append(pl.BlockSpec((p.shape[0], tile, columns), lambda i, place=place: (0, i, place)))
        else:
            specs.append(pl.BlockSpec((tile, columns), lambda i, place=place: (i, place)))
    return pl.pallas_call(
        functools.partial(flatten_kernel, starts),
        grid=(rows // tile,),
        in_specs=[pl.BlockSpec(lead.shape, lambda i: (0, 0))] + specs,
        out_specs=[pl.BlockSpec(memory_space=pl.ANY), pl.BlockSpec((1, 1), lambda i: (0, 0))],
        out_shape=[jax.ShapeDtypeStruct((1, size), F32), jax.ShapeDtypeStruct((1, 1), F32)],
        scratch_shapes=[pltpu.VMEM((2, tile * w, LANES), F32) for w in widths] + [pltpu.SemaphoreType.DMA((3, 4))],
        compiler_params=pltpu.CompilerParams(vmem_limit_bytes=48 * MIB),
        name="flatten",
    )(lead, *[p for p, _, _ in parts])

HALF_ROWS = 1056


def moments(grad, first, second, scale):
    clipped = grad * scale
    new_first = BETA_ONE * first + (1.0 - BETA_ONE) * clipped
    new_second = BETA_TWO * second + (1.0 - BETA_TWO) * clipped * clipped
    return new_first, new_second


def inner_step(new_first, new_second, weight):
    root = jnp.sqrt(new_second * (1.0 / (1.0 - BETA_TWO**STEP))) + ADAM_EPS
    return -INNER_RATE * (new_first * (1.0 / (1.0 - BETA_ONE**STEP)) / root + DECAY_RATE * weight)


def flat_chunks(rows):
    chunks, at, half_at = [], 0, 0
    while at < rows:
        size = min(2 * HALF_ROWS, rows - at)
        half = -(-size // 32) * 16
        chunks.append((at, size, half_at, half))
        at, half_at = at + size, half_at + half
    return chunks


def step_kernel(
    square_ref,
    g_ref,
    f_ref,
    s_ref,
    w_ref,
    norm_ref,
    total,
    g_buf,
    f_buf,
    s_buf,
    w_buf,
    step_buf,
    near_buf,
    far_buf,
    sum_buf,
    square_mine,
    square_all,
    in_sem,
    near_send,
    near_recv,
    far_send,
    far_recv,
    back_send,
    back_recv,
    own_sem,
    square_send,
    square_recv,
):
    rows = g_ref.shape[-1] // LANES
    chunks = flat_chunks(rows)
    count = len(chunks)
    shards = lax.axis_size("shard")
    shard, rep = lax.axis_index("shard"), lax.axis_index("rep")
    side = lax.rem(rep, 2)
    to_core, to_far = {"rep": rep + 1 - 2 * side}, {"rep": lax.rem(rep + 2, 4)}

    def other(k):
        return {"shard": lax.rem(shard + k, shards)}

    barrier = pltpu.get_barrier_semaphore()
    greeted = [to_core, to_far] + [other(k) for k in range(1, shards)]
    for device in greeted:
        pl.semaphore_signal(barrier, inc=1, device_id=device, device_id_type=MESH)

    def loads(i):
        at, size, _, _ = chunks[i]
        pairs = (g_ref, g_buf), (f_ref.at[0], f_buf), (s_ref.at[0], s_buf), (w_ref, w_buf)
        return [
            pltpu.make_async_copy(
                ref.at[:, pl.ds(at * LANES, size * LANES)],
                buf.at[i % 2, :, pl.ds(0, size * LANES)],
                in_sem.at[i % 2, n],
            )
            for n, (ref, buf) in enumerate(pairs)
        ]

    def remote(source, target, send, receive, device):
        return pltpu.make_async_remote_copy(
            src_ref=source, dst_ref=target, send_sem=send, recv_sem=receive, device_id=device, device_id_type=MESH
        )

    def near(i):
        _, _, at, half = chunks[i]
        span = pl.ds(at, half)
        return remote(step_buf.at[1 - side, span], near_buf.at[span], near_send.at[i], near_recv.at[i], to_core)

    def far(i):
        _, _, at, half = chunks[i]
        span = pl.ds(at, half)
        return remote(step_buf.at[side, span], far_buf.at[span], far_send.at[i], far_recv.at[i], to_far)

    def back(i):
        _, _, at, half = chunks[i]
        span = pl.ds(at, half)
        return remote(sum_buf.at[span], total.at[side, span], back_send.at[i], back_recv.at[i], to_core)

    def keep(i):
        _, _, at, half = chunks[i]
        span = pl.ds(at, half)
        return pltpu.make_async_copy(sum_buf.at[span], total.at[side, span], own_sem.at[i])

    for copy in loads(0):
        copy.start()
    pl.semaphore_wait(barrier, len(greeted))

    def square_copy(k):
        return remote(square_mine, square_all.at[shard], square_send.at[k], square_recv.at[shard], other(k))

    square_mine[...] = jnp.broadcast_to(square_ref[...], square_mine.shape)
    square_all[shard] = square_mine[...]
    for k in range(1, shards):
        square_copy(k).start()
    for k in range(1, shards):
        source = lax.rem(shard + k, shards)
        remote(
            square_mine, square_all.at[source], square_send.at[k], square_recv.at[source], other(k)
        ).wait_recv()
    norm = jnp.sqrt(jnp.sum(square_all[...], axis=0))
    norm_ref[...] = norm[:1, :1]
    scale = (CLIP_NORM / jnp.maximum(norm, CLIP_NORM))[:1]

    def blocks(size):
        return 48 if size % 48 == 0 else 16

    def compute(i):
        _, _, at, half = chunks[i]
        block = blocks(half)
        for h in (0, 1):

            def body(j, carry):
                here = pl.multiple_of(j * block, 16)
                span = pl.ds(pl.multiple_of((h * half + here) * LANES, LANES), block * LANES)
                grad, first, second, weight = (
                    buf[i % 2, :, span].reshape(block, LANES) for buf in (g_buf, f_buf, s_buf, w_buf)
                )
                new_first, new_second = moments(grad, first, second, scale)
                step = inner_step(new_first, new_second, weight)
                step_buf[h, pl.ds(at + here, block)] = step.astype(BF16)
                return carry

            lax.fori_loop(0, half // block, body, 0)

    def add(i, left, right, target):
        _, _, at, half = chunks[i]
        block = blocks(half)

        def body(j, carry):
            span = pl.ds(pl.multiple_of(at + j * block, 16), block)
            target[span] = (left[span].astype(F32) + right[span].astype(F32)).astype(BF16)
            return carry

        lax.fori_loop(0, half // block, body, 0)

    for i in range(count + 2):
        if i < count:
            for copy in loads(i):
                copy.wait()
            if i + 1 < count:
                for copy in loads(i + 1):
                    copy.start()
            compute(i)
            near(i).start()
        if 1 <= i <= count:
            near(i - 1).wait_recv()
            add(i - 1, step_buf.at[side], near_buf, step_buf.at[side])
            far(i - 1).start()
        if i >= 2:
            far(i - 2).wait_recv()
            add(i - 2, step_buf.at[side], far_buf, sum_buf)
            back(i - 2).start()
            keep(i - 2).start()
    for k in range(1, shards):
        square_copy(k).wait_send()
    for i in range(count):
        near(i).wait_send()
        far(i).wait_send()
        back(i).wait_send()
        keep(i).wait()
        _, _, at, half = chunks[i]
        span = pl.ds(at, half)
        remote(
            sum_buf.at[span], total.at[1 - side, span], back_send.at[i], back_recv.at[i], to_core
        ).wait_recv()


def summed_step(square, grad, first, second, weight):
    rows = grad.shape[-1] // LANES
    chunks = flat_chunks(rows)
    count = len(chunks)
    halves = sum(chunk[3] for chunk in chunks)
    size = chunks[0][3] * 2
    shards = lax.axis_size("shard")
    dma = pltpu.SemaphoreType.DMA
    anywhere = pl.BlockSpec(memory_space=pl.ANY)
    return pl.pallas_call(
        step_kernel,
        in_specs=[pl.BlockSpec(memory_space=pltpu.VMEM)] + [anywhere] * 4,
        out_specs=[pl.BlockSpec(memory_space=pltpu.VMEM), anywhere],
        out_shape=[jax.ShapeDtypeStruct((1, 1), F32), jax.ShapeDtypeStruct((2, halves, LANES), BF16)],
        scratch_shapes=[pltpu.VMEM((2, 1, size * LANES), F32)] * 4
        + [
            pltpu.VMEM((2, halves, LANES), BF16),
            pltpu.VMEM((halves, LANES), BF16),
            pltpu.VMEM((halves, LANES), BF16),
            pltpu.VMEM((halves, LANES), BF16),
            pltpu.VMEM((8, LANES), F32),
            pltpu.VMEM((shards, 8, LANES), F32),
            dma((2, 4)),
        ]
        + [dma((count,))] * 7
        + [dma((shards,))] * 2,
        compiler_params=pltpu.CompilerParams(
            vmem_limit_bytes=48 * MIB, collective_id=3, has_side_effects=True
        ),
        cost_estimate=pl.CostEstimate(flops=0, bytes_accessed=4 * MIB, transcendentals=0),
        name="summed_step",
    )(square, grad, first, second, weight)


def update_kernel(
    reps, norm_ref, g, f, s, total, mom, nf, ns, nm, up, tg, tf, ts, tm, tt, tnf, tns, tnm, tup, sems
):
    rows = g.shape[-1] // LANES
    chunks = flat_chunks(rows)
    whole = [c for c in chunks if c[1] == 2 * HALF_ROWS]
    scale = CLIP_NORM / jnp.maximum(norm_ref[...], CLIP_NORM)

    def body(g_ref, f_ref, s_ref, t_ref, m_ref, nf_ref, ns_ref, nm_ref, up_ref):
        half = t_ref.shape[1]
        size = g_ref.shape[0]
        nf_ref[...], ns_ref[...] = moments(g_ref[...], f_ref[...], s_ref[...], scale)
        for h in (0, 1):
            span = slice(h * half, min((h + 1) * half, size))
            pseudo = t_ref[h, : span.stop - span.start].astype(F32) * (-1.0 / reps)
            new = OUTER_MOMENTUM * m_ref[span] + pseudo
            nm_ref[span] = new
            up_ref[span] = -OUTER_RATE * (pseudo + OUTER_MOMENTUM * new)

    def view(ref):
        return ref.reshape(rows, LANES)

    ins, outs = [view(g), view(f), view(s), total, view(mom)], [view(r) for r in (nf, ns, nm, up)]
    wide = pl.BlockSpec((2 * HALF_ROWS, LANES), lambda i: (i, 0))
    halves = pl.BlockSpec((2, HALF_ROWS, LANES), lambda i: (0, i, 0))
    if whole:
        pltpu.emit_pipeline(
            body, grid=(len(whole),), in_specs=[wide, wide, wide, halves, wide], out_specs=[wide] * 4
        )(*ins, *outs)
    for at, size, half_at, half in chunks[len(whole) :]:

        def part(n, ref):
            return ref.at[:, pl.ds(half_at, half)] if n == 3 else ref.at[pl.ds(at, size)]

        copies = [
            pltpu.make_async_copy(part(n, ref), buf, sems.at[n]) for n, (ref, buf) in enumerate(zip(ins, (tg, tf, ts, tt, tm)))
        ]
        for copy in copies:
            copy.start()
        for copy in copies:
            copy.wait()
        body(tg, tf, ts, tt, tm, tnf, tns, tnm, tup)
        copies = [
            pltpu.make_async_copy(buf, ref.at[pl.ds(at, size)], sems.at[n])
            for n, (buf, ref) in enumerate(zip((tnf, tns, tnm, tup), outs))
        ]
        for copy in copies:
            copy.start()
        for copy in copies:
            copy.wait()


def update(reps, norm, grad, first, second, total, mom):
    _, size, _, half = flat_chunks(grad.shape[-1] // LANES)[-1]
    anywhere = pl.BlockSpec(memory_space=pl.ANY)
    tail = pltpu.VMEM((size, LANES), F32)
    return pl.pallas_call(
        functools.partial(update_kernel, reps),
        in_specs=[pl.BlockSpec(memory_space=pltpu.VMEM)] + [anywhere] * 5,
        out_specs=[anywhere] * 4,
        out_shape=[jax.ShapeDtypeStruct(ref.shape, F32) for ref in (first, second, mom, mom)],
        scratch_shapes=[tail] * 4
        + [pltpu.VMEM((2, half, LANES), BF16)]
        + [tail] * 4
        + [pltpu.SemaphoreType.DMA((5,))],
        compiler_params=pltpu.CompilerParams(vmem_limit_bytes=48 * MIB),
        cost_estimate=pl.CostEstimate(flops=0, bytes_accessed=120 * MIB, transcendentals=0),
        name="update",
    )(norm, grad, first, second, total, mom)


def rms_scale(rows):
    return lax.rsqrt(jnp.mean(rows * rows, axis=-1, keepdims=True) + EPSILON)


def rms_backward(rows, scale, gain, grad_out):
    grad_gain = jnp.sum(grad_out * rows * scale, axis=0)
    inner = jnp.sum(grad_out * gain * rows, axis=-1, keepdims=True)
    grad_in = scale * gain * grad_out - rows * scale * scale * scale * inner / rows.shape[-1]
    return grad_in, grad_gain


def rotate(rows, cosine, sine):
    half = HEAD_SIZE // 2
    front, back = rows[:, :half], rows[:, half:]
    return jnp.concatenate([front * cosine - back * sine, back * cosine + front * sine], axis=1)


def per_device(
    tokens,
    cotangent,
    routes,
    branch,
    attn_gain,
    query_key_value_weight,
    w_attn_out,
    ffn_gain,
    w_router,
    w_in,
    w_out,
    adam_first,
    adam_second,
    outer_mom,
):
    shards = lax.axis_size("shard")
    reps = lax.axis_size("rep")
    count = tokens.shape[2]
    width = tokens.shape[3]
    prompt = count - CONTINUATION_LEN
    local = EXPERTS // reps
    groups = None
    if shards > GROUP_SIZE:
        groups = [list(range(i, i + GROUP_SIZE)) for i in range(0, shards, GROUP_SIZE)]
    shard_pos = lax.axis_index("shard") % GROUP_SIZE
    rep_pos = lax.axis_index("rep")
    branch_len = branch.reshape(())
    x_in = tokens.reshape(count, width).astype(F32)
    top_low = cotangent.reshape(count, width)
    grad_top = top_low.astype(F32)
    route_ids = routes.reshape(count, TOP)
    gather = functools.partial(lax.all_gather, axis_name="shard", axis=0, tiled=True)
    rows = width // shards
    qkv_columns = Q_WIDTH + 2 * KV_WIDTH
    fast = shards == 2 * LINE and reps == 4 and rows == LANES
    flat_path = fast and outer_mom.shape[-1] % LANES == 0

    small = jnp.concatenate(
        [query_key_value_weight, w_attn_out, w_router, attn_gain[:, None], ffn_gain[:, None]], axis=1
    )
    small = jnp.pad(small, ((0, 0), (0, -small.shape[1] % LANES)))
    tokens_low = tokens.reshape(count, width)
    if fast:
        prompt_low, small_full, all_top = start_gather(tokens_low, small, top_low)
        small_full = small_full.reshape(width, small.shape[1])
    else:
        prompt_low = lax.all_gather(tokens_low[:prompt], "shard", axis=0, tiled=False, axis_index_groups=groups)
        small_full = gather(small)
        by_rep = lax.all_gather(top_low, "rep", axis=0, tiled=False)
        core_pos = rep_pos + 1 - 2 * (rep_pos % 2)
        all_top = jnp.stack([top_low] + [by_rep[i] for i in (core_pos, (rep_pos + 2) % 4, 3 - rep_pos)])
    prompt_low = prompt_low.reshape(GROUP_SIZE * prompt, width)
    qkv_full = small_full[:, :qkv_columns]
    attn_out_full = small_full[:, qkv_columns : qkv_columns + Q_WIDTH]
    router_full = small_full[:, qkv_columns + Q_WIDTH : qkv_columns + Q_WIDTH + EXPERTS]
    gains = small_full[:, qkv_columns + Q_WIDTH + EXPERTS :].astype(F32)
    attn_gain_full, ffn_gain_full = gains[:, 0], gains[:, 1]
    w_both = jnp.concatenate(
        [
            lax.dynamic_slice_in_dim(w_in, rep_pos * local * 2 * F, local * 2 * F, 1),
            lax.dynamic_slice_in_dim(w_out, rep_pos * local * F, local * F, 1),
        ],
        axis=1,
    )
    w_both, prompt_low = lax.optimization_barrier((w_both, prompt_low))
    w_both = gather(w_both)

    def normed(values):
        scale = rms_scale(values)
        return (values * scale * attn_gain_full).astype(BF16), scale

    def angles_of(positions):
        half = HEAD_SIZE // 2
        inverse_freq = ROPE_BASE ** (-(jnp.arange(half, dtype=F32) * 2.0) / HEAD_SIZE)
        angles = inverse_freq[:, None] * positions.astype(F32)[None, :]
        return jnp.cos(angles)[None], jnp.sin(angles)[None]

    def project(source, start, size, turn):
        rows = dot(qkv_full[:, start : start + size], source, (0, 1))
        rows = rows.reshape(size // HEAD_SIZE, HEAD_SIZE, source.shape[0])
        return (rotate(rows, *turn) if turn is not None else rows).astype(BF16)

    def keys_values(source, turn):
        return project(source, Q_WIDTH, KV_WIDTH, turn), project(source, Q_WIDTH + KV_WIDTH, KV_WIDTH, None)

    normed_attn, attn_scale = normed(x_in)
    normed_prompt, _ = normed(prompt_low.astype(F32))
    prompt_turn = angles_of(jnp.arange(GROUP_SIZE * prompt, dtype=jnp.int32))
    own_turn = angles_of(
        jnp.concatenate(
            [
                shard_pos * prompt + jnp.arange(prompt, dtype=jnp.int32),
                branch_len + jnp.arange(CONTINUATION_LEN, dtype=jnp.int32),
            ]
        )
    )
    continued_turn = tuple(part[..., prompt:] for part in own_turn)
    prompt_kv = keys_values(normed_prompt, prompt_turn)
    own_kv = jnp.stack(keys_values(normed_attn[prompt:], continued_turn))
    query = project(normed_attn, 0, Q_WIDTH, own_turn)
    where = jnp.stack([shard_pos.astype(jnp.int32), branch_len])
    if flat_path:
        size = outer_mom.shape[-1]

        def lead(first, second, rest):
            parts = [first[None].astype(F32), second[None].astype(F32), rest.reshape(-1, LANES).astype(F32)]
            return jnp.concatenate(parts, axis=0)

        def whole(values):
            return values, values.shape[-1], 0

        weight_flat, _ = flatten(
            size,
            lead(attn_gain, ffn_gain, w_router),
            [whole(query_key_value_weight), whole(w_attn_out), whole(w_in), whole(w_out)],
        )
        weight_flat, query = lax.optimization_barrier((weight_flat, query))
    attn, lse = attn_forward(where, query, prompt_kv, own_kv)
    attn_low = attn.reshape(Q_WIDTH, count)
    x_mid = x_in + dot(attn_low, attn_out_full, (0, 1))

    ffn_scale = rms_scale(x_mid)
    normed_ffn = (x_mid * ffn_scale * ffn_gain_full).astype(BF16)
    logits = dot(normed_ffn, router_full, (1, 0))
    chosen = jnp.any(route_ids[:, :, None] == jnp.arange(EXPERTS, dtype=jnp.int32), axis=1)
    gates = jax.nn.softmax(jnp.where(chosen, logits, NEGATIVE), axis=-1)
    gates = jnp.where(chosen, gates, 0.0)

    gates_out = jnp.pad(gates.T.reshape(reps, local, count), ((0, 0), (0, 8 - local), (0, 0)))
    _, dx_own, dx_core, dx_far, y_keep, y_give, normed_t, top_t, dgu, gated, dgate_part = experts(
        normed_ffn, all_top, gates_out, w_both
    )
    grad_from_experts = dx_own.astype(F32) + dx_core.astype(F32) + dx_far.astype(F32)
    grad_gates = dgate_part[:, :local].reshape(EXPERTS, count).T
    to_core = [(i, i + 1 - 2 * (i % 2)) for i in range(reps)]
    to_far = [(i, (i + 2) % reps) for i in range(reps)]
    y_core = lax.ppermute(y_give, "rep", to_core)

    def rep_sum(values):
        for pairs in (to_core, to_far):
            values = (values.astype(F32) + lax.ppermute(values, "rep", pairs).astype(F32)).astype(BF16)
        return values

    def expert_term(left, right):
        return dot(left, right.reshape(reps * count, -1), (1, 0)).astype(BF16)

    grad_logits = (gates * (grad_gates - jnp.sum(gates * grad_gates, axis=-1, keepdims=True))).astype(BF16)
    grad_router_w = dot(normed_ffn, grad_logits, (0, 0))
    grad_normed_ffn = grad_from_experts + dot(grad_logits, router_full, (1, 1))
    grad_mid_norm, grad_ffn_gain = rms_backward(x_mid, ffn_scale, ffn_gain_full, grad_normed_ffn)
    grad_mid = grad_top + grad_mid_norm
    grad_branch = grad_mid.astype(BF16)
    grad_attn_w = dot(grad_branch, attn_low, (0, 1))
    grad_attn = dot(attn_out_full, grad_branch, (0, 1)).astype(BF16).reshape(QUERY_HEADS, HEAD_SIZE, count)
    expert_columns = local * 3 * F
    if fast:
        expert_rows = expert_grads(
            normed_t,
            top_t,
            dgu.reshape(reps * count, -1),
            gated.reshape(reps * count, -1),
        )
    else:
        terms = jnp.concatenate([expert_term(normed_t, dgu), expert_term(top_t, gated)], axis=1)
        terms = lax.psum_scatter(terms, "shard", scatter_dimension=0, tiled=True)
        expert_rows = lax.all_gather(terms, "rep", axis=0, tiled=False)
    y_core, expert_rows = lax.optimization_barrier((y_core, expert_rows))
    y_near = y_keep.astype(F32) + y_core.astype(F32)
    y_far = lax.ppermute(y_near[1].astype(BF16), "rep", to_far)

    blank = jnp.zeros((width, -(Q_WIDTH + EXPERTS + 1) % LANES), BF16)
    early = jnp.concatenate(
        [grad_attn_w.astype(BF16), grad_router_w.astype(BF16), grad_ffn_gain[:, None].astype(BF16), blank], axis=1
    )
    grad_attn, early, expert_rows = lax.optimization_barrier((grad_attn, early, expert_rows))
    early = lax.psum_scatter(early, "shard", scatter_dimension=0, tiled=True)

    grad_query, grad_prompt_kv, grad_own_kv = attn_backward(
        where, query, prompt_kv, own_kv, grad_attn, attn, lse, jnp.concatenate(prompt_turn), jnp.concatenate(own_turn)
    )

    early, y_far, grad_query, grad_prompt_kv, grad_own_kv = lax.optimization_barrier(
        (early, y_far, grad_query, grad_prompt_kv, grad_own_kv)
    )
    block_out = (x_mid + y_near[0] + y_far.astype(F32)).astype(BF16)
    grad_query = grad_query.reshape(Q_WIDTH, count)
    grad_prompt_kv = grad_prompt_kv.reshape(2 * KV_WIDTH, GROUP_SIZE * prompt)
    grad_own_kv = grad_own_kv.reshape(2 * KV_WIDTH, CONTINUATION_LEN)
    late_kv = dot(normed_prompt, grad_prompt_kv, (0, 1)) + dot(normed_attn[prompt:], grad_own_kv, (0, 1))
    late = jnp.concatenate([dot(normed_attn, grad_query, (0, 1)).astype(BF16), late_kv.astype(BF16)], axis=1)
    if fast:
        qkv_rows, early = late_reduce(late, early)
    else:
        qkv_rows = rep_sum(lax.psum_scatter(late, "shard", scatter_dimension=0, tiled=True))
        early = rep_sum(early)
    attn_rows, router_rows = early[:, :Q_WIDTH], early[:, Q_WIDTH : Q_WIDTH + EXPERTS]
    ffn_gain_rows = early[:, Q_WIDTH + EXPERTS]
    attn_gain_rows = jnp.sum(
        qkv_rows.astype(F32) * query_key_value_weight.astype(F32), axis=1
    ) / attn_gain.astype(F32)

    in_columns = local * 2 * F
    if flat_path:
        total_grad, square = flatten(
            size,
            lead(attn_gain_rows, ffn_gain_rows, router_rows),
            [
                whole(qkv_rows),
                whole(attn_rows),
                (expert_rows, in_columns, 0),
                (expert_rows, expert_columns - in_columns, in_columns // (expert_columns - in_columns)),
            ],
        )
    else:
        weight_flat = jnp.concatenate(
            [
                portion.astype(F32).reshape(-1)
                for portion in (attn_gain, query_key_value_weight, w_attn_out, ffn_gain, w_router, w_in, w_out)
            ]
        )
        total_grad = jnp.concatenate(
            [
                portion.astype(F32).reshape(-1)
                for portion in (
                    attn_gain_rows,
                    qkv_rows,
                    attn_rows,
                    ffn_gain_rows,
                    router_rows,
                    expert_rows[:, :, :in_columns].transpose(1, 0, 2),
                    expert_rows[:, :, in_columns:].transpose(1, 0, 2),
                )
            ]
        )

    def scatter(shared):
        return lax.psum_scatter(shared, "shard", scatter_dimension=1, tiled=True, axis_index_groups=groups)

    reduced_kv = scatter(grad_prompt_kv)
    if flat_path:
        grad_norm, step_sum = summed_step(square, total_grad, adam_first, adam_second, weight_flat)
        step_sum, reduced_kv = lax.optimization_barrier((step_sum, reduced_kv))
    grad_projected = jnp.concatenate([grad_query, jnp.concatenate([reduced_kv, grad_own_kv], axis=1)], axis=0)
    grad_normed_attn = dot(grad_projected, qkv_full, (0, 1))
    grad_x_norm, _ = rms_backward(x_in, attn_scale, attn_gain_full, grad_normed_attn)
    grad_input = grad_mid + grad_x_norm

    if flat_path:
        new_first, new_second, new_mom, weight_update = update(
            reps, grad_norm, total_grad, adam_first, adam_second, step_sum, outer_mom
        )
        grad_norm = grad_norm.reshape(())
    else:
        grad_norm = jnp.sqrt(lax.psum(jnp.sum(total_grad * total_grad), "shard"))
        new_first, new_second = moments(
            total_grad,
            adam_first.reshape(-1),
            adam_second.reshape(-1),
            CLIP_NORM / jnp.maximum(grad_norm, CLIP_NORM),
        )
        step = inner_step(new_first, new_second, weight_flat)
        pseudo = -(lax.psum(step.astype(BF16), "rep").astype(F32) / reps)
        new_mom = OUTER_MOMENTUM * outer_mom.reshape(-1) + pseudo
        weight_update = -OUTER_RATE * (pseudo + OUTER_MOMENTUM * new_mom)
    return (
        block_out.reshape(tokens.shape),
        grad_input.reshape(tokens.shape),
        total_grad.reshape(outer_mom.shape),
        grad_norm,
        new_first.reshape(adam_first.shape),
        new_second.reshape(adam_second.shape),
        new_mom.reshape(outer_mom.shape),
        weight_update.reshape(outer_mom.shape),
    )


def solution(mesh):
    by_token = P("rep", "shard", None, None)
    by_state = P("rep", "shard", None)
    by_row = P("shard", None)
    placed = (
        by_token,
        by_token,
        by_token,
        P("rep", "shard"),
        P("shard"),
        by_row,
        by_row,
        P("shard"),
        by_row,
        by_row,
        by_row,
        by_state,
        by_state,
        by_row,
    )
    return jax.shard_map(
        per_device,
        mesh=mesh,
        in_specs=placed,
        out_specs=(by_token, by_token, by_row, P(), by_state, by_state, by_row, by_row),
        check_vma=False,
    )
```
